32 devices in a mesh: group: 2 (over y), afd: 16 (over z, x, core).
Axes of the slice: x: 2, y: 2, z: 4, core: 2. Of those that a mesh axis runs over, the one named last changes fastest.
Arguments:
- queries: bfloat16 [2, 128, 7168], P(None, ('group', 'afd')), parts along dimension 1, may hold values from -27 to 27
- fresh: bfloat16 [2, 128, 448], P(None, ('group', 'afd')), parts along dimension 1, may hold values from -12 to 12
- kv_cache: bfloat16 [128, 128, 448], P(('group', 'afd')), parts along dimension 0, may hold values from -12 to 12
- cache_len: int32 [128], P(('group', 'afd')), parts along dimension 0, may hold values from 1 to 128, 4096 in all
- hidden_state: bfloat16 [2, 128, 7168], P(None, ('group', 'afd')), parts along dimension 1, may hold values from -40 to 40
- norm_gain: bfloat16 [7168], replicated, may hold values from 0.099609375 to 1.8984375
- expert_ids: int32 [2, 128, 3], P(None, ('group', 'afd')), parts along dimension 1, may hold values from 0 to 7, as said below
- route_weight: float32 [2, 128, 3], P(None, ('group', 'afd')), parts along dimension 1, may hold values from 0.3 to 1.5
- gate_up: bfloat16 [16, 2, 256, 7168], P('afd'), may hold values from -0.0625 to 0.0625
- down: bfloat16 [16, 256, 7168], P('afd'), may hold values from -0.25 to 0.25
Outputs:
- layer_out: bfloat16 [2, 128, 7168], P(None, ('group', 'afd')), parts along dimension 1
The draws below stay inside these ranges and needn't reach their ends.
There are 2 independent parts, one for each index of `group`. The reference program is written for one: setup_inputs(seed, part) draws one part's arguments, and reference() takes and returns one part's arrays. A program takes and returns all parts, laid end to end along the dimension named above; an argument that names none is the same for every part. Nothing has to cross between parts.
Inputs may be any that keep to these rules, and one draw needn't show every extreme that they name: `expert_ids`: A row names 3 different experts. In each step the 4 rows of one device name every expert at most 2 times and at least 2 - 1 times, and the experts named 2 times are the same on all devices of that step.
All inputs are finite; a program needn't handle non-finite values. No bound on the sum of `cache_len` on one device may be relied on, other than what follows from the above.
Results may differ from the reference program's by a relative error of at most 0.0052.
Values may be sent and summed in bfloat16 or wider, within the bound.
No kernel may reach another device: no remote copies, remote signals or barrier semaphores. Data moves between devices by JAX's collectives and lax.ppermute only.
A program may use at most 128 MiB of HBM per device.

```python
import math
import jax
import jax.numpy as jnp
import numpy as np
from jax import lax

D = 7168
HEADS = 32
HEAD = 224
H_DEV = 256
EXPERTS = 8
TOP = 3
STEPS = 2
ROWS_DEV = 4
L_MAX = 128
TPN = 2
OWNERS = 16
TOKENS = 64
CAP = 2


def draw_kv_cache(key, part):
    key = jax.random.fold_in(key, 1)
    shape = (TOKENS, L_MAX, 2 * HEAD)
    values = jnp.clip(jax.random.normal(key, shape, jnp.float32), -4.0, 4.0)
    return values.astype(jnp.bfloat16)


def draw_fresh(key, part):
    key = jax.random.fold_in(key, 2)
    shape = (STEPS, TOKENS, 2 * HEAD)
    values = jnp.clip(jax.random.normal(key, shape, jnp.float32), -4.0, 4.0)
    return values.astype(jnp.bfloat16)


def draw_queries(key, part):
    key = jax.random.fold_in(key, 3)
    shape = (STEPS, TOKENS, D)
    values = jnp.clip(jax.random.normal(key, shape, jnp.float32), -4.0, 4.0)
    return values.astype(jnp.bfloat16)


def draw_hidden_state(key, part):
    key = jax.random.fold_in(key, 5)
    shape = (STEPS, TOKENS, D)
    row_scale = jnp.exp(jax.random.uniform(jax.random.fold_in(key, 1), (STEPS, TOKENS, 1), jnp.float32, -1.15, 1.15))
    col_scale = jnp.exp(jax.random.uniform(jax.random.fold_in(key, 2), (D,), jnp.float32, -1.15, 1.15))
    base = jnp.clip(jax.random.normal(key, shape, jnp.float32), -4.0, 4.0)
    return (base * row_scale * col_scale).astype(jnp.bfloat16)


def draw_expert_ids(key, part):
    key = jax.random.fold_in(key, 7)
    blocks = TOKENS // ROWS_DEV
    pattern = (jnp.arange(ROWS_DEV * TOP, dtype=jnp.int32) % EXPERTS).reshape(ROWS_DEV, TOP)
    result = []
    for step in range(STEPS):
        order = jax.random.permutation(jax.random.fold_in(key, step), EXPERTS).astype(jnp.int32)
        named = order[pattern]
        step_key = jax.random.fold_in(key, 1000 + step)

        def one_block(block):
            shuffle = jax.random.permutation(jax.random.fold_in(step_key, block), ROWS_DEV)
            return named[shuffle]
        result.append(jax.vmap(one_block)(jnp.arange(blocks)).reshape(TOKENS, TOP))
    return jnp.stack(result).astype(jnp.int32)


def block_scale(rng, extent, shards, least, largest):
    def one(position, blocks):
        heights = jax.random.uniform(jax.random.fold_in(jax.random.fold_in(rng, 6), position), (blocks,), jnp.float32, least / len(shards), largest / len(shards))
        return jnp.repeat(jnp.exp(heights), extent[position] // blocks).reshape((-1,) + (1,) * (len(extent) - position - 1))

    level = one(*shards[0])
    for cut in shards[1:]:
        level = level * one(*cut)
    return level


def profile(amount, total, most, slope):
    portions = [(1 << 20) // math.isqrt(grade ** slope) + 1 for grade in range(2, amount + 1)]
    spare, given = total - most - (amount - 1), [1] * (amount - 1)
    while spare > 0:
        free = [i for i in range(amount - 1) if given[i] < most]
        mass, left = sum([portions[i] for i in free]), spare
        for i in free:
            more = min(most - given[i], max(1, left * portions[i] // mass), spare)
            given[i] = given[i] + more
            spare = spare - more
    return np.array([most] + given)


def ragged(rng, amount, total, limit, slope):
    if amount == 2:
        one = jax.random.randint(rng, (), max(1, total - limit), min(limit, total - 1) + 1)
        return jnp.stack([one, total - one])
    sizes = jnp.asarray(profile(amount, total, limit, slope), jnp.int32)
    couples = (amount - 1) // 2
    giver, taker = sizes[1:1 + 2 * couples:2], sizes[2:2 + 2 * couples:2]
    margin = jnp.minimum(giver - 1, limit - taker)
    shifted = jax.random.randint(jax.random.fold_in(rng, 1), (couples,), 0, 1 << 20) % (margin + 1)
    sizes = sizes.at[1:1 + 2 * couples:2].set(giver - shifted).at[2:2 + 2 * couples:2].set(taker + shifted)
    return sizes[jax.random.permutation(jax.random.fold_in(rng, 2), amount)]


def bell_draw(own_key, dims, width, bound, pieces=(), held_as=jnp.bfloat16):
    entries = jax.random.normal(own_key, dims, jnp.float32) * width
    if len(pieces) > 0:
        entries = block_scale(own_key, dims, pieces, -0.22, 0.18) * entries
    return jnp.clip(entries, min=-bound, max=bound).astype(held_as)


def setup_inputs(seed: int = 0, part: int = 0) -> dict:
    streams_of = jax.random.split(jax.random.key(seed), 11)
    part_splits = jax.random.split(jax.random.fold_in(streams_of[10], part), 11)
    queries = draw_queries(jax.random.fold_in(jax.random.fold_in(streams_of[10], part), 71), part)
    fresh = draw_fresh(jax.random.fold_in(jax.random.fold_in(streams_of[10], part), 71), part)
    kv_cache = draw_kv_cache(jax.random.fold_in(jax.random.fold_in(streams_of[10], part), 71), part)
    cache_len = ragged(part_splits[3], TOKENS, TOKENS * L_MAX // 2, L_MAX, 2).astype(jnp.int32)
    hidden_state = draw_hidden_state(jax.random.fold_in(jax.random.fold_in(streams_of[10], part), 71), part)
    norm_gain = jnp.clip(1.0 + 0.18 * jax.random.normal(streams_of[5], (D,), jnp.float32), 0.099609375, 1.8984375).astype(jnp.bfloat16)
    expert_ids = draw_expert_ids(jax.random.fold_in(jax.random.fold_in(streams_of[10], part), 71), part)
    route_weight = jnp.clip(0.3 + 1.2 * jax.random.uniform(part_splits[7], (STEPS, TOKENS, TOP), jnp.float32) ** block_scale(part_splits[7], (STEPS, TOKENS, TOP), ((1, 16),), -0.2, 0.2), 0.3, 1.5)
    gate_up = bell_draw(streams_of[8], (OWNERS, 2, H_DEV, D), D ** -0.5, 0.0625, ((0, 16),))
    down = bell_draw(streams_of[9], (OWNERS, H_DEV, D), (H_DEV * TPN) ** -0.5, 0.25, ((0, 16),))
    return dict(queries=queries, fresh=fresh, kv_cache=kv_cache, cache_len=cache_len, hidden_state=hidden_state, norm_gain=norm_gain, expert_ids=expert_ids, route_weight=route_weight, gate_up=gate_up, down=down)


def attend_rows(block):
    query, cache, fresh_part, length = block
    keys = jnp.concatenate([cache[:, :, :HEAD], jnp.swapaxes(fresh_part[:, :, :HEAD], 0, 1)], axis=1).astype(jnp.float32)
    values = jnp.concatenate([cache[:, :, HEAD:], jnp.swapaxes(fresh_part[:, :, HEAD:], 0, 1)], axis=1).astype(jnp.float32)
    scores = jnp.einsum('rhd,rld->rhl', query.astype(jnp.float32), keys) * HEAD ** (-0.5)
    places = jnp.arange(keys.shape[1], dtype=jnp.int32)
    valid = (places[None, :] < length[:, None]) | (places[None, :] >= cache.shape[1])
    scores = jnp.where(valid[:, None, :], scores, -1e+30)
    top = lax.optimization_barrier(jnp.max(scores, axis=-1, keepdims=True))
    expo = jnp.exp(scores - top)
    weights = (expo / lax.optimization_barrier(jnp.sum(expo, axis=-1, keepdims=True))).astype(jnp.bfloat16)
    return jnp.einsum('rhl,rld->rhd', weights.astype(jnp.float32), values)

def reference(queries, fresh, kv_cache, cache_len, hidden_state, norm_gain, expert_ids, route_weight, gate_up, down):
    blocks = TOKENS // ROWS_DEV
    most_rows = blocks * CAP
    outputs = []
    for step in range(STEPS):
        query = queries[step].reshape(blocks, ROWS_DEV, HEADS, HEAD)
        cache = kv_cache.reshape(blocks, ROWS_DEV, L_MAX, 2 * HEAD)
        fresh_part = jnp.swapaxes(fresh[:step + 1].reshape(step + 1, blocks, ROWS_DEV, 2 * HEAD), 0, 1)
        length = cache_len.reshape(blocks, ROWS_DEV)
        attended = lax.map(attend_rows, (query, cache, fresh_part, length)).reshape(TOKENS, D)
        resid = hidden_state[step].astype(jnp.float32) + attended
        meansq = lax.optimization_barrier(jnp.mean(resid * resid, axis=-1, keepdims=True))
        normed = (resid * lax.rsqrt(meansq + 1e-06) * norm_gain.astype(jnp.float32)).astype(jnp.bfloat16)
        ids_now = expert_ids[step]
        weight_now = route_weight[step]

        def one_expert(expert, combined):
            named = ids_now == expert
            weight = lax.optimization_barrier(jnp.sum(jnp.where(named, weight_now, 0.0), axis=1))
            hit = jnp.any(named, axis=1)
            order = jnp.argsort(jnp.where(hit, 0, 1).astype(jnp.int32), stable=True)[:most_rows].astype(jnp.int32)
            rows = normed[order]

            def one_shard(shard, total):
                index = expert * TPN + shard
                pair = lax.dynamic_index_in_dim(gate_up, index, 0, keepdims=False)
                w_down = lax.dynamic_index_in_dim(down, index, 0, keepdims=False)
                gate = jnp.dot(rows, pair[0].T, preferred_element_type=jnp.float32)
                upper = jnp.dot(rows, pair[1].T, preferred_element_type=jnp.float32)
                act = (jax.nn.silu(gate) * upper).astype(jnp.bfloat16)
                part = jnp.dot(act, w_down, preferred_element_type=jnp.float32).astype(jnp.bfloat16)
                return total + part.astype(jnp.float32)
            summed = lax.fori_loop(0, TPN, one_shard, jnp.zeros((most_rows, D), jnp.float32))
            return combined.at[order].add(weight[order][:, None] * summed)
        combined = lax.fori_loop(0, EXPERTS, one_expert, jnp.zeros((TOKENS, D), jnp.float32))
        outputs.append((resid + combined).astype(jnp.bfloat16))
    return jnp.stack(outputs)
```

```python
import functools
import jax
import jax.numpy as jnp
from jax import lax
from jax.experimental import pallas as pl
from jax.experimental.pallas import tpu as pltpu
from jax.sharding import PartitionSpec as P

HEADS = 32
HEAD = 224
EXPERTS = 8
TOP = 3
CAP = 2
PIECES = 4
F32 = jnp.float32
BF16 = jnp.bfloat16
MIB = 1 << 20


def iota(shape, dim):
    return lax.broadcasted_iota(jnp.int32, shape, dim)


def nt_dot(a, b):
    return lax.dot_general(a, b, (((1,), (1,)), ((), ())), preferred_element_type=F32)


def dot(a, b):
    return jnp.dot(a, b, preferred_element_type=F32)


def spread(ids_ref, where, steps, rows, k):
    out = jnp.full(where.shape, -1, jnp.int32)
    for s in range(steps):
        for r in range(rows):
            out = jnp.where(where == s * rows + r, ids_ref[s, r, k], out)
    return out


def attend_kernel(
    len_ref, ids_ref, q_ref, fresh_ref, kv_ref, hid_ref, gain_ref, resid_ref, out_ref, merged
):
    steps, rows, width = q_ref.shape
    length = kv_ref.shape[1]
    both = steps * rows
    piece = width // PIECES
    scale = HEAD ** (-0.5)
    q = jnp.concatenate([q_ref[s].astype(F32) for s in range(steps)], axis=0)
    heads = jnp.concatenate([q[:, h * HEAD : (h + 1) * HEAD] for h in range(HEADS)], axis=0)
    heads = heads.astype(BF16)
    kv = jnp.concatenate([kv_ref[r] for r in range(rows)], axis=0)
    new = jnp.concatenate([fresh_ref[s].astype(F32) for s in range(steps)], axis=0).astype(BF16)

    sub = iota((both, rows * length), 0)
    lane = iota((both, rows * length), 1)
    limit = jnp.zeros_like(lane)
    for r in range(rows):
        limit = jnp.where(lane // length == r, len_ref[r], limit)
    valid = (lane // length == sub % rows) & (lane % length < limit)
    sub = iota((both, both), 0)
    lane = iota((both, both), 1)
    valid_new = (lane % rows == sub % rows) & (lane // rows <= sub // rows)

    old_s = (nt_dot(heads, kv[:, :HEAD]) * scale).reshape(HEADS, both, rows * length)
    new_s = (nt_dot(heads, new[:, :HEAD]) * scale).reshape(HEADS, both, both)
    old_s = jnp.where(valid[None], old_s, -1e30)
    new_s = jnp.where(valid_new[None], new_s, -1e30)
    top = jnp.maximum(
        jnp.max(old_s, axis=-1, keepdims=True), jnp.max(new_s, axis=-1, keepdims=True)
    )
    old_e = jnp.exp(old_s - top)
    new_e = jnp.exp(new_s - top)
    total = jnp.sum(old_e, axis=-1, keepdims=True) + jnp.sum(new_e, axis=-1, keepdims=True)
    old_w = (old_e / total).reshape(HEADS * both, rows * length).astype(BF16)
    new_w = (new_e / total).reshape(HEADS * both, both).astype(BF16)
    attended = dot(old_w, kv[:, HEAD:]) + dot(new_w, new[:, HEAD:])
    for h in range(HEADS):
        merged[:, h * HEAD : (h + 1) * HEAD] = attended[h * both : (h + 1) * both]
    hidden = jnp.concatenate([hid_ref[s].astype(F32) for s in range(steps)], axis=0)
    resid = hidden + merged[...]
    resid_ref[...] = resid
    meansq = jnp.mean(resid * resid, axis=-1, keepdims=True)
    normed = resid * lax.rsqrt(meansq + 1e-06) * gain_ref[...].astype(F32)
    stacked = jnp.concatenate(
        [normed[:, k * piece : (k + 1) * piece] for k in range(PIECES)], axis=0
    ).astype(BF16)

    lines = PIECES * steps * CAP
    shape = (EXPERTS * lines, PIECES * both)
    line = iota(shape, 0)
    col = iota(shape, 1)
    where = iota((1, PIECES * both), 1) % both
    named = jnp.zeros(shape, jnp.bool_)
    for k in range(TOP):
        named = named | (spread(ids_ref, where, steps, rows, k) == line // lines)
    at = iota((PIECES * both, PIECES * both), 0)
    to = iota((PIECES * both, PIECES * both), 1)
    before = jnp.where((at // rows == to // rows) & (at < to), 1.0, 0.0).astype(BF16)
    rank = dot(jnp.where(named, 1.0, 0.0).astype(BF16), before)
    slot = (line % CAP).astype(F32)
    same = (line // CAP) % (PIECES * steps) == col // rows
    picks = jnp.where(named & same & (rank == slot), 1.0, 0.0).astype(BF16)
    out_ref[...] = dot(picks, stacked).astype(BF16).reshape(out_ref.shape)


def attend(cache_len, expert_ids, queries, fresh, kv_cache, hidden_state, norm_gain):
    steps, rows, width = queries.shape
    lines = PIECES * steps * CAP
    smem = pl.BlockSpec(memory_space=pltpu.SMEM)
    vmem = pl.BlockSpec(memory_space=pltpu.VMEM)
    return pl.pallas_call(
        attend_kernel,
        out_shape=(
            jax.ShapeDtypeStruct((steps * rows, width), F32),
            jax.ShapeDtypeStruct((EXPERTS, lines, width // PIECES), BF16),
        ),
        in_specs=[smem, smem, vmem, vmem, vmem, vmem, vmem],
        out_specs=(vmem, vmem),
        scratch_shapes=[pltpu.VMEM((steps * rows, width), F32)],
        compiler_params=pltpu.CompilerParams(vmem_limit_bytes=32 * MIB),
        cost_estimate=pl.CostEstimate(
            flops=300_000_000, bytes_accessed=2_000_000, transcendentals=131072
        ),
        name="attend",
    )(cache_len, expert_ids, queries, fresh, kv_cache, hidden_state, norm_gain.reshape(1, width))


def regroup(chips, lines, per):
    n = chips * lines
    row = iota((n, n), 0)
    col = iota((n, n), 1)
    k, p, x = row // (chips * per), (row // per) % chips, row % per
    return jnp.where(col == p * lines + k * per + x, 1.0, 0.0).astype(BF16)


def expert_kernel(
    own_ref, other_ref, gate_up_ref, down_ref, mine_ref, theirs_ref, gu, dn, gu_sem, dn_sem
):
    chips, lines, piece = own_ref.shape
    per = lines // PIECES
    hidden = down_ref.shape[1]
    half = chips * per
    cols = [pl.ds(k * piece, piece) for k in range(PIECES)]
    gu_copies = [
        pltpu.make_async_copy(gate_up_ref.at[0, :, :, cols[k]], gu.at[k], gu_sem.at[k])
        for k in range(PIECES)
    ]
    dn_copies = [
        pltpu.make_async_copy(down_ref.at[0, :, cols[k]], dn.at[k], dn_sem.at[k])
        for k in range(PIECES)
    ]
    for copy in gu_copies + dn_copies:
        copy.start()
    order = regroup(chips, lines, per)
    own = dot(order, own_ref[...].reshape(chips * lines, piece)).astype(BF16)
    other = dot(order, other_ref[...].reshape(chips * lines, piece)).astype(BF16)
    gate = jnp.zeros((2 * half, hidden), F32)
    upper = jnp.zeros((2 * half, hidden), F32)
    for k in range(PIECES):
        rows = jnp.concatenate(
            [own[k * half : (k + 1) * half], other[k * half : (k + 1) * half]], axis=0
        )
        gu_copies[k].wait()
        gate = gate + nt_dot(rows, gu[k, 0])
        upper = upper + nt_dot(rows, gu[k, 1])
    act = (gate / (1.0 + jnp.exp(-gate)) * upper).astype(BF16)
    mine = []
    theirs = []
    for k in range(PIECES):
        dn_copies[k].wait()
        part = dot(act, dn[k]).astype(BF16)
        mine.append(part[:half])
        theirs.append(part[half:])
    n = chips * lines
    row = iota((n, n), 0)
    col = iota((n, n), 1)
    k, p, x = col // half, (col // per) % chips, col % per
    back = jnp.where(row == p * lines + k * per + x, 1.0, 0.0).astype(BF16)
    mine = dot(back, jnp.concatenate(mine, axis=0)).astype(BF16)
    theirs = dot(back, jnp.concatenate(theirs, axis=0)).astype(BF16)
    mine_ref[...] = mine.reshape(chips, lines, piece)
    theirs_ref[...] = theirs.reshape(chips, lines, piece)


def experts(own, other, gate_up, down):
    chips, lines, piece = own.shape
    hidden = down.shape[1]
    vmem = pl.BlockSpec(memory_space=pltpu.VMEM)
    hbm = pl.BlockSpec(memory_space=pl.ANY)
    return pl.pallas_call(
        expert_kernel,
        out_shape=(jax.ShapeDtypeStruct(own.shape, BF16),) * 2,
        in_specs=[vmem, vmem, hbm, hbm],
        out_specs=(vmem, vmem),
        scratch_shapes=[
            pltpu.VMEM((PIECES, 2, hidden, piece), BF16),
            pltpu.VMEM((PIECES, hidden, piece), BF16),
            pltpu.SemaphoreType.DMA((PIECES,)),
            pltpu.SemaphoreType.DMA((PIECES,)),
        ],
        compiler_params=pltpu.CompilerParams(vmem_limit_bytes=48 * MIB),
        cost_estimate=pl.CostEstimate(
            flops=800_000_000, bytes_accessed=12_000_000, transcendentals=16384
        ),
        name="experts",
    )(own, other, gate_up, down)


def combine_kernel(ids_ref, weight_ref, resid_ref, back_ref, out_ref):
    steps, rows, width = out_ref.shape
    chips, lines, piece = back_ref.shape
    both = steps * rows
    chips_per_expert = chips // EXPERTS
    shape = (both, chips * lines)
    line = iota(shape, 1)
    sub = iota(shape, 0)
    expert = line // (lines * chips_per_expert)
    where = iota((both, 1), 0)
    named = jnp.zeros(shape, F32)
    mix = jnp.zeros(shape, F32)
    for k in range(TOP):
        hit = spread(ids_ref, where, steps, rows, k) == expert
        weight = jnp.zeros((both, 1), F32)
        for s in range(steps):
            for r in range(rows):
                weight = jnp.where(where == s * rows + r, weight_ref[s, r, k], weight)
        named = named + jnp.where(hit, 1.0, 0.0)
        mix = mix + jnp.where(hit, weight, 0.0)
    at = iota((both, both), 1)
    to = iota((both, both), 0)
    before = jnp.where((at // rows == to // rows) & (at < to), 1.0, 0.0).astype(BF16)
    rank = dot(before, named.astype(BF16))
    same = (line // CAP) % steps == sub // rows
    mix = jnp.where((rank == (line % CAP).astype(F32)) & same, mix, 0.0)
    high = mix.astype(BF16)
    rest = mix - high.astype(F32)
    middle = rest.astype(BF16)
    low = (rest - middle.astype(F32)).astype(BF16)
    k_of = (line // (steps * CAP)) % PIECES
    parts = [
        jnp.where(k_of == k, part.astype(F32), 0.0)
        for part in (high, middle, low)
        for k in range(PIECES)
    ]
    left = jnp.concatenate(parts, axis=0).astype(BF16)
    product = dot(left, back_ref[...].reshape(chips * lines, piece))
    n = PIECES * both
    total = product[:n] + product[n : 2 * n] + product[2 * n :]
    for k in range(PIECES):
        cols = pl.ds(k * piece, piece)
        done = (resid_ref[:, cols] + total[k * both : (k + 1) * both]).astype(BF16)
        for s in range(steps):
            out_ref[s, :, cols] = done[s * rows : (s + 1) * rows]


def combine(expert_ids, route_weight, resid, back):
    steps, rows, _ = expert_ids.shape
    smem = pl.BlockSpec(memory_space=pltpu.SMEM)
    vmem = pl.BlockSpec(memory_space=pltpu.VMEM)
    return pl.pallas_call(
        combine_kernel,
        out_shape=jax.ShapeDtypeStruct((steps, rows, resid.shape[1]), BF16),
        in_specs=[smem, smem, vmem, vmem],
        out_specs=vmem,
        compiler_params=pltpu.CompilerParams(vmem_limit_bytes=32 * MIB),
        cost_estimate=pl.CostEstimate(
            flops=100_000_000, bytes_accessed=1_000_000, transcendentals=0
        ),
        name="combine",
    )(expert_ids, route_weight, resid, back)


def per_device(
    queries,
    fresh,
    kv_cache,
    cache_len,
    hidden_state,
    norm_gain,
    expert_ids,
    route_weight,
    gate_up,
    down,
):
    owners = lax.axis_size("afd")
    chips = owners // 2
    chips_per_expert = chips // EXPERTS
    same_core = [[2 * p + c for p in range(chips)] for c in range(2)]
    swap = [(i, i ^ 1) for i in range(owners)]
    resid, outgoing = attend(
        cache_len, expert_ids, queries, fresh, kv_cache, hidden_state, norm_gain
    )
    if chips_per_expert > 1:
        outgoing = jnp.repeat(outgoing, chips_per_expert, axis=0)
    own = lax.all_to_all(
        outgoing, "afd", split_axis=0, concat_axis=0, axis_index_groups=same_core, tiled=True
    )
    other = lax.ppermute(own, "afd", swap)
    mine, theirs = experts(own, other, gate_up, down)
    summed = (mine.astype(F32) + lax.ppermute(theirs, "afd", swap).astype(F32)).astype(BF16)
    back = lax.all_to_all(
        summed, "afd", split_axis=0, concat_axis=0, axis_index_groups=same_core, tiled=True
    )
    return combine(expert_ids, route_weight, resid, back)


def solution(mesh):
    placed = (
        P(None, ("group", "afd"), None),
        P(None, ("group", "afd"), None),
        P(("group", "afd"), None, None),
        P(("group", "afd")),
        P(None, ("group", "afd"), None),
        P(),
        P(None, ("group", "afd"), None),
        P(None, ("group", "afd"), None),
        P("afd", None, None, None),
        P("afd", None, None),
    )
    return jax.shard_map(
        per_device,
        mesh=mesh,
        in_specs=placed,
        out_specs=P(None, ("group", "afd"), None),
        check_vma=False,
    )
```

```python
import functools
import jax
import jax.numpy as jnp
from jax import lax
from jax.experimental import pallas as pl
from jax.experimental.pallas import tpu as pltpu
from jax.sharding import PartitionSpec as P

HEADS = 32
HEAD = 224
EXPERTS = 8
TOP = 3
CAP = 2
LINES = 16
LANES = 128
F32 = jnp.float32
BF16 = jnp.bfloat16
MIB = 1 << 20
VMEM = pl.BlockSpec(memory_space=pltpu.VMEM)
HBM = pl.BlockSpec(memory_space=pl.ANY)
BATCHES = ((0, 1),)


def iota(shape, dim):
    return lax.broadcasted_iota(jnp.int32, shape, dim)


def nt_dot(a, b):
    return lax.dot_general(a, b, (((1,), (1,)), ((), ())), preferred_element_type=F32)


def dot(a, b):
    return jnp.dot(a, b, preferred_element_type=F32)


def one_hot(mask):
    return jnp.where(mask, 1.0, 0.0).astype(BF16)


def spread(ref, k, where, steps, rows, empty):
    out = jnp.full(where.shape, empty)
    for s in range(steps):
        for r in range(rows):
            out = jnp.where(where == s * rows + r, ref[k, s, r], out)
    return out


def picks_of(ids_ref, batch, steps, rows, me):
    pieces = LINES // (len(batch) * CAP)
    both = steps * rows
    shape = (EXPERTS * LINES, pieces * both)
    line = iota(shape, 0)
    col = iota(shape, 1)
    where = iota((1, pieces * both), 1) % both
    expert = (line // LINES) ^ me
    named = jnp.zeros(shape, jnp.bool_)
    for k in range(TOP):
        named = named | (spread(ids_ref, k, where, steps, rows, -1) == expert)
    at = iota((pieces * both, pieces * both), 0)
    to = iota((pieces * both, pieces * both), 1)
    rank = dot(one_hot(named), one_hot((at // rows == to // rows) & (at < to)))
    slot = (line % CAP).astype(F32)
    step = (line // CAP) % len(batch) + batch[0]
    piece = line // (CAP * len(batch)) % pieces
    same = (step == col // rows % steps) & (piece == col // both)
    return one_hot(named & same & (rank == slot))


def attend_kernel(
    permuted, len_hbm, ids_hbm, q_hbm, fresh_hbm, kv_hbm, hid_hbm, gain_hbm, resid_ref, *rest
):
    outs = rest[: len(BATCHES) * EXPERTS]
    len_ref, ids_ref, q_ref, fresh_ref, kv_ref, hid_ref, gain_ref, merged, sems = rest[len(outs) :]
    copies = [
        pltpu.make_async_copy(source, target, sems.at[i])
        for i, (source, target) in enumerate(
            (
                (q_hbm, q_ref),
                (kv_hbm, kv_ref),
                (len_hbm, len_ref),
                (ids_hbm, ids_ref),
                (fresh_hbm, fresh_ref),
                (hid_hbm, hid_ref),
                (gain_hbm, gain_ref),
            )
        )
    ]
    for copy in copies:
        copy.start()
    steps, rows, width = q_ref.shape
    length = kv_ref.shape[2]
    both = steps * rows
    scale = HEAD ** (-0.5)
    me = lax.axis_index("afd") // 2 if permuted else 0
    for copy in copies:
        copy.wait()
    q = jnp.concatenate([q_ref[s].astype(F32) for s in range(steps)], axis=0)
    heads = jnp.concatenate([q[:, h * HEAD : (h + 1) * HEAD] for h in range(HEADS)], axis=0)
    heads = heads.astype(BF16)
    kv = jnp.concatenate([kv_ref[r] for r in range(rows)], axis=1)
    new = jnp.concatenate([fresh_ref[s].astype(F32) for s in range(steps)], axis=0).astype(BF16)

    sub = iota((both, rows * length), 0)
    lane = iota((both, rows * length), 1)
    limit = jnp.zeros_like(lane)
    for r in range(rows):
        limit = jnp.where(lane // length == r, len_ref[r], limit)
    valid = (lane // length == sub % rows) & (lane % length < limit)
    sub = iota((both, both), 0)
    lane = iota((both, both), 1)
    valid_new = (lane % rows == sub % rows) & (lane // rows <= sub // rows)

    old_s = (dot(heads, kv[:HEAD]) * scale).reshape(HEADS, both, rows * length)
    new_s = (nt_dot(heads, new[:, :HEAD]) * scale).reshape(HEADS, both, both)
    old_s = jnp.where(valid[None], old_s, -1e30)
    new_s = jnp.where(valid_new[None], new_s, -1e30)
    top = jnp.maximum(
        jnp.max(old_s, axis=-1, keepdims=True), jnp.max(new_s, axis=-1, keepdims=True)
    )
    old_e = jnp.exp(old_s - top)
    new_e = jnp.exp(new_s - top)
    total = jnp.sum(old_e, axis=-1, keepdims=True) + jnp.sum(new_e, axis=-1, keepdims=True)
    old_w = (old_e / total).reshape(HEADS * both, rows * length).astype(BF16)
    new_w = (new_e / total).reshape(HEADS * both, both).astype(BF16)
    attended = nt_dot(old_w, kv[HEAD:]) + dot(new_w, new[:, HEAD:])
    for h in range(HEADS):
        merged[:, h * HEAD : (h + 1) * HEAD] = attended[h * both : (h + 1) * both]
    hidden = jnp.concatenate([hid_ref[s].astype(F32) for s in range(steps)], axis=0)
    resid = hidden + merged[...]
    resid_ref[...] = resid
    meansq = jnp.mean(resid * resid, axis=-1, keepdims=True)
    gain = gain_ref[...].astype(F32)
    gain = jnp.concatenate([gain[i : i + 1] for i in range(width // LANES)], axis=1)
    normed = resid * lax.rsqrt(meansq + 1e-06) * gain
    for i, batch in enumerate(BATCHES):
        pieces = LINES // (len(batch) * CAP)
        piece = width // pieces
        stacked = jnp.concatenate(
            [normed[:, k * piece : (k + 1) * piece] for k in range(pieces)], axis=0
        ).astype(BF16)
        picks = picks_of(ids_ref, batch, steps, rows, me)
        sent = dot(picks, stacked).astype(BF16)
        for j in range(EXPERTS):
            outs[i * EXPERTS + j][0] = sent[j * LINES : (j + 1) * LINES]


def attend(permuted, cache_len, ids, queries, fresh, kv_cache, hidden_state, norm_gain):
    steps, rows, width = queries.shape
    chunks = []
    for batch in BATCHES:
        shape = (1, LINES, width * len(batch) * CAP // LINES)
        chunks += [jax.ShapeDtypeStruct(shape, BF16)] * EXPERTS
    kv = kv_cache.transpose(0, 2, 1)
    gain = norm_gain.reshape(width // LANES, LANES)
    results = pl.pallas_call(
        functools.partial(attend_kernel, permuted),
        out_shape=(jax.ShapeDtypeStruct((steps * rows, width), F32), *chunks),
        in_specs=[HBM] * 7,
        out_specs=(VMEM,) * (1 + len(chunks)),
        scratch_shapes=[
            pltpu.SMEM(cache_len.shape, jnp.int32),
            pltpu.SMEM(ids.shape, jnp.int32),
            pltpu.VMEM(queries.shape, BF16),
            pltpu.VMEM(fresh.shape, BF16),
            pltpu.VMEM(kv.shape, BF16),
            pltpu.VMEM(hidden_state.shape, BF16),
            pltpu.VMEM(gain.shape, BF16),
            pltpu.VMEM((steps * rows, width), F32),
            pltpu.SemaphoreType.DMA((7,)),
        ],
        compiler_params=pltpu.CompilerParams(vmem_limit_bytes=24 * MIB),
        cost_estimate=pl.CostEstimate(
            flops=300_000_000, bytes_accessed=2_000_000, transcendentals=131072
        ),
        name="attend",
    )(cache_len, ids, queries, fresh, kv, hidden_state, gain)
    resid, chunks = results[0], results[1:]
    return resid, [chunks[i * EXPERTS : (i + 1) * EXPERTS] for i in range(len(BATCHES))]


def mixing(ids_ref, weight_ref, batch, steps, rows, chips, me):
    pieces = LINES // (len(batch) * CAP)
    both = len(batch) * rows
    shape = (both, chips * LINES)
    line = iota(shape, 1)
    sub = iota(shape, 0)
    expert = (line // LINES ^ me) // (chips // EXPERTS)
    where = iota((both, 1), 0) + batch[0] * rows
    named = jnp.zeros(shape, F32)
    mix = jnp.zeros(shape, F32)
    for k in range(TOP):
        hit = spread(ids_ref, k, where, steps, rows, -1) == expert
        weight = spread(weight_ref, k, where, steps, rows, 0.0)
        named = named + jnp.where(hit, 1.0, 0.0)
        mix = mix + jnp.where(hit, weight, 0.0)
    at = iota((both, both), 1)
    to = iota((both, both), 0)
    rank = dot(one_hot((at // rows == to // rows) & (at < to)), named.astype(BF16))
    same = (line // CAP) % len(batch) == sub // rows
    mix = jnp.where((rank == (line % CAP).astype(F32)) & same, mix, 0.0)
    high = mix.astype(BF16).astype(F32)
    middle = (mix - high).astype(BF16).astype(F32)
    low = mix - high - middle
    k_of = line // (len(batch) * CAP) % pieces
    parts = [
        jnp.where(k_of == k, part, 0.0) for part in (high, middle, low) for k in range(pieces)
    ]
    return jnp.concatenate(parts, axis=0).astype(BF16)


def stage_kernel(
    permuted, chips, steps, rows, ids_hbm, weight_hbm, gu_hbm, dn_hbm, after, gu, dn, *rest
):
    mixes = rest[: len(BATCHES)]
    ids_ref, weight_ref, small, large = rest[len(BATCHES) :]
    first = [
        pltpu.make_async_copy(ids_hbm, ids_ref, small.at[0]),
        pltpu.make_async_copy(weight_hbm, weight_ref, small.at[1]),
    ]
    hidden = dn.shape[0]
    step = hidden // 4
    second = []
    for i in range(4):
        part = pl.ds(i * step, step)
        second.append((gu_hbm.at[0, 0, part], gu.at[0, part]))
        second.append((gu_hbm.at[0, 1, part], gu.at[1, part]))
        second.append((dn_hbm.at[0, part], dn.at[part]))
    second = [pltpu.make_async_copy(a, b, large.at[i]) for i, (a, b) in enumerate(second)]
    for copy in first + second:
        copy.start()
    for copy in first:
        copy.wait()
    me = lax.axis_index("afd") // 2 if permuted else 0
    for batch, mix in zip(BATCHES, mixes):
        mix[...] = mixing(ids_ref, weight_ref, batch, steps, rows, chips, me)
    for copy in second:
        copy.wait()


def stage(permuted, chips, ids, weights, gate_up, down, after):
    _, steps, rows = ids.shape
    mixes = [
        jax.ShapeDtypeStruct((3 * LINES // CAP * rows, chips * LINES), BF16) for _ in BATCHES
    ]
    gu, dn, *mixes = pl.pallas_call(
        functools.partial(stage_kernel, permuted, chips, steps, rows),
        out_shape=(
            jax.ShapeDtypeStruct(gate_up.shape[1:], BF16),
            jax.ShapeDtypeStruct(down.shape[1:], BF16),
            *mixes,
        ),
        in_specs=[HBM] * 5,
        out_specs=(VMEM,) * (2 + len(mixes)),
        scratch_shapes=[
            pltpu.SMEM(ids.shape, jnp.int32),
            pltpu.SMEM(weights.shape, F32),
            pltpu.SemaphoreType.DMA((2,)),
            pltpu.SemaphoreType.DMA((12,)),
        ],
        compiler_params=pltpu.CompilerParams(vmem_limit_bytes=24 * MIB),
        cost_estimate=pl.CostEstimate(
            flops=1_000_000, bytes_accessed=22_000_000, transcendentals=0
        ),
        name="stage",
    )(ids, weights, gate_up, down, after)
    return gu, dn, mixes


def expert_kernel(count, per, *refs):
    own_refs, other_refs = refs[:count], refs[count : 2 * count]
    gu, dn = refs[2 * count : 2 * count + 2]
    mine_refs = refs[2 * count + 2 : 3 * count + 2]
    theirs_refs = refs[3 * count + 2 :]
    piece = own_refs[0].shape[2]
    chips = sum(ref.shape[0] for ref in own_refs)
    pieces = LINES // per
    half = chips * per
    n = chips * LINES
    row = iota((n, n), 0)
    col = iota((n, n), 1)
    order = one_hot(col == row // per % chips * LINES + row // half * per + row % per)
    sides = []
    for refs_now in (own_refs, other_refs):
        lines = [ref[...].reshape(ref.shape[0] * LINES, piece) for ref in refs_now]
        sides.append(dot(order, jnp.concatenate(lines, axis=0)).astype(BF16))
    gate = upper = None
    for k in range(pieces):
        x = jnp.concatenate([side[k * half : (k + 1) * half] for side in sides], axis=0)
        cols = pl.ds(k * piece, piece)
        g, u = nt_dot(x, gu[0, :, cols]), nt_dot(x, gu[1, :, cols])
        gate, upper = (g, u) if k == 0 else (gate + g, upper + u)
    act = (gate / (1.0 + jnp.exp(-gate)) * upper).astype(BF16)
    mine = []
    theirs = []
    for k in range(pieces):
        part = dot(act, dn[:, k * piece : (k + 1) * piece]).astype(BF16)
        mine.append(part[:half])
        theirs.append(part[half:])
    back = one_hot(row == col // per % chips * LINES + col // half * per + col % per)
    for parts, refs_now in ((theirs, theirs_refs), (mine, mine_refs)):
        lines = dot(back, jnp.concatenate(parts, axis=0)).astype(BF16)
        start = 0
        for ref in refs_now:
            size = ref.shape[0] * LINES
            ref[...] = lines[start : start + size].reshape(ref.shape)
            start += size


def experts(own, other, gu, dn, per):
    count = len(own)
    shapes = tuple(jax.ShapeDtypeStruct(x.shape, BF16) for x in own)
    results = pl.pallas_call(
        functools.partial(expert_kernel, count, per),
        out_shape=shapes + shapes,
        in_specs=[VMEM] * (2 * count + 2),
        out_specs=(VMEM,) * (2 * count),
        compiler_params=pltpu.CompilerParams(vmem_limit_bytes=32 * MIB),
        cost_estimate=pl.CostEstimate(
            flops=800_000_000, bytes_accessed=12_000_000, transcendentals=16384
        ),
        name="experts",
    )(*own, *other, gu, dn)
    return results[:count], results[count:]


def combine_kernel(counts, resid_ref, *refs):
    out_ref = refs[-1]
    _, rows, width = out_ref.shape
    start = 0
    for batch, count in zip(BATCHES, counts):
        left = refs[start][...]
        back_refs = refs[start + 1 : start + 1 + count]
        start += 1 + count
        piece = back_refs[0].shape[2]
        pieces = width // piece
        both = len(batch) * rows
        lines = [ref[...].reshape(ref.shape[0] * LINES, piece) for ref in back_refs]
        product = dot(left, jnp.concatenate(lines, axis=0))
        n = pieces * both
        total = product[:n] + product[n : 2 * n] + product[2 * n :]
        first = batch[0] * rows
        for k in range(pieces):
            cols = pl.ds(k * piece, piece)
            done = resid_ref[first : first + both, cols] + total[k * both : (k + 1) * both]
            done = done.astype(BF16)
            for i, s in enumerate(batch):
                out_ref[s, :, cols] = done[i * rows : (i + 1) * rows]


def combine(shape, resid, mixes, backs):
    operands = [x for mix, back in zip(mixes, backs) for x in (mix, *back)]
    return pl.pallas_call(
        functools.partial(combine_kernel, [len(back) for back in backs]),
        out_shape=jax.ShapeDtypeStruct(shape, BF16),
        in_specs=[VMEM] * (1 + len(operands)),
        out_specs=VMEM,
        compiler_params=pltpu.CompilerParams(vmem_limit_bytes=24 * MIB),
        cost_estimate=pl.CostEstimate(
            flops=100_000_000, bytes_accessed=1_000_000, transcendentals=0
        ),
        name="combine",
    )(resid, *operands)


def per_device(
    queries,
    fresh,
    kv_cache,
    cache_len,
    hidden_state,
    norm_gain,
    expert_ids,
    route_weight,
    gate_up,
    down,
):
    owners = lax.axis_size("afd")
    chips = owners // 2
    chips_per_expert = chips // EXPERTS
    permuted = chips == EXPERTS
    swap = [(i, i ^ 1) for i in range(owners)]
    far_first = sorted(range(1, chips), reverse=True)

    def to_chips(chunks):
        if permuted:
            moved = {0: chunks[0]}
            for j in far_first:
                moved[j] = lax.ppermute(chunks[j], "afd", [(i, i ^ 2 * j) for i in range(owners)])
            return [moved[j] for j in range(chips)]
        same_core = [[2 * p + c for p in range(chips)] for c in range(2)]
        whole = jnp.concatenate(chunks, axis=0)
        return [
            lax.all_to_all(
                whole, "afd", split_axis=0, concat_axis=0, axis_index_groups=same_core, tiled=True
            )
        ]

    ids = expert_ids.transpose(2, 0, 1)
    weights = route_weight.transpose(2, 0, 1)
    resid, sent = attend(
        permuted, cache_len, ids, queries, fresh, kv_cache, hidden_state, norm_gain
    )
    gu, dn, mixes = stage(permuted, chips, ids, weights, gate_up, down, resid)
    backs = []
    for batch, chunks in zip(BATCHES, sent):
        if not permuted:
            chunks = [jnp.repeat(chunk, chips_per_expert, axis=0) for chunk in chunks]
        own = to_chips(chunks)
        other = [lax.ppermute(x, "afd", swap) for x in own]
        mine, theirs = experts(own, other, gu, dn, len(batch) * CAP)
        summed = [
            (a.astype(F32) + lax.ppermute(b, "afd", swap).astype(F32)).astype(BF16)
            for a, b in zip(mine, theirs)
        ]
        backs.append(to_chips(summed))
    return combine(queries.shape, resid, mixes, backs)


def solution(mesh):
    placed = (
        P(None, ("group", "afd"), None),
        P(None, ("group", "afd"), None),
        P(("group", "afd"), None, None),
        P(("group", "afd")),
        P(None, ("group", "afd"), None),
        P(),
        P(None, ("group", "afd"), None),
        P(None, ("group", "afd"), None),
        P("afd", None, None, None),
        P("afd", None, None),
    )
    return jax.shard_map(
        per_device,
        mesh=mesh,
        in_specs=placed,
        out_specs=P(None, ("group", "afd"), None),
        check_vma=False,
    )
```

```python
import functools
import jax
import jax.numpy as jnp
from jax import lax
from jax.experimental import pallas as pl
from jax.experimental.pallas import tpu as pltpu
from jax.sharding import PartitionSpec as P

HEADS = 32
HEAD = 224
EXPERTS = 8
TOP = 3
LANES = 128
PARTS = 3
F32 = jnp.float32
BF16 = jnp.bfloat16
MIB = 1 << 20
VMEM = pl.BlockSpec(memory_space=pltpu.VMEM)
HBM = pl.BlockSpec(memory_space=pltpu.HBM)


def iota(shape, dim):
    return lax.broadcasted_iota(jnp.int32, shape, dim)


def nt_dot(a, b):
    return lax.dot_general(a, b, (((1,), (1,)), ((), ())), preferred_element_type=F32)


def dot(a, b):
    return jnp.dot(a, b, preferred_element_type=F32)


def one_hot(mask):
    return jnp.where(mask, 1.0, 0.0).astype(BF16)


def spread(ref, k, where, steps, rows, empty):
    out = jnp.full(where.shape, empty)
    for s in range(steps):
        for r in range(rows):
            out = jnp.where(where == s * rows + r, ref[k, s, r], out)
    return out


def tail(ids_ref, weight_ref, steps, rows):
    both = steps * rows
    lane = iota((both, LANES), 1)
    where = iota((both, 1), 0)
    mix = jnp.zeros((both, LANES), F32)
    for k in range(TOP):
        hit = spread(ids_ref, k, where, steps, rows, -1) == lane % EXPERTS
        mix = mix + jnp.where(hit, spread(weight_ref, k, where, steps, rows, 0.0), 0.0)
    out = jnp.zeros((both, LANES), F32)
    for part in range(PARTS):
        term = mix.astype(BF16).astype(F32)
        out = jnp.where(lane // EXPERTS == part, term, out)
        mix = mix - term
    return out.astype(BF16)


def attend_kernel(
    len_hbm,
    ids_hbm,
    weight_hbm,
    q_hbm,
    fresh_hbm,
    kv_hbm,
    hid_hbm,
    gain_hbm,
    resid_ref,
    out_ref,
    len_ref,
    ids_ref,
    weight_ref,
    q_ref,
    fresh_ref,
    kv_ref,
    hid_ref,
    gain_ref,
    merged,
    sems,
):
    copies = [
        pltpu.make_async_copy(source, target, sems.at[i])
        for i, (source, target) in enumerate(
            (
                (q_hbm, q_ref),
                (kv_hbm, kv_ref),
                (len_hbm, len_ref),
                (ids_hbm, ids_ref),
                (weight_hbm, weight_ref),
                (fresh_hbm, fresh_ref),
                (hid_hbm, hid_ref),
                (gain_hbm, gain_ref),
            )
        )
    ]
    for copy in copies:
        copy.start()
    steps, rows, width = q_ref.shape
    length = kv_ref.shape[2]
    both = steps * rows
    scale = HEAD ** (-0.5)
    for copy in copies:
        copy.wait()
    q = jnp.concatenate([q_ref[s].astype(F32) for s in range(steps)], axis=0)
    heads = jnp.concatenate([q[:, h * HEAD : (h + 1) * HEAD] for h in range(HEADS)], axis=0)
    heads = heads.astype(BF16)
    kv = jnp.concatenate([kv_ref[r] for r in range(rows)], axis=1)
    new = jnp.concatenate([fresh_ref[s].astype(F32) for s in range(steps)], axis=0).astype(BF16)

    sub = iota((both, rows * length), 0)
    lane = iota((both, rows * length), 1)
    limit = jnp.zeros_like(lane)
    for r in range(rows):
        limit = jnp.where(lane // length == r, len_ref[r], limit)
    valid = (lane // length == sub % rows) & (lane % length < limit)
    sub = iota((both, both), 0)
    lane = iota((both, both), 1)
    valid_new = (lane % rows == sub % rows) & (lane // rows <= sub // rows)

    old_s = (dot(heads, kv[:HEAD]) * scale).reshape(HEADS, both, rows * length)
    new_s = (nt_dot(heads, new[:, :HEAD]) * scale).reshape(HEADS, both, both)
    old_s = jnp.where(valid[None], old_s, -1e30)
    new_s = jnp.where(valid_new[None], new_s, -1e30)
    top = jnp.maximum(
        jnp.max(old_s, axis=-1, keepdims=True), jnp.max(new_s, axis=-1, keepdims=True)
    )
    old_e = jnp.exp(old_s - top)
    new_e = jnp.exp(new_s - top)
    total = jnp.sum(old_e, axis=-1, keepdims=True) + jnp.sum(new_e, axis=-1, keepdims=True)
    old_w = (old_e / total).reshape(HEADS * both, rows * length).astype(BF16)
    new_w = (new_e / total).reshape(HEADS * both, both).astype(BF16)
    attended = nt_dot(old_w, kv[HEAD:]) + dot(new_w, new[:, HEAD:])
    for h in range(HEADS):
        merged[:, h * HEAD : (h + 1) * HEAD] = attended[h * both : (h + 1) * both]
    hidden = jnp.concatenate([hid_ref[s].astype(F32) for s in range(steps)], axis=0)
    resid = hidden + merged[...]
    resid_ref[...] = resid
    meansq = jnp.mean(resid * resid, axis=-1, keepdims=True)
    gain = gain_ref[...].astype(F32)
    gain = jnp.concatenate([gain[i : i + 1] for i in range(width // LANES)], axis=1)
    normed = resid * lax.rsqrt(meansq + 1e-06) * gain
    out_ref[:, :width] = normed.astype(BF16)
    out_ref[:, width:] = tail(ids_ref, weight_ref, steps, rows)


def attend(cache_len, ids, weights, queries, fresh, kv_cache, hidden_state, norm_gain):
    steps, rows, width = queries.shape
    kv = kv_cache.transpose(0, 2, 1)
    gain = norm_gain.reshape(width // LANES, LANES)
    return pl.pallas_call(
        attend_kernel,
        out_shape=(
            jax.ShapeDtypeStruct((steps * rows, width), F32),
            jax.ShapeDtypeStruct((steps * rows, width + LANES), BF16),
        ),
        in_specs=[HBM] * 8,
        out_specs=(VMEM, VMEM),
        scratch_shapes=[
            pltpu.SMEM(cache_len.shape, jnp.int32),
            pltpu.SMEM(ids.shape, jnp.int32),
            pltpu.SMEM(weights.shape, F32),
            pltpu.VMEM(queries.shape, BF16),
            pltpu.VMEM(fresh.shape, BF16),
            pltpu.VMEM(kv.shape, BF16),
            pltpu.VMEM(hidden_state.shape, BF16),
            pltpu.VMEM(gain.shape, BF16),
            pltpu.VMEM((steps * rows, width), F32),
            pltpu.SemaphoreType.DMA((8,)),
        ],
        compiler_params=pltpu.CompilerParams(vmem_limit_bytes=24 * MIB),
        cost_estimate=pl.CostEstimate(
            flops=300_000_000, bytes_accessed=2_000_000, transcendentals=131072
        ),
        name="attend",
    )(cache_len, ids, weights, queries, fresh, kv, hidden_state, gain)


def stage_kernel(gu_hbm, dn_hbm, after, gu, dn, sems):
    step = dn.shape[0] // 4
    pairs = []
    for i in range(4):
        part = pl.ds(i * step, step)
        pairs.append((gu_hbm.at[0, 0, part], gu.at[0, part]))
        pairs.append((gu_hbm.at[0, 1, part], gu.at[1, part]))
        pairs.append((dn_hbm.at[0, part], dn.at[part]))
    copies = [pltpu.make_async_copy(a, b, sems.at[i]) for i, (a, b) in enumerate(pairs)]
    for copy in copies:
        copy.start()
    for copy in copies:
        copy.wait()


def stage(gate_up, down, after):
    return pl.pallas_call(
        stage_kernel,
        out_shape=(
            jax.ShapeDtypeStruct(gate_up.shape[1:], BF16),
            jax.ShapeDtypeStruct(down.shape[1:], BF16),
        ),
        in_specs=[HBM, HBM, VMEM],
        out_specs=(VMEM, VMEM),
        scratch_shapes=[pltpu.SemaphoreType.DMA((12,))],
        compiler_params=pltpu.CompilerParams(vmem_limit_bytes=24 * MIB),
        cost_estimate=pl.CostEstimate(flops=0, bytes_accessed=22_000_000, transcendentals=0),
        name="stage",
    )(gate_up, down, after)


def expert_kernel(rows_ref, gu, dn, out_ref):
    width = out_ref.shape[1]
    expert = lax.axis_index("afd") // (lax.axis_size("afd") // EXPERTS)
    ends = rows_ref[:, width:].astype(F32)
    lane = iota(ends.shape, 1)
    mine = (lane % EXPERTS == expert) & (lane < PARTS * EXPERTS)
    weight = jnp.sum(jnp.where(mine, ends, 0.0), axis=1, keepdims=True)
    x = rows_ref[:, :width]
    gate = nt_dot(x, gu[0])
    upper = nt_dot(x, gu[1])
    act = (gate / (1.0 + jnp.exp(-gate)) * upper).astype(BF16)
    part = dot(act, dn[...]).astype(BF16).astype(F32)
    out_ref[...] = (part * weight).astype(BF16)


def experts(rows, gu, dn):
    count, width = rows.shape[0], dn.shape[1]
    return pl.pallas_call(
        expert_kernel,
        out_shape=jax.ShapeDtypeStruct((count, width), BF16),
        in_specs=[VMEM] * 3,
        out_specs=VMEM,
        compiler_params=pltpu.CompilerParams(vmem_limit_bytes=32 * MIB),
        cost_estimate=pl.CostEstimate(
            flops=1_500_000_000, bytes_accessed=12_000_000, transcendentals=16384
        ),
        name="experts",
    )(rows, gu, dn)


def per_device(
    queries,
    fresh,
    kv_cache,
    cache_len,
    hidden_state,
    norm_gain,
    expert_ids,
    route_weight,
    gate_up,
    down,
):
    ids = expert_ids.transpose(2, 0, 1)
    weights = route_weight.transpose(2, 0, 1)
    resid, packed = attend(
        cache_len, ids, weights, queries, fresh, kv_cache, hidden_state, norm_gain
    )
    gathered = lax.all_gather(packed, "afd", axis=0, tiled=True)
    gu, dn = stage(gate_up, down, resid)
    weighted = experts(gathered, gu, dn)
    combined = lax.psum_scatter(weighted, "afd", scatter_dimension=0, tiled=True)
    return (resid + combined.astype(F32)).astype(BF16).reshape(queries.shape)


def solution(mesh):
    placed = (
        P(None, ("group", "afd"), None),
        P(None, ("group", "afd"), None),
        P(("group", "afd"), None, None),
        P(("group", "afd")),
        P(None, ("group", "afd"), None),
        P(),
        P(None, ("group", "afd"), None),
        P(None, ("group", "afd"), None),
        P("afd", None, None, None),
        P("afd", None, None),
    )
    return jax.shard_map(
        per_device,
        mesh=mesh,
        in_specs=placed,
        out_specs=P(None, ("group", "afd"), None),
        check_vma=False,
    )
```

```python
import functools
import jax
import jax.numpy as jnp
from jax import lax
from jax.experimental import pallas as pl
from jax.experimental.pallas import tpu as pltpu
from jax.sharding import PartitionSpec as P

HEADS = 32
HEAD = 224
EXPERTS = 8
TOP = 3
CAP = 2
LINES = 16
LANES = 128
F32 = jnp.float32
BF16 = jnp.bfloat16
MIB = 1 << 20
VMEM = pl.BlockSpec(memory_space=pltpu.VMEM)
HBM = pl.BlockSpec(memory_space=pltpu.HBM)
BATCHES = ((0,), (1,))


def iota(shape, dim):
    return lax.broadcasted_iota(jnp.int32, shape, dim)


def in_hbm(*arrays):
    return [pltpu.with_memory_space_constraint(x, pltpu.HBM) for x in arrays]


def nt_dot(a, b):
    return lax.dot_general(a, b, (((1,), (1,)), ((), ())), preferred_element_type=F32)


def dot(a, b):
    return jnp.dot(a, b, preferred_element_type=F32)


def one_hot(mask):
    return jnp.where(mask, 1.0, 0.0).astype(BF16)


def spread(ref, k, where, steps, rows, empty):
    out = jnp.full(where.shape, empty)
    for s in range(steps):
        for r in range(rows):
            out = jnp.where(where == s * rows + r, ref[k, s, r], out)
    return out


def picks_of(ids_ref, batch, steps, rows):
    pieces = LINES // (len(batch) * CAP)
    both = steps * rows
    shape = (EXPERTS * LINES, pieces * both)
    line = iota(shape, 0)
    col = iota(shape, 1)
    where = iota((1, pieces * both), 1) % both
    expert = line // LINES
    named = jnp.zeros(shape, jnp.bool_)
    for k in range(TOP):
        named = named | (spread(ids_ref, k, where, steps, rows, -1) == expert)
    at = iota((pieces * both, pieces * both), 0)
    to = iota((pieces * both, pieces * both), 1)
    rank = dot(one_hot(named), one_hot((at // rows == to // rows) & (at < to)))
    slot = (line % CAP).astype(F32)
    step = (line // CAP) % len(batch) + batch[0]
    piece = line // (CAP * len(batch)) % pieces
    same = (step == col // rows % steps) & (piece == col // both)
    return one_hot(named & same & (rank == slot))


def attend_kernel(
    len_hbm,
    ids_hbm,
    q_hbm,
    fresh_hbm,
    kv_hbm,
    hid_hbm,
    gain_hbm,
    gu_hbm,
    dn_hbm,
    gu_ref,
    dn_ref,
    resid_ref,
    *rest,
):
    outs = rest[: len(BATCHES)]
    len_ref, ids_ref, q_ref, fresh_ref, kv_ref, hid_ref, gain_ref, merged, sems, large = rest[
        len(outs) :
    ]
    copies = [
        pltpu.make_async_copy(source, target, sems.at[i])
        for i, (source, target) in enumerate(
            (
                (q_hbm, q_ref),
                (kv_hbm, kv_ref),
                (len_hbm, len_ref),
                (ids_hbm, ids_ref),
                (fresh_hbm, fresh_ref),
                (hid_hbm, hid_ref),
                (gain_hbm, gain_ref),
            )
        )
    ]
    step = dn_ref.shape[0] // 4
    weights = []
    for i in range(4):
        part = pl.ds(i * step, step)
        weights.append((gu_hbm.at[0, 0, part], gu_ref.at[0, part]))
        weights.append((gu_hbm.at[0, 1, part], gu_ref.at[1, part]))
        weights.append((dn_hbm.at[0, part], dn_ref.at[part]))
    weights = [pltpu.make_async_copy(a, b, large.at[i]) for i, (a, b) in enumerate(weights)]
    for copy in copies + weights:
        copy.start()
    steps, rows, width = q_ref.shape
    length = kv_ref.shape[2]
    both = steps * rows
    scale = HEAD ** (-0.5)
    for copy in copies:
        copy.wait()
    q = jnp.concatenate([q_ref[s].astype(F32) for s in range(steps)], axis=0)
    heads = jnp.concatenate([q[:, h * HEAD : (h + 1) * HEAD] for h in range(HEADS)], axis=0)
    heads = heads.astype(BF16)
    kv = jnp.concatenate([kv_ref[r] for r in range(rows)], axis=1)
    new = jnp.concatenate([fresh_ref[s].astype(F32) for s in range(steps)], axis=0).astype(BF16)

    sub = iota((both, rows * length), 0)
    lane = iota((both, rows * length), 1)
    limit = jnp.zeros_like(lane)
    for r in range(rows):
        limit = jnp.where(lane // length == r, len_ref[r], limit)
    valid = (lane // length == sub % rows) & (lane % length < limit)
    sub = iota((both, both), 0)
    lane = iota((both, both), 1)
    valid_new = (lane % rows == sub % rows) & (lane // rows <= sub // rows)

    old_s = (dot(heads, kv[:HEAD]) * scale).reshape(HEADS, both, rows * length)
    new_s = (nt_dot(heads, new[:, :HEAD]) * scale).reshape(HEADS, both, both)
    old_s = jnp.where(valid[None], old_s, -1e30)
    new_s = jnp.where(valid_new[None], new_s, -1e30)
    top = jnp.maximum(
        jnp.max(old_s, axis=-1, keepdims=True), jnp.max(new_s, axis=-1, keepdims=True)
    )
    old_e = jnp.exp(old_s - top)
    new_e = jnp.exp(new_s - top)
    total = jnp.sum(old_e, axis=-1, keepdims=True) + jnp.sum(new_e, axis=-1, keepdims=True)
    old_w = (old_e / total).reshape(HEADS * both, rows * length).astype(BF16)
    new_w = (new_e / total).reshape(HEADS * both, both).astype(BF16)
    attended = nt_dot(old_w, kv[HEAD:]) + dot(new_w, new[:, HEAD:])
    for h in range(HEADS):
        merged[:, h * HEAD : (h + 1) * HEAD] = attended[h * both : (h + 1) * both]
    hidden = jnp.concatenate([hid_ref[s].astype(F32) for s in range(steps)], axis=0)
    resid = hidden + merged[...]
    resid_ref[...] = resid
    meansq = jnp.mean(resid * resid, axis=-1, keepdims=True)
    gain = gain_ref[...].astype(F32)
    gain = jnp.concatenate([gain[i : i + 1] for i in range(width // LANES)], axis=1)
    normed = resid * lax.rsqrt(meansq + 1e-06) * gain
    for batch, out in zip(BATCHES, outs):
        pieces = LINES // (len(batch) * CAP)
        piece = width // pieces
        stacked = jnp.concatenate(
            [normed[:, k * piece : (k + 1) * piece] for k in range(pieces)], axis=0
        ).astype(BF16)
        picks = picks_of(ids_ref, batch, steps, rows)
        out[...] = dot(picks, stacked).astype(BF16).reshape(out.shape)
    for copy in weights:
        copy.wait()


def attend(cache_len, ids, queries, fresh, kv_cache, hidden_state, norm_gain, gate_up, down):
    steps, rows, width = queries.shape
    chunks = []
    for batch in BATCHES:
        shape = (EXPERTS, LINES, width * len(batch) * CAP // LINES)
        chunks.append(jax.ShapeDtypeStruct(shape, BF16))
    kv = kv_cache.transpose(0, 2, 1)
    gain = norm_gain.reshape(width // LANES, LANES)
    gu, dn, resid, *chunks = pl.pallas_call(
        attend_kernel,
        out_shape=(
            jax.ShapeDtypeStruct(gate_up.shape[1:], BF16),
            jax.ShapeDtypeStruct(down.shape[1:], BF16),
            jax.ShapeDtypeStruct((steps * rows, width), F32),
            *chunks,
        ),
        in_specs=[HBM] * 9,
        out_specs=(VMEM,) * (3 + len(chunks)),
        scratch_shapes=[
            pltpu.SMEM(cache_len.shape, jnp.int32),
            pltpu.SMEM(ids.shape, jnp.int32),
            pltpu.VMEM(queries.shape, BF16),
            pltpu.VMEM(fresh.shape, BF16),
            pltpu.VMEM(kv.shape, BF16),
            pltpu.VMEM(hidden_state.shape, BF16),
            pltpu.VMEM(gain.shape, BF16),
            pltpu.VMEM((steps * rows, width), F32),
            pltpu.SemaphoreType.DMA((7,)),
            pltpu.SemaphoreType.DMA((12,)),
        ],
        compiler_params=pltpu.CompilerParams(vmem_limit_bytes=32 * MIB),
        cost_estimate=pl.CostEstimate(
            flops=300_000_000, bytes_accessed=24_000_000, transcendentals=131072
        ),
        name="attend",
    )(*in_hbm(cache_len, ids, queries, fresh, kv, hidden_state, gain, gate_up, down))
    return gu, dn, resid, chunks


def mixing(ids_ref, weight_ref, batch, steps, rows, chips):
    pieces = LINES // (len(batch) * CAP)
    both = len(batch) * rows
    shape = (both, chips * LINES)
    line = iota(shape, 1)
    sub = iota(shape, 0)
    expert = line // LINES // (chips // EXPERTS)
    where = iota((both, 1), 0) + batch[0] * rows
    named = jnp.zeros(shape, F32)
    mix = jnp.zeros(shape, F32)
    for k in range(TOP):
        hit = spread(ids_ref, k, where, steps, rows, -1) == expert
        weight = spread(weight_ref, k, where, steps, rows, 0.0)
        named = named + jnp.where(hit, 1.0, 0.0)
        mix = mix + jnp.where(hit, weight, 0.0)
    at = iota((both, both), 1)
    to = iota((both, both), 0)
    rank = dot(one_hot((at // rows == to // rows) & (at < to)), named.astype(BF16))
    same = (line // CAP) % len(batch) == sub // rows
    mix = jnp.where((rank == (line % CAP).astype(F32)) & same, mix, 0.0)
    high = mix.astype(BF16).astype(F32)
    middle = (mix - high).astype(BF16).astype(F32)
    low = mix - high - middle
    k_of = line // (len(batch) * CAP) % pieces
    parts = [
        jnp.where(k_of == k, part, 0.0) for part in (high, middle, low) for k in range(pieces)
    ]
    return jnp.concatenate(parts, axis=0).astype(BF16)


def mix_kernel(chips, ids_hbm, weight_hbm, *refs):
    mixes = refs[: len(BATCHES)]
    ids_ref, weight_ref, sems = refs[len(BATCHES) :]
    copies = [
        pltpu.make_async_copy(ids_hbm, ids_ref, sems.at[0]),
        pltpu.make_async_copy(weight_hbm, weight_ref, sems.at[1]),
    ]
    for copy in copies:
        copy.start()
    for copy in copies:
        copy.wait()
    _, steps, rows = ids_ref.shape
    for batch, mix in zip(BATCHES, mixes):
        mix[...] = mixing(ids_ref, weight_ref, batch, steps, rows, chips)


def mixers(chips, ids, weights):
    rows = ids.shape[2]
    mixes = [
        jax.ShapeDtypeStruct((3 * LINES // CAP * rows, chips * LINES), BF16) for _ in BATCHES
    ]
    return pl.pallas_call(
        functools.partial(mix_kernel, chips),
        out_shape=mixes,
        in_specs=[HBM] * 2,
        out_specs=[VMEM] * len(mixes),
        scratch_shapes=[
            pltpu.SMEM(ids.shape, jnp.int32),
            pltpu.SMEM(weights.shape, F32),
            pltpu.SemaphoreType.DMA((2,)),
        ],
        compiler_params=pltpu.CompilerParams(vmem_limit_bytes=16 * MIB),
        cost_estimate=pl.CostEstimate(flops=100_000_000, bytes_accessed=4_000_000, transcendentals=0),
        name="mixers",
    )(*in_hbm(ids, weights))


def expert_kernel(per, own_ref, other_ref, gu, dn, mine_ref, theirs_ref):
    chips, lines, piece = own_ref.shape
    pieces = lines // per
    half = chips * per
    n = chips * lines
    row = iota((n, n), 0)
    col = iota((n, n), 1)
    order = one_hot(col == row // per % chips * lines + row // half * per + row % per)
    sides = [dot(order, ref[...].reshape(n, piece)).astype(BF16) for ref in (own_ref, other_ref)]
    gate = upper = None
    for k in range(pieces):
        x = jnp.concatenate([side[k * half : (k + 1) * half] for side in sides], axis=0)
        cols = pl.ds(k * piece, piece)
        g, u = nt_dot(x, gu[0, :, cols]), nt_dot(x, gu[1, :, cols])
        gate, upper = (g, u) if k == 0 else (gate + g, upper + u)
    act = (gate / (1.0 + jnp.exp(-gate)) * upper).astype(BF16)
    mine = []
    theirs = []
    for k in range(pieces):
        part = dot(act, dn[:, k * piece : (k + 1) * piece]).astype(BF16)
        mine.append(part[:half])
        theirs.append(part[half:])
    back = one_hot(row == col // per % chips * lines + col // half * per + col % per)
    for parts, ref in ((theirs, theirs_ref), (mine, mine_ref)):
        lines_now = dot(back, jnp.concatenate(parts, axis=0)).astype(BF16)
        ref[...] = lines_now.reshape(ref.shape)


def experts(own, other, gu, dn, per):
    shape = jax.ShapeDtypeStruct(own.shape, BF16)
    return pl.pallas_call(
        functools.partial(expert_kernel, per),
        out_shape=(shape, shape),
        in_specs=[VMEM] * 4,
        out_specs=(VMEM, VMEM),
        compiler_params=pltpu.CompilerParams(vmem_limit_bytes=32 * MIB),
        cost_estimate=pl.CostEstimate(
            flops=800_000_000, bytes_accessed=12_000_000, transcendentals=16384
        ),
        name="experts",
    )(own, other, gu, dn)


def combine_kernel(resid_ref, *refs):
    out_ref = refs[-1]
    _, rows, width = out_ref.shape
    for i, batch in enumerate(BATCHES):
        left = refs[2 * i][...]
        back_ref = refs[2 * i + 1]
        chips, lines, piece = back_ref.shape
        pieces = width // piece
        both = len(batch) * rows
        product = dot(left, back_ref[...].reshape(chips * lines, piece))
        n = pieces * both
        total = product[:n] + product[n : 2 * n] + product[2 * n :]
        first = batch[0] * rows
        for k in range(pieces):
            cols = pl.ds(k * piece, piece)
            done = resid_ref[first : first + both, cols] + total[k * both : (k + 1) * both]
            done = done.astype(BF16)
            for j, s in enumerate(batch):
                out_ref[s, :, cols] = done[j * rows : (j + 1) * rows]


def combine(shape, resid, mixes, backs):
    operands = [x for pair in zip(mixes, backs) for x in pair]
    return pl.pallas_call(
        combine_kernel,
        out_shape=jax.ShapeDtypeStruct(shape, BF16),
        in_specs=[VMEM] * (1 + len(operands)),
        out_specs=VMEM,
        compiler_params=pltpu.CompilerParams(vmem_limit_bytes=24 * MIB),
        cost_estimate=pl.CostEstimate(
            flops=100_000_000, bytes_accessed=1_000_000, transcendentals=0
        ),
        name="combine",
    )(resid, *operands)


def per_device(
    queries,
    fresh,
    kv_cache,
    cache_len,
    hidden_state,
    norm_gain,
    expert_ids,
    route_weight,
    gate_up,
    down,
):
    owners = lax.axis_size("afd")
    chips = owners // 2
    swap = [(i, i ^ 1) for i in range(owners)]
    same_core = [[2 * p + c for p in range(chips)] for c in range(2)]

    def to_chips(chunks):
        return lax.all_to_all(
            chunks, "afd", split_axis=0, concat_axis=0, axis_index_groups=same_core, tiled=True
        )

    ids = expert_ids.transpose(2, 0, 1)
    weights = route_weight.transpose(2, 0, 1)
    gu, dn, resid, sent = attend(
        cache_len, ids, queries, fresh, kv_cache, hidden_state, norm_gain, gate_up, down
    )
    mixes = mixers(chips, ids, weights)
    if chips > EXPERTS:
        sent = [jnp.repeat(chunks, chips // EXPERTS, axis=0) for chunks in sent]
    received = [to_chips(chunks) for chunks in sent]
    backs = []
    for batch, own in zip(BATCHES, received):
        other = lax.ppermute(own, "afd", swap)
        mine, theirs = experts(own, other, gu, dn, len(batch) * CAP)
        summed = mine.astype(F32) + lax.ppermute(theirs, "afd", swap).astype(F32)
        backs.append(to_chips(summed.astype(BF16)))
    return combine(queries.shape, resid, mixes, backs)


def solution(mesh):
    placed = (
        P(None, ("group", "afd"), None),
        P(None, ("group", "afd"), None),
        P(("group", "afd"), None, None),
        P(("group", "afd")),
        P(None, ("group", "afd"), None),
        P(),
        P(None, ("group", "afd"), None),
        P(None, ("group", "afd"), None),
        P("afd", None, None, None),
        P("afd", None, None),
    )
    return jax.shard_map(
        per_device,
        mesh=mesh,
        in_specs=placed,
        out_specs=P(None, ("group", "afd"), None),
        check_vma=False,
    )
```

```python
import functools
import jax
import jax.numpy as jnp
from jax import lax
from jax.experimental import pallas as pl
from jax.experimental.pallas import tpu as pltpu
from jax.sharding import PartitionSpec as P

HEADS = 32
HEAD = 224
EXPERTS = 8
TOP = 3
CAP = 2
LINES = 16
LANES = 128
STAGED = 5
F32 = jnp.float32
BF16 = jnp.bfloat16
MIB = 1 << 20
VMEM = pl.BlockSpec(memory_space=pltpu.VMEM)
HBM = pl.BlockSpec(memory_space=pltpu.HBM)
BATCHES = ((0, 1),)
TURNS = ((0, 7, 1, 5, 2, 6, 3, 4), (0, 4, 6, 1, 7, 2, 5, 3))


def iota(shape, dim):
    return lax.broadcasted_iota(jnp.int32, shape, dim)


def in_hbm(*arrays):
    return [pltpu.with_memory_space_constraint(x, pltpu.HBM) for x in arrays]


def partner(permuted, turn):
    if not permuted:
        return turn
    place = lax.axis_index("afd")
    out = jnp.zeros_like(turn)
    for n in range(1, len(TURNS[0])):
        out = jnp.where(turn == n, jnp.where(place % 2 == 0, TURNS[0][n], TURNS[1][n]), out)
    return out ^ (place // 2)


def nt_dot(a, b):
    return lax.dot_general(a, b, (((1,), (1,)), ((), ())), preferred_element_type=F32)


def dot(a, b):
    return jnp.dot(a, b, preferred_element_type=F32)


def one_hot(mask):
    return jnp.where(mask, 1.0, 0.0).astype(BF16)


def spread(ref, k, where, steps, rows, empty):
    out = jnp.full(where.shape, empty)
    for s in range(steps):
        for r in range(rows):
            out = jnp.where(where == s * rows + r, ref[k, s, r], out)
    return out


def picks_of(ids_ref, batch, steps, rows, permuted):
    pieces = LINES // (len(batch) * CAP)
    both = steps * rows
    shape = (EXPERTS * LINES, pieces * both)
    line = iota(shape, 0)
    col = iota(shape, 1)
    where = iota((1, pieces * both), 1) % both
    expert = partner(permuted, line // LINES)
    named = jnp.zeros(shape, jnp.bool_)
    for k in range(TOP):
        named = named | (spread(ids_ref, k, where, steps, rows, -1) == expert)
    at = iota((pieces * both, pieces * both), 0)
    to = iota((pieces * both, pieces * both), 1)
    rank = dot(one_hot(named), one_hot((at // rows == to // rows) & (at < to)))
    slot = (line % CAP).astype(F32)
    step = (line // CAP) % len(batch) + batch[0]
    piece = line // (CAP * len(batch)) % pieces
    same = (step == col // rows % steps) & (piece == col // both)
    return one_hot(named & same & (rank == slot))


def attend_kernel(
    permuted, len_hbm, ids_hbm, q_hbm, fresh_hbm, kv_hbm, hid_hbm, gain_hbm, resid_ref, *rest
):
    outs = rest[: len(BATCHES) * EXPERTS]
    len_ref, ids_ref, q_ref, fresh_ref, kv_ref, hid_ref, gain_ref, merged, sems = rest[len(outs) :]
    copies = [
        pltpu.make_async_copy(source, target, sems.at[i])
        for i, (source, target) in enumerate(
            (
                (q_hbm, q_ref),
                (kv_hbm, kv_ref),
                (len_hbm, len_ref),
                (ids_hbm, ids_ref),
                (fresh_hbm, fresh_ref),
                (hid_hbm, hid_ref),
                (gain_hbm, gain_ref),
            )
        )
    ]
    for copy in copies:
        copy.start()
    steps, rows, width = q_ref.shape
    length = kv_ref.shape[2]
    both = steps * rows
    scale = HEAD ** (-0.5)
    for copy in copies:
        copy.wait()
    q = jnp.concatenate([q_ref[s].astype(F32) for s in range(steps)], axis=0)
    heads = jnp.concatenate([q[:, h * HEAD : (h + 1) * HEAD] for h in range(HEADS)], axis=0)
    heads = heads.astype(BF16)
    kv = jnp.concatenate([kv_ref[r] for r in range(rows)], axis=1)
    new = jnp.concatenate([fresh_ref[s].astype(F32) for s in range(steps)], axis=0).astype(BF16)

    sub = iota((both, rows * length), 0)
    lane = iota((both, rows * length), 1)
    limit = jnp.zeros_like(lane)
    for r in range(rows):
        limit = jnp.where(lane // length == r, len_ref[r], limit)
    valid = (lane // length == sub % rows) & (lane % length < limit)
    sub = iota((both, both), 0)
    lane = iota((both, both), 1)
    valid_new = (lane % rows == sub % rows) & (lane // rows <= sub // rows)

    old_s = (dot(heads, kv[:HEAD]) * scale).reshape(HEADS, both, rows * length)
    new_s = (nt_dot(heads, new[:, :HEAD]) * scale).reshape(HEADS, both, both)
    old_s = jnp.where(valid[None], old_s, -1e30)
    new_s = jnp.where(valid_new[None], new_s, -1e30)
    top = jnp.maximum(
        jnp.max(old_s, axis=-1, keepdims=True), jnp.max(new_s, axis=-1, keepdims=True)
    )
    old_e = jnp.exp(old_s - top)
    new_e = jnp.exp(new_s - top)
    total = jnp.sum(old_e, axis=-1, keepdims=True) + jnp.sum(new_e, axis=-1, keepdims=True)
    old_w = (old_e / total).reshape(HEADS * both, rows * length).astype(BF16)
    new_w = (new_e / total).reshape(HEADS * both, both).astype(BF16)
    attended = nt_dot(old_w, kv[HEAD:]) + dot(new_w, new[:, HEAD:])
    for h in range(HEADS):
        merged[:, h * HEAD : (h + 1) * HEAD] = attended[h * both : (h + 1) * both]
    hidden = jnp.concatenate([hid_ref[s].astype(F32) for s in range(steps)], axis=0)
    resid = hidden + merged[...]
    resid_ref[...] = resid
    meansq = jnp.mean(resid * resid, axis=-1, keepdims=True)
    gain = gain_ref[...].astype(F32)
    gain = jnp.concatenate([gain[i : i + 1] for i in range(width // LANES)], axis=1)
    normed = resid * lax.rsqrt(meansq + 1e-06) * gain
    for i, batch in enumerate(BATCHES):
        pieces = LINES // (len(batch) * CAP)
        piece = width // pieces
        stacked = jnp.concatenate(
            [normed[:, k * piece : (k + 1) * piece] for k in range(pieces)], axis=0
        ).astype(BF16)
        picks = picks_of(ids_ref, batch, steps, rows, permuted)
        sent = dot(picks, stacked).astype(BF16)
        for j in range(EXPERTS):
            outs[i * EXPERTS + j][0] = sent[j * LINES : (j + 1) * LINES]


def attend(permuted, cache_len, ids, queries, fresh, kv_cache, hidden_state, norm_gain):
    steps, rows, width = queries.shape
    chunks = []
    for batch in BATCHES:
        shape = (1, LINES, width * len(batch) * CAP // LINES)
        chunks += [jax.ShapeDtypeStruct(shape, BF16)] * EXPERTS
    kv = kv_cache.transpose(0, 2, 1)
    gain = norm_gain.reshape(width // LANES, LANES)
    results = pl.pallas_call(
        functools.partial(attend_kernel, permuted),
        out_shape=(jax.ShapeDtypeStruct((steps * rows, width), F32), *chunks),
        in_specs=[HBM] * 7,
        out_specs=(VMEM,) * (1 + len(chunks)),
        scratch_shapes=[
            pltpu.SMEM(cache_len.shape, jnp.int32),
            pltpu.SMEM(ids.shape, jnp.int32),
            pltpu.VMEM(queries.shape, BF16),
            pltpu.VMEM(fresh.shape, BF16),
            pltpu.VMEM(kv.shape, BF16),
            pltpu.VMEM(hidden_state.shape, BF16),
            pltpu.VMEM(gain.shape, BF16),
            pltpu.VMEM((steps * rows, width), F32),
            pltpu.SemaphoreType.DMA((7,)),
        ],
        compiler_params=pltpu.CompilerParams(vmem_limit_bytes=24 * MIB),
        cost_estimate=pl.CostEstimate(
            flops=300_000_000, bytes_accessed=2_000_000, transcendentals=131072
        ),
        name="attend",
    )(*in_hbm(cache_len, ids, queries, fresh, kv, hidden_state, gain))
    resid, chunks = results[0], results[1:]
    return resid, [chunks[i * EXPERTS : (i + 1) * EXPERTS] for i in range(len(BATCHES))]


def mixing(ids_ref, weight_ref, batch, steps, rows, chips, permuted):
    pieces = LINES // (len(batch) * CAP)
    both = len(batch) * rows
    shape = (both, chips * LINES)
    line = iota(shape, 1)
    sub = iota(shape, 0)
    expert = partner(permuted, line // LINES) // (chips // EXPERTS)
    where = iota((both, 1), 0) + batch[0] * rows
    named = jnp.zeros(shape, F32)
    mix = jnp.zeros(shape, F32)
    for k in range(TOP):
        hit = spread(ids_ref, k, where, steps, rows, -1) == expert
        weight = spread(weight_ref, k, where, steps, rows, 0.0)
        named = named + jnp.where(hit, 1.0, 0.0)
        mix = mix + jnp.where(hit, weight, 0.0)
    at = iota((both, both), 1)
    to = iota((both, both), 0)
    rank = dot(one_hot((at // rows == to // rows) & (at < to)), named.astype(BF16))
    same = (line // CAP) % len(batch) == sub // rows
    mix = jnp.where((rank == (line % CAP).astype(F32)) & same, mix, 0.0)
    high = mix.astype(BF16).astype(F32)
    middle = (mix - high).astype(BF16).astype(F32)
    low = mix - high - middle
    k_of = line // (len(batch) * CAP) % pieces
    parts = [
        jnp.where(k_of == k, part, 0.0) for part in (high, middle, low) for k in range(pieces)
    ]
    return jnp.concatenate(parts, axis=0).astype(BF16)


def stage_kernel(
    permuted, chips, steps, rows, ids_hbm, weight_hbm, gu_hbm, dn_hbm, gu, dn, *rest
):
    mixes = rest[: len(BATCHES)]
    ids_ref, weight_ref, small, large = rest[len(BATCHES) :]
    first = [
        pltpu.make_async_copy(ids_hbm, ids_ref, small.at[0]),
        pltpu.make_async_copy(weight_hbm, weight_ref, small.at[1]),
    ]
    hidden = dn.shape[0]
    step = hidden // 4
    second = []
    for i in range(4):
        part = pl.ds(i * step, step)
        second.append((gu_hbm.at[0, 0, part], gu.at[0, part]))
        second.append((gu_hbm.at[0, 1, part], gu.at[1, part]))
        second.append((dn_hbm.at[0, part], dn.at[part]))
    second = [pltpu.make_async_copy(a, b, large.at[i]) for i, (a, b) in enumerate(second)]
    for copy in first + second:
        copy.start()
    for copy in first:
        copy.wait()
    for batch, mix in zip(BATCHES, mixes):
        mix[...] = mixing(ids_ref, weight_ref, batch, steps, rows, chips, permuted)
    for copy in second:
        copy.wait()


def stage(permuted, chips, ids, weights, gate_up, down):
    _, steps, rows = ids.shape
    mixes = [
        jax.ShapeDtypeStruct((3 * LINES // CAP * rows, chips * LINES), BF16) for _ in BATCHES
    ]
    gu, dn, *mixes = pl.pallas_call(
        functools.partial(stage_kernel, permuted, chips, steps, rows),
        out_shape=(
            jax.ShapeDtypeStruct(gate_up.shape[1:], BF16),
            jax.ShapeDtypeStruct(down.shape[1:], BF16),
            *mixes,
        ),
        in_specs=[HBM] * 4,
        out_specs=(VMEM,) * (2 + len(mixes)),
        scratch_shapes=[
            pltpu.SMEM(ids.shape, jnp.int32),
            pltpu.SMEM(weights.shape, F32),
            pltpu.SemaphoreType.DMA((2,)),
            pltpu.SemaphoreType.DMA((12,)),
        ],
        compiler_params=pltpu.CompilerParams(vmem_limit_bytes=24 * MIB),
        cost_estimate=pl.CostEstimate(
            flops=1_000_000, bytes_accessed=22_000_000, transcendentals=0
        ),
        name="stage",
    )(*in_hbm(ids, weights, gate_up, down))
    return gu, dn, mixes


def expert_kernel(count, per, *refs):
    own_refs, other_refs = refs[:count], refs[count : 2 * count]
    gu, dn = refs[2 * count : 2 * count + 2]
    mine_refs = refs[2 * count + 2 : 3 * count + 2]
    theirs_refs = refs[3 * count + 2 :]
    piece = own_refs[0].shape[2]
    chips = sum(ref.shape[0] for ref in own_refs)
    pieces = LINES // per
    half = chips * per
    n = chips * LINES
    row = iota((n, n), 0)
    col = iota((n, n), 1)
    order = one_hot(col == row // per % chips * LINES + row // half * per + row % per)
    sides = []
    for refs_now in (own_refs, other_refs):
        lines = [ref[...].reshape(ref.shape[0] * LINES, piece) for ref in refs_now]
        sides.append(dot(order, jnp.concatenate(lines, axis=0)).astype(BF16))
    gate = upper = None
    for k in range(pieces):
        x = jnp.concatenate([side[k * half : (k + 1) * half] for side in sides], axis=0)
        cols = pl.ds(k * piece, piece)
        g, u = nt_dot(x, gu[0, :, cols]), nt_dot(x, gu[1, :, cols])
        gate, upper = (g, u) if k == 0 else (gate + g, upper + u)
    act = (gate / (1.0 + jnp.exp(-gate)) * upper).astype(BF16)
    mine = []
    theirs = []
    for k in range(pieces):
        part = dot(act, dn[:, k * piece : (k + 1) * piece]).astype(BF16)
        mine.append(part[:half])
        theirs.append(part[half:])
    back = one_hot(row == col // per % chips * LINES + col // half * per + col % per)
    for parts, refs_now in ((theirs, theirs_refs), (mine, mine_refs)):
        lines = dot(back, jnp.concatenate(parts, axis=0)).astype(BF16)
        start = 0
        for ref in refs_now:
            size = ref.shape[0] * LINES
            ref[...] = lines[start : start + size].reshape(ref.shape)
            start += size


def experts(own, other, gu, dn, per):
    count = len(own)
    shapes = tuple(jax.ShapeDtypeStruct(x.shape, BF16) for x in own)
    results = pl.pallas_call(
        functools.partial(expert_kernel, count, per),
        out_shape=shapes + shapes,
        in_specs=[VMEM] * (2 * count + 2),
        out_specs=(VMEM,) * (2 * count),
        compiler_params=pltpu.CompilerParams(vmem_limit_bytes=32 * MIB),
        cost_estimate=pl.CostEstimate(
            flops=800_000_000, bytes_accessed=12_000_000, transcendentals=16384
        ),
        name="experts",
    )(*own, *other, gu, dn)
    return results[:count], results[count:]


def combine_kernel(counts, resid_ref, *refs):
    out_ref = refs[-1]
    _, rows, width = out_ref.shape
    start = 0
    for batch, count in zip(BATCHES, counts):
        left = refs[start][...]
        back_refs = refs[start + 1 : start + 1 + count]
        start += 1 + count
        piece = back_refs[0].shape[2]
        pieces = width // piece
        both = len(batch) * rows
        lines = [ref[...].reshape(ref.shape[0] * LINES, piece) for ref in back_refs]
        product = dot(left, jnp.concatenate(lines, axis=0))
        n = pieces * both
        total = product[:n] + product[n : 2 * n] + product[2 * n :]
        first = batch[0] * rows
        for k in range(pieces):
            cols = pl.ds(k * piece, piece)
            done = resid_ref[first : first + both, cols] + total[k * both : (k + 1) * both]
            done = done.astype(BF16)
            for i, s in enumerate(batch):
                out_ref[s, :, cols] = done[i * rows : (i + 1) * rows]


def combine(shape, resid, mixes, backs):
    operands = [x for mix, back in zip(mixes, backs) for x in (mix, *back)]
    return pl.pallas_call(
        functools.partial(combine_kernel, [len(back) for back in backs]),
        out_shape=jax.ShapeDtypeStruct(shape, BF16),
        in_specs=[VMEM] * (1 + len(operands)),
        out_specs=VMEM,
        compiler_params=pltpu.CompilerParams(vmem_limit_bytes=24 * MIB),
        cost_estimate=pl.CostEstimate(
            flops=100_000_000, bytes_accessed=1_000_000, transcendentals=0
        ),
        name="combine",
    )(resid, *operands)


def per_device(
    queries,
    fresh,
    kv_cache,
    cache_len,
    hidden_state,
    norm_gain,
    expert_ids,
    route_weight,
    gate_up,
    down,
):
    owners = lax.axis_size("afd")
    chips = owners // 2
    chips_per_expert = chips // EXPERTS
    permuted = chips == EXPERTS
    swap = [(i, i ^ 1) for i in range(owners)]

    def trade(chunk, n):
        turns = [(i, ((i // 2) ^ TURNS[i % 2][n]) * 2 + i % 2) for i in range(owners)]
        return lax.ppermute(chunk, "afd", turns)

    def to_chips(chunks):
        same_core = [[2 * p + c for p in range(chips)] for c in range(2)]
        whole = jnp.concatenate(chunks, axis=0)
        return [
            lax.all_to_all(
                whole, "afd", split_axis=0, concat_axis=0, axis_index_groups=same_core, tiled=True
            )
        ]

    ids = expert_ids.transpose(2, 0, 1)
    weights = route_weight.transpose(2, 0, 1)
    resid, sent = attend(
        permuted, cache_len, ids, queries, fresh, kv_cache, hidden_state, norm_gain
    )
    gu, dn, mixes = stage(permuted, chips, ids, weights, gate_up, down)
    backs = []
    for batch, chunks in zip(BATCHES, sent):
        if permuted:
            *late, gu, dn = lax.optimization_barrier((*chunks[STAGED:], gu, dn))
            chunks = [*chunks[:STAGED], *late]
            own = [chunks[0]] + [trade(chunks[n], n) for n in range(1, chips)]
        else:
            own = to_chips([jnp.repeat(chunk, chips_per_expert, axis=0) for chunk in chunks])
        other = [lax.ppermute(x, "afd", swap) for x in own]
        mine, theirs = experts(own, other, gu, dn, len(batch) * CAP)
        summed = [
            (a.astype(F32) + lax.ppermute(b, "afd", swap).astype(F32)).astype(BF16)
            for a, b in zip(mine, theirs)
        ]
        if permuted:
            backs.append([summed[0]] + [trade(summed[n], n) for n in range(1, chips)])
        else:
            backs.append(to_chips(summed))
    return combine(queries.shape, resid, mixes, backs)


def solution(mesh):
    placed = (
        P(None, ("group", "afd"), None),
        P(None, ("group", "afd"), None),
        P(("group", "afd"), None, None),
        P(("group", "afd")),
        P(None, ("group", "afd"), None),
        P(),
        P(None, ("group", "afd"), None),
        P(None, ("group", "afd"), None),
        P("afd", None, None, None),
        P("afd", None, None),
    )
    return jax.shard_map(
        per_device,
        mesh=mesh,
        in_specs=placed,
        out_specs=P(None, ("group", "afd"), None),
        check_vma=False,
    )
```

```python
import functools
import jax
import jax.numpy as jnp
from jax import lax
from jax.experimental import pallas as pl
from jax.experimental.pallas import tpu as pltpu
from jax.sharding import PartitionSpec as P

HEADS = 32
HEAD = 224
EXPERTS = 8
TOP = 3
CAP = 2
PIECES = 4
LANES = 128
PARTS = 3
F32 = jnp.float32
BF16 = jnp.bfloat16
MIB = 1 << 20
VMEM = pl.BlockSpec(memory_space=pltpu.VMEM)
HBM = pl.BlockSpec(memory_space=pltpu.HBM)
TOGETHER = 4


def iota(shape, dim):
    return lax.broadcasted_iota(jnp.int32, shape, dim)


def in_hbm(*arrays):
    return [pltpu.with_memory_space_constraint(x, pltpu.HBM) for x in arrays]


def nt_dot(a, b):
    return lax.dot_general(a, b, (((1,), (1,)), ((), ())), preferred_element_type=F32)


def dot(a, b):
    return jnp.dot(a, b, preferred_element_type=F32)


def one_hot(mask):
    return jnp.where(mask, 1.0, 0.0).astype(BF16)


def distance(turn, core, chips):
    return (2 * turn) ^ (core * (chips - 1))


def expert_at(turn, chips):
    place = lax.axis_index("afd")
    return (distance(turn, place % 2, chips) ^ (place // 2)) // (chips // EXPERTS)


def spread(ref, k, where, steps, rows, empty):
    out = jnp.full(where.shape, empty)
    for s in range(steps):
        for r in range(rows):
            out = jnp.where(where == s * rows + r, ref[k, s, r], out)
    return out


def tail(ids_ref, weight_ref, steps, rows):
    both = steps * rows
    lane = iota((both, LANES), 1)
    where = iota((both, 1), 0)
    mix = jnp.zeros((both, LANES), F32)
    named = jnp.zeros((both, LANES), F32)
    for k in range(TOP):
        hit = spread(ids_ref, k, where, steps, rows, -1) == lane % EXPERTS
        mix = mix + jnp.where(hit, spread(weight_ref, k, where, steps, rows, 0.0), 0.0)
        named = named + jnp.where(hit, 1.0, 0.0)
    out = jnp.where(lane // EXPERTS == PARTS, named, 0.0)
    for part in range(PARTS):
        term = mix.astype(BF16).astype(F32)
        out = jnp.where(lane // EXPERTS == part, term, out)
        mix = mix - term
    return out.astype(BF16)


def attend_kernel(
    len_hbm,
    ids_hbm,
    weight_hbm,
    q_hbm,
    fresh_hbm,
    kv_hbm,
    hid_hbm,
    gain_hbm,
    resid_ref,
    out_ref,
    len_ref,
    ids_ref,
    weight_ref,
    q_ref,
    fresh_ref,
    kv_ref,
    hid_ref,
    gain_ref,
    merged,
    sems,
):
    copies = [
        pltpu.make_async_copy(source, target, sems.at[i])
        for i, (source, target) in enumerate(
            (
                (q_hbm, q_ref),
                (kv_hbm, kv_ref),
                (len_hbm, len_ref),
                (ids_hbm, ids_ref),
                (weight_hbm, weight_ref),
                (fresh_hbm, fresh_ref),
                (hid_hbm, hid_ref),
                (gain_hbm, gain_ref),
            )
        )
    ]
    for copy in copies:
        copy.start()
    steps, rows, width = q_ref.shape
    length = kv_ref.shape[2]
    both = steps * rows
    scale = HEAD ** (-0.5)
    for copy in copies:
        copy.wait()
    q = jnp.concatenate([q_ref[s].astype(F32) for s in range(steps)], axis=0)
    heads = jnp.concatenate([q[:, h * HEAD : (h + 1) * HEAD] for h in range(HEADS)], axis=0)
    heads = heads.astype(BF16)
    kv = jnp.concatenate([kv_ref[r] for r in range(rows)], axis=1)
    new = jnp.concatenate([fresh_ref[s].astype(F32) for s in range(steps)], axis=0).astype(BF16)

    sub = iota((both, rows * length), 0)
    lane = iota((both, rows * length), 1)
    limit = jnp.zeros_like(lane)
    for r in range(rows):
        limit = jnp.where(lane // length == r, len_ref[r], limit)
    valid = (lane // length == sub % rows) & (lane % length < limit)
    sub = iota((both, both), 0)
    lane = iota((both, both), 1)
    valid_new = (lane % rows == sub % rows) & (lane // rows <= sub // rows)

    old_s = (dot(heads, kv[:HEAD]) * scale).reshape(HEADS, both, rows * length)
    new_s = (nt_dot(heads, new[:, :HEAD]) * scale).reshape(HEADS, both, both)
    old_s = jnp.where(valid[None], old_s, -1e30)
    new_s = jnp.where(valid_new[None], new_s, -1e30)
    top = jnp.maximum(
        jnp.max(old_s, axis=-1, keepdims=True), jnp.max(new_s, axis=-1, keepdims=True)
    )
    old_e = jnp.exp(old_s - top)
    new_e = jnp.exp(new_s - top)
    total = jnp.sum(old_e, axis=-1, keepdims=True) + jnp.sum(new_e, axis=-1, keepdims=True)
    old_w = (old_e / total).reshape(HEADS * both, rows * length).astype(BF16)
    new_w = (new_e / total).reshape(HEADS * both, both).astype(BF16)
    attended = nt_dot(old_w, kv[HEAD:]) + dot(new_w, new[:, HEAD:])
    for h in range(HEADS):
        merged[:, h * HEAD : (h + 1) * HEAD] = attended[h * both : (h + 1) * both]
    hidden = jnp.concatenate([hid_ref[s].astype(F32) for s in range(steps)], axis=0)
    resid = hidden + merged[...]
    resid_ref[...] = resid
    meansq = jnp.mean(resid * resid, axis=-1, keepdims=True)
    gain = gain_ref[...].astype(F32)
    gain = jnp.concatenate([gain[i : i + 1] for i in range(width // LANES)], axis=1)
    normed = resid * lax.rsqrt(meansq + 1e-06) * gain
    out_ref[:, :width] = normed.astype(BF16)
    out_ref[:, width:] = tail(ids_ref, weight_ref, steps, rows)


def attend(cache_len, ids, weights, queries, fresh, kv_cache, hidden_state, norm_gain):
    steps, rows, width = queries.shape
    kv = kv_cache.transpose(0, 2, 1)
    gain = norm_gain.reshape(width // LANES, LANES)
    return pl.pallas_call(
        attend_kernel,
        out_shape=(
            jax.ShapeDtypeStruct((steps * rows, width), F32),
            jax.ShapeDtypeStruct((steps * rows, width + LANES), BF16),
        ),
        in_specs=[HBM] * 8,
        out_specs=(VMEM, VMEM),
        scratch_shapes=[
            pltpu.SMEM(cache_len.shape, jnp.int32),
            pltpu.SMEM(ids.shape, jnp.int32),
            pltpu.SMEM(weights.shape, F32),
            pltpu.VMEM(queries.shape, BF16),
            pltpu.VMEM(fresh.shape, BF16),
            pltpu.VMEM(kv.shape, BF16),
            pltpu.VMEM(hidden_state.shape, BF16),
            pltpu.VMEM(gain.shape, BF16),
            pltpu.VMEM((steps * rows, width), F32),
            pltpu.SemaphoreType.DMA((8,)),
        ],
        compiler_params=pltpu.CompilerParams(vmem_limit_bytes=24 * MIB),
        cost_estimate=pl.CostEstimate(
            flops=300_000_000, bytes_accessed=2_000_000, transcendentals=131072
        ),
        name="attend",
    )(*in_hbm(cache_len, ids, weights, queries, fresh, kv, hidden_state, gain))


def pack_kernel(steps, chips, own_ref, other_ref, *outs):
    both, width = own_ref.shape
    width -= LANES
    rows = both // steps
    piece = width // PIECES
    side_lines = steps * CAP
    lines = PIECES * 2 * side_lines
    tails = [ref[:, width:].astype(F32) for ref in (own_ref, other_ref)]
    tails = jnp.concatenate(tails * PIECES, axis=0).astype(BF16)
    count = 2 * both * PIECES
    row = iota((len(outs) * lines, LANES), 0)
    lane = iota((len(outs) * lines, LANES), 1)
    wanted = one_hot(lane == PARTS * EXPERTS + expert_at(row // lines, chips))
    named = nt_dot(wanted, tails)
    at = iota((count, count), 0)
    to = iota((count, count), 1)
    before = one_hot((at // rows == to // rows) & (at < to))
    rank = dot(named.astype(BF16), before)
    line = iota(named.shape, 0)
    col = iota(named.shape, 1)
    same = (line // CAP) % (lines // CAP) == col // rows
    picks = one_hot(same & (named > 0.5) & (rank == (line % CAP).astype(F32)))
    parts = [ref[:, :width].astype(F32) for ref in (own_ref, other_ref)]
    stacked = jnp.concatenate(
        [part[:, k * piece : (k + 1) * piece] for k in range(PIECES) for part in parts], axis=0
    ).astype(BF16)
    sent = dot(picks, stacked).astype(BF16)
    for t, out in enumerate(outs):
        out[...] = sent[t * lines : (t + 1) * lines]


def pack(steps, chips, own, other):
    both, width = own.shape
    shape = (PIECES * 2 * steps * CAP, (width - LANES) // PIECES)
    turns = chips // 2
    return pl.pallas_call(
        functools.partial(pack_kernel, steps, chips),
        out_shape=[jax.ShapeDtypeStruct(shape, BF16)] * turns,
        in_specs=[VMEM] * 2,
        out_specs=[VMEM] * turns,
        compiler_params=pltpu.CompilerParams(vmem_limit_bytes=24 * MIB),
        cost_estimate=pl.CostEstimate(
            flops=50_000_000, bytes_accessed=2_000_000, transcendentals=0
        ),
        name="pack",
    )(own, other)


def mixing(steps, chips, own_ref, other_ref):
    both, width = own_ref.shape
    width -= LANES
    rows = both // steps
    lines = PIECES * 2 * steps * CAP
    tails = [ref[:, width:].astype(F32) for ref in (own_ref, other_ref)]
    tails = jnp.concatenate(tails, axis=0).astype(BF16)
    count = chips // 2 * lines
    lane = iota((LANES, count), 0)
    expert = expert_at(iota((LANES, count), 1) // lines, chips)
    found = [dot(tails, one_hot(lane == part * EXPERTS + expert)) for part in range(PARTS + 1)]
    at = iota((2 * both, 2 * both), 1)
    to = iota((2 * both, 2 * both), 0)
    rank = dot(one_hot((at // rows == to // rows) & (at < to)), found[PARTS].astype(BF16))
    line = iota((2 * both, count), 1)
    row = iota((2 * both, count), 0)
    same = (line // CAP) % (2 * steps) == row // rows
    slot = same & (rank == (line % CAP).astype(F32))
    k_of = line // (2 * steps * CAP) % PIECES
    parts = [
        jnp.where(slot & (k_of == k), found[part], 0.0)
        for part in range(PARTS)
        for k in range(PIECES)
    ]
    return jnp.concatenate(parts, axis=0).astype(BF16)


def stage_kernel(steps, chips, own_ref, other_ref, gu_hbm, dn_hbm, gu, dn, mix_ref, sems):
    step = dn.shape[0] // 4
    pairs = []
    for i in range(4):
        part = pl.ds(i * step, step)
        pairs.append((gu_hbm.at[0, 0, part], gu.at[0, part]))
        pairs.append((gu_hbm.at[0, 1, part], gu.at[1, part]))
        pairs.append((dn_hbm.at[0, part], dn.at[part]))
    copies = [pltpu.make_async_copy(a, b, sems.at[i]) for i, (a, b) in enumerate(pairs)]
    for copy in copies:
        copy.start()
    mix_ref[...] = mixing(steps, chips, own_ref, other_ref)
    for copy in copies:
        copy.wait()


def stage(steps, chips, own, other, gate_up, down):
    lines = PIECES * 2 * steps * CAP
    return pl.pallas_call(
        functools.partial(stage_kernel, steps, chips),
        out_shape=(
            jax.ShapeDtypeStruct(gate_up.shape[1:], BF16),
            jax.ShapeDtypeStruct(down.shape[1:], BF16),
            jax.ShapeDtypeStruct((PARTS * PIECES * 2 * own.shape[0], chips // 2 * lines), BF16),
        ),
        in_specs=[VMEM, VMEM, HBM, HBM],
        out_specs=(VMEM,) * 3,
        scratch_shapes=[pltpu.SemaphoreType.DMA((12,))],
        compiler_params=pltpu.CompilerParams(vmem_limit_bytes=24 * MIB),
        cost_estimate=pl.CostEstimate(
            flops=10_000_000, bytes_accessed=22_000_000, transcendentals=0
        ),
        name="stage",
    )(own, other, *in_hbm(gate_up, down))


def expert_kernel(turns, *refs):
    own_refs, other_refs = refs[:turns], refs[turns : 2 * turns]
    gu, dn = refs[2 * turns : 2 * turns + 2]
    mine_refs = refs[2 * turns + 2 : 3 * turns + 2]
    theirs_refs = refs[3 * turns + 2 :]
    lines, piece = own_refs[0].shape
    per = lines // PIECES
    half = turns * per
    n = turns * lines
    row = iota((n, n), 0)
    col = iota((n, n), 1)
    order = one_hot(col == row // per % turns * lines + row // half * per + row % per)
    sides = [
        dot(order, jnp.concatenate([ref[...] for ref in now], axis=0)).astype(BF16)
        for now in (own_refs, other_refs)
    ]
    gate = upper = None
    for k in range(PIECES):
        x = jnp.concatenate([side[k * half : (k + 1) * half] for side in sides], axis=0)
        cols = pl.ds(k * piece, piece)
        g, u = nt_dot(x, gu[0, :, cols]), nt_dot(x, gu[1, :, cols])
        gate, upper = (g, u) if k == 0 else (gate + g, upper + u)
    act = (gate / (1.0 + jnp.exp(-gate)) * upper).astype(BF16)
    mine = []
    theirs = []
    for k in range(PIECES):
        part = dot(act, dn[:, k * piece : (k + 1) * piece]).astype(BF16)
        mine.append(part[:half])
        theirs.append(part[half:])
    back = one_hot(row == col // per % turns * lines + col // half * per + col % per)
    for parts, now in ((theirs, theirs_refs), (mine, mine_refs)):
        out = dot(back, jnp.concatenate(parts, axis=0)).astype(BF16)
        for t, ref in enumerate(now):
            ref[...] = out[t * lines : (t + 1) * lines]


def experts(own, other, gu, dn):
    turns = len(own)
    shape = jax.ShapeDtypeStruct(own[0].shape, BF16)
    results = pl.pallas_call(
        functools.partial(expert_kernel, turns),
        out_shape=[shape] * (2 * turns),
        in_specs=[VMEM] * (2 * turns + 2),
        out_specs=[VMEM] * (2 * turns),
        compiler_params=pltpu.CompilerParams(vmem_limit_bytes=32 * MIB),
        cost_estimate=pl.CostEstimate(
            flops=800_000_000, bytes_accessed=12_000_000, transcendentals=16384
        ),
        name="experts",
    )(*own, *other, gu, dn)
    return results[:turns], results[turns:]


def combine_kernel(mix_ref, resid_ref, *refs):
    back_refs, (kept_ref, sent_ref) = refs[:-2], refs[-2:]
    both = resid_ref.shape[0]
    piece = back_refs[0].shape[1]
    product = dot(mix_ref[...], jnp.concatenate([ref[...] for ref in back_refs], axis=0))
    n = PIECES * 2 * both
    total = product[:n] + product[n : 2 * n] + product[2 * n :]
    for k in range(PIECES):
        cols = pl.ds(k * piece, piece)
        first = k * 2 * both
        kept_ref[:, cols] = resid_ref[:, cols] + total[first : first + both]
        sent_ref[:, cols] = total[first + both : first + 2 * both].astype(BF16)


def combine(mix, resid, backs):
    return pl.pallas_call(
        combine_kernel,
        out_shape=(
            jax.ShapeDtypeStruct(resid.shape, F32),
            jax.ShapeDtypeStruct(resid.shape, BF16),
        ),
        in_specs=[VMEM] * (2 + len(backs)),
        out_specs=(VMEM, VMEM),
        compiler_params=pltpu.CompilerParams(vmem_limit_bytes=24 * MIB),
        cost_estimate=pl.CostEstimate(
            flops=100_000_000, bytes_accessed=1_000_000, transcendentals=0
        ),
        name="combine",
    )(mix, resid, *backs)


def finish_kernel(kept_ref, other_ref, out_ref):
    steps, rows, _ = out_ref.shape
    done = (kept_ref[...] + other_ref[...].astype(F32)).astype(BF16)
    for s in range(steps):
        out_ref[s] = done[s * rows : (s + 1) * rows]


def finish(shape, kept, other):
    return pl.pallas_call(
        finish_kernel,
        out_shape=jax.ShapeDtypeStruct(shape, BF16),
        in_specs=[VMEM, VMEM],
        out_specs=VMEM,
        compiler_params=pltpu.CompilerParams(vmem_limit_bytes=24 * MIB),
        cost_estimate=pl.CostEstimate(flops=100_000, bytes_accessed=500_000, transcendentals=0),
        name="finish",
    )(kept, other)


def per_device(
    queries,
    fresh,
    kv_cache,
    cache_len,
    hidden_state,
    norm_gain,
    expert_ids,
    route_weight,
    gate_up,
    down,
):
    steps = queries.shape[0]
    owners = lax.axis_size("afd")
    chips = owners // 2
    turns = chips // 2
    cores = [(i, i ^ 1) for i in range(owners)]

    def swap(x):
        return lax.ppermute(x, "afd", cores)

    def trade(x, t):
        to = [(i, (i // 2 ^ distance(t, i % 2, chips)) * 2 + i % 2) for i in range(owners)]
        return lax.ppermute(x, "afd", to)

    ids = expert_ids.transpose(2, 0, 1)
    weights = route_weight.transpose(2, 0, 1)
    resid, normed = attend(
        cache_len, ids, weights, queries, fresh, kv_cache, hidden_state, norm_gain
    )
    normed_other = swap(normed)
    sent = pack(steps, chips, normed, normed_other)
    own = [trade(sent[t], t) for t in range(turns)]
    gu, dn, mix = stage(steps, chips, normed, normed_other, gate_up, down)
    own[0], gu, dn = lax.optimization_barrier((own[0], gu, dn))
    other = [swap(x) for x in own]
    summed = []
    for t in range(0, turns, TOGETHER):
        mine, theirs = experts(own[t : t + TOGETHER], other[t : t + TOGETHER], gu, dn)
        summed += [
            (a.astype(F32) + swap(b).astype(F32)).astype(BF16) for a, b in zip(mine, theirs)
        ]
    backs = [trade(summed[t], t) for t in range(turns)]
    kept, given = combine(mix, resid, backs)
    return finish(queries.shape, kept, swap(given))


def solution(mesh):
    placed = (
        P(None, ("group", "afd"), None),
        P(None, ("group", "afd"), None),
        P(("group", "afd"), None, None),
        P(("group", "afd")),
        P(None, ("group", "afd"), None),
        P(),
        P(None, ("group", "afd"), None),
        P(None, ("group", "afd"), None),
        P("afd", None, None, None),
        P("afd", None, None),
    )
    return jax.shard_map(
        per_device,
        mesh=mesh,
        in_specs=placed,
        out_specs=P(None, ("group", "afd"), None),
        check_vma=False,
    )
```

```python
import functools
import jax
import jax.numpy as jnp
from jax import lax
from jax.experimental import pallas as pl
from jax.experimental.pallas import tpu as pltpu
from jax.sharding import PartitionSpec as P

HEADS = 32
HEAD = 224
EXPERTS = 8
TOP = 3
CAP = 2
PIECES = 4
LANES = 128
PARTS = 3
F32 = jnp.float32
BF16 = jnp.bfloat16
MIB = 1 << 20
VMEM = pl.BlockSpec(memory_space=pltpu.VMEM)
HBM = pl.BlockSpec(memory_space=pltpu.HBM)
TOGETHER = 4


def iota(shape, dim):
    return lax.broadcasted_iota(jnp.int32, shape, dim)


def in_hbm(*arrays):
    return [pltpu.with_memory_space_constraint(x, pltpu.HBM) for x in arrays]


def nt_dot(a, b):
    return lax.dot_general(a, b, (((1,), (1,)), ((), ())), preferred_element_type=F32)


def dot(a, b):
    return jnp.dot(a, b, preferred_element_type=F32)


def one_hot(mask):
    return jnp.where(mask, 1.0, 0.0).astype(BF16)


def distance(turn, core, chips):
    return (2 * turn) ^ (core * (chips - 1))


def expert_at(turn, chips):
    place = lax.axis_index("afd")
    return (distance(turn, place % 2, chips) ^ (place // 2)) // (chips // EXPERTS)


def spread(ref, k, where, steps, rows, empty):
    out = jnp.full(where.shape, empty)
    for s in range(steps):
        for r in range(rows):
            out = jnp.where(where == s * rows + r, ref[k, s, r], out)
    return out


def tail(ids_ref, weight_ref, steps, rows):
    both = steps * rows
    lane = iota((both, LANES), 1)
    where = iota((both, 1), 0)
    mix = jnp.zeros((both, LANES), F32)
    named = jnp.zeros((both, LANES), F32)
    for k in range(TOP):
        hit = spread(ids_ref, k, where, steps, rows, -1) == lane % EXPERTS
        mix = mix + jnp.where(hit, spread(weight_ref, k, where, steps, rows, 0.0), 0.0)
        named = named + jnp.where(hit, 1.0, 0.0)
    out = jnp.where(lane // EXPERTS == PARTS, named, 0.0)
    for part in range(PARTS):
        term = mix.astype(BF16).astype(F32)
        out = jnp.where(lane // EXPERTS == part, term, out)
        mix = mix - term
    return out.astype(BF16)


def attend_kernel(
    len_hbm,
    ids_hbm,
    weight_hbm,
    q_hbm,
    fresh_hbm,
    kv_hbm,
    hid_hbm,
    gain_hbm,
    resid_ref,
    out_ref,
    len_ref,
    ids_ref,
    weight_ref,
    q_ref,
    fresh_ref,
    kv_ref,
    hid_ref,
    gain_ref,
    merged,
    sems,
):
    copies = [
        pltpu.make_async_copy(source, target, sems.at[i])
        for i, (source, target) in enumerate(
            (
                (q_hbm, q_ref),
                (kv_hbm, kv_ref),
                (len_hbm, len_ref),
                (ids_hbm, ids_ref),
                (weight_hbm, weight_ref),
                (fresh_hbm, fresh_ref),
                (hid_hbm, hid_ref),
                (gain_hbm, gain_ref),
            )
        )
    ]
    for copy in copies:
        copy.start()
    steps, rows, width = q_ref.shape
    length = kv_ref.shape[2]
    both = steps * rows
    scale = HEAD ** (-0.5)
    for copy in copies:
        copy.wait()
    q = jnp.concatenate([q_ref[s].astype(F32) for s in range(steps)], axis=0)
    heads = jnp.concatenate([q[:, h * HEAD : (h + 1) * HEAD] for h in range(HEADS)], axis=0)
    heads = heads.astype(BF16)
    kv = jnp.concatenate([kv_ref[r] for r in range(rows)], axis=1)
    new = jnp.concatenate([fresh_ref[s].astype(F32) for s in range(steps)], axis=0).astype(BF16)

    sub = iota((both, rows * length), 0)
    lane = iota((both, rows * length), 1)
    limit = jnp.zeros_like(lane)
    for r in range(rows):
        limit = jnp.where(lane // length == r, len_ref[r], limit)
    valid = (lane // length == sub % rows) & (lane % length < limit)
    sub = iota((both, both), 0)
    lane = iota((both, both), 1)
    valid_new = (lane % rows == sub % rows) & (lane // rows <= sub // rows)

    old_s = (dot(heads, kv[:HEAD]) * scale).reshape(HEADS, both, rows * length)
    new_s = (nt_dot(heads, new[:, :HEAD]) * scale).reshape(HEADS, both, both)
    old_s = jnp.where(valid[None], old_s, -1e30)
    new_s = jnp.where(valid_new[None], new_s, -1e30)
    top = jnp.maximum(
        jnp.max(old_s, axis=-1, keepdims=True), jnp.max(new_s, axis=-1, keepdims=True)
    )
    old_e = jnp.exp(old_s - top)
    new_e = jnp.exp(new_s - top)
    total = jnp.sum(old_e, axis=-1, keepdims=True) + jnp.sum(new_e, axis=-1, keepdims=True)
    old_w = (old_e / total).reshape(HEADS * both, rows * length).astype(BF16)
    new_w = (new_e / total).reshape(HEADS * both, both).astype(BF16)
    attended = nt_dot(old_w, kv[HEAD:]) + dot(new_w, new[:, HEAD:])
    for h in range(HEADS):
        merged[:, h * HEAD : (h + 1) * HEAD] = attended[h * both : (h + 1) * both]
    hidden = jnp.concatenate([hid_ref[s].astype(F32) for s in range(steps)], axis=0)
    resid = hidden + merged[...]
    resid_ref[...] = resid
    meansq = jnp.mean(resid * resid, axis=-1, keepdims=True)
    gain = gain_ref[...].astype(F32)
    gain = jnp.concatenate([gain[i : i + 1] for i in range(width // LANES)], axis=1)
    normed = resid * lax.rsqrt(meansq + 1e-06) * gain
    out_ref[:, :width] = normed.astype(BF16)
    out_ref[:, width:] = tail(ids_ref, weight_ref, steps, rows)


def attend(cache_len, ids, weights, queries, fresh, kv_cache, hidden_state, norm_gain):
    steps, rows, width = queries.shape
    kv = kv_cache.transpose(0, 2, 1)
    gain = norm_gain.reshape(width // LANES, LANES)
    return pl.pallas_call(
        attend_kernel,
        out_shape=(
            jax.ShapeDtypeStruct((steps * rows, width), F32),
            jax.ShapeDtypeStruct((steps * rows, width + LANES), BF16),
        ),
        in_specs=[HBM] * 8,
        out_specs=(VMEM, VMEM),
        scratch_shapes=[
            pltpu.SMEM(cache_len.shape, jnp.int32),
            pltpu.SMEM(ids.shape, jnp.int32),
            pltpu.SMEM(weights.shape, F32),
            pltpu.VMEM(queries.shape, BF16),
            pltpu.VMEM(fresh.shape, BF16),
            pltpu.VMEM(kv.shape, BF16),
            pltpu.VMEM(hidden_state.shape, BF16),
            pltpu.VMEM(gain.shape, BF16),
            pltpu.VMEM((steps * rows, width), F32),
            pltpu.SemaphoreType.DMA((8,)),
        ],
        compiler_params=pltpu.CompilerParams(vmem_limit_bytes=24 * MIB),
        cost_estimate=pl.CostEstimate(
            flops=300_000_000, bytes_accessed=2_000_000, transcendentals=131072
        ),
        name="attend",
    )(*in_hbm(cache_len, ids, weights, queries, fresh, kv, hidden_state, gain))


def pack_kernel(steps, chips, own_ref, other_ref, *outs):
    both, width = own_ref.shape
    width -= LANES
    rows = both // steps
    piece = width // PIECES
    side_lines = steps * CAP
    lines = PIECES * 2 * side_lines
    tails = [ref[:, width:].astype(F32) for ref in (own_ref, other_ref)]
    tails = jnp.concatenate(tails * PIECES, axis=0).astype(BF16)
    count = 2 * both * PIECES
    row = iota((len(outs) * lines, LANES), 0)
    lane = iota((len(outs) * lines, LANES), 1)
    wanted = one_hot(lane == PARTS * EXPERTS + expert_at(row // lines, chips))
    named = nt_dot(wanted, tails)
    at = iota((count, count), 0)
    to = iota((count, count), 1)
    before = one_hot((at // rows == to // rows) & (at < to))
    rank = dot(named.astype(BF16), before)
    line = iota(named.shape, 0)
    col = iota(named.shape, 1)
    same = (line // CAP) % (lines // CAP) == col // rows
    picks = one_hot(same & (named > 0.5) & (rank == (line % CAP).astype(F32)))
    parts = [ref[:, :width].astype(F32) for ref in (own_ref, other_ref)]
    stacked = jnp.concatenate(
        [part[:, k * piece : (k + 1) * piece] for k in range(PIECES) for part in parts], axis=0
    ).astype(BF16)
    sent = dot(picks, stacked).astype(BF16)
    for t, out in enumerate(outs):
        out[...] = sent[t * lines : (t + 1) * lines]


def pack(steps, chips, own, other):
    both, width = own.shape
    shape = (PIECES * 2 * steps * CAP, (width - LANES) // PIECES)
    turns = chips // 2
    return pl.pallas_call(
        functools.partial(pack_kernel, steps, chips),
        out_shape=[jax.ShapeDtypeStruct(shape, BF16)] * turns,
        in_specs=[VMEM] * 2,
        out_specs=[VMEM] * turns,
        compiler_params=pltpu.CompilerParams(vmem_limit_bytes=24 * MIB),
        cost_estimate=pl.CostEstimate(
            flops=50_000_000, bytes_accessed=2_000_000, transcendentals=0
        ),
        name="pack",
    )(own, other)


def mixing(steps, chips, own_ref, other_ref):
    both, width = own_ref.shape
    width -= LANES
    rows = both // steps
    lines = PIECES * 2 * steps * CAP
    tails = [ref[:, width:].astype(F32) for ref in (own_ref, other_ref)]
    tails = jnp.concatenate(tails, axis=0).astype(BF16)
    count = chips // 2 * lines
    lane = iota((LANES, count), 0)
    expert = expert_at(iota((LANES, count), 1) // lines, chips)
    found = [dot(tails, one_hot(lane == part * EXPERTS + expert)) for part in range(PARTS + 1)]
    at = iota((2 * both, 2 * both), 1)
    to = iota((2 * both, 2 * both), 0)
    rank = dot(one_hot((at // rows == to // rows) & (at < to)), found[PARTS].astype(BF16))
    line = iota((2 * both, count), 1)
    row = iota((2 * both, count), 0)
    same = (line // CAP) % (2 * steps) == row // rows
    slot = same & (rank == (line % CAP).astype(F32))
    k_of = line // (2 * steps * CAP) % PIECES
    parts = [
        jnp.where(slot & (k_of == k), found[part], 0.0)
        for part in range(PARTS)
        for k in range(PIECES)
    ]
    return jnp.concatenate(parts, axis=0).astype(BF16)


def stage_kernel(steps, chips, own_ref, other_ref, gu_hbm, dn_hbm, gu, dn, mix_ref, sems):
    step = dn.shape[0] // 4
    pairs = []
    for i in range(4):
        part = pl.ds(i * step, step)
        pairs.append((gu_hbm.at[0, 0, part], gu.at[0, part]))
        pairs.append((gu_hbm.at[0, 1, part], gu.at[1, part]))
        pairs.append((dn_hbm.at[0, part], dn.at[part]))
    copies = [pltpu.make_async_copy(a, b, sems.at[i]) for i, (a, b) in enumerate(pairs)]
    for copy in copies:
        copy.start()
    mix_ref[...] = mixing(steps, chips, own_ref, other_ref)
    for copy in copies:
        copy.wait()


def stage(steps, chips, own, other, gate_up, down):
    lines = PIECES * 2 * steps * CAP
    return pl.pallas_call(
        functools.partial(stage_kernel, steps, chips),
        out_shape=(
            jax.ShapeDtypeStruct(gate_up.shape[1:], BF16),
            jax.ShapeDtypeStruct(down.shape[1:], BF16),
            jax.ShapeDtypeStruct((PARTS * PIECES * 2 * own.shape[0], chips // 2 * lines), BF16),
        ),
        in_specs=[VMEM, VMEM, HBM, HBM],
        out_specs=(VMEM,) * 3,
        scratch_shapes=[pltpu.SemaphoreType.DMA((12,))],
        compiler_params=pltpu.CompilerParams(vmem_limit_bytes=24 * MIB),
        cost_estimate=pl.CostEstimate(
            flops=10_000_000, bytes_accessed=22_000_000, transcendentals=0
        ),
        name="stage",
    )(own, other, *in_hbm(gate_up, down))


def expert_kernel(turns, *refs):
    own_refs, other_refs = refs[:turns], refs[turns : 2 * turns]
    gu, dn = refs[2 * turns : 2 * turns + 2]
    mine_refs = refs[2 * turns + 2 : 3 * turns + 2]
    theirs_refs = refs[3 * turns + 2 :]
    lines, piece = own_refs[0].shape
    per = lines // PIECES
    half = turns * per
    n = turns * lines
    row = iota((n, n), 0)
    col = iota((n, n), 1)
    order = one_hot(col == row // per % turns * lines + row // half * per + row % per)
    sides = [
        dot(order, jnp.concatenate([ref[...] for ref in now], axis=0)).astype(BF16)
        for now in (own_refs, other_refs)
    ]
    gate = upper = None
    for k in range(PIECES):
        x = jnp.concatenate([side[k * half : (k + 1) * half] for side in sides], axis=0)
        cols = pl.ds(k * piece, piece)
        g, u = nt_dot(x, gu[0, :, cols]), nt_dot(x, gu[1, :, cols])
        gate, upper = (g, u) if k == 0 else (gate + g, upper + u)
    act = (gate / (1.0 + jnp.exp(-gate)) * upper).astype(BF16)
    mine = []
    theirs = []
    for k in range(PIECES):
        part = dot(act, dn[:, k * piece : (k + 1) * piece]).astype(BF16)
        mine.append(part[:half])
        theirs.append(part[half:])
    back = one_hot(row == col // per % turns * lines + col // half * per + col % per)
    for parts, now in ((theirs, theirs_refs), (mine, mine_refs)):
        out = dot(back, jnp.concatenate(parts, axis=0)).astype(BF16)
        for t, ref in enumerate(now):
            ref[...] = out[t * lines : (t + 1) * lines]


def experts(own, other, gu, dn):
    turns = len(own)
    shape = jax.ShapeDtypeStruct(own[0].shape, BF16)
    results = pl.pallas_call(
        functools.partial(expert_kernel, turns),
        out_shape=[shape] * (2 * turns),
        in_specs=[VMEM] * (2 * turns + 2),
        out_specs=[VMEM] * (2 * turns),
        compiler_params=pltpu.CompilerParams(vmem_limit_bytes=32 * MIB),
        cost_estimate=pl.CostEstimate(
            flops=800_000_000, bytes_accessed=12_000_000, transcendentals=16384
        ),
        name="experts",
    )(*own, *other, gu, dn)
    return results[:turns], results[turns:]


def combine_kernel(mix_ref, resid_ref, *refs):
    back_refs, (kept_ref, sent_ref) = refs[:-2], refs[-2:]
    both = resid_ref.shape[0]
    piece = back_refs[0].shape[1]
    product = dot(mix_ref[...], jnp.concatenate([ref[...] for ref in back_refs], axis=0))
    n = PIECES * 2 * both
    total = product[:n] + product[n : 2 * n] + product[2 * n :]
    for k in range(PIECES):
        cols = pl.ds(k * piece, piece)
        first = k * 2 * both
        kept_ref[:, cols] = resid_ref[:, cols] + total[first : first + both]
        sent_ref[:, cols] = total[first + both : first + 2 * both].astype(BF16)


def combine(mix, resid, backs):
    return pl.pallas_call(
        combine_kernel,
        out_shape=(
            jax.ShapeDtypeStruct(resid.shape, F32),
            jax.ShapeDtypeStruct(resid.shape, BF16),
        ),
        in_specs=[VMEM] * (2 + len(backs)),
        out_specs=(VMEM, VMEM),
        compiler_params=pltpu.CompilerParams(vmem_limit_bytes=24 * MIB),
        cost_estimate=pl.CostEstimate(
            flops=100_000_000, bytes_accessed=1_000_000, transcendentals=0
        ),
        name="combine",
    )(mix, resid, *backs)


def finish_kernel(kept_ref, other_ref, out_ref):
    steps, rows, _ = out_ref.shape
    done = (kept_ref[...] + other_ref[...].astype(F32)).astype(BF16)
    for s in range(steps):
        out_ref[s] = done[s * rows : (s + 1) * rows]


def finish(shape, kept, other):
    return pl.pallas_call(
        finish_kernel,
        out_shape=jax.ShapeDtypeStruct(shape, BF16),
        in_specs=[VMEM, VMEM],
        out_specs=VMEM,
        compiler_params=pltpu.CompilerParams(vmem_limit_bytes=24 * MIB),
        cost_estimate=pl.CostEstimate(flops=100_000, bytes_accessed=500_000, transcendentals=0),
        name="finish",
    )(kept, other)


def per_device(
    queries,
    fresh,
    kv_cache,
    cache_len,
    hidden_state,
    norm_gain,
    expert_ids,
    route_weight,
    gate_up,
    down,
):
    steps = queries.shape[0]
    owners = lax.axis_size("afd")
    chips = owners // 2
    turns = chips // 2
    cores = [(i, i ^ 1) for i in range(owners)]

    def swap(x):
        return lax.ppermute(x, "afd", cores)

    def route(t):
        return [(i, (i // 2 ^ distance(t, i % 2, chips)) * 2 + 1 - i % 2) for i in range(owners)]

    def send(x, t):
        return lax.ppermute(x, "afd", route(t))

    def send_back(x, t):
        return lax.ppermute(x, "afd", [(j, i) for i, j in route(t)])

    ids = expert_ids.transpose(2, 0, 1)
    weights = route_weight.transpose(2, 0, 1)
    resid, normed = attend(
        cache_len, ids, weights, queries, fresh, kv_cache, hidden_state, norm_gain
    )
    normed_other = swap(normed)
    sent = pack(steps, chips, normed, normed_other)
    own = [send(sent[t], t) for t in range(turns)]
    gu, dn, mix = stage(steps, chips, normed, normed_other, gate_up, down)
    own[0], gu, dn = lax.optimization_barrier((own[0], gu, dn))
    other = [swap(x) for x in own]
    summed = []
    for t in range(0, turns, TOGETHER):
        mine, theirs = experts(own[t : t + TOGETHER], other[t : t + TOGETHER], gu, dn)
        summed += [
            (a.astype(F32) + swap(b).astype(F32)).astype(BF16) for a, b in zip(mine, theirs)
        ]
    backs = [send_back(summed[t], t) for t in range(turns)]
    kept, given = combine(mix, resid, backs)
    return finish(queries.shape, kept, swap(given))


def solution(mesh):
    placed = (
        P(None, ("group", "afd"), None),
        P(None, ("group", "afd"), None),
        P(("group", "afd"), None, None),
        P(("group", "afd")),
        P(None, ("group", "afd"), None),
        P(),
        P(None, ("group", "afd"), None),
        P(None, ("group", "afd"), None),
        P("afd", None, None, None),
        P("afd", None, None),
    )
    return jax.shard_map(
        per_device,
        mesh=mesh,
        in_specs=placed,
        out_specs=P(None, ("group", "afd"), None),
        check_vma=False,
    )
```

```python
import functools
import jax
import jax.numpy as jnp
from jax import lax
from jax.experimental import pallas as pl
from jax.experimental.pallas import tpu as pltpu
from jax.sharding import PartitionSpec as P

HEADS = 32
HEAD = 224
EXPERTS = 8
TOP = 3
CAP = 2
PIECES = 4
LANES = 128
PARTS = 3
F32 = jnp.float32
BF16 = jnp.bfloat16
MIB = 1 << 20
VMEM = pl.BlockSpec(memory_space=pltpu.VMEM)
HBM = pl.BlockSpec(memory_space=pltpu.HBM)
TOGETHER = 4
STAGED = 2


def iota(shape, dim):
    return lax.broadcasted_iota(jnp.int32, shape, dim)


def in_hbm(*arrays):
    return [pltpu.with_memory_space_constraint(x, pltpu.HBM) for x in arrays]


def nt_dot(a, b):
    return lax.dot_general(a, b, (((1,), (1,)), ((), ())), preferred_element_type=F32)


def dot(a, b):
    return jnp.dot(a, b, preferred_element_type=F32)


def one_hot(mask):
    return jnp.where(mask, 1.0, 0.0).astype(BF16)


def distance(turn, core, chips):
    return ((chips - 2 * turn) % chips) ^ core


def expert_at(turn, chips):
    place = lax.axis_index("afd")
    return (distance(turn, place % 2, chips) ^ (place // 2)) // (chips // EXPERTS)


def spread(ref, k, where, steps, rows, empty):
    out = jnp.full(where.shape, empty)
    for s in range(steps):
        for r in range(rows):
            out = jnp.where(where == s * rows + r, ref[k, s, r], out)
    return out


def tail(ids_ref, weight_ref, steps, rows):
    both = steps * rows
    lane = iota((both, LANES), 1)
    where = iota((both, 1), 0)
    mix = jnp.zeros((both, LANES), F32)
    named = jnp.zeros((both, LANES), F32)
    for k in range(TOP):
        hit = spread(ids_ref, k, where, steps, rows, -1) == lane % EXPERTS
        mix = mix + jnp.where(hit, spread(weight_ref, k, where, steps, rows, 0.0), 0.0)
        named = named + jnp.where(hit, 1.0, 0.0)
    out = jnp.where(lane // EXPERTS == PARTS, named, 0.0)
    for part in range(PARTS):
        term = mix.astype(BF16).astype(F32)
        out = jnp.where(lane // EXPERTS == part, term, out)
        mix = mix - term
    return out.astype(BF16)


def attend_kernel(
    len_hbm,
    ids_hbm,
    weight_hbm,
    q_hbm,
    fresh_hbm,
    kv_hbm,
    hid_hbm,
    gain_hbm,
    resid_ref,
    out_ref,
    len_ref,
    ids_ref,
    weight_ref,
    q_ref,
    fresh_ref,
    kv_ref,
    hid_ref,
    gain_ref,
    merged,
    sems,
):
    copies = [
        pltpu.make_async_copy(source, target, sems.at[i])
        for i, (source, target) in enumerate(
            (
                (q_hbm, q_ref),
                (kv_hbm, kv_ref),
                (len_hbm, len_ref),
                (ids_hbm, ids_ref),
                (weight_hbm, weight_ref),
                (fresh_hbm, fresh_ref),
                (hid_hbm, hid_ref),
                (gain_hbm, gain_ref),
            )
        )
    ]
    for copy in copies:
        copy.start()
    steps, rows, width = q_ref.shape
    length = kv_ref.shape[2]
    both = steps * rows
    scale = HEAD ** (-0.5)
    for copy in copies:
        copy.wait()
    q = jnp.concatenate([q_ref[s].astype(F32) for s in range(steps)], axis=0)
    heads = jnp.concatenate([q[:, h * HEAD : (h + 1) * HEAD] for h in range(HEADS)], axis=0)
    heads = heads.astype(BF16)
    kv = jnp.concatenate([kv_ref[r] for r in range(rows)], axis=1)
    new = jnp.concatenate([fresh_ref[s].astype(F32) for s in range(steps)], axis=0).astype(BF16)

    sub = iota((both, rows * length), 0)
    lane = iota((both, rows * length), 1)
    limit = jnp.zeros_like(lane)
    for r in range(rows):
        limit = jnp.where(lane // length == r, len_ref[r], limit)
    valid = (lane // length == sub % rows) & (lane % length < limit)
    sub = iota((both, both), 0)
    lane = iota((both, both), 1)
    valid_new = (lane % rows == sub % rows) & (lane // rows <= sub // rows)

    old_s = (dot(heads, kv[:HEAD]) * scale).reshape(HEADS, both, rows * length)
    new_s = (nt_dot(heads, new[:, :HEAD]) * scale).reshape(HEADS, both, both)
    old_s = jnp.where(valid[None], old_s, -1e30)
    new_s = jnp.where(valid_new[None], new_s, -1e30)
    top = jnp.maximum(
        jnp.max(old_s, axis=-1, keepdims=True), jnp.max(new_s, axis=-1, keepdims=True)
    )
    old_e = jnp.exp(old_s - top)
    new_e = jnp.exp(new_s - top)
    total = jnp.sum(old_e, axis=-1, keepdims=True) + jnp.sum(new_e, axis=-1, keepdims=True)
    old_w = (old_e / total).reshape(HEADS * both, rows * length).astype(BF16)
    new_w = (new_e / total).reshape(HEADS * both, both).astype(BF16)
    attended = nt_dot(old_w, kv[HEAD:]) + dot(new_w, new[:, HEAD:])
    for h in range(HEADS):
        merged[:, h * HEAD : (h + 1) * HEAD] = attended[h * both : (h + 1) * both]
    hidden = jnp.concatenate([hid_ref[s].astype(F32) for s in range(steps)], axis=0)
    resid = hidden + merged[...]
    resid_ref[...] = resid
    meansq = jnp.mean(resid * resid, axis=-1, keepdims=True)
    gain = gain_ref[...].astype(F32)
    gain = jnp.concatenate([gain[i : i + 1] for i in range(width // LANES)], axis=1)
    normed = resid * lax.rsqrt(meansq + 1e-06) * gain
    out_ref[:, :width] = normed.astype(BF16)
    out_ref[:, width:] = tail(ids_ref, weight_ref, steps, rows)


def attend(cache_len, ids, weights, queries, fresh, kv_cache, hidden_state, norm_gain):
    steps, rows, width = queries.shape
    kv = kv_cache.transpose(0, 2, 1)
    gain = norm_gain.reshape(width // LANES, LANES)
    return pl.pallas_call(
        attend_kernel,
        out_shape=(
            jax.ShapeDtypeStruct((steps * rows, width), F32),
            jax.ShapeDtypeStruct((steps * rows, width + LANES), BF16),
        ),
        in_specs=[HBM] * 8,
        out_specs=(VMEM, VMEM),
        scratch_shapes=[
            pltpu.SMEM(cache_len.shape, jnp.int32),
            pltpu.SMEM(ids.shape, jnp.int32),
            pltpu.SMEM(weights.shape, F32),
            pltpu.VMEM(queries.shape, BF16),
            pltpu.VMEM(fresh.shape, BF16),
            pltpu.VMEM(kv.shape, BF16),
            pltpu.VMEM(hidden_state.shape, BF16),
            pltpu.VMEM(gain.shape, BF16),
            pltpu.VMEM((steps * rows, width), F32),
            pltpu.SemaphoreType.DMA((8,)),
        ],
        compiler_params=pltpu.CompilerParams(vmem_limit_bytes=24 * MIB),
        cost_estimate=pl.CostEstimate(
            flops=300_000_000, bytes_accessed=2_000_000, transcendentals=131072
        ),
        name="attend",
    )(*in_hbm(cache_len, ids, weights, queries, fresh, kv, hidden_state, gain))


def pack_kernel(steps, chips, own_ref, other_ref, *outs):
    both, width = own_ref.shape
    width -= LANES
    rows = both // steps
    piece = width // PIECES
    side_lines = steps * CAP
    lines = PIECES * 2 * side_lines
    tails = [ref[:, width:].astype(F32) for ref in (own_ref, other_ref)]
    tails = jnp.concatenate(tails * PIECES, axis=0).astype(BF16)
    count = 2 * both * PIECES
    row = iota((len(outs) * lines, LANES), 0)
    lane = iota((len(outs) * lines, LANES), 1)
    wanted = one_hot(lane == PARTS * EXPERTS + expert_at(row // lines, chips))
    named = nt_dot(wanted, tails)
    at = iota((count, count), 0)
    to = iota((count, count), 1)
    before = one_hot((at // rows == to // rows) & (at < to))
    rank = dot(named.astype(BF16), before)
    line = iota(named.shape, 0)
    col = iota(named.shape, 1)
    same = (line // CAP) % (lines // CAP) == col // rows
    picks = one_hot(same & (named > 0.5) & (rank == (line % CAP).astype(F32)))
    parts = [ref[:, :width].astype(F32) for ref in (own_ref, other_ref)]
    stacked = jnp.concatenate(
        [part[:, k * piece : (k + 1) * piece] for k in range(PIECES) for part in parts], axis=0
    ).astype(BF16)
    sent = dot(picks, stacked).astype(BF16)
    for t, out in enumerate(outs):
        out[...] = sent[t * lines : (t + 1) * lines]


def pack(steps, chips, own, other):
    both, width = own.shape
    shape = (PIECES * 2 * steps * CAP, (width - LANES) // PIECES)
    turns = chips // 2
    return pl.pallas_call(
        functools.partial(pack_kernel, steps, chips),
        out_shape=[jax.ShapeDtypeStruct(shape, BF16)] * turns,
        in_specs=[VMEM] * 2,
        out_specs=[VMEM] * turns,
        compiler_params=pltpu.CompilerParams(vmem_limit_bytes=24 * MIB),
        cost_estimate=pl.CostEstimate(
            flops=50_000_000, bytes_accessed=2_000_000, transcendentals=0
        ),
        name="pack",
    )(own, other)


def mixing(steps, chips, own_ref, other_ref):
    both, width = own_ref.shape
    width -= LANES
    rows = both // steps
    lines = PIECES * 2 * steps * CAP
    tails = [ref[:, width:].astype(F32) for ref in (own_ref, other_ref)]
    tails = jnp.concatenate(tails, axis=0).astype(BF16)
    count = chips // 2 * lines
    lane = iota((LANES, count), 0)
    expert = expert_at(iota((LANES, count), 1) // lines, chips)
    found = [dot(tails, one_hot(lane == part * EXPERTS + expert)) for part in range(PARTS + 1)]
    at = iota((2 * both, 2 * both), 1)
    to = iota((2 * both, 2 * both), 0)
    rank = dot(one_hot((at // rows == to // rows) & (at < to)), found[PARTS].astype(BF16))
    line = iota((2 * both, count), 1)
    row = iota((2 * both, count), 0)
    same = (line // CAP) % (2 * steps) == row // rows
    slot = same & (rank == (line % CAP).astype(F32))
    k_of = line // (2 * steps * CAP) % PIECES
    parts = [
        jnp.where(slot & (k_of == k), found[part], 0.0)
        for part in range(PARTS)
        for k in range(PIECES)
    ]
    return jnp.concatenate(parts, axis=0).astype(BF16)


def stage_kernel(steps, chips, own_ref, other_ref, gu_hbm, dn_hbm, gu, dn, mix_ref, sems):
    step = dn.shape[0] // 4
    pairs = []
    for i in range(4):
        part = pl.ds(i * step, step)
        pairs.append((gu_hbm.at[0, 0, part], gu.at[0, part]))
        pairs.append((gu_hbm.at[0, 1, part], gu.at[1, part]))
        pairs.append((dn_hbm.at[0, part], dn.at[part]))
    copies = [pltpu.make_async_copy(a, b, sems.at[i]) for i, (a, b) in enumerate(pairs)]
    for copy in copies:
        copy.start()
    mix_ref[...] = mixing(steps, chips, own_ref, other_ref)
    for copy in copies:
        copy.wait()


def stage(steps, chips, own, other, gate_up, down):
    lines = PIECES * 2 * steps * CAP
    return pl.pallas_call(
        functools.partial(stage_kernel, steps, chips),
        out_shape=(
            jax.ShapeDtypeStruct(gate_up.shape[1:], BF16),
            jax.ShapeDtypeStruct(down.shape[1:], BF16),
            jax.ShapeDtypeStruct((PARTS * PIECES * 2 * own.shape[0], chips // 2 * lines), BF16),
        ),
        in_specs=[VMEM, VMEM, HBM, HBM],
        out_specs=(VMEM,) * 3,
        scratch_shapes=[pltpu.SemaphoreType.DMA((12,))],
        compiler_params=pltpu.CompilerParams(vmem_limit_bytes=24 * MIB),
        cost_estimate=pl.CostEstimate(
            flops=10_000_000, bytes_accessed=22_000_000, transcendentals=0
        ),
        name="stage",
    )(own, other, *in_hbm(gate_up, down))


def expert_kernel(turns, *refs):
    own_refs, other_refs = refs[:turns], refs[turns : 2 * turns]
    gu, dn = refs[2 * turns : 2 * turns + 2]
    mine_refs = refs[2 * turns + 2 : 3 * turns + 2]
    theirs_refs = refs[3 * turns + 2 :]
    lines, piece = own_refs[0].shape
    per = lines // PIECES
    half = turns * per
    n = turns * lines
    row = iota((n, n), 0)
    col = iota((n, n), 1)
    order = one_hot(col == row // per % turns * lines + row // half * per + row % per)
    sides = [
        dot(order, jnp.concatenate([ref[...] for ref in now], axis=0)).astype(BF16)
        for now in (own_refs, other_refs)
    ]
    gate = upper = None
    for k in range(PIECES):
        x = jnp.concatenate([side[k * half : (k + 1) * half] for side in sides], axis=0)
        cols = pl.ds(k * piece, piece)
        g, u = nt_dot(x, gu[0, :, cols]), nt_dot(x, gu[1, :, cols])
        gate, upper = (g, u) if k == 0 else (gate + g, upper + u)
    act = (gate / (1.0 + jnp.exp(-gate)) * upper).astype(BF16)
    mine = []
    theirs = []
    for k in range(PIECES):
        part = dot(act, dn[:, k * piece : (k + 1) * piece]).astype(BF16)
        mine.append(part[:half])
        theirs.append(part[half:])
    back = one_hot(row == col // per % turns * lines + col // half * per + col % per)
    for parts, now in ((theirs, theirs_refs), (mine, mine_refs)):
        out = dot(back, jnp.concatenate(parts, axis=0)).astype(BF16)
        for t, ref in enumerate(now):
            ref[...] = out[t * lines : (t + 1) * lines]


def experts(own, other, gu, dn):
    turns = len(own)
    shape = jax.ShapeDtypeStruct(own[0].shape, BF16)
    results = pl.pallas_call(
        functools.partial(expert_kernel, turns),
        out_shape=[shape] * (2 * turns),
        in_specs=[VMEM] * (2 * turns + 2),
        out_specs=[VMEM] * (2 * turns),
        compiler_params=pltpu.CompilerParams(vmem_limit_bytes=32 * MIB),
        cost_estimate=pl.CostEstimate(
            flops=800_000_000, bytes_accessed=12_000_000, transcendentals=16384
        ),
        name="experts",
    )(*own, *other, gu, dn)
    return results[:turns], results[turns:]


def combine_kernel(mix_ref, resid_ref, *refs):
    back_refs, (kept_ref, sent_ref) = refs[:-2], refs[-2:]
    both = resid_ref.shape[0]
    piece = back_refs[0].shape[1]
    product = dot(mix_ref[...], jnp.concatenate([ref[...] for ref in back_refs], axis=0))
    n = PIECES * 2 * both
    total = product[:n] + product[n : 2 * n] + product[2 * n :]
    for k in range(PIECES):
        cols = pl.ds(k * piece, piece)
        first = k * 2 * both
        kept_ref[:, cols] = resid_ref[:, cols] + total[first : first + both]
        sent_ref[:, cols] = total[first + both : first + 2 * both].astype(BF16)


def combine(mix, resid, backs):
    return pl.pallas_call(
        combine_kernel,
        out_shape=(
            jax.ShapeDtypeStruct(resid.shape, F32),
            jax.ShapeDtypeStruct(resid.shape, BF16),
        ),
        in_specs=[VMEM] * (2 + len(backs)),
        out_specs=(VMEM, VMEM),
        compiler_params=pltpu.CompilerParams(vmem_limit_bytes=24 * MIB),
        cost_estimate=pl.CostEstimate(
            flops=100_000_000, bytes_accessed=1_000_000, transcendentals=0
        ),
        name="combine",
    )(mix, resid, *backs)


def finish_kernel(kept_ref, other_ref, out_ref):
    steps, rows, _ = out_ref.shape
    done = (kept_ref[...] + other_ref[...].astype(F32)).astype(BF16)
    for s in range(steps):
        out_ref[s] = done[s * rows : (s + 1) * rows]


def finish(shape, kept, other):
    return pl.pallas_call(
        finish_kernel,
        out_shape=jax.ShapeDtypeStruct(shape, BF16),
        in_specs=[VMEM, VMEM],
        out_specs=VMEM,
        compiler_params=pltpu.CompilerParams(vmem_limit_bytes=24 * MIB),
        cost_estimate=pl.CostEstimate(flops=100_000, bytes_accessed=500_000, transcendentals=0),
        name="finish",
    )(kept, other)


def per_device(
    queries,
    fresh,
    kv_cache,
    cache_len,
    hidden_state,
    norm_gain,
    expert_ids,
    route_weight,
    gate_up,
    down,
):
    steps = queries.shape[0]
    owners = lax.axis_size("afd")
    chips = owners // 2
    turns = chips // 2
    cores = [(i, i ^ 1) for i in range(owners)]

    def swap(x):
        return lax.ppermute(x, "afd", cores)

    def route(t):
        return [(i, (i // 2 ^ distance(t, i % 2, chips)) * 2 + 1 - i % 2) for i in range(owners)]

    def send(x, t):
        return lax.ppermute(x, "afd", route(t))

    def send_back(x, t):
        return lax.ppermute(x, "afd", [(j, i) for i, j in route(t)])

    ids = expert_ids.transpose(2, 0, 1)
    weights = route_weight.transpose(2, 0, 1)
    resid, normed = attend(
        cache_len, ids, weights, queries, fresh, kv_cache, hidden_state, norm_gain
    )
    normed_other = swap(normed)
    sent = pack(steps, chips, normed, normed_other)
    gu, dn, mix = stage(steps, chips, normed, normed_other, gate_up, down)
    *late, gu, dn = lax.optimization_barrier((*sent[STAGED:], gu, dn))
    sent = [*sent[:STAGED], *late]
    own = [send(sent[t], t) for t in range(turns)]
    other = [swap(x) for x in own]
    summed = []
    for t in range(0, turns, TOGETHER):
        mine, theirs = experts(own[t : t + TOGETHER], other[t : t + TOGETHER], gu, dn)
        summed += [
            (a.astype(F32) + swap(b).astype(F32)).astype(BF16) for a, b in zip(mine, theirs)
        ]
    backs = [send_back(summed[t], t) for t in range(turns)]
    kept, given = combine(mix, resid, backs)
    return finish(queries.shape, kept, swap(given))


def solution(mesh):
    placed = (
        P(None, ("group", "afd"), None),
        P(None, ("group", "afd"), None),
        P(("group", "afd"), None, None),
        P(("group", "afd")),
        P(None, ("group", "afd"), None),
        P(),
        P(None, ("group", "afd"), None),
        P(None, ("group", "afd"), None),
        P("afd", None, None, None),
        P("afd", None, None),
    )
    return jax.shard_map(
        per_device,
        mesh=mesh,
        in_specs=placed,
        out_specs=P(None, ("group", "afd"), None),
        check_vma=False,
    )
```

```python
import functools
import jax
import jax.numpy as jnp
from jax import lax
from jax.experimental import pallas as pl
from jax.experimental.pallas import tpu as pltpu
from jax.sharding import PartitionSpec as P

HEADS = 32
HEAD = 224
EXPERTS = 8
TOP = 3
CAP = 2
PIECES = 4
LANES = 128
PARTS = 3
F32 = jnp.float32
BF16 = jnp.bfloat16
MIB = 1 << 20
LIGHT = pl.CostEstimate(flops=1, bytes_accessed=1, transcendentals=0)
VMEM = pl.BlockSpec(memory_space=pltpu.VMEM)
HBM = pl.BlockSpec(memory_space=pltpu.HBM)
TOGETHER = 2


def iota(shape, dim):
    return lax.broadcasted_iota(jnp.int32, shape, dim)


def in_hbm(*arrays):
    return [pltpu.with_memory_space_constraint(x, pltpu.HBM) for x in arrays]


def nt_dot(a, b):
    return lax.dot_general(a, b, (((1,), (1,)), ((), ())), preferred_element_type=F32)


def dot(a, b):
    return jnp.dot(a, b, preferred_element_type=F32)


def one_hot(mask):
    return jnp.where(mask, 1.0, 0.0).astype(BF16)


def distance(turn, core, chips):
    return (2 * turn) ^ (core * (chips - 1))


def expert_at(turn, chips):
    place = lax.axis_index("afd")
    return (distance(turn, place % 2, chips) ^ (place // 2)) // (chips // EXPERTS)


def spread(ref, k, where, steps, rows, empty):
    out = jnp.full(where.shape, empty)
    for s in range(steps):
        for r in range(rows):
            out = jnp.where(where == s * rows + r, ref[k, s, r], out)
    return out


def tail(ids_ref, weight_ref, steps, rows):
    both = steps * rows
    lane = iota((both, LANES), 1)
    where = iota((both, 1), 0)
    mix = jnp.zeros((both, LANES), F32)
    named = jnp.zeros((both, LANES), F32)
    for k in range(TOP):
        hit = spread(ids_ref, k, where, steps, rows, -1) == lane % EXPERTS
        mix = mix + jnp.where(hit, spread(weight_ref, k, where, steps, rows, 0.0), 0.0)
        named = named + jnp.where(hit, 1.0, 0.0)
    out = jnp.where(lane // EXPERTS == PARTS, named, 0.0)
    for part in range(PARTS):
        term = mix.astype(BF16).astype(F32)
        out = jnp.where(lane // EXPERTS == part, term, out)
        mix = mix - term
    return out.astype(BF16)


def attend_kernel(
    len_hbm,
    ids_hbm,
    weight_hbm,
    q_hbm,
    fresh_hbm,
    kv_hbm,
    hid_hbm,
    gain_hbm,
    resid_ref,
    out_ref,
    len_ref,
    ids_ref,
    weight_ref,
    q_ref,
    fresh_ref,
    kv_ref,
    hid_ref,
    gain_ref,
    merged,
    sems,
):
    copies = [
        pltpu.make_async_copy(source, target, sems.at[i])
        for i, (source, target) in enumerate(
            (
                (q_hbm, q_ref),
                (kv_hbm, kv_ref),
                (len_hbm, len_ref),
                (ids_hbm, ids_ref),
                (weight_hbm, weight_ref),
                (fresh_hbm, fresh_ref),
                (hid_hbm, hid_ref),
                (gain_hbm, gain_ref),
            )
        )
    ]
    for copy in copies:
        copy.start()
    steps, rows, width = q_ref.shape
    length = kv_ref.shape[2]
    both = steps * rows
    scale = HEAD ** (-0.5)
    for copy in copies:
        copy.wait()
    q = jnp.concatenate([q_ref[s].astype(F32) for s in range(steps)], axis=0)
    heads = jnp.concatenate([q[:, h * HEAD : (h + 1) * HEAD] for h in range(HEADS)], axis=0)
    heads = heads.astype(BF16)
    kv = jnp.concatenate([kv_ref[r] for r in range(rows)], axis=1)
    new = jnp.concatenate([fresh_ref[s].astype(F32) for s in range(steps)], axis=0).astype(BF16)

    sub = iota((both, rows * length), 0)
    lane = iota((both, rows * length), 1)
    limit = jnp.zeros_like(lane)
    for r in range(rows):
        limit = jnp.where(lane // length == r, len_ref[r], limit)
    valid = (lane // length == sub % rows) & (lane % length < limit)
    sub = iota((both, both), 0)
    lane = iota((both, both), 1)
    valid_new = (lane % rows == sub % rows) & (lane // rows <= sub // rows)

    old_s = (dot(heads, kv[:HEAD]) * scale).reshape(HEADS, both, rows * length)
    new_s = (nt_dot(heads, new[:, :HEAD]) * scale).reshape(HEADS, both, both)
    old_s = jnp.where(valid[None], old_s, -1e30)
    new_s = jnp.where(valid_new[None], new_s, -1e30)
    top = jnp.maximum(
        jnp.max(old_s, axis=-1, keepdims=True), jnp.max(new_s, axis=-1, keepdims=True)
    )
    old_e = jnp.exp(old_s - top)
    new_e = jnp.exp(new_s - top)
    total = jnp.sum(old_e, axis=-1, keepdims=True) + jnp.sum(new_e, axis=-1, keepdims=True)
    old_w = (old_e / total).reshape(HEADS * both, rows * length).astype(BF16)
    new_w = (new_e / total).reshape(HEADS * both, both).astype(BF16)
    attended = nt_dot(old_w, kv[HEAD:]) + dot(new_w, new[:, HEAD:])
    for h in range(HEADS):
        merged[:, h * HEAD : (h + 1) * HEAD] = attended[h * both : (h + 1) * both]
    hidden = jnp.concatenate([hid_ref[s].astype(F32) for s in range(steps)], axis=0)
    resid = hidden + merged[...]
    resid_ref[...] = resid
    meansq = jnp.mean(resid * resid, axis=-1, keepdims=True)
    gain = gain_ref[...].astype(F32)
    gain = jnp.concatenate([gain[i : i + 1] for i in range(width // LANES)], axis=1)
    normed = resid * lax.rsqrt(meansq + 1e-06) * gain
    out_ref[:, :width] = normed.astype(BF16)
    out_ref[:, width:] = tail(ids_ref, weight_ref, steps, rows)


def attend(cache_len, ids, weights, queries, fresh, kv_cache, hidden_state, norm_gain):
    steps, rows, width = queries.shape
    kv = kv_cache.transpose(0, 2, 1)
    gain = norm_gain.reshape(width // LANES, LANES)
    return pl.pallas_call(
        attend_kernel,
        out_shape=(
            jax.ShapeDtypeStruct((steps * rows, width), F32),
            jax.ShapeDtypeStruct((steps * rows, width + LANES), BF16),
        ),
        in_specs=[HBM] * 8,
        out_specs=(VMEM, VMEM),
        scratch_shapes=[
            pltpu.SMEM(cache_len.shape, jnp.int32),
            pltpu.SMEM(ids.shape, jnp.int32),
            pltpu.SMEM(weights.shape, F32),
            pltpu.VMEM(queries.shape, BF16),
            pltpu.VMEM(fresh.shape, BF16),
            pltpu.VMEM(kv.shape, BF16),
            pltpu.VMEM(hidden_state.shape, BF16),
            pltpu.VMEM(gain.shape, BF16),
            pltpu.VMEM((steps * rows, width), F32),
            pltpu.SemaphoreType.DMA((8,)),
        ],
        compiler_params=pltpu.CompilerParams(vmem_limit_bytes=24 * MIB),
        cost_estimate=pl.CostEstimate(
            flops=300_000_000, bytes_accessed=2_000_000, transcendentals=131072
        ),
        name="attend",
    )(*in_hbm(cache_len, ids, weights, queries, fresh, kv, hidden_state, gain))


def pack_kernel(steps, chips, own_ref, other_ref, *outs):
    both, width = own_ref.shape
    width -= LANES
    rows = both // steps
    piece = width // PIECES
    side_lines = steps * CAP
    lines = PIECES * 2 * side_lines
    tails = [ref[:, width:].astype(F32) for ref in (own_ref, other_ref)]
    tails = jnp.concatenate(tails * PIECES, axis=0).astype(BF16)
    count = 2 * both * PIECES
    row = iota((len(outs) * lines, LANES), 0)
    lane = iota((len(outs) * lines, LANES), 1)
    wanted = one_hot(lane == PARTS * EXPERTS + expert_at(row // lines, chips))
    named = nt_dot(wanted, tails)
    at = iota((count, count), 0)
    to = iota((count, count), 1)
    before = one_hot((at // rows == to // rows) & (at < to))
    rank = dot(named.astype(BF16), before)
    line = iota(named.shape, 0)
    col = iota(named.shape, 1)
    same = (line // CAP) % (lines // CAP) == col // rows
    picks = one_hot(same & (named > 0.5) & (rank == (line % CAP).astype(F32)))
    parts = [ref[:, :width].astype(F32) for ref in (own_ref, other_ref)]
    stacked = jnp.concatenate(
        [part[:, k * piece : (k + 1) * piece] for k in range(PIECES) for part in parts], axis=0
    ).astype(BF16)
    sent = dot(picks, stacked).astype(BF16)
    for t, out in enumerate(outs):
        out[...] = sent[t * lines : (t + 1) * lines]


def pack(steps, chips, own, other):
    both, width = own.shape
    shape = (PIECES * 2 * steps * CAP, (width - LANES) // PIECES)
    turns = chips // 2
    return pl.pallas_call(
        functools.partial(pack_kernel, steps, chips),
        out_shape=[jax.ShapeDtypeStruct(shape, BF16)] * turns,
        in_specs=[VMEM] * 2,
        out_specs=[VMEM] * turns,
        compiler_params=pltpu.CompilerParams(vmem_limit_bytes=24 * MIB),
        cost_estimate=LIGHT,
        name="pack",
    )(own, other)


def mixing(steps, chips, own_ref, other_ref):
    both, width = own_ref.shape
    width -= LANES
    rows = both // steps
    lines = PIECES * 2 * steps * CAP
    tails = [ref[:, width:].astype(F32) for ref in (own_ref, other_ref)]
    tails = jnp.concatenate(tails, axis=0).astype(BF16)
    count = chips // 2 * lines
    lane = iota((LANES, count), 0)
    expert = expert_at(iota((LANES, count), 1) // lines, chips)
    found = [dot(tails, one_hot(lane == part * EXPERTS + expert)) for part in range(PARTS + 1)]
    at = iota((2 * both, 2 * both), 1)
    to = iota((2 * both, 2 * both), 0)
    rank = dot(one_hot((at // rows == to // rows) & (at < to)), found[PARTS].astype(BF16))
    line = iota((2 * both, count), 1)
    row = iota((2 * both, count), 0)
    same = (line // CAP) % (2 * steps) == row // rows
    slot = same & (rank == (line % CAP).astype(F32))
    k_of = line // (2 * steps * CAP) % PIECES
    parts = [
        jnp.where(slot & (k_of == k), found[part], 0.0)
        for part in range(PARTS)
        for k in range(PIECES)
    ]
    return jnp.concatenate(parts, axis=0).astype(BF16)


def stage_kernel(steps, chips, own_ref, other_ref, gu_hbm, dn_hbm, gu, dn, mix_ref, sems):
    step = dn.shape[0] // 4
    pairs = []
    for i in range(4):
        part = pl.ds(i * step, step)
        pairs.append((gu_hbm.at[0, 0, part], gu.at[0, part]))
        pairs.append((gu_hbm.at[0, 1, part], gu.at[1, part]))
        pairs.append((dn_hbm.at[0, part], dn.at[part]))
    copies = [pltpu.make_async_copy(a, b, sems.at[i]) for i, (a, b) in enumerate(pairs)]
    for copy in copies:
        copy.start()
    mix_ref[...] = mixing(steps, chips, own_ref, other_ref)
    for copy in copies:
        copy.wait()


def stage(steps, chips, own, other, gate_up, down):
    lines = PIECES * 2 * steps * CAP
    return pl.pallas_call(
        functools.partial(stage_kernel, steps, chips),
        out_shape=(
            jax.ShapeDtypeStruct(gate_up.shape[1:], BF16),
            jax.ShapeDtypeStruct(down.shape[1:], BF16),
            jax.ShapeDtypeStruct((PARTS * PIECES * 2 * own.shape[0], chips // 2 * lines), BF16),
        ),
        in_specs=[VMEM, VMEM, HBM, HBM],
        out_specs=(VMEM,) * 3,
        scratch_shapes=[pltpu.SemaphoreType.DMA((12,))],
        compiler_params=pltpu.CompilerParams(vmem_limit_bytes=24 * MIB),
        cost_estimate=LIGHT,
        name="stage",
    )(own, other, *in_hbm(gate_up, down))


def expert_kernel(turns, *refs):
    own_refs, other_refs = refs[:turns], refs[turns : 2 * turns]
    gu, dn = refs[2 * turns : 2 * turns + 2]
    mine_refs = refs[2 * turns + 2 : 3 * turns + 2]
    theirs_refs = refs[3 * turns + 2 :]
    lines, piece = own_refs[0].shape
    per = lines // PIECES
    half = turns * per
    n = turns * lines
    row = iota((n, n), 0)
    col = iota((n, n), 1)
    order = one_hot(col == row // per % turns * lines + row // half * per + row % per)
    sides = [
        dot(order, jnp.concatenate([ref[...] for ref in now], axis=0)).astype(BF16)
        for now in (own_refs, other_refs)
    ]
    gate = upper = None
    for k in range(PIECES):
        x = jnp.concatenate([side[k * half : (k + 1) * half] for side in sides], axis=0)
        cols = pl.ds(k * piece, piece)
        g, u = nt_dot(x, gu[0, :, cols]), nt_dot(x, gu[1, :, cols])
        gate, upper = (g, u) if k == 0 else (gate + g, upper + u)
    act = (gate / (1.0 + jnp.exp(-gate)) * upper).astype(BF16)
    mine = []
    theirs = []
    for k in range(PIECES):
        part = dot(act, dn[:, k * piece : (k + 1) * piece]).astype(BF16)
        mine.append(part[:half])
        theirs.append(part[half:])
    back = one_hot(row == col // per % turns * lines + col // half * per + col % per)
    for parts, now in ((theirs, theirs_refs), (mine, mine_refs)):
        out = dot(back, jnp.concatenate(parts, axis=0)).astype(BF16)
        for t, ref in enumerate(now):
            ref[...] = out[t * lines : (t + 1) * lines]


def experts(own, other, gu, dn):
    turns = len(own)
    shape = jax.ShapeDtypeStruct(own[0].shape, BF16)
    results = pl.pallas_call(
        functools.partial(expert_kernel, turns),
        out_shape=[shape] * (2 * turns),
        in_specs=[VMEM] * (2 * turns + 2),
        out_specs=[VMEM] * (2 * turns),
        compiler_params=pltpu.CompilerParams(vmem_limit_bytes=32 * MIB),
        cost_estimate=LIGHT,
        name="experts",
    )(*own, *other, gu, dn)
    return results[:turns], results[turns:]


def combine_kernel(mix_ref, resid_ref, *refs):
    back_refs, (kept_ref, sent_ref) = refs[:-2], refs[-2:]
    both = resid_ref.shape[0]
    piece = back_refs[0].shape[1]
    product = dot(mix_ref[...], jnp.concatenate([ref[...] for ref in back_refs], axis=0))
    n = PIECES * 2 * both
    total = product[:n] + product[n : 2 * n] + product[2 * n :]
    for k in range(PIECES):
        cols = pl.ds(k * piece, piece)
        first = k * 2 * both
        kept_ref[:, cols] = resid_ref[:, cols] + total[first : first + both]
        sent_ref[:, cols] = total[first + both : first + 2 * both].astype(BF16)


def combine(mix, resid, backs):
    return pl.pallas_call(
        combine_kernel,
        out_shape=(
            jax.ShapeDtypeStruct(resid.shape, F32),
            jax.ShapeDtypeStruct(resid.shape, BF16),
        ),
        in_specs=[VMEM] * (2 + len(backs)),
        out_specs=(VMEM, VMEM),
        compiler_params=pltpu.CompilerParams(vmem_limit_bytes=24 * MIB),
        cost_estimate=pl.CostEstimate(
            flops=100_000_000, bytes_accessed=1_000_000, transcendentals=0
        ),
        name="combine",
    )(mix, resid, *backs)


def finish_kernel(kept_ref, other_ref, out_ref):
    steps, rows, _ = out_ref.shape
    done = (kept_ref[...] + other_ref[...].astype(F32)).astype(BF16)
    for s in range(steps):
        out_ref[s] = done[s * rows : (s + 1) * rows]


def finish(shape, kept, other):
    return pl.pallas_call(
        finish_kernel,
        out_shape=jax.ShapeDtypeStruct(shape, BF16),
        in_specs=[VMEM, VMEM],
        out_specs=VMEM,
        compiler_params=pltpu.CompilerParams(vmem_limit_bytes=24 * MIB),
        cost_estimate=pl.CostEstimate(flops=100_000, bytes_accessed=500_000, transcendentals=0),
        name="finish",
    )(kept, other)


def per_device(
    queries,
    fresh,
    kv_cache,
    cache_len,
    hidden_state,
    norm_gain,
    expert_ids,
    route_weight,
    gate_up,
    down,
):
    steps = queries.shape[0]
    owners = lax.axis_size("afd")
    chips = owners // 2
    turns = chips // 2
    cores = [(i, i ^ 1) for i in range(owners)]

    def swap(x):
        return lax.ppermute(x, "afd", cores)

    def route(t):
        return [(i, (i // 2 ^ distance(t, i % 2, chips)) * 2 + 1 - i % 2) for i in range(owners)]

    def send(x, t):
        return lax.ppermute(x, "afd", route(t))

    def send_back(x, t):
        return lax.ppermute(x, "afd", [(j, i) for i, j in route(t)])

    ids = expert_ids.transpose(2, 0, 1)
    weights = route_weight.transpose(2, 0, 1)
    resid, normed = attend(
        cache_len, ids, weights, queries, fresh, kv_cache, hidden_state, norm_gain
    )
    normed_other = swap(normed)
    sent = pack(steps, chips, normed, normed_other)
    gu, dn, mix = stage(steps, chips, normed, normed_other, gate_up, down)
    *late, gu, dn = lax.optimization_barrier((*sent[TOGETHER:], gu, dn))
    sent = [*sent[:TOGETHER], *late]
    own = [send(sent[t], t) for t in range(turns)]
    own[:TOGETHER], gu, dn = lax.optimization_barrier((own[:TOGETHER], gu, dn))
    backs = []
    for first in range(0, turns, TOGETHER):
        now = own[first : first + TOGETHER]
        mine, theirs = experts(now, [swap(x) for x in now], gu, dn)
        theirs, backs = lax.optimization_barrier((theirs, backs))
        rest = own[first + TOGETHER :]
        mine, own[first + TOGETHER :] = lax.optimization_barrier((mine, rest))
        summed = [
            (a.astype(F32) + swap(b).astype(F32)).astype(BF16) for a, b in zip(mine, theirs)
        ]
        backs = backs + [send_back(x, first + i) for i, x in enumerate(summed)]
    kept, given = combine(mix, resid, backs)
    return finish(queries.shape, kept, swap(given))


def solution(mesh):
    placed = (
        P(None, ("group", "afd"), None),
        P(None, ("group", "afd"), None),
        P(("group", "afd"), None, None),
        P(("group", "afd")),
        P(None, ("group", "afd"), None),
        P(),
        P(None, ("group", "afd"), None),
        P(None, ("group", "afd"), None),
        P("afd", None, None, None),
        P("afd", None, None),
    )
    return jax.shard_map(
        per_device,
        mesh=mesh,
        in_specs=placed,
        out_specs=P(None, ("group", "afd"), None),
        check_vma=False,
    )
```

```python
import functools
import jax
import jax.numpy as jnp
from jax import lax
from jax.experimental import pallas as pl
from jax.experimental.pallas import tpu as pltpu
from jax.sharding import PartitionSpec as P

HEADS = 32
HEAD = 224
EXPERTS = 8
TOP = 3
CAP = 2
LINES = 16
LANES = 128
STAGED = 5
F32 = jnp.float32
BF16 = jnp.bfloat16
MIB = 1 << 20
VMEM = pl.BlockSpec(memory_space=pltpu.VMEM)
HBM = pl.BlockSpec(memory_space=pltpu.HBM)
BATCHES = ((0, 1),)
TURNS = ((0, 7, 1, 5, 2, 6, 3, 4), (0, 4, 6, 1, 7, 2, 5, 3))


def iota(shape, dim):
    return lax.broadcasted_iota(jnp.int32, shape, dim)


def in_hbm(*arrays):
    return [pltpu.with_memory_space_constraint(x, pltpu.HBM) for x in arrays]


def partner(permuted, turn):
    if not permuted:
        return turn
    place = lax.axis_index("afd")
    out = jnp.zeros_like(turn)
    for n in range(1, len(TURNS[0])):
        out = jnp.where(turn == n, jnp.where(place % 2 == 0, TURNS[0][n], TURNS[1][n]), out)
    return out ^ (place // 2)


def nt_dot(a, b):
    return lax.dot_general(a, b, (((1,), (1,)), ((), ())), preferred_element_type=F32)


def dot(a, b):
    return jnp.dot(a, b, preferred_element_type=F32)


def one_hot(mask):
    return jnp.where(mask, 1.0, 0.0).astype(BF16)


def spread(ref, k, where, steps, rows, empty):
    out = jnp.full(where.shape, empty)
    for s in range(steps):
        for r in range(rows):
            out = jnp.where(where == s * rows + r, ref[k, s, r], out)
    return out


def picks_of(ids_ref, batch, steps, rows, permuted):
    pieces = LINES // (len(batch) * CAP)
    both = steps * rows
    shape = (EXPERTS * LINES, pieces * both)
    line = iota(shape, 0)
    col = iota(shape, 1)
    where = iota((1, pieces * both), 1) % both
    expert = partner(permuted, line // LINES)
    named = jnp.zeros(shape, jnp.bool_)
    for k in range(TOP):
        named = named | (spread(ids_ref, k, where, steps, rows, -1) == expert)
    at = iota((pieces * both, pieces * both), 0)
    to = iota((pieces * both, pieces * both), 1)
    rank = dot(one_hot(named), one_hot((at // rows == to // rows) & (at < to)))
    slot = (line % CAP).astype(F32)
    step = (line // CAP) % len(batch) + batch[0]
    piece = line // (CAP * len(batch)) % pieces
    same = (step == col // rows % steps) & (piece == col // both)
    return one_hot(named & same & (rank == slot))


def attend_kernel(
    permuted, len_hbm, ids_hbm, q_hbm, fresh_hbm, kv_hbm, hid_hbm, gain_hbm, resid_ref, *rest
):
    outs = rest[: len(BATCHES) * EXPERTS]
    len_ref, ids_ref, q_ref, fresh_ref, kv_ref, hid_ref, gain_ref, merged, sems = rest[len(outs) :]
    copies = [
        pltpu.make_async_copy(source, target, sems.at[i])
        for i, (source, target) in enumerate(
            (
                (q_hbm, q_ref),
                (kv_hbm, kv_ref),
                (len_hbm, len_ref),
                (ids_hbm, ids_ref),
                (fresh_hbm, fresh_ref),
                (hid_hbm, hid_ref),
                (gain_hbm, gain_ref),
            )
        )
    ]
    for copy in copies:
        copy.start()
    steps, rows, width = q_ref.shape
    length = kv_ref.shape[2]
    both = steps * rows
    scale = HEAD ** (-0.5)
    for copy in copies:
        copy.wait()
    q = jnp.concatenate([q_ref[s].astype(F32) for s in range(steps)], axis=0)
    heads = jnp.concatenate([q[:, h * HEAD : (h + 1) * HEAD] for h in range(HEADS)], axis=0)
    heads = heads.astype(BF16)
    kv = jnp.concatenate([kv_ref[r] for r in range(rows)], axis=1)
    new = jnp.concatenate([fresh_ref[s].astype(F32) for s in range(steps)], axis=0).astype(BF16)

    sub = iota((both, rows * length), 0)
    lane = iota((both, rows * length), 1)
    limit = jnp.zeros_like(lane)
    for r in range(rows):
        limit = jnp.where(lane // length == r, len_ref[r], limit)
    valid = (lane // length == sub % rows) & (lane % length < limit)
    sub = iota((both, both), 0)
    lane = iota((both, both), 1)
    valid_new = (lane % rows == sub % rows) & (lane // rows <= sub // rows)

    old_s = (dot(heads, kv[:HEAD]) * scale).reshape(HEADS, both, rows * length)
    new_s = (nt_dot(heads, new[:, :HEAD]) * scale).reshape(HEADS, both, both)
    old_s = jnp.where(valid[None], old_s, -1e30)
    new_s = jnp.where(valid_new[None], new_s, -1e30)
    top = jnp.maximum(
        jnp.max(old_s, axis=-1, keepdims=True), jnp.max(new_s, axis=-1, keepdims=True)
    )
    old_e = jnp.exp(old_s - top)
    new_e = jnp.exp(new_s - top)
    total = jnp.sum(old_e, axis=-1, keepdims=True) + jnp.sum(new_e, axis=-1, keepdims=True)
    old_w = (old_e / total).reshape(HEADS * both, rows * length).astype(BF16)
    new_w = (new_e / total).reshape(HEADS * both, both).astype(BF16)
    attended = nt_dot(old_w, kv[HEAD:]) + dot(new_w, new[:, HEAD:])
    for h in range(HEADS):
        merged[:, h * HEAD : (h + 1) * HEAD] = attended[h * both : (h + 1) * both]
    hidden = jnp.concatenate([hid_ref[s].astype(F32) for s in range(steps)], axis=0)
    resid = hidden + merged[...]
    resid_ref[...] = resid
    meansq = jnp.mean(resid * resid, axis=-1, keepdims=True)
    gain = gain_ref[...].astype(F32)
    gain = jnp.concatenate([gain[i : i + 1] for i in range(width // LANES)], axis=1)
    normed = resid * lax.rsqrt(meansq + 1e-06) * gain
    for i, batch in enumerate(BATCHES):
        pieces = LINES // (len(batch) * CAP)
        piece = width // pieces
        stacked = jnp.concatenate(
            [normed[:, k * piece : (k + 1) * piece] for k in range(pieces)], axis=0
        ).astype(BF16)
        picks = picks_of(ids_ref, batch, steps, rows, permuted)
        sent = dot(picks, stacked).astype(BF16)
        for j in range(EXPERTS):
            outs[i * EXPERTS + j][0] = sent[j * LINES : (j + 1) * LINES]


def attend(permuted, cache_len, ids, queries, fresh, kv_cache, hidden_state, norm_gain):
    steps, rows, width = queries.shape
    chunks = []
    for batch in BATCHES:
        shape = (1, LINES, width * len(batch) * CAP // LINES)
        chunks += [jax.ShapeDtypeStruct(shape, BF16)] * EXPERTS
    kv = kv_cache.transpose(0, 2, 1)
    gain = norm_gain.reshape(width // LANES, LANES)
    results = pl.pallas_call(
        functools.partial(attend_kernel, permuted),
        out_shape=(jax.ShapeDtypeStruct((steps * rows, width), F32), *chunks),
        in_specs=[HBM] * 7,
        out_specs=(VMEM,) * (1 + len(chunks)),
        scratch_shapes=[
            pltpu.SMEM(cache_len.shape, jnp.int32),
            pltpu.SMEM(ids.shape, jnp.int32),
            pltpu.VMEM(queries.shape, BF16),
            pltpu.VMEM(fresh.shape, BF16),
            pltpu.VMEM(kv.shape, BF16),
            pltpu.VMEM(hidden_state.shape, BF16),
            pltpu.VMEM(gain.shape, BF16),
            pltpu.VMEM((steps * rows, width), F32),
            pltpu.SemaphoreType.DMA((7,)),
        ],
        compiler_params=pltpu.CompilerParams(vmem_limit_bytes=24 * MIB),
        cost_estimate=pl.CostEstimate(
            flops=300_000_000, bytes_accessed=2_000_000, transcendentals=131072
        ),
        name="attend",
    )(*in_hbm(cache_len, ids, queries, fresh, kv, hidden_state, gain))
    resid, chunks = results[0], results[1:]
    return resid, [chunks[i * EXPERTS : (i + 1) * EXPERTS] for i in range(len(BATCHES))]


def mixing(ids_ref, weight_ref, batch, steps, rows, chips, permuted):
    pieces = LINES // (len(batch) * CAP)
    both = len(batch) * rows
    shape = (both, chips * LINES)
    line = iota(shape, 1)
    sub = iota(shape, 0)
    expert = partner(permuted, line // LINES) // (chips // EXPERTS)
    where = iota((both, 1), 0) + batch[0] * rows
    named = jnp.zeros(shape, F32)
    mix = jnp.zeros(shape, F32)
    for k in range(TOP):
        hit = spread(ids_ref, k, where, steps, rows, -1) == expert
        weight = spread(weight_ref, k, where, steps, rows, 0.0)
        named = named + jnp.where(hit, 1.0, 0.0)
        mix = mix + jnp.where(hit, weight, 0.0)
    at = iota((both, both), 1)
    to = iota((both, both), 0)
    rank = dot(one_hot((at // rows == to // rows) & (at < to)), named.astype(BF16))
    same = (line // CAP) % len(batch) == sub // rows
    mix = jnp.where((rank == (line % CAP).astype(F32)) & same, mix, 0.0)
    high = mix.astype(BF16).astype(F32)
    middle = (mix - high).astype(BF16).astype(F32)
    low = mix - high - middle
    k_of = line // (len(batch) * CAP) % pieces
    parts = [
        jnp.where(k_of == k, part, 0.0) for part in (high, middle, low) for k in range(pieces)
    ]
    return jnp.concatenate(parts, axis=0).astype(BF16)


def stage_kernel(
    permuted, chips, steps, rows, ids_hbm, weight_hbm, gu_hbm, dn_hbm, gu, dn, *rest
):
    mixes = rest[: len(BATCHES)]
    ids_ref, weight_ref, small, large = rest[len(BATCHES) :]
    first = [
        pltpu.make_async_copy(ids_hbm, ids_ref, small.at[0]),
        pltpu.make_async_copy(weight_hbm, weight_ref, small.at[1]),
    ]
    hidden = dn.shape[0]
    step = hidden // 4
    second = []
    for i in range(4):
        part = pl.ds(i * step, step)
        second.append((gu_hbm.at[0, 0, part], gu.at[0, part]))
        second.append((gu_hbm.at[0, 1, part], gu.at[1, part]))
        second.append((dn_hbm.at[0, part], dn.at[part]))
    second = [pltpu.make_async_copy(a, b, large.at[i]) for i, (a, b) in enumerate(second)]
    for copy in first + second:
        copy.start()
    for copy in first:
        copy.wait()
    for batch, mix in zip(BATCHES, mixes):
        mix[...] = mixing(ids_ref, weight_ref, batch, steps, rows, chips, permuted)
    for copy in second:
        copy.wait()


def stage(permuted, chips, ids, weights, gate_up, down):
    _, steps, rows = ids.shape
    mixes = [
        jax.ShapeDtypeStruct((3 * LINES // CAP * rows, chips * LINES), BF16) for _ in BATCHES
    ]
    gu, dn, *mixes = pl.pallas_call(
        functools.partial(stage_kernel, permuted, chips, steps, rows),
        out_shape=(
            jax.ShapeDtypeStruct(gate_up.shape[1:], BF16),
            jax.ShapeDtypeStruct(down.shape[1:], BF16),
            *mixes,
        ),
        in_specs=[HBM] * 4,
        out_specs=(VMEM,) * (2 + len(mixes)),
        scratch_shapes=[
            pltpu.SMEM(ids.shape, jnp.int32),
            pltpu.SMEM(weights.shape, F32),
            pltpu.SemaphoreType.DMA((2,)),
            pltpu.SemaphoreType.DMA((12,)),
        ],
        compiler_params=pltpu.CompilerParams(vmem_limit_bytes=24 * MIB),
        cost_estimate=pl.CostEstimate(
            flops=1_000_000, bytes_accessed=22_000_000, transcendentals=0
        ),
        name="stage",
    )(*in_hbm(ids, weights, gate_up, down))
    return gu, dn, mixes


def expert_kernel(count, per, *refs):
    own_refs, other_refs = refs[:count], refs[count : 2 * count]
    gu, dn = refs[2 * count : 2 * count + 2]
    mine_refs = refs[2 * count + 2 : 3 * count + 2]
    theirs_refs = refs[3 * count + 2 :]
    piece = own_refs[0].shape[2]
    chips = sum(ref.shape[0] for ref in own_refs)
    pieces = LINES // per
    half = chips * per
    n = chips * LINES
    row = iota((n, n), 0)
    col = iota((n, n), 1)
    order = one_hot(col == row // per % chips * LINES + row // half * per + row % per)
    sides = []
    for refs_now in (own_refs, other_refs):
        lines = [ref[...].reshape(ref.shape[0] * LINES, piece) for ref in refs_now]
        sides.append(dot(order, jnp.concatenate(lines, axis=0)).astype(BF16))
    gate = upper = None
    for k in range(pieces):
        x = jnp.concatenate([side[k * half : (k + 1) * half] for side in sides], axis=0)
        cols = pl.ds(k * piece, piece)
        g, u = nt_dot(x, gu[0, :, cols]), nt_dot(x, gu[1, :, cols])
        gate, upper = (g, u) if k == 0 else (gate + g, upper + u)
    act = (gate / (1.0 + jnp.exp(-gate)) * upper).astype(BF16)
    mine = []
    theirs = []
    for k in range(pieces):
        part = dot(act, dn[:, k * piece : (k + 1) * piece]).astype(BF16)
        mine.append(part[:half])
        theirs.append(part[half:])
    back = one_hot(row == col // per % chips * LINES + col // half * per + col % per)
    for parts, refs_now in ((theirs, theirs_refs), (mine, mine_refs)):
        lines = dot(back, jnp.concatenate(parts, axis=0)).astype(BF16)
        start = 0
        for ref in refs_now:
            size = ref.shape[0] * LINES
            ref[...] = lines[start : start + size].reshape(ref.shape)
            start += size


def experts(own, other, gu, dn, per):
    count = len(own)
    shapes = tuple(jax.ShapeDtypeStruct(x.shape, BF16) for x in own)
    results = pl.pallas_call(
        functools.partial(expert_kernel, count, per),
        out_shape=shapes + shapes,
        in_specs=[VMEM] * (2 * count + 2),
        out_specs=(VMEM,) * (2 * count),
        compiler_params=pltpu.CompilerParams(vmem_limit_bytes=32 * MIB),
        cost_estimate=pl.CostEstimate(
            flops=800_000_000, bytes_accessed=12_000_000, transcendentals=16384
        ),
        name="experts",
    )(*own, *other, gu, dn)
    return results[:count], results[count:]


def combine_kernel(counts, resid_ref, *refs):
    out_ref = refs[-1]
    _, rows, width = out_ref.shape
    start = 0
    for batch, count in zip(BATCHES, counts):
        left = refs[start][...]
        back_refs = refs[start + 1 : start + 1 + count]
        start += 1 + count
        piece = back_refs[0].shape[2]
        pieces = width // piece
        both = len(batch) * rows
        lines = [ref[...].reshape(ref.shape[0] * LINES, piece) for ref in back_refs]
        product = dot(left, jnp.concatenate(lines, axis=0))
        n = pieces * both
        total = product[:n] + product[n : 2 * n] + product[2 * n :]
        first = batch[0] * rows
        for k in range(pieces):
            cols = pl.ds(k * piece, piece)
            done = resid_ref[first : first + both, cols] + total[k * both : (k + 1) * both]
            done = done.astype(BF16)
            for i, s in enumerate(batch):
                out_ref[s, :, cols] = done[i * rows : (i + 1) * rows]


def combine(shape, resid, mixes, backs):
    operands = [x for mix, back in zip(mixes, backs) for x in (mix, *back)]
    return pl.pallas_call(
        functools.partial(combine_kernel, [len(back) for back in backs]),
        out_shape=jax.ShapeDtypeStruct(shape, BF16),
        in_specs=[VMEM] * (1 + len(operands)),
        out_specs=VMEM,
        compiler_params=pltpu.CompilerParams(vmem_limit_bytes=24 * MIB),
        cost_estimate=pl.CostEstimate(
            flops=100_000_000, bytes_accessed=1_000_000, transcendentals=0
        ),
        name="combine",
    )(resid, *operands)


def per_device(
    queries,
    fresh,
    kv_cache,
    cache_len,
    hidden_state,
    norm_gain,
    expert_ids,
    route_weight,
    gate_up,
    down,
):
    owners = lax.axis_size("afd")
    chips = owners // 2
    chips_per_expert = chips // EXPERTS
    permuted = chips == EXPERTS
    swap = [(i, i ^ 1) for i in range(owners)]

    def route(n):
        return [(i, (i // 2 ^ TURNS[i % 2][n]) * 2 + 1 - i % 2) for i in range(owners)]

    def send(chunk, n):
        return lax.ppermute(chunk, "afd", route(n))

    def send_back(chunk, n):
        return lax.ppermute(chunk, "afd", [(j, i) for i, j in route(n)])

    def to_chips(chunks):
        same_core = [[2 * p + c for p in range(chips)] for c in range(2)]
        whole = jnp.concatenate(chunks, axis=0)
        return [
            lax.all_to_all(
                whole, "afd", split_axis=0, concat_axis=0, axis_index_groups=same_core, tiled=True
            )
        ]

    ids = expert_ids.transpose(2, 0, 1)
    weights = route_weight.transpose(2, 0, 1)
    resid, sent = attend(
        permuted, cache_len, ids, queries, fresh, kv_cache, hidden_state, norm_gain
    )
    gu, dn, mixes = stage(permuted, chips, ids, weights, gate_up, down)
    backs = []
    for batch, chunks in zip(BATCHES, sent):
        if permuted:
            *late, gu, dn = lax.optimization_barrier((*chunks[STAGED:], gu, dn))
            chunks = [*chunks[:STAGED], *late]
            own = [chunks[0]] + [send(chunks[n], n) for n in range(1, chips)]
        else:
            own = to_chips([jnp.repeat(chunk, chips_per_expert, axis=0) for chunk in chunks])
        other = [lax.ppermute(x, "afd", swap) for x in own]
        mine, theirs = experts(own, other, gu, dn, len(batch) * CAP)
        summed = [
            (a.astype(F32) + lax.ppermute(b, "afd", swap).astype(F32)).astype(BF16)
            for a, b in zip(mine, theirs)
        ]
        if permuted:
            backs.append([summed[0]] + [send_back(summed[n], n) for n in range(1, chips)])
        else:
            backs.append(to_chips(summed))
    return combine(queries.shape, resid, mixes, backs)


def solution(mesh):
    placed = (
        P(None, ("group", "afd"), None),
        P(None, ("group", "afd"), None),
        P(("group", "afd"), None, None),
        P(("group", "afd")),
        P(None, ("group", "afd"), None),
        P(),
        P(None, ("group", "afd"), None),
        P(None, ("group", "afd"), None),
        P("afd", None, None, None),
        P("afd", None, None),
    )
    return jax.shard_map(
        per_device,
        mesh=mesh,
        in_specs=placed,
        out_specs=P(None, ("group", "afd"), None),
        check_vma=False,
    )
```

```python
import functools
import jax
import jax.numpy as jnp
from jax import lax
from jax.experimental import pallas as pl
from jax.experimental.pallas import tpu as pltpu
from jax.sharding import PartitionSpec as P

HEADS = 32
HEAD = 224
EXPERTS = 8
TOP = 3
CAP = 2
PIECES = 4
LANES = 128
PARTS = 3
F32 = jnp.float32
BF16 = jnp.bfloat16
MIB = 1 << 20
VMEM = pl.BlockSpec(memory_space=pltpu.VMEM)
HBM = pl.BlockSpec(memory_space=pltpu.HBM)
TOGETHER = 4


def iota(shape, dim):
    return lax.broadcasted_iota(jnp.int32, shape, dim)


def in_hbm(*arrays):
    return [pltpu.with_memory_space_constraint(x, pltpu.HBM) for x in arrays]


def nt_dot(a, b):
    return lax.dot_general(a, b, (((1,), (1,)), ((), ())), preferred_element_type=F32)


def dot(a, b):
    return jnp.dot(a, b, preferred_element_type=F32)


def one_hot(mask):
    return jnp.where(mask, 1.0, 0.0).astype(BF16)


def distance(turn, core, chips):
    return (2 * turn) ^ (core * (chips - 1))


def expert_at(turn, chips):
    place = lax.axis_index("afd")
    return (distance(turn, place % 2, chips) ^ (place // 2)) // (chips // EXPERTS)


def spread(ref, k, where, steps, rows, empty):
    out = jnp.full(where.shape, empty)
    for s in range(steps):
        for r in range(rows):
            out = jnp.where(where == s * rows + r, ref[k, s, r], out)
    return out


def tail(ids_ref, weight_ref, steps, rows):
    both = steps * rows
    lane = iota((both, LANES), 1)
    where = iota((both, 1), 0)
    mix = jnp.zeros((both, LANES), F32)
    named = jnp.zeros((both, LANES), F32)
    for k in range(TOP):
        hit = spread(ids_ref, k, where, steps, rows, -1) == lane % EXPERTS
        mix = mix + jnp.where(hit, spread(weight_ref, k, where, steps, rows, 0.0), 0.0)
        named = named + jnp.where(hit, 1.0, 0.0)
    out = jnp.where(lane // EXPERTS == PARTS, named, 0.0)
    for part in range(PARTS):
        term = mix.astype(BF16).astype(F32)
        out = jnp.where(lane // EXPERTS == part, term, out)
        mix = mix - term
    return out.astype(BF16)


def attend_kernel(
    len_hbm,
    ids_hbm,
    weight_hbm,
    q_hbm,
    fresh_hbm,
    kv_hbm,
    hid_hbm,
    gain_hbm,
    dn_hbm,
    resid_ref,
    out_ref,
    dn_ref,
    len_ref,
    ids_ref,
    weight_ref,
    q_ref,
    fresh_ref,
    kv_ref,
    hid_ref,
    gain_ref,
    merged,
    sems,
):
    copies = [
        pltpu.make_async_copy(source, target, sems.at[i])
        for i, (source, target) in enumerate(
            (
                (q_hbm, q_ref),
                (kv_hbm, kv_ref),
                (len_hbm, len_ref),
                (ids_hbm, ids_ref),
                (weight_hbm, weight_ref),
                (fresh_hbm, fresh_ref),
                (hid_hbm, hid_ref),
                (gain_hbm, gain_ref),
            )
        )
    ]
    down = pltpu.make_async_copy(dn_hbm.at[0], dn_ref, sems.at[len(copies)])
    for copy in [*copies, down]:
        copy.start()
    steps, rows, width = q_ref.shape
    length = kv_ref.shape[2]
    both = steps * rows
    scale = HEAD ** (-0.5)
    for copy in copies:
        copy.wait()
    q = jnp.concatenate([q_ref[s].astype(F32) for s in range(steps)], axis=0)
    heads = jnp.concatenate([q[:, h * HEAD : (h + 1) * HEAD] for h in range(HEADS)], axis=0)
    heads = heads.astype(BF16)
    kv = jnp.concatenate([kv_ref[r] for r in range(rows)], axis=1)
    new = jnp.concatenate([fresh_ref[s].astype(F32) for s in range(steps)], axis=0).astype(BF16)

    sub = iota((both, rows * length), 0)
    lane = iota((both, rows * length), 1)
    limit = jnp.zeros_like(lane)
    for r in range(rows):
        limit = jnp.where(lane // length == r, len_ref[r], limit)
    valid = (lane // length == sub % rows) & (lane % length < limit)
    sub = iota((both, both), 0)
    lane = iota((both, both), 1)
    valid_new = (lane % rows == sub % rows) & (lane // rows <= sub // rows)

    old_s = (dot(heads, kv[:HEAD]) * scale).reshape(HEADS, both, rows * length)
    new_s = (nt_dot(heads, new[:, :HEAD]) * scale).reshape(HEADS, both, both)
    old_s = jnp.where(valid[None], old_s, -1e30)
    new_s = jnp.where(valid_new[None], new_s, -1e30)
    top = jnp.maximum(
        jnp.max(old_s, axis=-1, keepdims=True), jnp.max(new_s, axis=-1, keepdims=True)
    )
    old_e = jnp.exp(old_s - top)
    new_e = jnp.exp(new_s - top)
    total = jnp.sum(old_e, axis=-1, keepdims=True) + jnp.sum(new_e, axis=-1, keepdims=True)
    old_w = (old_e / total).reshape(HEADS * both, rows * length).astype(BF16)
    new_w = (new_e / total).reshape(HEADS * both, both).astype(BF16)
    attended = nt_dot(old_w, kv[HEAD:]) + dot(new_w, new[:, HEAD:])
    for h in range(HEADS):
        merged[:, h * HEAD : (h + 1) * HEAD] = attended[h * both : (h + 1) * both]
    hidden = jnp.concatenate([hid_ref[s].astype(F32) for s in range(steps)], axis=0)
    resid = hidden + merged[...]
    resid_ref[...] = resid
    meansq = jnp.mean(resid * resid, axis=-1, keepdims=True)
    gain = gain_ref[...].astype(F32)
    gain = jnp.concatenate([gain[i : i + 1] for i in range(width // LANES)], axis=1)
    normed = resid * lax.rsqrt(meansq + 1e-06) * gain
    out_ref[:, :width] = normed.astype(BF16)
    out_ref[:, width:] = tail(ids_ref, weight_ref, steps, rows)
    down.wait()


def attend(cache_len, ids, weights, queries, fresh, kv_cache, hidden_state, norm_gain, down):
    steps, rows, width = queries.shape
    kv = kv_cache.transpose(0, 2, 1)
    gain = norm_gain.reshape(width // LANES, LANES)
    return pl.pallas_call(
        attend_kernel,
        out_shape=(
            jax.ShapeDtypeStruct((steps * rows, width), F32),
            jax.ShapeDtypeStruct((steps * rows, width + LANES), BF16),
            jax.ShapeDtypeStruct(down.shape[1:], BF16),
        ),
        in_specs=[HBM] * 9,
        out_specs=(VMEM, VMEM, VMEM),
        scratch_shapes=[
            pltpu.SMEM(cache_len.shape, jnp.int32),
            pltpu.SMEM(ids.shape, jnp.int32),
            pltpu.SMEM(weights.shape, F32),
            pltpu.VMEM(queries.shape, BF16),
            pltpu.VMEM(fresh.shape, BF16),
            pltpu.VMEM(kv.shape, BF16),
            pltpu.VMEM(hidden_state.shape, BF16),
            pltpu.VMEM(gain.shape, BF16),
            pltpu.VMEM((steps * rows, width), F32),
            pltpu.SemaphoreType.DMA((9,)),
        ],
        compiler_params=pltpu.CompilerParams(vmem_limit_bytes=24 * MIB),
        cost_estimate=pl.CostEstimate(
            flops=300_000_000, bytes_accessed=2_000_000, transcendentals=131072
        ),
        name="attend",
    )(*in_hbm(cache_len, ids, weights, queries, fresh, kv, hidden_state, gain, down))


def pack_kernel(steps, chips, own_ref, other_ref, *outs):
    both, width = own_ref.shape
    width -= LANES
    rows = both // steps
    piece = width // PIECES
    side_lines = steps * CAP
    lines = PIECES * 2 * side_lines
    tails = [ref[:, width:].astype(F32) for ref in (own_ref, other_ref)]
    tails = jnp.concatenate(tails * PIECES, axis=0).astype(BF16)
    count = 2 * both * PIECES
    row = iota((len(outs) * lines, LANES), 0)
    lane = iota((len(outs) * lines, LANES), 1)
    wanted = one_hot(lane == PARTS * EXPERTS + expert_at(row // lines, chips))
    named = nt_dot(wanted, tails)
    at = iota((count, count), 0)
    to = iota((count, count), 1)
    before = one_hot((at // rows == to // rows) & (at < to))
    rank = dot(named.astype(BF16), before)
    line = iota(named.shape, 0)
    col = iota(named.shape, 1)
    same = (line // CAP) % (lines // CAP) == col // rows
    picks = one_hot(same & (named > 0.5) & (rank == (line % CAP).astype(F32)))
    parts = [ref[:, :width].astype(F32) for ref in (own_ref, other_ref)]
    stacked = jnp.concatenate(
        [part[:, k * piece : (k + 1) * piece] for k in range(PIECES) for part in parts], axis=0
    ).astype(BF16)
    sent = dot(picks, stacked).astype(BF16)
    for t, out in enumerate(outs):
        out[...] = sent[t * lines : (t + 1) * lines]


def pack(steps, chips, own, other):
    both, width = own.shape
    shape = (PIECES * 2 * steps * CAP, (width - LANES) // PIECES)
    turns = chips // 2
    return pl.pallas_call(
        functools.partial(pack_kernel, steps, chips),
        out_shape=[jax.ShapeDtypeStruct(shape, BF16)] * turns,
        in_specs=[VMEM] * 2,
        out_specs=[VMEM] * turns,
        compiler_params=pltpu.CompilerParams(vmem_limit_bytes=24 * MIB),
        cost_estimate=pl.CostEstimate(
            flops=50_000_000, bytes_accessed=2_000_000, transcendentals=0
        ),
        name="pack",
    )(own, other)


def mixing(steps, chips, own_ref, other_ref):
    both, width = own_ref.shape
    width -= LANES
    rows = both // steps
    lines = PIECES * 2 * steps * CAP
    tails = [ref[:, width:].astype(F32) for ref in (own_ref, other_ref)]
    tails = jnp.concatenate(tails, axis=0).astype(BF16)
    count = chips // 2 * lines
    lane = iota((LANES, count), 0)
    expert = expert_at(iota((LANES, count), 1) // lines, chips)
    found = [dot(tails, one_hot(lane == part * EXPERTS + expert)) for part in range(PARTS + 1)]
    at = iota((2 * both, 2 * both), 1)
    to = iota((2 * both, 2 * both), 0)
    rank = dot(one_hot((at // rows == to // rows) & (at < to)), found[PARTS].astype(BF16))
    line = iota((2 * both, count), 1)
    row = iota((2 * both, count), 0)
    same = (line // CAP) % (2 * steps) == row // rows
    slot = same & (rank == (line % CAP).astype(F32))
    k_of = line // (2 * steps * CAP) % PIECES
    parts = [
        jnp.where(slot & (k_of == k), found[part], 0.0)
        for part in range(PARTS)
        for k in range(PIECES)
    ]
    return jnp.concatenate(parts, axis=0).astype(BF16)


def stage_kernel(which, gu_hbm, out, sems):
    step = out.shape[0] // 4
    copies = []
    for i in range(4):
        part = pl.ds(i * step, step)
        copies.append(pltpu.make_async_copy(gu_hbm.at[0, which, part], out.at[part], sems.at[i]))
    for copy in copies:
        copy.start()
    for copy in copies:
        copy.wait()


def stage(which, gate_up):
    return pl.pallas_call(
        functools.partial(stage_kernel, which),
        out_shape=jax.ShapeDtypeStruct(gate_up.shape[2:], BF16),
        in_specs=[HBM],
        out_specs=VMEM,
        scratch_shapes=[pltpu.SemaphoreType.DMA((4,))],
        compiler_params=pltpu.CompilerParams(vmem_limit_bytes=16 * MIB),
        cost_estimate=pl.CostEstimate(flops=0, bytes_accessed=8_000_000, transcendentals=0),
        name="stage",
    )(*in_hbm(gate_up))


def mix_kernel(steps, chips, own_ref, other_ref, mix_ref):
    mix_ref[...] = mixing(steps, chips, own_ref, other_ref)


def mixer(steps, chips, own, other):
    lines = PIECES * 2 * steps * CAP
    shape = (PARTS * PIECES * 2 * own.shape[0], chips // 2 * lines)
    return pl.pallas_call(
        functools.partial(mix_kernel, steps, chips),
        out_shape=jax.ShapeDtypeStruct(shape, BF16),
        in_specs=[VMEM, VMEM],
        out_specs=VMEM,
        compiler_params=pltpu.CompilerParams(vmem_limit_bytes=24 * MIB),
        cost_estimate=pl.CostEstimate(
            flops=10_000_000, bytes_accessed=1_000_000, transcendentals=0
        ),
        name="mixer",
    )(own, other)


def expert_kernel(turns, *refs):
    own_refs, other_refs = refs[:turns], refs[turns : 2 * turns]
    w_gate, w_upper, w_down = refs[2 * turns : 2 * turns + 3]
    mine_refs = refs[2 * turns + 3 : 3 * turns + 3]
    theirs_refs = refs[3 * turns + 3 :]
    lines, piece = own_refs[0].shape
    per = lines // PIECES
    half = turns * per
    n = turns * lines
    row = iota((n, n), 0)
    col = iota((n, n), 1)
    order = one_hot(col == row // per % turns * lines + row // half * per + row % per)
    sides = [
        dot(order, jnp.concatenate([ref[...] for ref in now], axis=0)).astype(BF16)
        for now in (own_refs, other_refs)
    ]
    gate = upper = None
    for k in range(PIECES):
        x = jnp.concatenate([side[k * half : (k + 1) * half] for side in sides], axis=0)
        cols = pl.ds(k * piece, piece)
        g, u = nt_dot(x, w_gate[:, cols]), nt_dot(x, w_upper[:, cols])
        gate, upper = (g, u) if k == 0 else (gate + g, upper + u)
    act = (gate / (1.0 + jnp.exp(-gate)) * upper).astype(BF16)
    mine = []
    theirs = []
    for k in range(PIECES):
        part = dot(act, w_down[:, k * piece : (k + 1) * piece]).astype(BF16)
        mine.append(part[:half])
        theirs.append(part[half:])
    back = one_hot(row == col // per % turns * lines + col // half * per + col % per)
    for parts, now in ((theirs, theirs_refs), (mine, mine_refs)):
        out = dot(back, jnp.concatenate(parts, axis=0)).astype(BF16)
        for t, ref in enumerate(now):
            ref[...] = out[t * lines : (t + 1) * lines]


def experts(own, other, gate, upper, down):
    turns = len(own)
    shape = jax.ShapeDtypeStruct(own[0].shape, BF16)
    results = pl.pallas_call(
        functools.partial(expert_kernel, turns),
        out_shape=[shape] * (2 * turns),
        in_specs=[VMEM] * (2 * turns + 3),
        out_specs=[VMEM] * (2 * turns),
        compiler_params=pltpu.CompilerParams(vmem_limit_bytes=32 * MIB),
        cost_estimate=pl.CostEstimate(
            flops=800_000_000, bytes_accessed=12_000_000, transcendentals=16384
        ),
        name="experts",
    )(*own, *other, gate, upper, down)
    return results[:turns], results[turns:]


def combine_kernel(mix_ref, resid_ref, *refs):
    back_refs, (kept_ref, sent_ref) = refs[:-2], refs[-2:]
    both = resid_ref.shape[0]
    piece = back_refs[0].shape[1]
    product = dot(mix_ref[...], jnp.concatenate([ref[...] for ref in back_refs], axis=0))
    n = PIECES * 2 * both
    total = product[:n] + product[n : 2 * n] + product[2 * n :]
    for k in range(PIECES):
        cols = pl.ds(k * piece, piece)
        first = k * 2 * both
        kept_ref[:, cols] = resid_ref[:, cols] + total[first : first + both]
        sent_ref[:, cols] = total[first + both : first + 2 * both].astype(BF16)


def combine(mix, resid, backs):
    return pl.pallas_call(
        combine_kernel,
        out_shape=(
            jax.ShapeDtypeStruct(resid.shape, F32),
            jax.ShapeDtypeStruct(resid.shape, BF16),
        ),
        in_specs=[VMEM] * (2 + len(backs)),
        out_specs=(VMEM, VMEM),
        compiler_params=pltpu.CompilerParams(vmem_limit_bytes=24 * MIB),
        cost_estimate=pl.CostEstimate(
            flops=100_000_000, bytes_accessed=1_000_000, transcendentals=0
        ),
        name="combine",
    )(mix, resid, *backs)


def finish_kernel(kept_ref, other_ref, out_ref):
    steps, rows, _ = out_ref.shape
    done = (kept_ref[...] + other_ref[...].astype(F32)).astype(BF16)
    for s in range(steps):
        out_ref[s] = done[s * rows : (s + 1) * rows]


def finish(shape, kept, other):
    return pl.pallas_call(
        finish_kernel,
        out_shape=jax.ShapeDtypeStruct(shape, BF16),
        in_specs=[VMEM, VMEM],
        out_specs=VMEM,
        compiler_params=pltpu.CompilerParams(vmem_limit_bytes=24 * MIB),
        cost_estimate=pl.CostEstimate(flops=100_000, bytes_accessed=500_000, transcendentals=0),
        name="finish",
    )(kept, other)


def per_device(
    queries,
    fresh,
    kv_cache,
    cache_len,
    hidden_state,
    norm_gain,
    expert_ids,
    route_weight,
    gate_up,
    down,
):
    steps = queries.shape[0]
    owners = lax.axis_size("afd")
    chips = owners // 2
    turns = chips // 2
    cores = [(i, i ^ 1) for i in range(owners)]

    def swap(x):
        return lax.ppermute(x, "afd", cores)

    def route(t):
        return [(i, (i // 2 ^ distance(t, i % 2, chips)) * 2 + 1 - i % 2) for i in range(owners)]

    def send(x, t):
        return lax.ppermute(x, "afd", route(t))

    def send_back(x, t):
        return lax.ppermute(x, "afd", [(j, i) for i, j in route(t)])

    ids = expert_ids.transpose(2, 0, 1)
    weights = route_weight.transpose(2, 0, 1)
    resid, normed, w_down = attend(
        cache_len, ids, weights, queries, fresh, kv_cache, hidden_state, norm_gain, down
    )
    normed_other = swap(normed)
    w_gate = stage(0, gate_up)
    w_gate, normed_other = lax.optimization_barrier((w_gate, normed_other))
    sent = pack(steps, chips, normed, normed_other)
    own = [send(sent[t], t) for t in range(turns)]
    w_upper = stage(1, gate_up)
    mix = mixer(steps, chips, normed, normed_other)
    own[0], w_upper = lax.optimization_barrier((own[0], w_upper))
    other = [swap(x) for x in own]
    summed = []
    for t in range(0, turns, TOGETHER):
        now = slice(t, t + TOGETHER)
        mine, theirs = experts(own[now], other[now], w_gate, w_upper, w_down)
        summed += [
            (a.astype(F32) + swap(b).astype(F32)).astype(BF16) for a, b in zip(mine, theirs)
        ]
    backs = [send_back(summed[t], t) for t in range(turns)]
    kept, given = combine(mix, resid, backs)
    return finish(queries.shape, kept, swap(given))


def solution(mesh):
    placed = (
        P(None, ("group", "afd"), None),
        P(None, ("group", "afd"), None),
        P(("group", "afd"), None, None),
        P(("group", "afd")),
        P(None, ("group", "afd"), None),
        P(),
        P(None, ("group", "afd"), None),
        P(None, ("group", "afd"), None),
        P("afd", None, None, None),
        P("afd", None, None),
    )
    return jax.shard_map(
        per_device,
        mesh=mesh,
        in_specs=placed,
        out_specs=P(None, ("group", "afd"), None),
        check_vma=False,
    )
```

```python
import functools
import jax
import jax.numpy as jnp
from jax import lax
from jax.experimental import pallas as pl
from jax.experimental.pallas import tpu as pltpu
from jax.sharding import PartitionSpec as P

HEADS = 32
HEAD = 224
EXPERTS = 8
TOP = 3
CAP = 2
PIECES = 4
LANES = 128
PARTS = 3
F32 = jnp.float32
BF16 = jnp.bfloat16
MIB = 1 << 20
VMEM = pl.BlockSpec(memory_space=pltpu.VMEM)
HBM = pl.BlockSpec(memory_space=pltpu.HBM)
TOGETHER = 2


def iota(shape, dim):
    return lax.broadcasted_iota(jnp.int32, shape, dim)


def in_hbm(*arrays):
    return [pltpu.with_memory_space_constraint(x, pltpu.HBM) for x in arrays]


def nt_dot(a, b):
    return lax.dot_general(a, b, (((1,), (1,)), ((), ())), preferred_element_type=F32)


def dot(a, b):
    return jnp.dot(a, b, preferred_element_type=F32)


def one_hot(mask):
    return jnp.where(mask, 1.0, 0.0).astype(BF16)


def distance(turn, core, chips):
    return (2 * turn) ^ (core * (chips - 1))


def expert_at(turn, chips):
    place = lax.axis_index("afd")
    return (distance(turn, place % 2, chips) ^ (place // 2)) // (chips // EXPERTS)


def spread(ref, k, where, steps, rows, empty):
    out = jnp.full(where.shape, empty)
    for s in range(steps):
        for r in range(rows):
            out = jnp.where(where == s * rows + r, ref[k, s, r], out)
    return out


def tail(ids_ref, weight_ref, steps, rows):
    both = steps * rows
    lane = iota((both, LANES), 1)
    where = iota((both, 1), 0)
    mix = jnp.zeros((both, LANES), F32)
    named = jnp.zeros((both, LANES), F32)
    for k in range(TOP):
        hit = spread(ids_ref, k, where, steps, rows, -1) == lane % EXPERTS
        mix = mix + jnp.where(hit, spread(weight_ref, k, where, steps, rows, 0.0), 0.0)
        named = named + jnp.where(hit, 1.0, 0.0)
    out = jnp.where(lane // EXPERTS == PARTS, named, 0.0)
    for part in range(PARTS):
        term = mix.astype(BF16).astype(F32)
        out = jnp.where(lane // EXPERTS == part, term, out)
        mix = mix - term
    return out.astype(BF16)


def attend_kernel(
    len_hbm,
    ids_hbm,
    weight_hbm,
    q_hbm,
    fresh_hbm,
    kv_hbm,
    hid_hbm,
    gain_hbm,
    dn_hbm,
    resid_ref,
    out_ref,
    dn_ref,
    len_ref,
    ids_ref,
    weight_ref,
    q_ref,
    fresh_ref,
    kv_ref,
    hid_ref,
    gain_ref,
    merged,
    sems,
):
    copies = [
        pltpu.make_async_copy(source, target, sems.at[i])
        for i, (source, target) in enumerate(
            (
                (q_hbm, q_ref),
                (kv_hbm, kv_ref),
                (len_hbm, len_ref),
                (ids_hbm, ids_ref),
                (weight_hbm, weight_ref),
                (fresh_hbm, fresh_ref),
                (hid_hbm, hid_ref),
                (gain_hbm, gain_ref),
            )
        )
    ]
    down = pltpu.make_async_copy(dn_hbm.at[0], dn_ref, sems.at[len(copies)])
    for copy in [*copies, down]:
        copy.start()
    steps, rows, width = q_ref.shape
    length = kv_ref.shape[2]
    both = steps * rows
    scale = HEAD ** (-0.5)
    for copy in copies:
        copy.wait()
    q = jnp.concatenate([q_ref[s].astype(F32) for s in range(steps)], axis=0)
    heads = jnp.concatenate([q[:, h * HEAD : (h + 1) * HEAD] for h in range(HEADS)], axis=0)
    heads = heads.astype(BF16)
    kv = jnp.concatenate([kv_ref[r] for r in range(rows)], axis=1)
    new = jnp.concatenate([fresh_ref[s].astype(F32) for s in range(steps)], axis=0).astype(BF16)

    sub = iota((both, rows * length), 0)
    lane = iota((both, rows * length), 1)
    limit = jnp.zeros_like(lane)
    for r in range(rows):
        limit = jnp.where(lane // length == r, len_ref[r], limit)
    valid = (lane // length == sub % rows) & (lane % length < limit)
    sub = iota((both, both), 0)
    lane = iota((both, both), 1)
    valid_new = (lane % rows == sub % rows) & (lane // rows <= sub // rows)

    old_s = (dot(heads, kv[:HEAD]) * scale).reshape(HEADS, both, rows * length)
    new_s = (nt_dot(heads, new[:, :HEAD]) * scale).reshape(HEADS, both, both)
    old_s = jnp.where(valid[None], old_s, -1e30)
    new_s = jnp.where(valid_new[None], new_s, -1e30)
    top = jnp.maximum(
        jnp.max(old_s, axis=-1, keepdims=True), jnp.max(new_s, axis=-1, keepdims=True)
    )
    old_e = jnp.exp(old_s - top)
    new_e = jnp.exp(new_s - top)
    total = jnp.sum(old_e, axis=-1, keepdims=True) + jnp.sum(new_e, axis=-1, keepdims=True)
    old_w = (old_e / total).reshape(HEADS * both, rows * length).astype(BF16)
    new_w = (new_e / total).reshape(HEADS * both, both).astype(BF16)
    attended = nt_dot(old_w, kv[HEAD:]) + dot(new_w, new[:, HEAD:])
    for h in range(HEADS):
        merged[:, h * HEAD : (h + 1) * HEAD] = attended[h * both : (h + 1) * both]
    hidden = jnp.concatenate([hid_ref[s].astype(F32) for s in range(steps)], axis=0)
    resid = hidden + merged[...]
    resid_ref[...] = resid
    meansq = jnp.mean(resid * resid, axis=-1, keepdims=True)
    gain = gain_ref[...].astype(F32)
    gain = jnp.concatenate([gain[i : i + 1] for i in range(width // LANES)], axis=1)
    normed = resid * lax.rsqrt(meansq + 1e-06) * gain
    out_ref[:, :width] = normed.astype(BF16)
    out_ref[:, width:] = tail(ids_ref, weight_ref, steps, rows)
    down.wait()


def attend(cache_len, ids, weights, queries, fresh, kv_cache, hidden_state, norm_gain, down):
    steps, rows, width = queries.shape
    kv = kv_cache.transpose(0, 2, 1)
    gain = norm_gain.reshape(width // LANES, LANES)
    return pl.pallas_call(
        attend_kernel,
        out_shape=(
            jax.ShapeDtypeStruct((steps * rows, width), F32),
            jax.ShapeDtypeStruct((steps * rows, width + LANES), BF16),
            jax.ShapeDtypeStruct(down.shape[1:], BF16),
        ),
        in_specs=[HBM] * 9,
        out_specs=(VMEM, VMEM, VMEM),
        scratch_shapes=[
            pltpu.SMEM(cache_len.shape, jnp.int32),
            pltpu.SMEM(ids.shape, jnp.int32),
            pltpu.SMEM(weights.shape, F32),
            pltpu.VMEM(queries.shape, BF16),
            pltpu.VMEM(fresh.shape, BF16),
            pltpu.VMEM(kv.shape, BF16),
            pltpu.VMEM(hidden_state.shape, BF16),
            pltpu.VMEM(gain.shape, BF16),
            pltpu.VMEM((steps * rows, width), F32),
            pltpu.SemaphoreType.DMA((9,)),
        ],
        compiler_params=pltpu.CompilerParams(vmem_limit_bytes=24 * MIB),
        cost_estimate=pl.CostEstimate(
            flops=300_000_000, bytes_accessed=2_000_000, transcendentals=131072
        ),
        name="attend",
    )(*in_hbm(cache_len, ids, weights, queries, fresh, kv, hidden_state, gain, down))


def pack_kernel(steps, chips, own_ref, other_ref, *outs):
    both, width = own_ref.shape
    width -= LANES
    rows = both // steps
    piece = width // PIECES
    side_lines = steps * CAP
    lines = PIECES * 2 * side_lines
    tails = [ref[:, width:].astype(F32) for ref in (own_ref, other_ref)]
    tails = jnp.concatenate(tails * PIECES, axis=0).astype(BF16)
    count = 2 * both * PIECES
    row = iota((len(outs) * lines, LANES), 0)
    lane = iota((len(outs) * lines, LANES), 1)
    wanted = one_hot(lane == PARTS * EXPERTS + expert_at(row // lines, chips))
    named = nt_dot(wanted, tails)
    at = iota((count, count), 0)
    to = iota((count, count), 1)
    before = one_hot((at // rows == to // rows) & (at < to))
    rank = dot(named.astype(BF16), before)
    line = iota(named.shape, 0)
    col = iota(named.shape, 1)
    same = (line // CAP) % (lines // CAP) == col // rows
    picks = one_hot(same & (named > 0.5) & (rank == (line % CAP).astype(F32)))
    parts = [ref[:, :width].astype(F32) for ref in (own_ref, other_ref)]
    stacked = jnp.concatenate(
        [part[:, k * piece : (k + 1) * piece] for k in range(PIECES) for part in parts], axis=0
    ).astype(BF16)
    sent = dot(picks, stacked).astype(BF16)
    for t, out in enumerate(outs):
        out[...] = sent[t * lines : (t + 1) * lines]


def pack(steps, chips, own, other):
    both, width = own.shape
    shape = (PIECES * 2 * steps * CAP, (width - LANES) // PIECES)
    turns = chips // 2
    return pl.pallas_call(
        functools.partial(pack_kernel, steps, chips),
        out_shape=[jax.ShapeDtypeStruct(shape, BF16)] * turns,
        in_specs=[VMEM] * 2,
        out_specs=[VMEM] * turns,
        compiler_params=pltpu.CompilerParams(vmem_limit_bytes=24 * MIB),
        cost_estimate=pl.CostEstimate(
            flops=50_000_000, bytes_accessed=2_000_000, transcendentals=0
        ),
        name="pack",
    )(own, other)


def mixing(steps, chips, own_ref, other_ref):
    both, width = own_ref.shape
    width -= LANES
    rows = both // steps
    lines = PIECES * 2 * steps * CAP
    tails = [ref[:, width:].astype(F32) for ref in (own_ref, other_ref)]
    tails = jnp.concatenate(tails, axis=0).astype(BF16)
    count = chips // 2 * lines
    lane = iota((LANES, count), 0)
    expert = expert_at(iota((LANES, count), 1) // lines, chips)
    found = [dot(tails, one_hot(lane == part * EXPERTS + expert)) for part in range(PARTS + 1)]
    at = iota((2 * both, 2 * both), 1)
    to = iota((2 * both, 2 * both), 0)
    rank = dot(one_hot((at // rows == to // rows) & (at < to)), found[PARTS].astype(BF16))
    line = iota((2 * both, count), 1)
    row = iota((2 * both, count), 0)
    same = (line // CAP) % (2 * steps) == row // rows
    slot = same & (rank == (line % CAP).astype(F32))
    k_of = line // (2 * steps * CAP) % PIECES
    parts = [
        jnp.where(slot & (k_of == k), found[part], 0.0)
        for part in range(PARTS)
        for k in range(PIECES)
    ]
    return jnp.concatenate(parts, axis=0).astype(BF16)


def stage_kernel(which, gu_hbm, out, sems):
    step = out.shape[0] // 4
    copies = []
    for i in range(4):
        part = pl.ds(i * step, step)
        copies.append(pltpu.make_async_copy(gu_hbm.at[0, which, part], out.at[part], sems.at[i]))
    for copy in copies:
        copy.start()
    for copy in copies:
        copy.wait()


def stage(which, gate_up):
    return pl.pallas_call(
        functools.partial(stage_kernel, which),
        out_shape=jax.ShapeDtypeStruct(gate_up.shape[2:], BF16),
        in_specs=[HBM],
        out_specs=VMEM,
        scratch_shapes=[pltpu.SemaphoreType.DMA((4,))],
        compiler_params=pltpu.CompilerParams(vmem_limit_bytes=16 * MIB),
        cost_estimate=pl.CostEstimate(flops=0, bytes_accessed=8_000_000, transcendentals=0),
        name="stage",
    )(*in_hbm(gate_up))


def mix_kernel(steps, chips, own_ref, other_ref, mix_ref):
    mix_ref[...] = mixing(steps, chips, own_ref, other_ref)


def mixer(steps, chips, own, other):
    lines = PIECES * 2 * steps * CAP
    shape = (PARTS * PIECES * 2 * own.shape[0], chips // 2 * lines)
    return pl.pallas_call(
        functools.partial(mix_kernel, steps, chips),
        out_shape=jax.ShapeDtypeStruct(shape, BF16),
        in_specs=[VMEM, VMEM],
        out_specs=VMEM,
        compiler_params=pltpu.CompilerParams(vmem_limit_bytes=24 * MIB),
        cost_estimate=pl.CostEstimate(
            flops=10_000_000, bytes_accessed=1_000_000, transcendentals=0
        ),
        name="mixer",
    )(own, other)


def expert_kernel(turns, *refs):
    own_refs, other_refs = refs[:turns], refs[turns : -2 * turns - 3]
    w_gate, w_upper, w_down = refs[-2 * turns - 3 : -2 * turns]
    mine_refs, theirs_refs = refs[-2 * turns : -turns], refs[-turns:]
    lines, piece = own_refs[0].shape
    per = lines // PIECES
    half = turns * per
    n = turns * lines
    row = iota((n, n), 0)
    col = iota((n, n), 1)
    order = one_hot(col == row // per % turns * lines + row // half * per + row % per)
    sides = [
        dot(order, jnp.concatenate([ref[...] for ref in now], axis=0)).astype(BF16)
        for now in (own_refs, other_refs)
    ]
    gate = upper = None
    for k in range(PIECES):
        x = jnp.concatenate([side[k * half : (k + 1) * half] for side in sides], axis=0)
        cols = pl.ds(k * piece, piece)
        g, u = nt_dot(x, w_gate[:, cols]), nt_dot(x, w_upper[:, cols])
        gate, upper = (g, u) if k == 0 else (gate + g, upper + u)
    act = (gate / (1.0 + jnp.exp(-gate)) * upper).astype(BF16)
    mine = []
    theirs = []
    for k in range(PIECES):
        part = dot(act, w_down[:, k * piece : (k + 1) * piece]).astype(BF16)
        mine.append(part[:half])
        theirs.append(part[half:])
    back = one_hot(row == col // per % turns * lines + col // half * per + col % per)
    for parts, now in ((theirs, theirs_refs), (mine, mine_refs)):
        out = dot(back, jnp.concatenate(parts, axis=0)).astype(BF16)
        for t, ref in enumerate(now):
            ref[...] = out[t * lines : (t + 1) * lines]


def experts(own, other, gate, upper, down):
    turns = len(own)
    shape = jax.ShapeDtypeStruct(own[0].shape, BF16)
    results = pl.pallas_call(
        functools.partial(expert_kernel, turns),
        out_shape=[shape] * (2 * turns),
        in_specs=[VMEM] * (turns + len(other) + 3),
        out_specs=[VMEM] * (2 * turns),
        compiler_params=pltpu.CompilerParams(vmem_limit_bytes=32 * MIB),
        cost_estimate=pl.CostEstimate(
            flops=800_000_000, bytes_accessed=12_000_000, transcendentals=16384
        ),
        name="experts",
    )(*own, *other, gate, upper, down)
    return results[:turns], results[turns:]


def combine_kernel(mix_ref, resid_ref, *refs):
    back_refs, (kept_ref, sent_ref) = refs[:-2], refs[-2:]
    both = resid_ref.shape[0]
    piece = back_refs[0].shape[1]
    product = dot(mix_ref[...], jnp.concatenate([ref[...] for ref in back_refs], axis=0))
    n = PIECES * 2 * both
    total = product[:n] + product[n : 2 * n] + product[2 * n :]
    for k in range(PIECES):
        cols = pl.ds(k * piece, piece)
        first = k * 2 * both
        kept_ref[:, cols] = resid_ref[:, cols] + total[first : first + both]
        sent_ref[:, cols] = total[first + both : first + 2 * both].astype(BF16)


def combine(mix, resid, backs):
    return pl.pallas_call(
        combine_kernel,
        out_shape=(
            jax.ShapeDtypeStruct(resid.shape, F32),
            jax.ShapeDtypeStruct(resid.shape, BF16),
        ),
        in_specs=[VMEM] * (2 + len(backs)),
        out_specs=(VMEM, VMEM),
        compiler_params=pltpu.CompilerParams(vmem_limit_bytes=24 * MIB),
        cost_estimate=pl.CostEstimate(
            flops=100_000_000, bytes_accessed=1_000_000, transcendentals=0
        ),
        name="combine",
    )(mix, resid, *backs)


def finish_kernel(kept_ref, other_ref, out_ref):
    steps, rows, _ = out_ref.shape
    done = (kept_ref[...] + other_ref[...].astype(F32)).astype(BF16)
    for s in range(steps):
        out_ref[s] = done[s * rows : (s + 1) * rows]


def finish(shape, kept, other):
    return pl.pallas_call(
        finish_kernel,
        out_shape=jax.ShapeDtypeStruct(shape, BF16),
        in_specs=[VMEM, VMEM],
        out_specs=VMEM,
        compiler_params=pltpu.CompilerParams(vmem_limit_bytes=24 * MIB),
        cost_estimate=pl.CostEstimate(flops=100_000, bytes_accessed=500_000, transcendentals=0),
        name="finish",
    )(kept, other)


def per_device(
    queries,
    fresh,
    kv_cache,
    cache_len,
    hidden_state,
    norm_gain,
    expert_ids,
    route_weight,
    gate_up,
    down,
):
    steps = queries.shape[0]
    owners = lax.axis_size("afd")
    chips = owners // 2
    turns = chips // 2
    cores = [(i, i ^ 1) for i in range(owners)]

    def swap(x):
        return lax.ppermute(x, "afd", cores)

    def route(t):
        return [(i, (i // 2 ^ distance(t, i % 2, chips)) * 2 + 1 - i % 2) for i in range(owners)]

    def send(x, t):
        return lax.ppermute(x, "afd", route(t))

    def send_back(x, t):
        return lax.ppermute(x, "afd", [(j, i) for i, j in route(t)])

    ids = expert_ids.transpose(2, 0, 1)
    weights = route_weight.transpose(2, 0, 1)
    resid, normed, w_down = attend(
        cache_len, ids, weights, queries, fresh, kv_cache, hidden_state, norm_gain, down
    )
    normed_other = swap(normed)
    w_gate = stage(0, gate_up)
    w_gate, normed_other = lax.optimization_barrier((w_gate, normed_other))
    sent = pack(steps, chips, normed, normed_other)
    own = [send(sent[t], t) for t in range(turns)]
    w_upper = stage(1, gate_up)
    mix = mixer(steps, chips, normed, normed_other)
    own[:TOGETHER], w_upper = lax.optimization_barrier((own[:TOGETHER], w_upper))
    backs = []
    for first in range(0, turns, TOGETHER):
        now = own[first : first + TOGETHER]
        cut = 1 if first else 2
        other = [jnp.concatenate([swap(part) for part in jnp.split(x, cut)]) for x in now]
        mine, theirs = experts(now, other, w_gate, w_upper, w_down)
        theirs, backs = lax.optimization_barrier((theirs, backs))
        rest = own[first + TOGETHER :]
        mine, own[first + TOGETHER :] = lax.optimization_barrier((mine, rest))
        summed = [
            (a.astype(F32) + swap(b).astype(F32)).astype(BF16) for a, b in zip(mine, theirs)
        ]
        backs = backs + [send_back(x, first + i) for i, x in enumerate(summed)]
    kept, given = combine(mix, resid, backs)
    return finish(queries.shape, kept, swap(given))


def solution(mesh):
    placed = (
        P(None, ("group", "afd"), None),
        P(None, ("group", "afd"), None),
        P(("group", "afd"), None, None),
        P(("group", "afd")),
        P(None, ("group", "afd"), None),
        P(),
        P(None, ("group", "afd"), None),
        P(None, ("group", "afd"), None),
        P("afd", None, None, None),
        P("afd", None, None),
    )
    return jax.shard_map(
        per_device,
        mesh=mesh,
        in_specs=placed,
        out_specs=P(None, ("group", "afd"), None),
        check_vma=False,
    )
```

```python
import functools
import jax
import jax.numpy as jnp
from jax import lax
from jax.experimental import pallas as pl
from jax.experimental.pallas import tpu as pltpu
from jax.sharding import PartitionSpec as P

HEADS = 32
HEAD = 224
EXPERTS = 8
TOP = 3
CAP = 2
PIECES = 4
LANES = 128
PARTS = 3
F32 = jnp.float32
BF16 = jnp.bfloat16
MIB = 1 << 20
VMEM = pl.BlockSpec(memory_space=pltpu.VMEM)
HBM = pl.BlockSpec(memory_space=pltpu.HBM)
TOGETHER = 4


def iota(shape, dim):
    return lax.broadcasted_iota(jnp.int32, shape, dim)


def in_hbm(*arrays):
    return [pltpu.with_memory_space_constraint(x, pltpu.HBM) for x in arrays]


def nt_dot(a, b):
    return lax.dot_general(a, b, (((1,), (1,)), ((), ())), preferred_element_type=F32)


def dot(a, b):
    return jnp.dot(a, b, preferred_element_type=F32)


def one_hot(mask):
    return jnp.where(mask, 1.0, 0.0).astype(BF16)


def distance(turn, core, chips):
    bits = (chips // 2).bit_length() - 1
    even = 0
    for b in range(bits):
        even = even + ((turn >> b) % 2 << (bits - b))
    return even ^ (core * (chips - 1))


def expert_at(turn, chips):
    place = lax.axis_index("afd")
    return (distance(turn, place % 2, chips) ^ (place // 2)) // (chips // EXPERTS)


def spread(ref, k, where, steps, rows, empty):
    out = jnp.full(where.shape, empty)
    for s in range(steps):
        for r in range(rows):
            out = jnp.where(where == s * rows + r, ref[k, s, r], out)
    return out


def tail(ids_ref, weight_ref, steps, rows):
    both = steps * rows
    lane = iota((both, LANES), 1)
    where = iota((both, 1), 0)
    mix = jnp.zeros((both, LANES), F32)
    named = jnp.zeros((both, LANES), F32)
    for k in range(TOP):
        hit = spread(ids_ref, k, where, steps, rows, -1) == lane % EXPERTS
        mix = mix + jnp.where(hit, spread(weight_ref, k, where, steps, rows, 0.0), 0.0)
        named = named + jnp.where(hit, 1.0, 0.0)
    out = jnp.where(lane // EXPERTS == PARTS, named, 0.0)
    for part in range(PARTS):
        term = mix.astype(BF16).astype(F32)
        out = jnp.where(lane // EXPERTS == part, term, out)
        mix = mix - term
    return out.astype(BF16)


def attend_kernel(
    len_hbm,
    ids_hbm,
    weight_hbm,
    q_hbm,
    fresh_hbm,
    kv_hbm,
    hid_hbm,
    gain_hbm,
    dn_hbm,
    resid_ref,
    out_ref,
    dn_ref,
    len_ref,
    ids_ref,
    weight_ref,
    q_ref,
    fresh_ref,
    kv_ref,
    hid_ref,
    gain_ref,
    merged,
    sems,
):
    copies = [
        pltpu.make_async_copy(source, target, sems.at[i])
        for i, (source, target) in enumerate(
            (
                (q_hbm, q_ref),
                (kv_hbm, kv_ref),
                (len_hbm, len_ref),
                (ids_hbm, ids_ref),
                (weight_hbm, weight_ref),
                (fresh_hbm, fresh_ref),
                (hid_hbm, hid_ref),
                (gain_hbm, gain_ref),
            )
        )
    ]
    down = pltpu.make_async_copy(dn_hbm.at[0], dn_ref, sems.at[len(copies)])
    for copy in [*copies, down]:
        copy.start()
    steps, rows, width = q_ref.shape
    length = kv_ref.shape[2]
    both = steps * rows
    scale = HEAD ** (-0.5)
    for copy in copies:
        copy.wait()
    q = jnp.concatenate([q_ref[s].astype(F32) for s in range(steps)], axis=0)
    heads = jnp.concatenate([q[:, h * HEAD : (h + 1) * HEAD] for h in range(HEADS)], axis=0)
    heads = heads.astype(BF16)
    kv = jnp.concatenate([kv_ref[r] for r in range(rows)], axis=1)
    new = jnp.concatenate([fresh_ref[s].astype(F32) for s in range(steps)], axis=0).astype(BF16)

    sub = iota((both, rows * length), 0)
    lane = iota((both, rows * length), 1)
    limit = jnp.zeros_like(lane)
    for r in range(rows):
        limit = jnp.where(lane // length == r, len_ref[r], limit)
    valid = (lane // length == sub % rows) & (lane % length < limit)
    sub = iota((both, both), 0)
    lane = iota((both, both), 1)
    valid_new = (lane % rows == sub % rows) & (lane // rows <= sub // rows)

    old_s = (dot(heads, kv[:HEAD]) * scale).reshape(HEADS, both, rows * length)
    new_s = (nt_dot(heads, new[:, :HEAD]) * scale).reshape(HEADS, both, both)
    old_s = jnp.where(valid[None], old_s, -1e30)
    new_s = jnp.where(valid_new[None], new_s, -1e30)
    top = jnp.maximum(
        jnp.max(old_s, axis=-1, keepdims=True), jnp.max(new_s, axis=-1, keepdims=True)
    )
    old_e = jnp.exp(old_s - top)
    new_e = jnp.exp(new_s - top)
    total = jnp.sum(old_e, axis=-1, keepdims=True) + jnp.sum(new_e, axis=-1, keepdims=True)
    old_w = (old_e / total).reshape(HEADS * both, rows * length).astype(BF16)
    new_w = (new_e / total).reshape(HEADS * both, both).astype(BF16)
    attended = nt_dot(old_w, kv[HEAD:]) + dot(new_w, new[:, HEAD:])
    for h in range(HEADS):
        merged[:, h * HEAD : (h + 1) * HEAD] = attended[h * both : (h + 1) * both]
    hidden = jnp.concatenate([hid_ref[s].astype(F32) for s in range(steps)], axis=0)
    resid = hidden + merged[...]
    resid_ref[...] = resid
    meansq = jnp.mean(resid * resid, axis=-1, keepdims=True)
    gain = gain_ref[...].astype(F32)
    gain = jnp.concatenate([gain[i : i + 1] for i in range(width // LANES)], axis=1)
    normed = resid * lax.rsqrt(meansq + 1e-06) * gain
    out_ref[:, :width] = normed.astype(BF16)
    out_ref[:, width:] = tail(ids_ref, weight_ref, steps, rows)
    down.wait()


def attend(cache_len, ids, weights, queries, fresh, kv_cache, hidden_state, norm_gain, down):
    steps, rows, width = queries.shape
    kv = kv_cache.transpose(0, 2, 1)
    gain = norm_gain.reshape(width // LANES, LANES)
    return pl.pallas_call(
        attend_kernel,
        out_shape=(
            jax.ShapeDtypeStruct((steps * rows, width), F32),
            jax.ShapeDtypeStruct((steps * rows, width + LANES), BF16),
            jax.ShapeDtypeStruct(down.shape[1:], BF16),
        ),
        in_specs=[HBM] * 9,
        out_specs=(VMEM, VMEM, VMEM),
        scratch_shapes=[
            pltpu.SMEM(cache_len.shape, jnp.int32),
            pltpu.SMEM(ids.shape, jnp.int32),
            pltpu.SMEM(weights.shape, F32),
            pltpu.VMEM(queries.shape, BF16),
            pltpu.VMEM(fresh.shape, BF16),
            pltpu.VMEM(kv.shape, BF16),
            pltpu.VMEM(hidden_state.shape, BF16),
            pltpu.VMEM(gain.shape, BF16),
            pltpu.VMEM((steps * rows, width), F32),
            pltpu.SemaphoreType.DMA((9,)),
        ],
        compiler_params=pltpu.CompilerParams(vmem_limit_bytes=24 * MIB),
        cost_estimate=pl.CostEstimate(
            flops=300_000_000, bytes_accessed=2_000_000, transcendentals=131072
        ),
        name="attend",
    )(*in_hbm(cache_len, ids, weights, queries, fresh, kv, hidden_state, gain, down))


def pack_kernel(steps, chips, own_ref, other_ref, *outs):
    both, width = own_ref.shape
    width -= LANES
    rows = both // steps
    piece = width // PIECES
    side_lines = steps * CAP
    lines = PIECES * 2 * side_lines
    tails = [ref[:, width:].astype(F32) for ref in (own_ref, other_ref)]
    tails = jnp.concatenate(tails * PIECES, axis=0).astype(BF16)
    count = 2 * both * PIECES
    row = iota((len(outs) * lines, LANES), 0)
    lane = iota((len(outs) * lines, LANES), 1)
    wanted = one_hot(lane == PARTS * EXPERTS + expert_at(row // lines, chips))
    named = nt_dot(wanted, tails)
    at = iota((count, count), 0)
    to = iota((count, count), 1)
    before = one_hot((at // rows == to // rows) & (at < to))
    rank = dot(named.astype(BF16), before)
    line = iota(named.shape, 0)
    col = iota(named.shape, 1)
    same = (line // CAP) % (lines // CAP) == col // rows
    picks = one_hot(same & (named > 0.5) & (rank == (line % CAP).astype(F32)))
    parts = [ref[:, :width].astype(F32) for ref in (own_ref, other_ref)]
    stacked = jnp.concatenate(
        [part[:, k * piece : (k + 1) * piece] for k in range(PIECES) for part in parts], axis=0
    ).astype(BF16)
    sent = dot(picks, stacked).astype(BF16)
    for t, out in enumerate(outs):
        out[...] = sent[t * lines : (t + 1) * lines]


def pack(steps, chips, own, other):
    both, width = own.shape
    shape = (PIECES * 2 * steps * CAP, (width - LANES) // PIECES)
    turns = chips // 2
    return pl.pallas_call(
        functools.partial(pack_kernel, steps, chips),
        out_shape=[jax.ShapeDtypeStruct(shape, BF16)] * turns,
        in_specs=[VMEM] * 2,
        out_specs=[VMEM] * turns,
        compiler_params=pltpu.CompilerParams(vmem_limit_bytes=24 * MIB),
        cost_estimate=pl.CostEstimate(
            flops=50_000_000, bytes_accessed=2_000_000, transcendentals=0
        ),
        name="pack",
    )(own, other)


def mixing(steps, chips, own_ref, other_ref):
    both, width = own_ref.shape
    width -= LANES
    rows = both // steps
    lines = PIECES * 2 * steps * CAP
    tails = [ref[:, width:].astype(F32) for ref in (own_ref, other_ref)]
    tails = jnp.concatenate(tails, axis=0).astype(BF16)
    count = chips // 2 * lines
    lane = iota((LANES, count), 0)
    expert = expert_at(iota((LANES, count), 1) // lines, chips)
    found = [dot(tails, one_hot(lane == part * EXPERTS + expert)) for part in range(PARTS + 1)]
    at = iota((2 * both, 2 * both), 1)
    to = iota((2 * both, 2 * both), 0)
    rank = dot(one_hot((at // rows == to // rows) & (at < to)), found[PARTS].astype(BF16))
    line = iota((2 * both, count), 1)
    row = iota((2 * both, count), 0)
    same = (line // CAP) % (2 * steps) == row // rows
    slot = same & (rank == (line % CAP).astype(F32))
    k_of = line // (2 * steps * CAP) % PIECES
    parts = [
        jnp.where(slot & (k_of == k), found[part], 0.0)
        for part in range(PARTS)
        for k in range(PIECES)
    ]
    return jnp.concatenate(parts, axis=0).astype(BF16)


def stage_kernel(gu_hbm, out, sems):
    step = out.shape[1] // 4
    copies = []
    for i in range(8):
        part = pl.ds(i // 2 * step, step)
        copies.append(
            pltpu.make_async_copy(gu_hbm.at[0, i % 2, part], out.at[i % 2, part], sems.at[i])
        )
    for copy in copies:
        copy.start()
    for copy in copies:
        copy.wait()


def stage(gate_up):
    return pl.pallas_call(
        stage_kernel,
        out_shape=jax.ShapeDtypeStruct(gate_up.shape[1:], BF16),
        in_specs=[HBM],
        out_specs=VMEM,
        scratch_shapes=[pltpu.SemaphoreType.DMA((8,))],
        compiler_params=pltpu.CompilerParams(vmem_limit_bytes=16 * MIB),
        cost_estimate=pl.CostEstimate(flops=0, bytes_accessed=16_000_000, transcendentals=0),
        name="stage",
    )(*in_hbm(gate_up))


def mix_kernel(steps, chips, own_ref, other_ref, mix_ref):
    mix_ref[...] = mixing(steps, chips, own_ref, other_ref)


def mixer(steps, chips, own, other):
    lines = PIECES * 2 * steps * CAP
    shape = (PARTS * PIECES * 2 * own.shape[0], chips // 2 * lines)
    return pl.pallas_call(
        functools.partial(mix_kernel, steps, chips),
        out_shape=jax.ShapeDtypeStruct(shape, BF16),
        in_specs=[VMEM, VMEM],
        out_specs=VMEM,
        compiler_params=pltpu.CompilerParams(vmem_limit_bytes=24 * MIB),
        cost_estimate=pl.CostEstimate(
            flops=10_000_000, bytes_accessed=1_000_000, transcendentals=0
        ),
        name="mixer",
    )(own, other)


def expert_kernel(turns, *refs):
    own_refs, other_refs = refs[:turns], refs[turns : 2 * turns]
    w_in, w_down = refs[2 * turns : 2 * turns + 2]
    mine_refs = refs[2 * turns + 2 : 3 * turns + 2]
    theirs_refs = refs[3 * turns + 2 :]
    lines, piece = own_refs[0].shape
    per = lines // PIECES
    half = turns * per
    n = turns * lines
    row = iota((n, n), 0)
    col = iota((n, n), 1)
    order = one_hot(col == row // per % turns * lines + row // half * per + row % per)
    sides = [
        dot(order, jnp.concatenate([ref[...] for ref in now], axis=0)).astype(BF16)
        for now in (own_refs, other_refs)
    ]
    gate = upper = None
    for k in range(PIECES):
        x = jnp.concatenate([side[k * half : (k + 1) * half] for side in sides], axis=0)
        cols = pl.ds(k * piece, piece)
        g, u = nt_dot(x, w_in[0, :, cols]), nt_dot(x, w_in[1, :, cols])
        gate, upper = (g, u) if k == 0 else (gate + g, upper + u)
    act = (gate / (1.0 + jnp.exp(-gate)) * upper).astype(BF16)
    mine = []
    theirs = []
    for k in range(PIECES):
        part = dot(act, w_down[:, k * piece : (k + 1) * piece]).astype(BF16)
        mine.append(part[:half])
        theirs.append(part[half:])
    back = one_hot(row == col // per % turns * lines + col // half * per + col % per)
    for parts, now in ((theirs, theirs_refs), (mine, mine_refs)):
        out = dot(back, jnp.concatenate(parts, axis=0)).astype(BF16)
        for t, ref in enumerate(now):
            ref[...] = out[t * lines : (t + 1) * lines]


def experts(own, other, gate_up, down):
    turns = len(own)
    shape = jax.ShapeDtypeStruct(own[0].shape, BF16)
    results = pl.pallas_call(
        functools.partial(expert_kernel, turns),
        out_shape=[shape] * (2 * turns),
        in_specs=[VMEM] * (2 * turns + 2),
        out_specs=[VMEM] * (2 * turns),
        compiler_params=pltpu.CompilerParams(vmem_limit_bytes=32 * MIB),
        cost_estimate=pl.CostEstimate(
            flops=800_000_000, bytes_accessed=12_000_000, transcendentals=16384
        ),
        name="experts",
    )(*own, *other, gate_up, down)
    return results[:turns], results[turns:]


def combine_kernel(mix_ref, resid_ref, *refs):
    back_refs, (kept_ref, sent_ref) = refs[:-2], refs[-2:]
    both = resid_ref.shape[0]
    piece = back_refs[0].shape[1]
    product = dot(mix_ref[...], jnp.concatenate([ref[...] for ref in back_refs], axis=0))
    n = PIECES * 2 * both
    total = product[:n] + product[n : 2 * n] + product[2 * n :]
    for k in range(PIECES):
        cols = pl.ds(k * piece, piece)
        first = k * 2 * both
        kept_ref[:, cols] = resid_ref[:, cols] + total[first : first + both]
        sent_ref[:, cols] = total[first + both : first + 2 * both].astype(BF16)


def combine(mix, resid, backs):
    return pl.pallas_call(
        combine_kernel,
        out_shape=(
            jax.ShapeDtypeStruct(resid.shape, F32),
            jax.ShapeDtypeStruct(resid.shape, BF16),
        ),
        in_specs=[VMEM] * (2 + len(backs)),
        out_specs=(VMEM, VMEM),
        compiler_params=pltpu.CompilerParams(vmem_limit_bytes=24 * MIB),
        cost_estimate=pl.CostEstimate(
            flops=100_000_000, bytes_accessed=1_000_000, transcendentals=0
        ),
        name="combine",
    )(mix, resid, *backs)


def finish_kernel(kept_ref, other_ref, out_ref):
    steps, rows, _ = out_ref.shape
    done = (kept_ref[...] + other_ref[...].astype(F32)).astype(BF16)
    for s in range(steps):
        out_ref[s] = done[s * rows : (s + 1) * rows]


def finish(shape, kept, other):
    return pl.pallas_call(
        finish_kernel,
        out_shape=jax.ShapeDtypeStruct(shape, BF16),
        in_specs=[VMEM, VMEM],
        out_specs=VMEM,
        compiler_params=pltpu.CompilerParams(vmem_limit_bytes=24 * MIB),
        cost_estimate=pl.CostEstimate(flops=100_000, bytes_accessed=500_000, transcendentals=0),
        name="finish",
    )(kept, other)


def per_device(
    queries,
    fresh,
    kv_cache,
    cache_len,
    hidden_state,
    norm_gain,
    expert_ids,
    route_weight,
    gate_up,
    down,
):
    steps = queries.shape[0]
    owners = lax.axis_size("afd")
    chips = owners // 2
    turns = chips // 2
    cores = [(i, i ^ 1) for i in range(owners)]

    def swap(x):
        return lax.ppermute(x, "afd", cores)

    def route(t):
        return [(i, (i // 2 ^ distance(t, i % 2, chips)) * 2 + 1 - i % 2) for i in range(owners)]

    def send(x, t):
        return lax.ppermute(x, "afd", route(t))

    def send_back(x, t):
        return lax.ppermute(x, "afd", [(j, i) for i, j in route(t)])

    ids = expert_ids.transpose(2, 0, 1)
    weights = route_weight.transpose(2, 0, 1)
    resid, normed, w_down = attend(
        cache_len, ids, weights, queries, fresh, kv_cache, hidden_state, norm_gain, down
    )
    normed_other = swap(normed)
    sent = pack(steps, chips, normed, normed_other)
    own = [send(sent[t], t) for t in range(turns)]
    w_in = stage(gate_up)
    mix = mixer(steps, chips, normed, normed_other)
    own[0], w_in = lax.optimization_barrier((own[0], w_in))
    other = [swap(x) for x in own]
    summed = []
    for t in range(0, turns, TOGETHER):
        now = slice(t, t + TOGETHER)
        mine, theirs = experts(own[now], other[now], w_in, w_down)
        summed += [
            (a.astype(F32) + swap(b).astype(F32)).astype(BF16) for a, b in zip(mine, theirs)
        ]
    backs = [send_back(summed[t], t) for t in range(turns)]
    kept, given = combine(mix, resid, backs)
    return finish(queries.shape, kept, swap(given))


def solution(mesh):
    placed = (
        P(None, ("group", "afd"), None),
        P(None, ("group", "afd"), None),
        P(("group", "afd"), None, None),
        P(("group", "afd")),
        P(None, ("group", "afd"), None),
        P(),
        P(None, ("group", "afd"), None),
        P(None, ("group", "afd"), None),
        P("afd", None, None, None),
        P("afd", None, None),
    )
    return jax.shard_map(
        per_device,
        mesh=mesh,
        in_specs=placed,
        out_specs=P(None, ("group", "afd"), None),
        check_vma=False,
    )
```

```python
import functools
import jax
import jax.numpy as jnp
from jax import lax
from jax.experimental import pallas as pl
from jax.experimental.pallas import tpu as pltpu
from jax.sharding import PartitionSpec as P

HEADS = 32
HEAD = 224
EXPERTS = 8
TOP = 3
CAP = 2
PIECES = 4
LANES = 128
PARTS = 3
F32 = jnp.float32
BF16 = jnp.bfloat16
MIB = 1 << 20
VMEM = pl.BlockSpec(memory_space=pltpu.VMEM)
HBM = pl.BlockSpec(memory_space=pltpu.HBM)
TOGETHER = 4


def iota(shape, dim):
    return lax.broadcasted_iota(jnp.int32, shape, dim)


def in_hbm(*arrays):
    return [pltpu.with_memory_space_constraint(x, pltpu.HBM) for x in arrays]


def nt_dot(a, b):
    return lax.dot_general(a, b, (((1,), (1,)), ((), ())), preferred_element_type=F32)


def dot(a, b):
    return jnp.dot(a, b, preferred_element_type=F32)


def one_hot(mask):
    return jnp.where(mask, 1.0, 0.0).astype(BF16)


def distance(turn, core, chips):
    return jnp.where(turn == 0, 0, (2 * turn) ^ (core * (chips - 1)))


def expert_at(turn, chips):
    place = lax.axis_index("afd")
    return (distance(turn, place % 2, chips) ^ (place // 2)) // (chips // EXPERTS)


def expert_across(chips):
    return (lax.axis_index("afd") // 2 ^ (chips - 1)) // (chips // EXPERTS)


def spread(ref, k, where, steps, rows, empty):
    out = jnp.full(where.shape, empty)
    for s in range(steps):
        for r in range(rows):
            out = jnp.where(where == s * rows + r, ref[k, s, r], out)
    return out


def tail(ids_ref, weight_ref, steps, rows):
    both = steps * rows
    lane = iota((both, LANES), 1)
    where = iota((both, 1), 0)
    mix = jnp.zeros((both, LANES), F32)
    named = jnp.zeros((both, LANES), F32)
    for k in range(TOP):
        hit = spread(ids_ref, k, where, steps, rows, -1) == lane % EXPERTS
        mix = mix + jnp.where(hit, spread(weight_ref, k, where, steps, rows, 0.0), 0.0)
        named = named + jnp.where(hit, 1.0, 0.0)
    out = jnp.where(lane // EXPERTS == PARTS, named, 0.0)
    for part in range(PARTS):
        term = mix.astype(BF16).astype(F32)
        out = jnp.where(lane // EXPERTS == part, term, out)
        mix = mix - term
    return out.astype(BF16)


def choose(steps, expert, place, lines, tails, parts):
    both, width = parts[0].shape
    rows = both // steps
    piece = width // PIECES
    stacked = jnp.concatenate([x.astype(F32) for x in tails] * PIECES, axis=0).astype(BF16)
    count = stacked.shape[0]
    line = iota((lines, LANES), 0)
    named = nt_dot(one_hot(iota(line.shape, 1) == PARTS * EXPERTS + expert(line)), stacked)
    at = iota((count, count), 0)
    to = iota((count, count), 1)
    before = one_hot((at // rows == to // rows) & (at < to))
    rank = dot(named.astype(BF16), before)
    line = iota(named.shape, 0)
    same = place(line) == iota(named.shape, 1) // rows
    picks = one_hot(same & (named > 0.5) & (rank == (line % CAP).astype(F32)))
    data = [x[:, k * piece : (k + 1) * piece].astype(F32) for k in range(PIECES) for x in parts]
    return dot(picks, jnp.concatenate(data, axis=0).astype(BF16)).astype(BF16)


def attend_kernel(
    chips,
    len_hbm,
    ids_hbm,
    weight_hbm,
    q_hbm,
    fresh_hbm,
    kv_hbm,
    hid_hbm,
    gain_hbm,
    dn_hbm,
    resid_ref,
    out_ref,
    across_ref,
    dn_ref,
    len_ref,
    ids_ref,
    weight_ref,
    q_ref,
    fresh_ref,
    kv_ref,
    hid_ref,
    gain_ref,
    merged,
    sems,
):
    copies = [
        pltpu.make_async_copy(source, target, sems.at[i])
        for i, (source, target) in enumerate(
            (
                (q_hbm, q_ref),
                (kv_hbm, kv_ref),
                (len_hbm, len_ref),
                (ids_hbm, ids_ref),
                (weight_hbm, weight_ref),
                (fresh_hbm, fresh_ref),
                (hid_hbm, hid_ref),
                (gain_hbm, gain_ref),
            )
        )
    ]
    down = pltpu.make_async_copy(dn_hbm.at[0], dn_ref, sems.at[len(copies)])
    for copy in [*copies, down]:
        copy.start()
    steps, rows, width = q_ref.shape
    length = kv_ref.shape[2]
    both = steps * rows
    scale = HEAD ** (-0.5)
    for copy in copies:
        copy.wait()
    q = jnp.concatenate([q_ref[s].astype(F32) for s in range(steps)], axis=0)
    heads = jnp.concatenate([q[:, h * HEAD : (h + 1) * HEAD] for h in range(HEADS)], axis=0)
    heads = heads.astype(BF16)
    kv = jnp.concatenate([kv_ref[r] for r in range(rows)], axis=1)
    new = jnp.concatenate([fresh_ref[s].astype(F32) for s in range(steps)], axis=0).astype(BF16)

    sub = iota((both, rows * length), 0)
    lane = iota((both, rows * length), 1)
    limit = jnp.zeros_like(lane)
    for r in range(rows):
        limit = jnp.where(lane // length == r, len_ref[r], limit)
    valid = (lane // length == sub % rows) & (lane % length < limit)
    sub = iota((both, both), 0)
    lane = iota((both, both), 1)
    valid_new = (lane % rows == sub % rows) & (lane // rows <= sub // rows)

    old_s = (dot(heads, kv[:HEAD]) * scale).reshape(HEADS, both, rows * length)
    new_s = (nt_dot(heads, new[:, :HEAD]) * scale).reshape(HEADS, both, both)
    old_s = jnp.where(valid[None], old_s, -1e30)
    new_s = jnp.where(valid_new[None], new_s, -1e30)
    top = jnp.maximum(
        jnp.max(old_s, axis=-1, keepdims=True), jnp.max(new_s, axis=-1, keepdims=True)
    )
    old_e = jnp.exp(old_s - top)
    new_e = jnp.exp(new_s - top)
    total = jnp.sum(old_e, axis=-1, keepdims=True) + jnp.sum(new_e, axis=-1, keepdims=True)
    old_w = (old_e / total).reshape(HEADS * both, rows * length).astype(BF16)
    new_w = (new_e / total).reshape(HEADS * both, both).astype(BF16)
    attended = nt_dot(old_w, kv[HEAD:]) + dot(new_w, new[:, HEAD:])
    for h in range(HEADS):
        merged[:, h * HEAD : (h + 1) * HEAD] = attended[h * both : (h + 1) * both]
    hidden = jnp.concatenate([hid_ref[s].astype(F32) for s in range(steps)], axis=0)
    resid = hidden + merged[...]
    resid_ref[...] = resid
    meansq = jnp.mean(resid * resid, axis=-1, keepdims=True)
    gain = gain_ref[...].astype(F32)
    gain = jnp.concatenate([gain[i : i + 1] for i in range(width // LANES)], axis=1)
    normed = resid * lax.rsqrt(meansq + 1e-06) * gain
    out_ref[:, :width] = normed.astype(BF16)
    ends = tail(ids_ref, weight_ref, steps, rows)
    out_ref[:, width:] = ends
    lines = across_ref.shape[0]
    across_ref[...] = choose(
        steps, lambda n: expert_across(chips), lambda n: n // CAP, lines, [ends], [normed]
    )
    down.wait()


def attend(chips, cache_len, ids, weights, queries, fresh, kv_cache, hidden_state, norm_gain, down):
    steps, rows, width = queries.shape
    kv = kv_cache.transpose(0, 2, 1)
    gain = norm_gain.reshape(width // LANES, LANES)
    return pl.pallas_call(
        functools.partial(attend_kernel, chips),
        out_shape=(
            jax.ShapeDtypeStruct((steps * rows, width), F32),
            jax.ShapeDtypeStruct((steps * rows, width + LANES), BF16),
            jax.ShapeDtypeStruct((PIECES * steps * CAP, width // PIECES), BF16),
            jax.ShapeDtypeStruct(down.shape[1:], BF16),
        ),
        in_specs=[HBM] * 9,
        out_specs=(VMEM,) * 4,
        scratch_shapes=[
            pltpu.SMEM(cache_len.shape, jnp.int32),
            pltpu.SMEM(ids.shape, jnp.int32),
            pltpu.SMEM(weights.shape, F32),
            pltpu.VMEM(queries.shape, BF16),
            pltpu.VMEM(fresh.shape, BF16),
            pltpu.VMEM(kv.shape, BF16),
            pltpu.VMEM(hidden_state.shape, BF16),
            pltpu.VMEM(gain.shape, BF16),
            pltpu.VMEM((steps * rows, width), F32),
            pltpu.SemaphoreType.DMA((9,)),
        ],
        compiler_params=pltpu.CompilerParams(vmem_limit_bytes=24 * MIB),
        cost_estimate=pl.CostEstimate(
            flops=300_000_000, bytes_accessed=2_000_000, transcendentals=131072
        ),
        name="attend",
    )(*in_hbm(cache_len, ids, weights, queries, fresh, kv, hidden_state, gain, down))


def pack_kernel(steps, chips, own_ref, other_ref, home_ref, away_ref, *outs):
    width = own_ref.shape[1] - LANES
    lines = PIECES * 2 * steps * CAP

    def place(n):
        at = n // CAP % (lines // CAP)
        side, k = at // (PIECES * steps), at // steps % PIECES
        return jnp.where(n < lines, (k * 2 + side) * steps + at % steps, at)

    sent = choose(
        steps,
        lambda n: expert_at(n // lines, chips),
        place,
        (1 + len(outs)) * lines,
        [own_ref[:, width:], other_ref[:, width:]],
        [own_ref[:, :width], other_ref[:, :width]],
    )
    home_ref[...] = sent[: lines // 2]
    away_ref[...] = sent[lines // 2 : lines]
    for t, out in enumerate(outs):
        out[...] = sent[(t + 1) * lines : (t + 2) * lines]


def pack(steps, chips, own, other):
    lines, piece = PIECES * 2 * steps * CAP, (own.shape[1] - LANES) // PIECES
    half = jax.ShapeDtypeStruct((lines // 2, piece), BF16)
    turns = [jax.ShapeDtypeStruct((lines, piece), BF16)] * (chips // 2 - 1)
    return pl.pallas_call(
        functools.partial(pack_kernel, steps, chips),
        out_shape=[half, half, *turns],
        in_specs=[VMEM] * 2,
        out_specs=[VMEM] * (2 + len(turns)),
        compiler_params=pltpu.CompilerParams(vmem_limit_bytes=24 * MIB),
        cost_estimate=pl.CostEstimate(
            flops=50_000_000, bytes_accessed=2_000_000, transcendentals=0
        ),
        name="pack",
    )(own, other)


def mixing(steps, expert, sides, lines, count, tails):
    both = tails[0].shape[0]
    rows = both // steps
    tails = jnp.concatenate([x.astype(F32) for x in tails], axis=0).astype(BF16)
    lane = iota((LANES, count), 0)
    named_by = expert(iota((LANES, count), 1) // lines)
    found = [dot(tails, one_hot(lane == part * EXPERTS + named_by)) for part in range(PARTS + 1)]
    at = iota((sides * both, sides * both), 1)
    to = iota((sides * both, sides * both), 0)
    rank = dot(one_hot((at // rows == to // rows) & (at < to)), found[PARTS].astype(BF16))
    line = iota((sides * both, count), 1)
    row = iota((sides * both, count), 0)
    same = (line // CAP) % (sides * steps) == row // rows
    slot = same & (rank == (line % CAP).astype(F32))
    k_of = line // (sides * steps * CAP) % PIECES
    parts = [
        jnp.where(slot & (k_of == k), found[part], 0.0)
        for part in range(PARTS)
        for k in range(PIECES)
    ]
    return jnp.concatenate(parts, axis=0).astype(BF16)


def stage_kernel(gu_hbm, out, sems):
    step = out.shape[1] // 4
    copies = []
    for i in range(8):
        part = pl.ds(i // 2 * step, step)
        copies.append(
            pltpu.make_async_copy(gu_hbm.at[0, i % 2, part], out.at[i % 2, part], sems.at[i])
        )
    for copy in copies:
        copy.start()
    for copy in copies:
        copy.wait()


def stage(gate_up):
    return pl.pallas_call(
        stage_kernel,
        out_shape=jax.ShapeDtypeStruct(gate_up.shape[1:], BF16),
        in_specs=[HBM],
        out_specs=VMEM,
        scratch_shapes=[pltpu.SemaphoreType.DMA((8,))],
        compiler_params=pltpu.CompilerParams(vmem_limit_bytes=16 * MIB),
        cost_estimate=pl.CostEstimate(flops=0, bytes_accessed=16_000_000, transcendentals=0),
        name="stage",
    )(*in_hbm(gate_up))


def mix_kernel(steps, chips, own_ref, other_ref, mix_ref, last_ref):
    width = own_ref.shape[1] - LANES
    own, other = own_ref[:, width:], other_ref[:, width:]
    lines = PIECES * steps * CAP
    mix_ref[...] = mixing(
        steps, lambda t: expert_at(t + 1, chips), 2, 2 * lines, mix_ref.shape[1], [own, other]
    )
    last_ref[...] = mixing(
        steps,
        lambda t: jnp.where(t == 0, expert_across(chips), expert_at(0 * t, chips)),
        1,
        lines,
        last_ref.shape[1],
        [own],
    )


def mixer(steps, chips, own, other):
    both = own.shape[0]
    lines = PIECES * steps * CAP
    return pl.pallas_call(
        functools.partial(mix_kernel, steps, chips),
        out_shape=(
            jax.ShapeDtypeStruct(
                (PARTS * PIECES * 2 * both, (chips // 2 - 1) * 2 * lines), BF16
            ),
            jax.ShapeDtypeStruct((PARTS * PIECES * both, 2 * lines), BF16),
        ),
        in_specs=[VMEM, VMEM],
        out_specs=(VMEM, VMEM),
        compiler_params=pltpu.CompilerParams(vmem_limit_bytes=24 * MIB),
        cost_estimate=pl.CostEstimate(
            flops=10_000_000, bytes_accessed=1_000_000, transcendentals=0
        ),
        name="mixer",
    )(own, other)


def regroup(heights, back):
    n = sum(heights)
    per_k = n // PIECES
    target = iota((n, n), 1 if back else 0)
    source = iota((n, n), 0 if back else 1)
    k, x = target // per_k, target % per_k
    line = target
    start = 0
    for height in heights:
        per = height // PIECES
        at = start + k * per + x - start // PIECES
        line = jnp.where(x >= start // PIECES, at, line)
        start += height
    return one_hot(source == line)


def expert_kernel(count, *refs):
    sides = refs[:count], refs[count : 2 * count]
    w_in, w_down = refs[2 * count : 2 * count + 2]
    outs = refs[2 * count + 2 :]
    heights = [ref.shape[0] for ref in sides[0]]
    piece = sides[0][0].shape[1]
    half = sum(heights) // PIECES
    order = regroup(heights, False)
    rows = [
        dot(order, jnp.concatenate([ref[...] for ref in side], axis=0)).astype(BF16)
        for side in sides
    ]
    gate = upper = None
    for k in range(PIECES):
        x = jnp.concatenate([side[k * half : (k + 1) * half] for side in rows], axis=0)
        cols = pl.ds(k * piece, piece)
        g, u = nt_dot(x, w_in[0, :, cols]), nt_dot(x, w_in[1, :, cols])
        gate, upper = (g, u) if k == 0 else (gate + g, upper + u)
    act = (gate / (1.0 + jnp.exp(-gate)) * upper).astype(BF16)
    mine = []
    theirs = []
    for k in range(PIECES):
        part = dot(act, w_down[:, k * piece : (k + 1) * piece]).astype(BF16)
        mine.append(part[:half])
        theirs.append(part[half:])
    back = regroup(heights, True)
    for parts, now in ((theirs, outs[len(outs) // 2 :]), (mine, outs[: len(outs) // 2])):
        out = dot(back, jnp.concatenate(parts, axis=0)).astype(BF16)
        start = 0
        for ref in now:
            ref[...] = out[start : start + ref.shape[0]]
            start += ref.shape[0]


def experts(own, other, heights, gate_up, down):
    shapes = [jax.ShapeDtypeStruct((height, own[0].shape[1]), BF16) for height in heights]
    results = pl.pallas_call(
        functools.partial(expert_kernel, len(own)),
        out_shape=shapes + shapes,
        in_specs=[VMEM] * (2 * len(own) + 2),
        out_specs=[VMEM] * (2 * len(shapes)),
        compiler_params=pltpu.CompilerParams(vmem_limit_bytes=32 * MIB),
        cost_estimate=pl.CostEstimate(
            flops=800_000_000, bytes_accessed=12_000_000, transcendentals=16384
        ),
        name="experts",
    )(*own, *other, gate_up, down)
    return results[: len(shapes)], results[len(shapes) :]


def mixed(mix_ref, back_refs, rows):
    product = dot(mix_ref[...], jnp.concatenate([ref[...] for ref in back_refs], axis=0))
    n = PIECES * rows
    total = product[:n] + product[n : 2 * n] + product[2 * n :]
    return [total[k * rows : (k + 1) * rows] for k in range(PIECES)]


def combine_kernel(mix_ref, last_ref, resid_ref, across_ref, home_ref, *refs):
    back_refs, (kept_ref, given_ref) = refs[:-2], refs[-2:]
    both = resid_ref.shape[0]
    piece = home_ref.shape[1]
    turns = mixed(mix_ref, back_refs, 2 * both)
    last = mixed(last_ref, [across_ref, home_ref], both)
    for k in range(PIECES):
        cols = pl.ds(k * piece, piece)
        kept_ref[:, cols] = resid_ref[:, cols] + turns[k][:both] + last[k]
        given_ref[:, cols] = turns[k][both:].astype(BF16)


def combine(mix, mix_last, resid, across, home, backs):
    return pl.pallas_call(
        combine_kernel,
        out_shape=(
            jax.ShapeDtypeStruct(resid.shape, F32),
            jax.ShapeDtypeStruct(resid.shape, BF16),
        ),
        in_specs=[VMEM] * (5 + len(backs)),
        out_specs=(VMEM, VMEM),
        compiler_params=pltpu.CompilerParams(vmem_limit_bytes=24 * MIB),
        cost_estimate=pl.CostEstimate(
            flops=100_000_000, bytes_accessed=1_000_000, transcendentals=0
        ),
        name="combine",
    )(mix, mix_last, resid, across, home, *backs)


def finish_kernel(kept_ref, other_ref, out_ref):
    steps, rows, _ = out_ref.shape
    done = (kept_ref[...] + other_ref[...].astype(F32)).astype(BF16)
    for s in range(steps):
        out_ref[s] = done[s * rows : (s + 1) * rows]


def finish(shape, kept, other):
    return pl.pallas_call(
        finish_kernel,
        out_shape=jax.ShapeDtypeStruct(shape, BF16),
        in_specs=[VMEM, VMEM],
        out_specs=VMEM,
        compiler_params=pltpu.CompilerParams(vmem_limit_bytes=24 * MIB),
        cost_estimate=pl.CostEstimate(flops=100_000, bytes_accessed=500_000, transcendentals=0),
        name="finish",
    )(kept, other)


def per_device(
    queries,
    fresh,
    kv_cache,
    cache_len,
    hidden_state,
    norm_gain,
    expert_ids,
    route_weight,
    gate_up,
    down,
):
    steps = queries.shape[0]
    owners = lax.axis_size("afd")
    chips = owners // 2
    turns = chips // 2
    cores = [(i, i ^ 1) for i in range(owners)]

    def swap(x):
        return lax.ppermute(x, "afd", cores)

    def route(t):
        return [
            (i, ((i // 2 ^ 2 * t ^ i % 2 * (chips - 1)) * 2 + 1 - i % 2)) for i in range(owners)
        ]

    def route_across():
        return [
            (i, (i // 2 ^ (chips - 1)) * 2 + (i % 2 ^ (i // 2 >= turns))) for i in range(owners)
        ]

    def send(x, to):
        return lax.ppermute(x, "afd", to)

    def send_back(x, to):
        return lax.ppermute(x, "afd", [(j, i) for i, j in to])

    ids = expert_ids.transpose(2, 0, 1)
    weights = route_weight.transpose(2, 0, 1)
    resid, normed, sent_across, w_down = attend(
        chips, cache_len, ids, weights, queries, fresh, kv_cache, hidden_state, norm_gain, down
    )
    across = send(sent_across, route_across())
    normed_other = swap(normed)
    home, away, *sent = pack(steps, chips, normed, normed_other)
    across, sent = lax.optimization_barrier((across, sent))
    own = [send(x, route(t + 1)) for t, x in enumerate(sent)]
    w_in = stage(gate_up)
    mix, mix_last = mixer(steps, chips, normed, normed_other)
    own[0], w_in, mix = lax.optimization_barrier((own[0], w_in, mix))
    mines = [across, home, *own[: TOGETHER - 1]]
    others = [swap(across), away, *[swap(x) for x in own[: TOGETHER - 1]]]
    small, large = sent_across.shape[0], sent[0].shape[0]
    summed = []
    for first in range(0, turns, TOGETHER):
        heights = [large] * TOGETHER
        if first:
            now = slice(first - 1, first + TOGETHER - 1)
            mines = own[now]
            others = [swap(x) for x in mines]
        mine, theirs = experts(mines, others, heights, w_in, w_down)
        summed += [
            (a.astype(F32) + swap(b).astype(F32)).astype(BF16) for a, b in zip(mine, theirs)
        ]
    last, summed = summed[0], summed[1:]
    backs = [send_back(x, route(t + 1)) for t, x in enumerate(summed)]
    back_across = send_back(last[:small], route_across())
    kept, given = combine(mix, mix_last, resid, back_across, last[small:], backs)
    return finish(queries.shape, kept, swap(given))


def solution(mesh):
    placed = (
        P(None, ("group", "afd"), None),
        P(None, ("group", "afd"), None),
        P(("group", "afd"), None, None),
        P(("group", "afd")),
        P(None, ("group", "afd"), None),
        P(),
        P(None, ("group", "afd"), None),
        P(None, ("group", "afd"), None),
        P("afd", None, None, None),
        P("afd", None, None),
    )
    return jax.shard_map(
        per_device,
        mesh=mesh,
        in_specs=placed,
        out_specs=P(None, ("group", "afd"), None),
        check_vma=False,
    )
```

```python
import functools
import jax
import jax.numpy as jnp
from jax import lax
from jax.experimental import pallas as pl
from jax.experimental.pallas import tpu as pltpu
from jax.sharding import PartitionSpec as P

HEADS = 32
HEAD = 224
EXPERTS = 8
TOP = 3
CAP = 2
PIECES = 4
LANES = 128
PARTS = 3
F32 = jnp.float32
BF16 = jnp.bfloat16
MIB = 1 << 20
VMEM = pl.BlockSpec(memory_space=pltpu.VMEM)
HBM = pl.BlockSpec(memory_space=pltpu.HBM)
TOGETHER = 4


def iota(shape, dim):
    return lax.broadcasted_iota(jnp.int32, shape, dim)


def in_hbm(*arrays):
    return [pltpu.with_memory_space_constraint(x, pltpu.HBM) for x in arrays]


def nt_dot(a, b):
    return lax.dot_general(a, b, (((1,), (1,)), ((), ())), preferred_element_type=F32)


def dot(a, b):
    return jnp.dot(a, b, preferred_element_type=F32)


def one_hot(mask):
    return jnp.where(mask, 1.0, 0.0).astype(BF16)


def distance(turn, core, chips):
    bits = (chips // 2).bit_length() - 1
    even = 0
    for b in range(bits):
        even = even + ((turn >> b) % 2 << (bits - b))
    return even ^ (core * (chips - 1))


def expert_at(turn, chips):
    place = lax.axis_index("afd")
    return (distance(turn, place % 2, chips) ^ (place // 2)) // (chips // EXPERTS)


def spread(ref, k, where, steps, rows, empty):
    out = jnp.full(where.shape, empty)
    for s in range(steps):
        for r in range(rows):
            out = jnp.where(where == s * rows + r, ref[k, s, r], out)
    return out


def tail(ids_ref, weight_ref, steps, rows):
    both = steps * rows
    lane = iota((both, LANES), 1)
    where = iota((both, 1), 0)
    mix = jnp.zeros((both, LANES), F32)
    named = jnp.zeros((both, LANES), F32)
    for k in range(TOP):
        hit = spread(ids_ref, k, where, steps, rows, -1) == lane % EXPERTS
        mix = mix + jnp.where(hit, spread(weight_ref, k, where, steps, rows, 0.0), 0.0)
        named = named + jnp.where(hit, 1.0, 0.0)
    out = jnp.where(lane // EXPERTS == PARTS, named, 0.0)
    for part in range(PARTS):
        term = mix.astype(BF16).astype(F32)
        out = jnp.where(lane // EXPERTS == part, term, out)
        mix = mix - term
    return out.astype(BF16)


def attend_kernel(
    len_hbm,
    ids_hbm,
    weight_hbm,
    q_hbm,
    fresh_hbm,
    kv_hbm,
    hid_hbm,
    gain_hbm,
    dn_hbm,
    resid_ref,
    out_ref,
    dn_ref,
    len_ref,
    ids_ref,
    weight_ref,
    q_ref,
    fresh_ref,
    kv_ref,
    hid_ref,
    gain_ref,
    merged,
    sems,
):
    pairs = (
        (q_hbm, q_ref),
        (kv_hbm, kv_ref),
        (fresh_hbm, fresh_ref),
        (len_hbm, len_ref),
        (hid_hbm, hid_ref),
        (gain_hbm, gain_ref),
        (ids_hbm, ids_ref),
        (weight_hbm, weight_ref),
        (dn_hbm.at[0], dn_ref),
    )
    copies = [pltpu.make_async_copy(a, b, sems.at[i]) for i, (a, b) in enumerate(pairs)]
    for copy in copies:
        copy.start()
    steps, rows, width = q_ref.shape
    length = kv_ref.shape[2]
    both = steps * rows
    scale = HEAD ** (-0.5)
    copies[0].wait()
    q = jnp.concatenate([q_ref[s].astype(F32) for s in range(steps)], axis=0)
    heads = jnp.concatenate([q[:, h * HEAD : (h + 1) * HEAD] for h in range(HEADS)], axis=0)
    heads = heads.astype(BF16)
    for copy in copies[1:4]:
        copy.wait()
    kv = jnp.concatenate([kv_ref[r] for r in range(rows)], axis=1)
    new = jnp.concatenate([fresh_ref[s].astype(F32) for s in range(steps)], axis=0).astype(BF16)

    sub = iota((both, rows * length), 0)
    lane = iota((both, rows * length), 1)
    limit = jnp.zeros_like(lane)
    for r in range(rows):
        limit = jnp.where(lane // length == r, len_ref[r], limit)
    valid = (lane // length == sub % rows) & (lane % length < limit)
    sub = iota((both, both), 0)
    lane = iota((both, both), 1)
    valid_new = (lane % rows == sub % rows) & (lane // rows <= sub // rows)

    old_s = (dot(heads, kv[:HEAD]) * scale).reshape(HEADS, both, rows * length)
    new_s = (nt_dot(heads, new[:, :HEAD]) * scale).reshape(HEADS, both, both)
    old_s = jnp.where(valid[None], old_s, -1e30)
    new_s = jnp.where(valid_new[None], new_s, -1e30)
    top = jnp.maximum(
        jnp.max(old_s, axis=-1, keepdims=True), jnp.max(new_s, axis=-1, keepdims=True)
    )
    old_e = jnp.exp(old_s - top)
    new_e = jnp.exp(new_s - top)
    total = jnp.sum(old_e, axis=-1, keepdims=True) + jnp.sum(new_e, axis=-1, keepdims=True)
    share = 1.0 / total
    old_w = (old_e * share).reshape(HEADS * both, rows * length).astype(BF16)
    new_w = (new_e * share).reshape(HEADS * both, both).astype(BF16)
    attended = nt_dot(old_w, kv[HEAD:]) + dot(new_w, new[:, HEAD:])
    for h in range(HEADS):
        merged[:, h * HEAD : (h + 1) * HEAD] = attended[h * both : (h + 1) * both]
    for copy in copies[4:8]:
        copy.wait()
    hidden = jnp.concatenate([hid_ref[s].astype(F32) for s in range(steps)], axis=0)
    resid = hidden + merged[...]
    resid_ref[...] = resid
    meansq = jnp.mean(resid * resid, axis=-1, keepdims=True)
    gain = gain_ref[...].astype(F32)
    gain = jnp.concatenate([gain[i : i + 1] for i in range(width // LANES)], axis=1)
    normed = resid * lax.rsqrt(meansq + 1e-06) * gain
    out_ref[:, :width] = normed.astype(BF16)
    out_ref[:, width:] = tail(ids_ref, weight_ref, steps, rows)
    copies[8].wait()


def attend(cache_len, ids, weights, queries, fresh, kv_cache, hidden_state, norm_gain, down):
    steps, rows, width = queries.shape
    kv = kv_cache.transpose(0, 2, 1)
    gain = norm_gain.reshape(width // LANES, LANES)
    return pl.pallas_call(
        attend_kernel,
        out_shape=(
            jax.ShapeDtypeStruct((steps * rows, width), F32),
            jax.ShapeDtypeStruct((steps * rows, width + LANES), BF16),
            jax.ShapeDtypeStruct(down.shape[1:], BF16),
        ),
        in_specs=[HBM] * 9,
        out_specs=(VMEM, VMEM, VMEM),
        scratch_shapes=[
            pltpu.SMEM(cache_len.shape, jnp.int32),
            pltpu.SMEM(ids.shape, jnp.int32),
            pltpu.SMEM(weights.shape, F32),
            pltpu.VMEM(queries.shape, BF16),
            pltpu.VMEM(fresh.shape, BF16),
            pltpu.VMEM(kv.shape, BF16),
            pltpu.VMEM(hidden_state.shape, BF16),
            pltpu.VMEM(gain.shape, BF16),
            pltpu.VMEM((steps * rows, width), F32),
            pltpu.SemaphoreType.DMA((9,)),
        ],
        compiler_params=pltpu.CompilerParams(vmem_limit_bytes=24 * MIB),
        cost_estimate=pl.CostEstimate(
            flops=300_000_000, bytes_accessed=2_000_000, transcendentals=131072
        ),
        name="attend",
    )(*in_hbm(cache_len, ids, weights, queries, fresh, kv, hidden_state, gain, down))


def pack_kernel(steps, chips, own_ref, other_ref, *outs):
    both, width = own_ref.shape
    width -= LANES
    rows = both // steps
    piece = width // PIECES
    side_lines = steps * CAP
    lines = PIECES * 2 * side_lines
    tails = [ref[:, width:].astype(F32) for ref in (own_ref, other_ref)]
    tails = jnp.concatenate(tails * PIECES, axis=0).astype(BF16)
    count = 2 * both * PIECES
    row = iota((len(outs) * lines, LANES), 0)
    lane = iota((len(outs) * lines, LANES), 1)
    wanted = one_hot(lane == PARTS * EXPERTS + expert_at(row // lines, chips))
    named = nt_dot(wanted, tails)
    at = iota((count, count), 0)
    to = iota((count, count), 1)
    before = one_hot((at // rows == to // rows) & (at < to))
    rank = dot(named.astype(BF16), before)
    line = iota(named.shape, 0)
    col = iota(named.shape, 1)
    same = (line // CAP) % (lines // CAP) == col // rows
    picks = one_hot(same & (named > 0.5) & (rank == (line % CAP).astype(F32)))
    parts = [ref[:, :width].astype(F32) for ref in (own_ref, other_ref)]
    stacked = jnp.concatenate(
        [part[:, k * piece : (k + 1) * piece] for k in range(PIECES) for part in parts], axis=0
    ).astype(BF16)
    sent = dot(picks, stacked).astype(BF16)
    for t, out in enumerate(outs):
        out[...] = sent[t * lines : (t + 1) * lines]


def pack(steps, chips, own, other):
    both, width = own.shape
    shape = (PIECES * 2 * steps * CAP, (width - LANES) // PIECES)
    turns = chips // 2
    return pl.pallas_call(
        functools.partial(pack_kernel, steps, chips),
        out_shape=[jax.ShapeDtypeStruct(shape, BF16)] * turns,
        in_specs=[VMEM] * 2,
        out_specs=[VMEM] * turns,
        compiler_params=pltpu.CompilerParams(vmem_limit_bytes=24 * MIB),
        cost_estimate=pl.CostEstimate(
            flops=50_000_000, bytes_accessed=2_000_000, transcendentals=0
        ),
        name="pack",
    )(own, other)


def mixing(steps, chips, own_ref, other_ref):
    both, width = own_ref.shape
    width -= LANES
    rows = both // steps
    lines = PIECES * 2 * steps * CAP
    tails = [ref[:, width:].astype(F32) for ref in (own_ref, other_ref)]
    tails = jnp.concatenate(tails, axis=0).astype(BF16)
    count = chips // 2 * lines
    lane = iota((LANES, count), 0)
    expert = expert_at(iota((LANES, count), 1) // lines, chips)
    found = [dot(tails, one_hot(lane == part * EXPERTS + expert)) for part in range(PARTS + 1)]
    at = iota((2 * both, 2 * both), 1)
    to = iota((2 * both, 2 * both), 0)
    rank = dot(one_hot((at // rows == to // rows) & (at < to)), found[PARTS].astype(BF16))
    line = iota((2 * both, count), 1)
    row = iota((2 * both, count), 0)
    same = (line // CAP) % (2 * steps) == row // rows
    slot = same & (rank == (line % CAP).astype(F32))
    k_of = line // (2 * steps * CAP) % PIECES
    parts = [
        jnp.where(slot & (k_of == k), found[part], 0.0)
        for part in range(PARTS)
        for k in range(PIECES)
    ]
    return jnp.concatenate(parts, axis=0).astype(BF16)


def stage_kernel(gu_hbm, out, sems):
    step = out.shape[1] // 4
    copies = []
    for i in range(8):
        part = pl.ds(i // 2 * step, step)
        copies.append(
            pltpu.make_async_copy(gu_hbm.at[0, i % 2, part], out.at[i % 2, part], sems.at[i])
        )
    for copy in copies:
        copy.start()
    for copy in copies:
        copy.wait()


def stage(gate_up):
    return pl.pallas_call(
        stage_kernel,
        out_shape=jax.ShapeDtypeStruct(gate_up.shape[1:], BF16),
        in_specs=[HBM],
        out_specs=VMEM,
        scratch_shapes=[pltpu.SemaphoreType.DMA((8,))],
        compiler_params=pltpu.CompilerParams(vmem_limit_bytes=16 * MIB),
        cost_estimate=pl.CostEstimate(flops=0, bytes_accessed=16_000_000, transcendentals=0),
        name="stage",
    )(*in_hbm(gate_up))


def mix_kernel(steps, chips, own_ref, other_ref, mix_ref):
    mix_ref[...] = mixing(steps, chips, own_ref, other_ref)


def mixer(steps, chips, own, other):
    lines = PIECES * 2 * steps * CAP
    shape = (PARTS * PIECES * 2 * own.shape[0], chips // 2 * lines)
    return pl.pallas_call(
        functools.partial(mix_kernel, steps, chips),
        out_shape=jax.ShapeDtypeStruct(shape, BF16),
        in_specs=[VMEM, VMEM],
        out_specs=VMEM,
        compiler_params=pltpu.CompilerParams(vmem_limit_bytes=24 * MIB),
        cost_estimate=pl.CostEstimate(
            flops=10_000_000, bytes_accessed=1_000_000, transcendentals=0
        ),
        name="mixer",
    )(own, other)


def expert_kernel(turns, *refs):
    own_refs, other_refs = refs[:turns], refs[turns : 2 * turns]
    w_in, w_down = refs[2 * turns : 2 * turns + 2]
    mine_refs = refs[2 * turns + 2 : 3 * turns + 2]
    theirs_refs = refs[3 * turns + 2 :]
    lines, piece = own_refs[0].shape
    per = lines // PIECES
    half = turns * per
    arrays = [ref[...].astype(F32) for ref in own_refs + other_refs]
    gate = upper = None
    for k in range(PIECES):
        x = [array[k * per : (k + 1) * per] for array in arrays]
        x = jnp.concatenate(x, axis=0).astype(BF16)
        cols = pl.ds(k * piece, piece)
        g, u = nt_dot(x, w_in[0, :, cols]), nt_dot(x, w_in[1, :, cols])
        gate, upper = (g, u) if k == 0 else (gate + g, upper + u)
    act = (gate / (1.0 + jnp.exp(-gate)) * upper).astype(BF16)
    parts = [dot(act, w_down[:, k * piece : (k + 1) * piece]) for k in range(PIECES)]
    for first, now in ((half, theirs_refs), (0, mine_refs)):
        for t, ref in enumerate(now):
            start = first + t * per
            out = [part[start : start + per] for part in parts]
            ref[...] = jnp.concatenate(out, axis=0).astype(BF16)


def experts(own, other, gate_up, down):
    turns = len(own)
    shape = jax.ShapeDtypeStruct(own[0].shape, BF16)
    results = pl.pallas_call(
        functools.partial(expert_kernel, turns),
        out_shape=[shape] * (2 * turns),
        in_specs=[VMEM] * (2 * turns + 2),
        out_specs=[VMEM] * (2 * turns),
        compiler_params=pltpu.CompilerParams(vmem_limit_bytes=32 * MIB),
        cost_estimate=pl.CostEstimate(
            flops=800_000_000, bytes_accessed=12_000_000, transcendentals=16384
        ),
        name="experts",
    )(*own, *other, gate_up, down)
    return results[:turns], results[turns:]


def combine_kernel(mix_ref, resid_ref, *refs):
    back_refs, (kept_ref, sent_ref) = refs[:-2], refs[-2:]
    both = resid_ref.shape[0]
    piece = back_refs[0].shape[1]
    product = dot(mix_ref[...], jnp.concatenate([ref[...] for ref in back_refs], axis=0))
    n = PIECES * 2 * both
    total = product[:n] + product[n : 2 * n] + product[2 * n :]
    for k in range(PIECES):
        cols = pl.ds(k * piece, piece)
        first = k * 2 * both
        kept_ref[:, cols] = resid_ref[:, cols] + total[first : first + both]
        sent_ref[:, cols] = total[first + both : first + 2 * both].astype(BF16)


def combine(mix, resid, backs):
    return pl.pallas_call(
        combine_kernel,
        out_shape=(
            jax.ShapeDtypeStruct(resid.shape, F32),
            jax.ShapeDtypeStruct(resid.shape, BF16),
        ),
        in_specs=[VMEM] * (2 + len(backs)),
        out_specs=(VMEM, VMEM),
        compiler_params=pltpu.CompilerParams(vmem_limit_bytes=24 * MIB),
        cost_estimate=pl.CostEstimate(
            flops=100_000_000, bytes_accessed=1_000_000, transcendentals=0
        ),
        name="combine",
    )(mix, resid, *backs)


def finish_kernel(kept_ref, other_ref, out_ref):
    steps, rows, _ = out_ref.shape
    done = (kept_ref[...] + other_ref[...].astype(F32)).astype(BF16)
    for s in range(steps):
        out_ref[s] = done[s * rows : (s + 1) * rows]


def finish(shape, kept, other):
    return pl.pallas_call(
        finish_kernel,
        out_shape=jax.ShapeDtypeStruct(shape, BF16),
        in_specs=[VMEM, VMEM],
        out_specs=VMEM,
        compiler_params=pltpu.CompilerParams(vmem_limit_bytes=24 * MIB),
        cost_estimate=pl.CostEstimate(flops=100_000, bytes_accessed=500_000, transcendentals=0),
        name="finish",
    )(kept, other)


def per_device(
    queries,
    fresh,
    kv_cache,
    cache_len,
    hidden_state,
    norm_gain,
    expert_ids,
    route_weight,
    gate_up,
    down,
):
    steps = queries.shape[0]
    owners = lax.axis_size("afd")
    chips = owners // 2
    turns = chips // 2
    cores = [(i, i ^ 1) for i in range(owners)]

    def swap(x):
        return lax.ppermute(x, "afd", cores)

    def route(t):
        return [(i, (i // 2 ^ distance(t, i % 2, chips)) * 2 + 1 - i % 2) for i in range(owners)]

    def send(x, t):
        return lax.ppermute(x, "afd", route(t))

    def send_back(x, t):
        return lax.ppermute(x, "afd", [(j, i) for i, j in route(t)])

    ids = expert_ids.transpose(2, 0, 1)
    weights = route_weight.transpose(2, 0, 1)
    resid, normed, w_down = attend(
        cache_len, ids, weights, queries, fresh, kv_cache, hidden_state, norm_gain, down
    )
    normed_other = swap(normed)
    sent = pack(steps, chips, normed, normed_other)
    own = [send(sent[t], t) for t in range(turns)]
    w_in = stage(gate_up)
    mix = mixer(steps, chips, normed, normed_other)
    own[0], w_in = lax.optimization_barrier((own[0], w_in))
    other = [swap(x) for x in own]
    summed = []
    for t in range(0, turns, TOGETHER):
        now = slice(t, t + TOGETHER)
        mine, theirs = experts(own[now], other[now], w_in, w_down)
        summed += [
            (a.astype(F32) + swap(b).astype(F32)).astype(BF16) for a, b in zip(mine, theirs)
        ]
    backs = [send_back(summed[t], t) for t in range(turns)]
    kept, given = combine(mix, resid, backs)
    return finish(queries.shape, kept, swap(given))


def solution(mesh):
    placed = (
        P(None, ("group", "afd"), None),
        P(None, ("group", "afd"), None),
        P(("group", "afd"), None, None),
        P(("group", "afd")),
        P(None, ("group", "afd"), None),
        P(),
        P(None, ("group", "afd"), None),
        P(None, ("group", "afd"), None),
        P("afd", None, None, None),
        P("afd", None, None),
    )
    return jax.shard_map(
        per_device,
        mesh=mesh,
        in_specs=placed,
        out_specs=P(None, ("group", "afd"), None),
        check_vma=False,
    )
```

```python
import functools
import jax
import jax.numpy as jnp
from jax import lax
from jax.experimental import pallas as pl
from jax.experimental.pallas import tpu as pltpu
from jax.sharding import PartitionSpec as P

HEADS = 32
HEAD = 224
EXPERTS = 8
TOP = 3
CAP = 2
PIECES = 4
LANES = 128
PARTS = 3
F32 = jnp.float32
BF16 = jnp.bfloat16
MIB = 1 << 20
VMEM = pl.BlockSpec(memory_space=pltpu.VMEM)
HBM = pl.BlockSpec(memory_space=pltpu.HBM)
TOGETHER = 4


def iota(shape, dim):
    return lax.broadcasted_iota(jnp.int32, shape, dim)


def in_hbm(*arrays):
    return [pltpu.with_memory_space_constraint(x, pltpu.HBM) for x in arrays]


def nt_dot(a, b):
    return lax.dot_general(a, b, (((1,), (1,)), ((), ())), preferred_element_type=F32)


def dot(a, b):
    return jnp.dot(a, b, preferred_element_type=F32)


def one_hot(mask):
    return jnp.where(mask, 1.0, 0.0).astype(BF16)


def distance(turn, core, chips):
    bits = (chips // 2).bit_length() - 1
    even = 0
    for b in range(bits):
        even = even + ((turn >> b) % 2 << (bits - b))
    return even ^ (core * (chips - 1))


def expert_at(turn, chips):
    place = lax.axis_index("afd")
    return (distance(turn, place % 2, chips) ^ (place // 2)) // (chips // EXPERTS)


def spread(ref, k, where, steps, rows, empty):
    out = jnp.full(where.shape, empty)
    for s in range(steps):
        for r in range(rows):
            out = jnp.where(where == s * rows + r, ref[k, s, r], out)
    return out


def tail(ids_ref, weight_ref, steps, rows):
    both = steps * rows
    lane = iota((both, LANES), 1)
    where = iota((both, 1), 0)
    mix = jnp.zeros((both, LANES), F32)
    named = jnp.zeros((both, LANES), F32)
    for k in range(TOP):
        hit = spread(ids_ref, k, where, steps, rows, -1) == lane % EXPERTS
        mix = mix + jnp.where(hit, spread(weight_ref, k, where, steps, rows, 0.0), 0.0)
        named = named + jnp.where(hit, 1.0, 0.0)
    out = jnp.where(lane // EXPERTS == PARTS, named, 0.0)
    for part in range(PARTS):
        term = mix.astype(BF16).astype(F32)
        out = jnp.where(lane // EXPERTS == part, term, out)
        mix = mix - term
    return out.astype(BF16)


def attend_kernel(
    len_hbm,
    ids_hbm,
    weight_hbm,
    q_hbm,
    fresh_hbm,
    kv_hbm,
    hid_hbm,
    gain_hbm,
    resid_ref,
    out_ref,
    len_ref,
    ids_ref,
    weight_ref,
    q_ref,
    fresh_ref,
    kv_ref,
    hid_ref,
    gain_ref,
    merged,
    sems,
):
    pairs = (
        (q_hbm, q_ref),
        (kv_hbm, kv_ref),
        (fresh_hbm, fresh_ref),
        (len_hbm, len_ref),
        (hid_hbm, hid_ref),
        (gain_hbm, gain_ref),
        (ids_hbm, ids_ref),
        (weight_hbm, weight_ref),
    )
    copies = [pltpu.make_async_copy(a, b, sems.at[i]) for i, (a, b) in enumerate(pairs)]
    for copy in copies:
        copy.start()
    steps, rows, width = q_ref.shape
    length = kv_ref.shape[2]
    both = steps * rows
    scale = HEAD ** (-0.5)
    copies[0].wait()
    q = jnp.concatenate([q_ref[s].astype(F32) for s in range(steps)], axis=0)
    heads = jnp.concatenate([q[:, h * HEAD : (h + 1) * HEAD] for h in range(HEADS)], axis=0)
    heads = heads.astype(BF16)
    for copy in copies[1:4]:
        copy.wait()
    kv = jnp.concatenate([kv_ref[r] for r in range(rows)], axis=1)
    new = jnp.concatenate([fresh_ref[s].astype(F32) for s in range(steps)], axis=0).astype(BF16)

    sub = iota((both, rows * length), 0)
    lane = iota((both, rows * length), 1)
    limit = jnp.zeros_like(lane)
    for r in range(rows):
        limit = jnp.where(lane // length == r, len_ref[r], limit)
    valid = (lane // length == sub % rows) & (lane % length < limit)
    sub = iota((both, both), 0)
    lane = iota((both, both), 1)
    valid_new = (lane % rows == sub % rows) & (lane // rows <= sub // rows)

    old_s = (dot(heads, kv[:HEAD]) * scale).reshape(HEADS, both, rows * length)
    new_s = (nt_dot(heads, new[:, :HEAD]) * scale).reshape(HEADS, both, both)
    old_s = jnp.where(valid[None], old_s, -1e30)
    new_s = jnp.where(valid_new[None], new_s, -1e30)
    top = jnp.maximum(
        jnp.max(old_s, axis=-1, keepdims=True), jnp.max(new_s, axis=-1, keepdims=True)
    )
    old_e = jnp.exp(old_s - top)
    new_e = jnp.exp(new_s - top)
    total = jnp.sum(old_e, axis=-1, keepdims=True) + jnp.sum(new_e, axis=-1, keepdims=True)
    share = 1.0 / total
    old_w = (old_e * share).reshape(HEADS * both, rows * length).astype(BF16)
    new_w = (new_e * share).reshape(HEADS * both, both).astype(BF16)
    attended = nt_dot(old_w, kv[HEAD:]) + dot(new_w, new[:, HEAD:])
    for h in range(HEADS):
        merged[:, h * HEAD : (h + 1) * HEAD] = attended[h * both : (h + 1) * both]
    for copy in copies[4:8]:
        copy.wait()
    hidden = jnp.concatenate([hid_ref[s].astype(F32) for s in range(steps)], axis=0)
    resid = hidden + merged[...]
    resid_ref[...] = resid
    meansq = jnp.mean(resid * resid, axis=-1, keepdims=True)
    gain = gain_ref[...].astype(F32)
    gain = jnp.concatenate([gain[i : i + 1] for i in range(width // LANES)], axis=1)
    normed = resid * lax.rsqrt(meansq + 1e-06) * gain
    out_ref[:, :width] = normed.astype(BF16)
    out_ref[:, width:] = tail(ids_ref, weight_ref, steps, rows)


def attend(cache_len, ids, weights, queries, fresh, kv_cache, hidden_state, norm_gain):
    steps, rows, width = queries.shape
    kv = kv_cache.transpose(0, 2, 1)
    gain = norm_gain.reshape(width // LANES, LANES)
    return pl.pallas_call(
        attend_kernel,
        out_shape=(
            jax.ShapeDtypeStruct((steps * rows, width), F32),
            jax.ShapeDtypeStruct((steps * rows, width + LANES), BF16),
        ),
        in_specs=[HBM] * 8,
        out_specs=(VMEM, VMEM),
        scratch_shapes=[
            pltpu.SMEM(cache_len.shape, jnp.int32),
            pltpu.SMEM(ids.shape, jnp.int32),
            pltpu.SMEM(weights.shape, F32),
            pltpu.VMEM(queries.shape, BF16),
            pltpu.VMEM(fresh.shape, BF16),
            pltpu.VMEM(kv.shape, BF16),
            pltpu.VMEM(hidden_state.shape, BF16),
            pltpu.VMEM(gain.shape, BF16),
            pltpu.VMEM((steps * rows, width), F32),
            pltpu.SemaphoreType.DMA((8,)),
        ],
        compiler_params=pltpu.CompilerParams(vmem_limit_bytes=24 * MIB),
        cost_estimate=pl.CostEstimate(
            flops=300_000_000, bytes_accessed=2_000_000, transcendentals=131072
        ),
        name="attend",
    )(*in_hbm(cache_len, ids, weights, queries, fresh, kv, hidden_state, gain))


def pack_kernel(steps, chips, own_ref, other_ref, *outs):
    both, width = own_ref.shape
    width -= LANES
    rows = both // steps
    piece = width // PIECES
    side_lines = steps * CAP
    lines = PIECES * 2 * side_lines
    tails = [ref[:, width:].astype(F32) for ref in (own_ref, other_ref)]
    tails = jnp.concatenate(tails * PIECES, axis=0).astype(BF16)
    count = 2 * both * PIECES
    row = iota((len(outs) * lines, LANES), 0)
    lane = iota((len(outs) * lines, LANES), 1)
    wanted = one_hot(lane == PARTS * EXPERTS + expert_at(row // lines, chips))
    named = nt_dot(wanted, tails)
    at = iota((count, count), 0)
    to = iota((count, count), 1)
    before = one_hot((at // rows == to // rows) & (at < to))
    rank = dot(named.astype(BF16), before)
    line = iota(named.shape, 0)
    col = iota(named.shape, 1)
    same = (line // CAP) % (lines // CAP) == col // rows
    picks = one_hot(same & (named > 0.5) & (rank == (line % CAP).astype(F32)))
    parts = [ref[:, :width].astype(F32) for ref in (own_ref, other_ref)]
    stacked = jnp.concatenate(
        [part[:, k * piece : (k + 1) * piece] for k in range(PIECES) for part in parts], axis=0
    ).astype(BF16)
    sent = dot(picks, stacked).astype(BF16)
    for t, out in enumerate(outs):
        out[...] = sent[t * lines : (t + 1) * lines]


def pack(steps, chips, own, other):
    both, width = own.shape
    shape = (PIECES * 2 * steps * CAP, (width - LANES) // PIECES)
    turns = chips // 2
    return pl.pallas_call(
        functools.partial(pack_kernel, steps, chips),
        out_shape=[jax.ShapeDtypeStruct(shape, BF16)] * turns,
        in_specs=[VMEM] * 2,
        out_specs=[VMEM] * turns,
        compiler_params=pltpu.CompilerParams(vmem_limit_bytes=24 * MIB),
        cost_estimate=pl.CostEstimate(
            flops=50_000_000, bytes_accessed=2_000_000, transcendentals=0
        ),
        name="pack",
    )(own, other)


def mixing(steps, chips, own_ref, other_ref):
    both, width = own_ref.shape
    width -= LANES
    rows = both // steps
    lines = PIECES * 2 * steps * CAP
    tails = [ref[:, width:].astype(F32) for ref in (own_ref, other_ref)]
    tails = jnp.concatenate(tails, axis=0).astype(BF16)
    count = chips // 2 * lines
    lane = iota((LANES, count), 0)
    expert = expert_at(iota((LANES, count), 1) // lines, chips)
    found = [dot(tails, one_hot(lane == part * EXPERTS + expert)) for part in range(PARTS + 1)]
    at = iota((2 * both, 2 * both), 1)
    to = iota((2 * both, 2 * both), 0)
    rank = dot(one_hot((at // rows == to // rows) & (at < to)), found[PARTS].astype(BF16))
    line = iota((2 * both, count), 1)
    row = iota((2 * both, count), 0)
    same = (line // CAP) % (2 * steps) == row // rows
    slot = same & (rank == (line % CAP).astype(F32))
    k_of = line // (2 * steps * CAP) % PIECES
    parts = [
        jnp.where(slot & (k_of == k), found[part], 0.0)
        for part in range(PARTS)
        for k in range(PIECES)
    ]
    return jnp.concatenate(parts, axis=0).astype(BF16)


def stage_kernel(gu_hbm, dn_hbm, gu, dn, sems):
    step = dn.shape[0] // 4
    pairs = []
    for i in range(4):
        part = pl.ds(i * step, step)
        pairs.append((gu_hbm.at[0, 0, part], gu.at[0, part]))
        pairs.append((gu_hbm.at[0, 1, part], gu.at[1, part]))
        pairs.append((dn_hbm.at[0, part], dn.at[part]))
    copies = [pltpu.make_async_copy(a, b, sems.at[i]) for i, (a, b) in enumerate(pairs)]
    for copy in copies:
        copy.start()
    for copy in copies:
        copy.wait()


def stage(gate_up, down):
    return pl.pallas_call(
        stage_kernel,
        out_shape=(
            jax.ShapeDtypeStruct(gate_up.shape[1:], BF16),
            jax.ShapeDtypeStruct(down.shape[1:], BF16),
        ),
        in_specs=[HBM, HBM],
        out_specs=(VMEM, VMEM),
        scratch_shapes=[pltpu.SemaphoreType.DMA((12,))],
        compiler_params=pltpu.CompilerParams(vmem_limit_bytes=16 * MIB),
        cost_estimate=pl.CostEstimate(flops=0, bytes_accessed=22_000_000, transcendentals=0),
        name="stage",
    )(*in_hbm(gate_up, down))


def mix_kernel(steps, chips, own_ref, other_ref, mix_ref):
    mix_ref[...] = mixing(steps, chips, own_ref, other_ref)


def mixer(steps, chips, own, other):
    lines = PIECES * 2 * steps * CAP
    shape = (PARTS * PIECES * 2 * own.shape[0], chips // 2 * lines)
    return pl.pallas_call(
        functools.partial(mix_kernel, steps, chips),
        out_shape=jax.ShapeDtypeStruct(shape, BF16),
        in_specs=[VMEM, VMEM],
        out_specs=VMEM,
        compiler_params=pltpu.CompilerParams(vmem_limit_bytes=24 * MIB),
        cost_estimate=pl.CostEstimate(
            flops=10_000_000, bytes_accessed=1_000_000, transcendentals=0
        ),
        name="mixer",
    )(own, other)


def expert_kernel(turns, *refs):
    own_refs, other_refs = refs[:turns], refs[turns : 2 * turns]
    w_in, w_down = refs[2 * turns : 2 * turns + 2]
    mine_refs = refs[2 * turns + 2 : 3 * turns + 2]
    theirs_refs = refs[3 * turns + 2 :]
    lines, piece = own_refs[0].shape
    per = lines // PIECES
    half = turns * per
    arrays = [ref[...].astype(F32) for ref in own_refs + other_refs]
    gate = upper = None
    for k in range(PIECES):
        x = [array[k * per : (k + 1) * per] for array in arrays]
        x = jnp.concatenate(x, axis=0).astype(BF16)
        cols = pl.ds(k * piece, piece)
        g, u = nt_dot(w_in[0, :, cols], x), nt_dot(w_in[1, :, cols], x)
        gate, upper = (g, u) if k == 0 else (gate + g, upper + u)
    act = (gate / (1.0 + jnp.exp(-gate)) * upper).T.astype(BF16)
    parts = [dot(act, w_down[:, k * piece : (k + 1) * piece]) for k in range(PIECES)]
    for first, now in ((half, theirs_refs), (0, mine_refs)):
        for t, ref in enumerate(now):
            start = first + t * per
            out = [part[start : start + per] for part in parts]
            ref[...] = jnp.concatenate(out, axis=0).astype(BF16)


def experts(own, other, gate_up, down):
    turns = len(own)
    shape = jax.ShapeDtypeStruct(own[0].shape, BF16)
    results = pl.pallas_call(
        functools.partial(expert_kernel, turns),
        out_shape=[shape] * (2 * turns),
        in_specs=[VMEM] * (2 * turns + 2),
        out_specs=[VMEM] * (2 * turns),
        compiler_params=pltpu.CompilerParams(vmem_limit_bytes=32 * MIB),
        cost_estimate=pl.CostEstimate(
            flops=800_000_000, bytes_accessed=12_000_000, transcendentals=16384
        ),
        name="experts",
    )(*own, *other, gate_up, down)
    return results[:turns], results[turns:]


def combine_kernel(mix_ref, resid_ref, *refs):
    back_refs, (kept_ref, sent_ref) = refs[:-2], refs[-2:]
    both = resid_ref.shape[0]
    piece = back_refs[0].shape[1]
    product = dot(mix_ref[...], jnp.concatenate([ref[...] for ref in back_refs], axis=0))
    n = PIECES * 2 * both
    total = product[:n] + product[n : 2 * n] + product[2 * n :]
    for k in range(PIECES):
        cols = pl.ds(k * piece, piece)
        first = k * 2 * both
        kept_ref[:, cols] = resid_ref[:, cols] + total[first : first + both]
        sent_ref[:, cols] = total[first + both : first + 2 * both].astype(BF16)


def combine(mix, resid, backs):
    return pl.pallas_call(
        combine_kernel,
        out_shape=(
            jax.ShapeDtypeStruct(resid.shape, F32),
            jax.ShapeDtypeStruct(resid.shape, BF16),
        ),
        in_specs=[VMEM] * (2 + len(backs)),
        out_specs=(VMEM, VMEM),
        compiler_params=pltpu.CompilerParams(vmem_limit_bytes=24 * MIB),
        cost_estimate=pl.CostEstimate(
            flops=100_000_000, bytes_accessed=1_000_000, transcendentals=0
        ),
        name="combine",
    )(mix, resid, *backs)


def finish_kernel(kept_ref, other_ref, out_ref):
    steps, rows, _ = out_ref.shape
    done = (kept_ref[...] + other_ref[...].astype(F32)).astype(BF16)
    for s in range(steps):
        out_ref[s] = done[s * rows : (s + 1) * rows]


def finish(shape, kept, other):
    return pl.pallas_call(
        finish_kernel,
        out_shape=jax.ShapeDtypeStruct(shape, BF16),
        in_specs=[VMEM, VMEM],
        out_specs=VMEM,
        compiler_params=pltpu.CompilerParams(vmem_limit_bytes=24 * MIB),
        cost_estimate=pl.CostEstimate(flops=100_000, bytes_accessed=500_000, transcendentals=0),
        name="finish",
    )(kept, other)


def per_device(
    queries,
    fresh,
    kv_cache,
    cache_len,
    hidden_state,
    norm_gain,
    expert_ids,
    route_weight,
    gate_up,
    down,
):
    steps = queries.shape[0]
    owners = lax.axis_size("afd")
    chips = owners // 2
    turns = chips // 2
    cores = [(i, i ^ 1) for i in range(owners)]

    def swap(x):
        return lax.ppermute(x, "afd", cores)

    def route(t):
        return [(i, (i // 2 ^ distance(t, i % 2, chips)) * 2 + 1 - i % 2) for i in range(owners)]

    def send(x, t):
        return lax.ppermute(x, "afd", route(t))

    def send_back(x, t):
        return lax.ppermute(x, "afd", [(j, i) for i, j in route(t)])

    ids = expert_ids.transpose(2, 0, 1)
    weights = route_weight.transpose(2, 0, 1)
    resid, normed = attend(
        cache_len, ids, weights, queries, fresh, kv_cache, hidden_state, norm_gain
    )
    normed_other = swap(normed)
    sent = pack(steps, chips, normed, normed_other)
    own = [send(sent[t], t) for t in range(turns)]
    w_in, w_down = stage(gate_up, down)
    mix = mixer(steps, chips, normed, normed_other)
    own[0], w_in = lax.optimization_barrier((own[0], w_in))
    other = [swap(x) for x in own]
    summed = []
    for t in range(0, turns, TOGETHER):
        now = slice(t, t + TOGETHER)
        mine, theirs = experts(own[now], other[now], w_in, w_down)
        summed += [
            (a.astype(F32) + swap(b).astype(F32)).astype(BF16) for a, b in zip(mine, theirs)
        ]
    backs = [send_back(summed[t], t) for t in range(turns)]
    kept, given = combine(mix, resid, backs)
    return finish(queries.shape, kept, swap(given))


def solution(mesh):
    placed = (
        P(None, ("group", "afd"), None),
        P(None, ("group", "afd"), None),
        P(("group", "afd"), None, None),
        P(("group", "afd")),
        P(None, ("group", "afd"), None),
        P(),
        P(None, ("group", "afd"), None),
        P(None, ("group", "afd"), None),
        P("afd", None, None, None),
        P("afd", None, None),
    )
    return jax.shard_map(
        per_device,
        mesh=mesh,
        in_specs=placed,
        out_specs=P(None, ("group", "afd"), None),
        check_vma=False,
    )
```

```python
import functools
import jax
import jax.numpy as jnp
from jax import lax
from jax.experimental import pallas as pl
from jax.experimental.pallas import tpu as pltpu
from jax.sharding import PartitionSpec as P

HEADS = 32
HEAD = 224
EXPERTS = 8
TOP = 3
CAP = 2
PIECES = 4
LANES = 128
PARTS = 3
F32 = jnp.float32
BF16 = jnp.bfloat16
MIB = 1 << 20
VMEM = pl.BlockSpec(memory_space=pltpu.VMEM)
HBM = pl.BlockSpec(memory_space=pltpu.HBM)
TOGETHER = 4


def iota(shape, dim):
    return lax.broadcasted_iota(jnp.int32, shape, dim)


def in_hbm(*arrays):
    return [pltpu.with_memory_space_constraint(x, pltpu.HBM) for x in arrays]


def nt_dot(a, b):
    return lax.dot_general(a, b, (((1,), (1,)), ((), ())), preferred_element_type=F32)


def dot(a, b):
    return jnp.dot(a, b, preferred_element_type=F32)


def one_hot(mask):
    return jnp.where(mask, 1.0, 0.0).astype(BF16)


def distance(turn, core, chips):
    bits = (chips // 2).bit_length() - 1
    even = 0
    for b in range(bits):
        even = even + ((turn >> b) % 2 << (bits - b))
    return even ^ (core * (chips - 1))


def expert_at(turn, chips):
    place = lax.axis_index("afd")
    return (distance(turn, place % 2, chips) ^ (place // 2)) // (chips // EXPERTS)


def spread(ref, k, where, steps, rows, empty):
    out = jnp.full(where.shape, empty)
    for s in range(steps):
        for r in range(rows):
            out = jnp.where(where == s * rows + r, ref[k, s, r], out)
    return out


def tail(ids_ref, weight_ref, steps, rows):
    both = steps * rows
    lane = iota((both, LANES), 1)
    where = iota((both, 1), 0)
    mix = jnp.zeros((both, LANES), F32)
    named = jnp.zeros((both, LANES), F32)
    for k in range(TOP):
        hit = spread(ids_ref, k, where, steps, rows, -1) == lane % EXPERTS
        mix = mix + jnp.where(hit, spread(weight_ref, k, where, steps, rows, 0.0), 0.0)
        named = named + jnp.where(hit, 1.0, 0.0)
    out = jnp.where(lane // EXPERTS == PARTS, named, 0.0)
    for part in range(PARTS):
        term = mix.astype(BF16).astype(F32)
        out = jnp.where(lane // EXPERTS == part, term, out)
        mix = mix - term
    return out.astype(BF16)


def attend_kernel(
    len_hbm,
    ids_hbm,
    weight_hbm,
    q_hbm,
    fresh_hbm,
    kv_hbm,
    hid_hbm,
    gain_hbm,
    resid_ref,
    out_ref,
    len_ref,
    ids_ref,
    weight_ref,
    q_ref,
    fresh_ref,
    kv_ref,
    hid_ref,
    gain_ref,
    merged,
    sems,
):
    pairs = (
        (q_hbm, q_ref),
        (kv_hbm, kv_ref),
        (fresh_hbm, fresh_ref),
        (len_hbm, len_ref),
        (hid_hbm, hid_ref),
        (gain_hbm, gain_ref),
        (ids_hbm, ids_ref),
        (weight_hbm, weight_ref),
    )
    copies = [pltpu.make_async_copy(a, b, sems.at[i]) for i, (a, b) in enumerate(pairs)]
    for copy in copies:
        copy.start()
    steps, rows, width = q_ref.shape
    length = kv_ref.shape[2]
    both = steps * rows
    scale = HEAD ** (-0.5)
    copies[0].wait()
    q = jnp.concatenate([q_ref[s].astype(F32) for s in range(steps)], axis=0)
    heads = jnp.concatenate([q[:, h * HEAD : (h + 1) * HEAD] for h in range(HEADS)], axis=0)
    heads = heads.astype(BF16)
    for copy in copies[1:4]:
        copy.wait()
    kv = jnp.concatenate([kv_ref[r] for r in range(rows)], axis=1)
    new = jnp.concatenate([fresh_ref[s].astype(F32) for s in range(steps)], axis=0).astype(BF16)

    sub = iota((both, rows * length), 0)
    lane = iota((both, rows * length), 1)
    limit = jnp.zeros_like(lane)
    for r in range(rows):
        limit = jnp.where(lane // length == r, len_ref[r], limit)
    valid = (lane // length == sub % rows) & (lane % length < limit)
    sub = iota((both, both), 0)
    lane = iota((both, both), 1)
    valid_new = (lane % rows == sub % rows) & (lane // rows <= sub // rows)

    old_s = (dot(heads, kv[:HEAD]) * scale).reshape(HEADS, both, rows * length)
    new_s = (nt_dot(heads, new[:, :HEAD]) * scale).reshape(HEADS, both, both)
    old_s = jnp.where(valid[None], old_s, -1e30)
    new_s = jnp.where(valid_new[None], new_s, -1e30)
    top = jnp.maximum(
        jnp.max(old_s, axis=-1, keepdims=True), jnp.max(new_s, axis=-1, keepdims=True)
    )
    old_e = jnp.exp(old_s - top)
    new_e = jnp.exp(new_s - top)
    total = jnp.sum(old_e, axis=-1, keepdims=True) + jnp.sum(new_e, axis=-1, keepdims=True)
    share = 1.0 / total
    old_w = (old_e * share).reshape(HEADS * both, rows * length).astype(BF16)
    new_w = (new_e * share).reshape(HEADS * both, both).astype(BF16)
    attended = nt_dot(old_w, kv[HEAD:]) + dot(new_w, new[:, HEAD:])
    for h in range(HEADS):
        merged[:, h * HEAD : (h + 1) * HEAD] = attended[h * both : (h + 1) * both]
    for copy in copies[4:8]:
        copy.wait()
    hidden = jnp.concatenate([hid_ref[s].astype(F32) for s in range(steps)], axis=0)
    resid = hidden + merged[...]
    resid_ref[...] = resid
    meansq = jnp.mean(resid * resid, axis=-1, keepdims=True)
    gain = gain_ref[...].astype(F32)
    gain = jnp.concatenate([gain[i : i + 1] for i in range(width // LANES)], axis=1)
    normed = resid * lax.rsqrt(meansq + 1e-06) * gain
    out_ref[:, :width] = normed.astype(BF16)
    out_ref[:, width:] = tail(ids_ref, weight_ref, steps, rows)


def attend(cache_len, ids, weights, queries, fresh, kv_cache, hidden_state, norm_gain):
    steps, rows, width = queries.shape
    kv = kv_cache.transpose(0, 2, 1)
    gain = norm_gain.reshape(width // LANES, LANES)
    return pl.pallas_call(
        attend_kernel,
        out_shape=(
            jax.ShapeDtypeStruct((steps * rows, width), F32),
            jax.ShapeDtypeStruct((steps * rows, width + LANES), BF16),
        ),
        in_specs=[HBM] * 8,
        out_specs=(VMEM, VMEM),
        scratch_shapes=[
            pltpu.SMEM(cache_len.shape, jnp.int32),
            pltpu.SMEM(ids.shape, jnp.int32),
            pltpu.SMEM(weights.shape, F32),
            pltpu.VMEM(queries.shape, BF16),
            pltpu.VMEM(fresh.shape, BF16),
            pltpu.VMEM(kv.shape, BF16),
            pltpu.VMEM(hidden_state.shape, BF16),
            pltpu.VMEM(gain.shape, BF16),
            pltpu.VMEM((steps * rows, width), F32),
            pltpu.SemaphoreType.DMA((8,)),
        ],
        compiler_params=pltpu.CompilerParams(vmem_limit_bytes=24 * MIB),
        cost_estimate=pl.CostEstimate(
            flops=300_000_000, bytes_accessed=2_000_000, transcendentals=131072
        ),
        name="attend",
    )(*in_hbm(cache_len, ids, weights, queries, fresh, kv, hidden_state, gain))


def pack_kernel(steps, chips, own_ref, other_ref, *outs):
    both, width = own_ref.shape
    width -= LANES
    rows = both // steps
    piece = width // PIECES
    side_lines = steps * CAP
    lines = PIECES * 2 * side_lines
    tails = [ref[:, width:].astype(F32) for ref in (own_ref, other_ref)]
    tails = jnp.concatenate(tails * PIECES, axis=0).astype(BF16)
    count = 2 * both * PIECES
    row = iota((len(outs) * lines, LANES), 0)
    lane = iota((len(outs) * lines, LANES), 1)
    wanted = one_hot(lane == PARTS * EXPERTS + expert_at(row // lines, chips))
    named = nt_dot(wanted, tails)
    at = iota((count, count), 0)
    to = iota((count, count), 1)
    before = one_hot((at // rows == to // rows) & (at < to))
    rank = dot(named.astype(BF16), before)
    line = iota(named.shape, 0)
    col = iota(named.shape, 1)
    same = (line // CAP) % (lines // CAP) == col // rows
    picks = one_hot(same & (named > 0.5) & (rank == (line % CAP).astype(F32)))
    parts = [ref[:, :width].astype(F32) for ref in (own_ref, other_ref)]
    stacked = jnp.concatenate(
        [part[:, k * piece : (k + 1) * piece] for k in range(PIECES) for part in parts], axis=0
    ).astype(BF16)
    sent = dot(picks, stacked).astype(BF16)
    for t, out in enumerate(outs):
        out[...] = sent[t * lines : (t + 1) * lines]


def pack(steps, chips, own, other):
    both, width = own.shape
    shape = (PIECES * 2 * steps * CAP, (width - LANES) // PIECES)
    turns = chips // 2
    return pl.pallas_call(
        functools.partial(pack_kernel, steps, chips),
        out_shape=[jax.ShapeDtypeStruct(shape, BF16)] * turns,
        in_specs=[VMEM] * 2,
        out_specs=[VMEM] * turns,
        compiler_params=pltpu.CompilerParams(vmem_limit_bytes=24 * MIB),
        cost_estimate=pl.CostEstimate(
            flops=50_000_000, bytes_accessed=2_000_000, transcendentals=0
        ),
        name="pack",
    )(own, other)


def mixing(steps, chips, own_ref, other_ref):
    both, width = own_ref.shape
    width -= LANES
    rows = both // steps
    lines = PIECES * 2 * steps * CAP
    tails = [ref[:, width:].astype(F32) for ref in (own_ref, other_ref)]
    tails = jnp.concatenate(tails, axis=0).astype(BF16)
    count = chips // 2 * lines
    lane = iota((LANES, count), 0)
    expert = expert_at(iota((LANES, count), 1) // lines, chips)
    found = [dot(tails, one_hot(lane == part * EXPERTS + expert)) for part in range(PARTS + 1)]
    at = iota((2 * both, 2 * both), 1)
    to = iota((2 * both, 2 * both), 0)
    rank = dot(one_hot((at // rows == to // rows) & (at < to)), found[PARTS].astype(BF16))
    line = iota((2 * both, count), 1)
    row = iota((2 * both, count), 0)
    same = (line // CAP) % (2 * steps) == row // rows
    slot = same & (rank == (line % CAP).astype(F32))
    k_of = line // (2 * steps * CAP) % PIECES
    parts = [
        jnp.where(slot & (k_of == k), found[part], 0.0)
        for part in range(PARTS)
        for k in range(PIECES)
    ]
    return jnp.concatenate(parts, axis=0).astype(BF16)


def stage_kernel(gu_hbm, dn_hbm, gu, dn, sems):
    step = dn.shape[0] // 4
    pairs = []
    for i in range(4):
        part = pl.ds(i * step, step)
        pairs.append((gu_hbm.at[0, 0, part], gu.at[0, part]))
        pairs.append((gu_hbm.at[0, 1, part], gu.at[1, part]))
        pairs.append((dn_hbm.at[0, part], dn.at[part]))
    copies = [pltpu.make_async_copy(a, b, sems.at[i]) for i, (a, b) in enumerate(pairs)]
    for copy in copies:
        copy.start()
    for copy in copies:
        copy.wait()


def stage(gate_up, down):
    return pl.pallas_call(
        stage_kernel,
        out_shape=(
            jax.ShapeDtypeStruct(gate_up.shape[1:], BF16),
            jax.ShapeDtypeStruct(down.shape[1:], BF16),
        ),
        in_specs=[HBM, HBM],
        out_specs=(VMEM, VMEM),
        scratch_shapes=[pltpu.SemaphoreType.DMA((12,))],
        compiler_params=pltpu.CompilerParams(vmem_limit_bytes=16 * MIB),
        cost_estimate=pl.CostEstimate(flops=0, bytes_accessed=22_000_000, transcendentals=0),
        name="stage",
    )(*in_hbm(gate_up, down))


def mix_kernel(steps, chips, own_ref, other_ref, mix_ref):
    mix_ref[...] = mixing(steps, chips, own_ref, other_ref)


def mixer(steps, chips, own, other):
    lines = PIECES * 2 * steps * CAP
    shape = (PARTS * PIECES * 2 * own.shape[0], chips // 2 * lines)
    return pl.pallas_call(
        functools.partial(mix_kernel, steps, chips),
        out_shape=jax.ShapeDtypeStruct(shape, BF16),
        in_specs=[VMEM, VMEM],
        out_specs=VMEM,
        compiler_params=pltpu.CompilerParams(vmem_limit_bytes=24 * MIB),
        cost_estimate=pl.CostEstimate(
            flops=10_000_000, bytes_accessed=1_000_000, transcendentals=0
        ),
        name="mixer",
    )(own, other)


def expert_kernel(turns, *refs):
    own_refs, other_refs = refs[:turns], refs[turns : 2 * turns]
    w_in, w_down = refs[2 * turns : 2 * turns + 2]
    mine_refs = refs[2 * turns + 2 : 3 * turns + 2]
    theirs_refs = refs[3 * turns + 2 :]
    lines, piece = own_refs[0].shape
    per = lines // PIECES
    half = turns * per
    arrays = [ref[...].astype(F32) for ref in own_refs + other_refs]
    gate = upper = None
    for k in range(PIECES):
        x = [array[k * per : (k + 1) * per] for array in arrays]
        x = jnp.concatenate(x, axis=0).astype(BF16)
        cols = pl.ds(k * piece, piece)
        g, u = nt_dot(w_in[0, :, cols], x), nt_dot(w_in[1, :, cols], x)
        gate, upper = (g, u) if k == 0 else (gate + g, upper + u)
    act = (gate / (1.0 + jnp.exp(-gate)) * upper).T.astype(BF16)
    parts = [dot(act, w_down[:, k * piece : (k + 1) * piece]) for k in range(PIECES)]
    for first, now in ((half, theirs_refs), (0, mine_refs)):
        for t, ref in enumerate(now):
            start = first + t * per
            out = [part[start : start + per] for part in parts]
            ref[...] = jnp.concatenate(out, axis=0).astype(BF16)


def experts(own, other, gate_up, down):
    turns = len(own)
    shape = jax.ShapeDtypeStruct(own[0].shape, BF16)
    results = pl.pallas_call(
        functools.partial(expert_kernel, turns),
        out_shape=[shape] * (2 * turns),
        in_specs=[VMEM] * (2 * turns + 2),
        out_specs=[VMEM] * (2 * turns),
        compiler_params=pltpu.CompilerParams(vmem_limit_bytes=32 * MIB),
        cost_estimate=pl.CostEstimate(
            flops=800_000_000, bytes_accessed=12_000_000, transcendentals=16384
        ),
        name="experts",
    )(*own, *other, gate_up, down)
    return results[:turns], results[turns:]


def combine_kernel(mix_ref, resid_ref, *refs):
    back_refs, (kept_ref, sent_ref) = refs[:-2], refs[-2:]
    both = resid_ref.shape[0]
    piece = back_refs[0].shape[1]
    product = dot(mix_ref[...], jnp.concatenate([ref[...] for ref in back_refs], axis=0))
    n = PIECES * 2 * both
    total = product[:n] + product[n : 2 * n] + product[2 * n :]
    for k in range(PIECES):
        cols = pl.ds(k * piece, piece)
        first = k * 2 * both
        kept_ref[:, cols] = resid_ref[:, cols] + total[first : first + both]
        sent_ref[:, cols] = total[first + both : first + 2 * both].astype(BF16)


def combine(mix, resid, backs):
    return pl.pallas_call(
        combine_kernel,
        out_shape=(
            jax.ShapeDtypeStruct(resid.shape, F32),
            jax.ShapeDtypeStruct(resid.shape, BF16),
        ),
        in_specs=[VMEM] * (2 + len(backs)),
        out_specs=(VMEM, VMEM),
        compiler_params=pltpu.CompilerParams(vmem_limit_bytes=24 * MIB),
        cost_estimate=pl.CostEstimate(
            flops=100_000_000, bytes_accessed=1_000_000, transcendentals=0
        ),
        name="combine",
    )(mix, resid, *backs)


def finish_kernel(kept_ref, other_ref, out_ref):
    steps, rows, _ = out_ref.shape
    done = (kept_ref[...] + other_ref[...].astype(F32)).astype(BF16)
    for s in range(steps):
        out_ref[s] = done[s * rows : (s + 1) * rows]


def finish(shape, kept, other):
    return pl.pallas_call(
        finish_kernel,
        out_shape=jax.ShapeDtypeStruct(shape, BF16),
        in_specs=[VMEM, VMEM],
        out_specs=VMEM,
        compiler_params=pltpu.CompilerParams(vmem_limit_bytes=24 * MIB),
        cost_estimate=pl.CostEstimate(flops=100_000, bytes_accessed=500_000, transcendentals=0),
        name="finish",
    )(kept, other)


def per_device(
    queries,
    fresh,
    kv_cache,
    cache_len,
    hidden_state,
    norm_gain,
    expert_ids,
    route_weight,
    gate_up,
    down,
):
    steps = queries.shape[0]
    owners = lax.axis_size("afd")
    chips = owners // 2
    turns = chips // 2
    cores = [(i, i ^ 1) for i in range(owners)]

    def swap(x):
        return lax.ppermute(x, "afd", cores)

    def route(t):
        return [(i, (i // 2 ^ distance(t, i % 2, chips)) * 2 + 1 - i % 2) for i in range(owners)]

    def send(x, t):
        return lax.ppermute(x, "afd", route(t))

    def send_back(x, t):
        return lax.ppermute(x, "afd", [(j, i) for i, j in route(t)])

    ids = expert_ids.transpose(2, 0, 1)
    weights = route_weight.transpose(2, 0, 1)
    resid, normed = attend(
        cache_len, ids, weights, queries, fresh, kv_cache, hidden_state, norm_gain
    )
    normed_other = swap(normed)
    sent = pack(steps, chips, normed, normed_other)
    own = [send(sent[t], t) for t in range(turns)]
    w_in, w_down = stage(gate_up, down)
    mix = mixer(steps, chips, normed, normed_other)
    own[0], w_in = lax.optimization_barrier((own[0], w_in))
    other = [swap(x) for x in own]
    summed = []
    for t in range(0, turns, TOGETHER):
        now = slice(t, t + TOGETHER)
        mine, theirs = experts(own[now], other[now], w_in, w_down)
        head = (mine[0].astype(F32) + swap(theirs[0]).astype(F32)).astype(BF16)
        head, theirs = lax.optimization_barrier((head, theirs[1:]))
        summed += [head]
        summed += [
            (a.astype(F32) + swap(b).astype(F32)).astype(BF16) for a, b in zip(mine[1:], theirs)
        ]
    backs = [send_back(summed[t], t) for t in range(turns)]
    kept, given = combine(mix, resid, backs)
    return finish(queries.shape, kept, swap(given))


def solution(mesh):
    placed = (
        P(None, ("group", "afd"), None),
        P(None, ("group", "afd"), None),
        P(("group", "afd"), None, None),
        P(("group", "afd")),
        P(None, ("group", "afd"), None),
        P(),
        P(None, ("group", "afd"), None),
        P(None, ("group", "afd"), None),
        P("afd", None, None, None),
        P("afd", None, None),
    )
    return jax.shard_map(
        per_device,
        mesh=mesh,
        in_specs=placed,
        out_specs=P(None, ("group", "afd"), None),
        check_vma=False,
    )
```

```python
import functools
import jax
import jax.numpy as jnp
from jax import lax
from jax.experimental import pallas as pl
from jax.experimental.pallas import tpu as pltpu
from jax.sharding import PartitionSpec as P

HEADS = 32
HEAD = 224
EXPERTS = 8
TOP = 3
CAP = 2
PIECES = 4
LANES = 128
PARTS = 3
F32 = jnp.float32
BF16 = jnp.bfloat16
MIB = 1 << 20
VMEM = pl.BlockSpec(memory_space=pltpu.VMEM)
HBM = pl.BlockSpec(memory_space=pltpu.HBM)
TOGETHER = 4


def iota(shape, dim):
    return lax.broadcasted_iota(jnp.int32, shape, dim)


def in_hbm(*arrays):
    return [pltpu.with_memory_space_constraint(x, pltpu.HBM) for x in arrays]


def nt_dot(a, b):
    return lax.dot_general(a, b, (((1,), (1,)), ((), ())), preferred_element_type=F32)


def dot(a, b):
    return jnp.dot(a, b, preferred_element_type=F32)


def one_hot(mask):
    return jnp.where(mask, 1.0, 0.0).astype(BF16)


def distance(turn, core, chips):
    bits = (chips // 2).bit_length() - 1
    even = 0
    for b in range(bits):
        even = even + ((turn >> b) % 2 << (bits - b))
    return even ^ (core * (chips - 1))


def expert_at(turn, chips):
    place = lax.axis_index("afd")
    return (distance(turn, place % 2, chips) ^ (place // 2)) // (chips // EXPERTS)


def spread(ref, k, where, steps, rows, empty):
    out = jnp.full(where.shape, empty)
    for s in range(steps):
        for r in range(rows):
            out = jnp.where(where == s * rows + r, ref[k, s, r], out)
    return out


def tail(ids_ref, weight_ref, steps, rows):
    both = steps * rows
    lane = iota((both, LANES), 1)
    where = iota((both, 1), 0)
    mix = jnp.zeros((both, LANES), F32)
    named = jnp.zeros((both, LANES), F32)
    for k in range(TOP):
        hit = spread(ids_ref, k, where, steps, rows, -1) == lane % EXPERTS
        mix = mix + jnp.where(hit, spread(weight_ref, k, where, steps, rows, 0.0), 0.0)
        named = named + jnp.where(hit, 1.0, 0.0)
    out = jnp.where(lane // EXPERTS == PARTS, named, 0.0)
    for part in range(PARTS):
        term = mix.astype(BF16).astype(F32)
        out = jnp.where(lane // EXPERTS == part, term, out)
        mix = mix - term
    return out.astype(BF16)


def attend_kernel(
    len_hbm,
    ids_hbm,
    weight_hbm,
    q_hbm,
    fresh_hbm,
    kv_hbm,
    hid_hbm,
    gain_hbm,
    resid_ref,
    out_ref,
    len_ref,
    ids_ref,
    weight_ref,
    q_ref,
    fresh_ref,
    kv_ref,
    hid_ref,
    gain_ref,
    merged,
    sems,
):
    pairs = (
        (q_hbm, q_ref),
        (kv_hbm, kv_ref),
        (fresh_hbm, fresh_ref),
        (len_hbm, len_ref),
        (hid_hbm, hid_ref),
        (gain_hbm, gain_ref),
        (ids_hbm, ids_ref),
        (weight_hbm, weight_ref),
    )
    copies = [pltpu.make_async_copy(a, b, sems.at[i]) for i, (a, b) in enumerate(pairs)]
    for copy in copies:
        copy.start()
    steps, rows, width = q_ref.shape
    length = kv_ref.shape[2]
    both = steps * rows
    scale = HEAD ** (-0.5)
    copies[0].wait()
    q = jnp.concatenate([q_ref[s].astype(F32) for s in range(steps)], axis=0)
    heads = jnp.concatenate([q[:, h * HEAD : (h + 1) * HEAD] for h in range(HEADS)], axis=0)
    heads = heads.astype(BF16)
    for copy in copies[1:4]:
        copy.wait()
    kv = jnp.concatenate([kv_ref[r] for r in range(rows)], axis=1)
    new = jnp.concatenate([fresh_ref[s].astype(F32) for s in range(steps)], axis=0).astype(BF16)

    sub = iota((both, rows * length), 0)
    lane = iota((both, rows * length), 1)
    limit = jnp.zeros_like(lane)
    for r in range(rows):
        limit = jnp.where(lane // length == r, len_ref[r], limit)
    valid = (lane // length == sub % rows) & (lane % length < limit)
    sub = iota((both, both), 0)
    lane = iota((both, both), 1)
    valid_new = (lane % rows == sub % rows) & (lane // rows <= sub // rows)

    old_s = (dot(heads, kv[:HEAD]) * scale).reshape(HEADS, both, rows * length)
    new_s = (nt_dot(heads, new[:, :HEAD]) * scale).reshape(HEADS, both, both)
    old_s = jnp.where(valid[None], old_s, -1e30)
    new_s = jnp.where(valid_new[None], new_s, -1e30)
    top = jnp.maximum(
        jnp.max(old_s, axis=-1, keepdims=True), jnp.max(new_s, axis=-1, keepdims=True)
    )
    old_e = jnp.exp(old_s - top)
    new_e = jnp.exp(new_s - top)
    total = jnp.sum(old_e, axis=-1, keepdims=True) + jnp.sum(new_e, axis=-1, keepdims=True)
    share = 1.0 / total
    old_w = (old_e * share).reshape(HEADS * both, rows * length).astype(BF16)
    new_w = (new_e * share).reshape(HEADS * both, both).astype(BF16)
    attended = nt_dot(old_w, kv[HEAD:]) + dot(new_w, new[:, HEAD:])
    for h in range(HEADS):
        merged[:, h * HEAD : (h + 1) * HEAD] = attended[h * both : (h + 1) * both]
    for copy in copies[4:8]:
        copy.wait()
    hidden = jnp.concatenate([hid_ref[s].astype(F32) for s in range(steps)], axis=0)
    resid = hidden + merged[...]
    resid_ref[...] = resid
    meansq = jnp.mean(resid * resid, axis=-1, keepdims=True)
    gain = gain_ref[...].astype(F32)
    gain = jnp.concatenate([gain[i : i + 1] for i in range(width // LANES)], axis=1)
    normed = resid * lax.rsqrt(meansq + 1e-06) * gain
    out_ref[:, :width] = normed.astype(BF16)
    out_ref[:, width:] = tail(ids_ref, weight_ref, steps, rows)


def attend(cache_len, ids, weights, queries, fresh, kv_cache, hidden_state, norm_gain):
    steps, rows, width = queries.shape
    kv = kv_cache.transpose(0, 2, 1)
    gain = norm_gain.reshape(width // LANES, LANES)
    return pl.pallas_call(
        attend_kernel,
        out_shape=(
            jax.ShapeDtypeStruct((steps * rows, width), F32),
            jax.ShapeDtypeStruct((steps * rows, width + LANES), BF16),
        ),
        in_specs=[HBM] * 8,
        out_specs=(VMEM, VMEM),
        scratch_shapes=[
            pltpu.SMEM(cache_len.shape, jnp.int32),
            pltpu.SMEM(ids.shape, jnp.int32),
            pltpu.SMEM(weights.shape, F32),
            pltpu.VMEM(queries.shape, BF16),
            pltpu.VMEM(fresh.shape, BF16),
            pltpu.VMEM(kv.shape, BF16),
            pltpu.VMEM(hidden_state.shape, BF16),
            pltpu.VMEM(gain.shape, BF16),
            pltpu.VMEM((steps * rows, width), F32),
            pltpu.SemaphoreType.DMA((8,)),
        ],
        compiler_params=pltpu.CompilerParams(vmem_limit_bytes=24 * MIB),
        cost_estimate=pl.CostEstimate(
            flops=300_000_000, bytes_accessed=2_000_000, transcendentals=131072
        ),
        name="attend",
    )(*in_hbm(cache_len, ids, weights, queries, fresh, kv, hidden_state, gain))


def pack_kernel(steps, chips, own_ref, other_ref, *outs):
    both, width = own_ref.shape
    width -= LANES
    rows = both // steps
    piece = width // PIECES
    side_lines = steps * CAP
    lines = PIECES * 2 * side_lines
    tails = [ref[:, width:].astype(F32) for ref in (own_ref, other_ref)]
    tails = jnp.concatenate(tails * PIECES, axis=0).astype(BF16)
    count = 2 * both * PIECES
    row = iota((len(outs) * lines, LANES), 0)
    lane = iota((len(outs) * lines, LANES), 1)
    wanted = one_hot(lane == PARTS * EXPERTS + expert_at(row // lines, chips))
    named = nt_dot(wanted, tails)
    at = iota((count, count), 0)
    to = iota((count, count), 1)
    before = one_hot((at // rows == to // rows) & (at < to))
    rank = dot(named.astype(BF16), before)
    line = iota(named.shape, 0)
    col = iota(named.shape, 1)
    same = (line // CAP) % (lines // CAP) == col // rows
    picks = one_hot(same & (named > 0.5) & (rank == (line % CAP).astype(F32)))
    parts = [ref[:, :width].astype(F32) for ref in (own_ref, other_ref)]
    stacked = jnp.concatenate(
        [part[:, k * piece : (k + 1) * piece] for k in range(PIECES) for part in parts], axis=0
    ).astype(BF16)
    sent = dot(picks, stacked).astype(BF16)
    for t, out in enumerate(outs):
        out[...] = sent[t * lines : (t + 1) * lines]


def pack(steps, chips, own, other):
    both, width = own.shape
    shape = (PIECES * 2 * steps * CAP, (width - LANES) // PIECES)
    turns = chips // 2
    return pl.pallas_call(
        functools.partial(pack_kernel, steps, chips),
        out_shape=[jax.ShapeDtypeStruct(shape, BF16)] * turns,
        in_specs=[VMEM] * 2,
        out_specs=[VMEM] * turns,
        compiler_params=pltpu.CompilerParams(vmem_limit_bytes=24 * MIB),
        cost_estimate=pl.CostEstimate(
            flops=50_000_000, bytes_accessed=2_000_000, transcendentals=0
        ),
        name="pack",
    )(own, other)


def mixing(steps, chips, own_ref, other_ref):
    both, width = own_ref.shape
    width -= LANES
    rows = both // steps
    lines = PIECES * 2 * steps * CAP
    tails = [ref[:, width:].astype(F32) for ref in (own_ref, other_ref)]
    tails = jnp.concatenate(tails, axis=0).astype(BF16)
    count = chips // 2 * lines
    lane = iota((LANES, count), 0)
    expert = expert_at(iota((LANES, count), 1) // lines, chips)
    found = [dot(tails, one_hot(lane == part * EXPERTS + expert)) for part in range(PARTS + 1)]
    at = iota((2 * both, 2 * both), 1)
    to = iota((2 * both, 2 * both), 0)
    rank = dot(one_hot((at // rows == to // rows) & (at < to)), found[PARTS].astype(BF16))
    line = iota((2 * both, count), 1)
    row = iota((2 * both, count), 0)
    same = (line // CAP) % (2 * steps) == row // rows
    slot = same & (rank == (line % CAP).astype(F32))
    k_of = line // (2 * steps * CAP) % PIECES
    parts = [
        jnp.where(slot & (k_of == k), found[part], 0.0)
        for part in range(PARTS)
        for k in range(PIECES)
    ]
    return jnp.concatenate(parts, axis=0).astype(BF16)


def stage_kernel(gu_hbm, dn_hbm, gu, dn, sems):
    step = dn.shape[0] // 4
    pairs = []
    for i in range(4):
        part = pl.ds(i * step, step)
        pairs.append((gu_hbm.at[0, 0, part], gu.at[0, part]))
        pairs.append((gu_hbm.at[0, 1, part], gu.at[1, part]))
        pairs.append((dn_hbm.at[0, part], dn.at[part]))
    copies = [pltpu.make_async_copy(a, b, sems.at[i]) for i, (a, b) in enumerate(pairs)]
    for copy in copies:
        copy.start()
    for copy in copies:
        copy.wait()


def stage(gate_up, down):
    return pl.pallas_call(
        stage_kernel,
        out_shape=(
            jax.ShapeDtypeStruct(gate_up.shape[1:], BF16),
            jax.ShapeDtypeStruct(down.shape[1:], BF16),
        ),
        in_specs=[HBM, HBM],
        out_specs=(VMEM, VMEM),
        scratch_shapes=[pltpu.SemaphoreType.DMA((12,))],
        compiler_params=pltpu.CompilerParams(vmem_limit_bytes=16 * MIB),
        cost_estimate=pl.CostEstimate(flops=0, bytes_accessed=22_000_000, transcendentals=0),
        name="stage",
    )(*in_hbm(gate_up, down))


def mix_kernel(steps, chips, own_ref, other_ref, mix_ref):
    mix_ref[...] = mixing(steps, chips, own_ref, other_ref)


def mixer(steps, chips, own, other):
    lines = PIECES * 2 * steps * CAP
    shape = (PARTS * PIECES * 2 * own.shape[0], chips // 2 * lines)
    return pl.pallas_call(
        functools.partial(mix_kernel, steps, chips),
        out_shape=jax.ShapeDtypeStruct(shape, BF16),
        in_specs=[VMEM, VMEM],
        out_specs=VMEM,
        compiler_params=pltpu.CompilerParams(vmem_limit_bytes=24 * MIB),
        cost_estimate=pl.CostEstimate(
            flops=10_000_000, bytes_accessed=1_000_000, transcendentals=0
        ),
        name="mixer",
    )(own, other)


def expert_kernel(turns, *refs):
    own_refs, other_refs = refs[:turns], refs[turns : 2 * turns]
    w_in, w_down = refs[2 * turns : 2 * turns + 2]
    mine_refs = refs[2 * turns + 2 : 3 * turns + 2]
    theirs_refs = refs[3 * turns + 2 :]
    lines, piece = own_refs[0].shape
    per = lines // PIECES
    half = turns * per
    arrays = [ref[...].astype(F32) for ref in own_refs + other_refs]
    gate = upper = None
    for k in range(PIECES):
        x = [array[k * per : (k + 1) * per] for array in arrays]
        x = jnp.concatenate(x, axis=0).astype(BF16)
        cols = pl.ds(k * piece, piece)
        g, u = nt_dot(w_in[0, :, cols], x), nt_dot(w_in[1, :, cols], x)
        gate, upper = (g, u) if k == 0 else (gate + g, upper + u)
    act = (gate / (1.0 + jnp.exp(-gate)) * upper).T.astype(BF16)
    parts = [dot(act, w_down[:, k * piece : (k + 1) * piece]) for k in range(PIECES)]
    for first, now in ((half, theirs_refs), (0, mine_refs)):
        for t, ref in enumerate(now):
            start = first + t * per
            out = [part[start : start + per] for part in parts]
            ref[...] = jnp.concatenate(out, axis=0).astype(BF16)


def experts(own, other, gate_up, down):
    turns = len(own)
    shape = jax.ShapeDtypeStruct(own[0].shape, BF16)
    results = pl.pallas_call(
        functools.partial(expert_kernel, turns),
        out_shape=[shape] * (2 * turns),
        in_specs=[VMEM] * (2 * turns + 2),
        out_specs=[VMEM] * (2 * turns),
        compiler_params=pltpu.CompilerParams(vmem_limit_bytes=32 * MIB),
        cost_estimate=pl.CostEstimate(
            flops=800_000_000, bytes_accessed=12_000_000, transcendentals=16384
        ),
        name="experts",
    )(*own, *other, gate_up, down)
    return results[:turns], results[turns:]


def combine_kernel(mix_ref, resid_ref, *refs):
    back_refs, (kept_ref, sent_ref) = refs[:-2], refs[-2:]
    both = resid_ref.shape[0]
    piece = back_refs[0].shape[1]
    product = dot(mix_ref[...], jnp.concatenate([ref[...] for ref in back_refs], axis=0))
    n = PIECES * 2 * both
    total = product[:n] + product[n : 2 * n] + product[2 * n :]
    for k in range(PIECES):
        cols = pl.ds(k * piece, piece)
        first = k * 2 * both
        kept_ref[:, cols] = resid_ref[:, cols] + total[first : first + both]
        sent_ref[:, cols] = total[first + both : first + 2 * both].astype(BF16)


def combine(mix, resid, backs):
    return pl.pallas_call(
        combine_kernel,
        out_shape=(
            jax.ShapeDtypeStruct(resid.shape, F32),
            jax.ShapeDtypeStruct(resid.shape, BF16),
        ),
        in_specs=[VMEM] * (2 + len(backs)),
        out_specs=(VMEM, VMEM),
        compiler_params=pltpu.CompilerParams(vmem_limit_bytes=24 * MIB),
        cost_estimate=pl.CostEstimate(
            flops=100_000_000, bytes_accessed=1_000_000, transcendentals=0
        ),
        name="combine",
    )(mix, resid, *backs)


def finish_kernel(kept_ref, other_ref, out_ref):
    steps, rows, _ = out_ref.shape
    done = (kept_ref[...] + other_ref[...].astype(F32)).astype(BF16)
    for s in range(steps):
        out_ref[s] = done[s * rows : (s + 1) * rows]


def finish(shape, kept, other):
    return pl.pallas_call(
        finish_kernel,
        out_shape=jax.ShapeDtypeStruct(shape, BF16),
        in_specs=[VMEM, VMEM],
        out_specs=VMEM,
        compiler_params=pltpu.CompilerParams(vmem_limit_bytes=24 * MIB),
        cost_estimate=pl.CostEstimate(flops=100_000, bytes_accessed=500_000, transcendentals=0),
        name="finish",
    )(kept, other)


def per_device(
    queries,
    fresh,
    kv_cache,
    cache_len,
    hidden_state,
    norm_gain,
    expert_ids,
    route_weight,
    gate_up,
    down,
):
    steps = queries.shape[0]
    owners = lax.axis_size("afd")
    chips = owners // 2
    turns = chips // 2
    cores = [(i, i ^ 1) for i in range(owners)]

    def swap(x):
        return lax.ppermute(x, "afd", cores)

    def route(t):
        return [(i, (i // 2 ^ distance(t, i % 2, chips)) * 2 + 1 - i % 2) for i in range(owners)]

    def send(x, t):
        return lax.ppermute(x, "afd", route(t))

    def send_back(x, t):
        return lax.ppermute(x, "afd", [(j, i) for i, j in route(t)])

    ids = expert_ids.transpose(2, 0, 1)
    weights = route_weight.transpose(2, 0, 1)
    resid, normed = attend(
        cache_len, ids, weights, queries, fresh, kv_cache, hidden_state, norm_gain
    )
    normed_other = swap(normed)
    sent = pack(steps, chips, normed, normed_other)
    w_in, w_down = stage(gate_up, down)
    last, w_in = lax.optimization_barrier((sent[-1], w_in))
    own = [send(x, t) for t, x in enumerate([*sent[:-1], last])]
    mix = mixer(steps, chips, normed, normed_other)
    other = [swap(x) for x in own]
    summed = []
    for t in range(0, turns, TOGETHER):
        now = slice(t, t + TOGETHER)
        mine, theirs = experts(own[now], other[now], w_in, w_down)
        summed += [
            (a.astype(F32) + swap(b).astype(F32)).astype(BF16) for a, b in zip(mine, theirs)
        ]
    backs = [send_back(summed[t], t) for t in range(turns)]
    kept, given = combine(mix, resid, backs)
    return finish(queries.shape, kept, swap(given))


def solution(mesh):
    placed = (
        P(None, ("group", "afd"), None),
        P(None, ("group", "afd"), None),
        P(("group", "afd"), None, None),
        P(("group", "afd")),
        P(None, ("group", "afd"), None),
        P(),
        P(None, ("group", "afd"), None),
        P(None, ("group", "afd"), None),
        P("afd", None, None, None),
        P("afd", None, None),
    )
    return jax.shard_map(
        per_device,
        mesh=mesh,
        in_specs=placed,
        out_specs=P(None, ("group", "afd"), None),
        check_vma=False,
    )
```

```python
import functools
import jax
import jax.numpy as jnp
from jax import lax
from jax.experimental import pallas as pl
from jax.experimental.pallas import tpu as pltpu
from jax.sharding import PartitionSpec as P

HEADS = 32
HEAD = 224
EXPERTS = 8
TOP = 3
CAP = 2
PIECES = 4
LANES = 128
PARTS = 3
F32 = jnp.float32
BF16 = jnp.bfloat16
MIB = 1 << 20
VMEM = pl.BlockSpec(memory_space=pltpu.VMEM)
HBM = pl.BlockSpec(memory_space=pltpu.HBM)
TOGETHER = 4


def iota(shape, dim):
    return lax.broadcasted_iota(jnp.int32, shape, dim)


def in_hbm(*arrays):
    return [pltpu.with_memory_space_constraint(x, pltpu.HBM) for x in arrays]


def nt_dot(a, b):
    return lax.dot_general(a, b, (((1,), (1,)), ((), ())), preferred_element_type=F32)


def dot(a, b):
    return jnp.dot(a, b, preferred_element_type=F32)


def one_hot(mask):
    return jnp.where(mask, 1.0, 0.0).astype(BF16)


def distance(turn, core, chips):
    bits = (chips // 2).bit_length() - 1
    even = 0
    for b in range(bits):
        even = even + ((turn >> b) % 2 << (bits - b))
    return even ^ (core * (chips - 1))


def expert_at(turn, chips):
    place = lax.axis_index("afd")
    return (distance(turn, place % 2, chips) ^ (place // 2)) // (chips // EXPERTS)


def spread(ref, k, where, steps, rows, empty):
    out = jnp.full(where.shape, empty)
    for s in range(steps):
        for r in range(rows):
            out = jnp.where(where == s * rows + r, ref[k, s, r], out)
    return out


def tail(ids_ref, weight_ref, steps, rows):
    both = steps * rows
    lane = iota((both, LANES), 1)
    where = iota((both, 1), 0)
    mix = jnp.zeros((both, LANES), F32)
    named = jnp.zeros((both, LANES), F32)
    for k in range(TOP):
        hit = spread(ids_ref, k, where, steps, rows, -1) == lane % EXPERTS
        mix = mix + jnp.where(hit, spread(weight_ref, k, where, steps, rows, 0.0), 0.0)
        named = named + jnp.where(hit, 1.0, 0.0)
    out = jnp.where(lane // EXPERTS == PARTS, named, 0.0)
    for part in range(PARTS):
        term = mix.astype(BF16).astype(F32)
        out = jnp.where(lane // EXPERTS == part, term, out)
        mix = mix - term
    return out.astype(BF16)


def attend_kernel(
    len_hbm,
    ids_hbm,
    weight_hbm,
    q_hbm,
    fresh_hbm,
    kv_hbm,
    hid_hbm,
    gain_hbm,
    resid_ref,
    out_ref,
    len_ref,
    ids_ref,
    weight_ref,
    q_ref,
    fresh_ref,
    kv_ref,
    hid_ref,
    gain_ref,
    merged,
    sems,
):
    pairs = (
        (q_hbm, q_ref),
        (kv_hbm, kv_ref),
        (fresh_hbm, fresh_ref),
        (len_hbm, len_ref),
        (hid_hbm, hid_ref),
        (gain_hbm, gain_ref),
        (ids_hbm, ids_ref),
        (weight_hbm, weight_ref),
    )
    copies = [pltpu.make_async_copy(a, b, sems.at[i]) for i, (a, b) in enumerate(pairs)]
    for copy in copies:
        copy.start()
    steps, rows, width = q_ref.shape
    length = kv_ref.shape[2]
    both = steps * rows
    scale = HEAD ** (-0.5)
    copies[0].wait()
    q = jnp.concatenate([q_ref[s].astype(F32) for s in range(steps)], axis=0)
    heads = jnp.concatenate([q[:, h * HEAD : (h + 1) * HEAD] for h in range(HEADS)], axis=0)
    heads = heads.astype(BF16)
    for copy in copies[1:]:
        copy.wait()
    kv = jnp.concatenate([kv_ref[r] for r in range(rows)], axis=1)
    new = jnp.concatenate([fresh_ref[s].astype(F32) for s in range(steps)], axis=0).astype(BF16)

    sub = iota((both, rows * length), 0)
    lane = iota((both, rows * length), 1)
    limit = jnp.zeros_like(lane)
    for r in range(rows):
        limit = jnp.where(lane // length == r, len_ref[r], limit)
    valid = (lane // length == sub % rows) & (lane % length < limit)
    sub = iota((both, both), 0)
    lane = iota((both, both), 1)
    valid_new = (lane % rows == sub % rows) & (lane // rows <= sub // rows)

    old_s = (dot(heads, kv[:HEAD]) * scale).reshape(HEADS, both, rows * length)
    new_s = (nt_dot(heads, new[:, :HEAD]) * scale).reshape(HEADS, both, both)
    old_s = jnp.where(valid[None], old_s, -1e30)
    new_s = jnp.where(valid_new[None], new_s, -1e30)
    top = jnp.maximum(
        jnp.max(old_s, axis=-1, keepdims=True), jnp.max(new_s, axis=-1, keepdims=True)
    )
    old_e = jnp.exp(old_s - top)
    new_e = jnp.exp(new_s - top)
    total = jnp.sum(old_e, axis=-1, keepdims=True) + jnp.sum(new_e, axis=-1, keepdims=True)
    share = 1.0 / total
    old_w = (old_e * share).reshape(HEADS * both, rows * length).astype(BF16)
    new_w = (new_e * share).reshape(HEADS * both, both).astype(BF16)
    attended = nt_dot(old_w, kv[HEAD:]) + dot(new_w, new[:, HEAD:])
    for h in range(HEADS):
        merged[:, h * HEAD : (h + 1) * HEAD] = attended[h * both : (h + 1) * both]
    hidden = jnp.concatenate([hid_ref[s].astype(F32) for s in range(steps)], axis=0)
    resid = hidden + merged[...]
    resid_ref[...] = resid
    meansq = jnp.mean(resid * resid, axis=-1, keepdims=True)
    gain = gain_ref[...].astype(F32)
    gain = jnp.concatenate([gain[i : i + 1] for i in range(width // LANES)], axis=1)
    normed = resid * lax.rsqrt(meansq + 1e-06) * gain
    out_ref[:, :width] = normed.astype(BF16)
    out_ref[:, width:] = tail(ids_ref, weight_ref, steps, rows)


def attend(cache_len, ids, weights, queries, fresh, kv_cache, hidden_state, norm_gain):
    steps, rows, width = queries.shape
    kv = kv_cache.transpose(0, 2, 1)
    gain = norm_gain.reshape(width // LANES, LANES)
    return pl.pallas_call(
        attend_kernel,
        out_shape=(
            jax.ShapeDtypeStruct((steps * rows, width), F32),
            jax.ShapeDtypeStruct((steps * rows, width + LANES), BF16),
        ),
        in_specs=[HBM] * 8,
        out_specs=(VMEM, VMEM),
        scratch_shapes=[
            pltpu.SMEM(cache_len.shape, jnp.int32),
            pltpu.SMEM(ids.shape, jnp.int32),
            pltpu.SMEM(weights.shape, F32),
            pltpu.VMEM(queries.shape, BF16),
            pltpu.VMEM(fresh.shape, BF16),
            pltpu.VMEM(kv.shape, BF16),
            pltpu.VMEM(hidden_state.shape, BF16),
            pltpu.VMEM(gain.shape, BF16),
            pltpu.VMEM((steps * rows, width), F32),
            pltpu.SemaphoreType.DMA((8,)),
        ],
        compiler_params=pltpu.CompilerParams(vmem_limit_bytes=24 * MIB),
        cost_estimate=pl.CostEstimate(
            flops=300_000_000, bytes_accessed=2_000_000, transcendentals=131072
        ),
        name="attend",
    )(*in_hbm(cache_len, ids, weights, queries, fresh, kv, hidden_state, gain))


def pack_kernel(steps, chips, own_ref, other_ref, *outs):
    both, width = own_ref.shape
    width -= LANES
    rows = both // steps
    piece = width // PIECES
    side_lines = steps * CAP
    lines = PIECES * 2 * side_lines
    tails = [ref[:, width:].astype(F32) for ref in (own_ref, other_ref)]
    tails = jnp.concatenate(tails * PIECES, axis=0).astype(BF16)
    count = 2 * both * PIECES
    row = iota((len(outs) * lines, LANES), 0)
    lane = iota((len(outs) * lines, LANES), 1)
    wanted = one_hot(lane == PARTS * EXPERTS + expert_at(row // lines, chips))
    named = nt_dot(wanted, tails)
    at = iota((count, count), 0)
    to = iota((count, count), 1)
    before = one_hot((at // rows == to // rows) & (at < to))
    rank = dot(named.astype(BF16), before)
    line = iota(named.shape, 0)
    col = iota(named.shape, 1)
    same = (line // CAP) % (lines // CAP) == col // rows
    picks = one_hot(same & (named > 0.5) & (rank == (line % CAP).astype(F32)))
    parts = [ref[:, :width].astype(F32) for ref in (own_ref, other_ref)]
    stacked = jnp.concatenate(
        [part[:, k * piece : (k + 1) * piece] for k in range(PIECES) for part in parts], axis=0
    ).astype(BF16)
    sent = dot(picks, stacked).astype(BF16)
    for t, out in enumerate(outs):
        out[...] = sent[t * lines : (t + 1) * lines]


def pack(steps, chips, own, other):
    both, width = own.shape
    shape = (PIECES * 2 * steps * CAP, (width - LANES) // PIECES)
    turns = chips // 2
    return pl.pallas_call(
        functools.partial(pack_kernel, steps, chips),
        out_shape=[jax.ShapeDtypeStruct(shape, BF16)] * turns,
        in_specs=[VMEM] * 2,
        out_specs=[VMEM] * turns,
        compiler_params=pltpu.CompilerParams(vmem_limit_bytes=24 * MIB),
        cost_estimate=pl.CostEstimate(
            flops=50_000_000, bytes_accessed=2_000_000, transcendentals=0
        ),
        name="pack",
    )(own, other)


def mixing(steps, chips, own_ref, other_ref):
    both, width = own_ref.shape
    width -= LANES
    rows = both // steps
    lines = PIECES * 2 * steps * CAP
    tails = [ref[:, width:].astype(F32) for ref in (own_ref, other_ref)]
    tails = jnp.concatenate(tails, axis=0).astype(BF16)
    count = chips // 2 * lines
    lane = iota((LANES, count), 0)
    expert = expert_at(iota((LANES, count), 1) // lines, chips)
    found = [dot(tails, one_hot(lane == part * EXPERTS + expert)) for part in range(PARTS + 1)]
    at = iota((2 * both, 2 * both), 1)
    to = iota((2 * both, 2 * both), 0)
    rank = dot(one_hot((at // rows == to // rows) & (at < to)), found[PARTS].astype(BF16))
    line = iota((2 * both, count), 1)
    row = iota((2 * both, count), 0)
    same = (line // CAP) % (2 * steps) == row // rows
    slot = same & (rank == (line % CAP).astype(F32))
    k_of = line // (2 * steps * CAP) % PIECES
    parts = [
        jnp.where(slot & (k_of == k), found[part], 0.0)
        for part in range(PARTS)
        for k in range(PIECES)
    ]
    return jnp.concatenate(parts, axis=0).astype(BF16)


def stage_kernel(gu_hbm, dn_hbm, gu, dn, sems):
    step = dn.shape[0] // 4
    pairs = []
    for i in range(4):
        part = pl.ds(i * step, step)
        pairs.append((gu_hbm.at[0, 0, part], gu.at[0, part]))
        pairs.append((gu_hbm.at[0, 1, part], gu.at[1, part]))
        pairs.append((dn_hbm.at[0, part], dn.at[part]))
    copies = [pltpu.make_async_copy(a, b, sems.at[i]) for i, (a, b) in enumerate(pairs)]
    for copy in copies:
        copy.start()
    for copy in copies:
        copy.wait()


def stage(gate_up, down):
    return pl.pallas_call(
        stage_kernel,
        out_shape=(
            jax.ShapeDtypeStruct(gate_up.shape[1:], BF16),
            jax.ShapeDtypeStruct(down.shape[1:], BF16),
        ),
        in_specs=[HBM, HBM],
        out_specs=(VMEM, VMEM),
        scratch_shapes=[pltpu.SemaphoreType.DMA((12,))],
        compiler_params=pltpu.CompilerParams(vmem_limit_bytes=16 * MIB),
        cost_estimate=pl.CostEstimate(flops=0, bytes_accessed=22_000_000, transcendentals=0),
        name="stage",
    )(*in_hbm(gate_up, down))


def mix_kernel(steps, chips, own_ref, other_ref, mix_ref):
    mix_ref[...] = mixing(steps, chips, own_ref, other_ref)


def mixer(steps, chips, own, other):
    lines = PIECES * 2 * steps * CAP
    shape = (PARTS * PIECES * 2 * own.shape[0], chips // 2 * lines)
    return pl.pallas_call(
        functools.partial(mix_kernel, steps, chips),
        out_shape=jax.ShapeDtypeStruct(shape, BF16),
        in_specs=[VMEM, VMEM],
        out_specs=VMEM,
        compiler_params=pltpu.CompilerParams(vmem_limit_bytes=24 * MIB),
        cost_estimate=pl.CostEstimate(
            flops=10_000_000, bytes_accessed=1_000_000, transcendentals=0
        ),
        name="mixer",
    )(own, other)


def expert_kernel(turns, *refs):
    own_refs, other_refs = refs[:turns], refs[turns : 2 * turns]
    w_in, w_down = refs[2 * turns : 2 * turns + 2]
    mine_refs = refs[2 * turns + 2 : 3 * turns + 2]
    theirs_refs = refs[3 * turns + 2 :]
    lines, piece = own_refs[0].shape
    per = lines // PIECES
    half = turns * per
    arrays = [ref[...].astype(F32) for ref in own_refs + other_refs]
    x = []
    for k in range(PIECES):
        rows = [array[k * per : (k + 1) * per] for array in arrays]
        x.append(jnp.concatenate(rows, axis=0).astype(BF16))
    _, hidden, width = w_in.shape
    both = nt_dot(w_in[...].reshape(2 * hidden, width), jnp.concatenate(x, axis=1))
    gate, upper = both[:hidden], both[hidden:]
    act = (gate / (1.0 + jnp.exp(-gate)) * upper).T.astype(BF16)
    parts = [dot(act, w_down[:, k * piece : (k + 1) * piece]) for k in range(PIECES)]
    for first, now in ((half, theirs_refs), (0, mine_refs)):
        for t, ref in enumerate(now):
            start = first + t * per
            out = [part[start : start + per] for part in parts]
            ref[...] = jnp.concatenate(out, axis=0).astype(BF16)


def experts(own, other, gate_up, down):
    turns = len(own)
    shape = jax.ShapeDtypeStruct(own[0].shape, BF16)
    results = pl.pallas_call(
        functools.partial(expert_kernel, turns),
        out_shape=[shape] * (2 * turns),
        in_specs=[VMEM] * (2 * turns + 2),
        out_specs=[VMEM] * (2 * turns),
        compiler_params=pltpu.CompilerParams(vmem_limit_bytes=32 * MIB),
        cost_estimate=pl.CostEstimate(
            flops=800_000_000, bytes_accessed=12_000_000, transcendentals=16384
        ),
        name="experts",
    )(*own, *other, gate_up, down)
    return results[:turns], results[turns:]


def combine_kernel(mix_ref, resid_ref, *refs):
    back_refs, (kept_ref, sent_ref) = refs[:-2], refs[-2:]
    both = resid_ref.shape[0]
    piece = back_refs[0].shape[1]
    product = dot(mix_ref[...], jnp.concatenate([ref[...] for ref in back_refs], axis=0))
    n = PIECES * 2 * both
    total = product[:n] + product[n : 2 * n] + product[2 * n :]
    for k in range(PIECES):
        cols = pl.ds(k * piece, piece)
        first = k * 2 * both
        kept_ref[:, cols] = resid_ref[:, cols] + total[first : first + both]
        sent_ref[:, cols] = total[first + both : first + 2 * both].astype(BF16)


def combine(mix, resid, backs):
    return pl.pallas_call(
        combine_kernel,
        out_shape=(
            jax.ShapeDtypeStruct(resid.shape, F32),
            jax.ShapeDtypeStruct(resid.shape, BF16),
        ),
        in_specs=[VMEM] * (2 + len(backs)),
        out_specs=(VMEM, VMEM),
        compiler_params=pltpu.CompilerParams(vmem_limit_bytes=24 * MIB),
        cost_estimate=pl.CostEstimate(
            flops=100_000_000, bytes_accessed=1_000_000, transcendentals=0
        ),
        name="combine",
    )(mix, resid, *backs)


def finish_kernel(kept_ref, other_ref, out_ref):
    steps, rows, _ = out_ref.shape
    done = (kept_ref[...] + other_ref[...].astype(F32)).astype(BF16)
    for s in range(steps):
        out_ref[s] = done[s * rows : (s + 1) * rows]


def finish(shape, kept, other):
    return pl.pallas_call(
        finish_kernel,
        out_shape=jax.ShapeDtypeStruct(shape, BF16),
        in_specs=[VMEM, VMEM],
        out_specs=VMEM,
        compiler_params=pltpu.CompilerParams(vmem_limit_bytes=24 * MIB),
        cost_estimate=pl.CostEstimate(flops=100_000, bytes_accessed=500_000, transcendentals=0),
        name="finish",
    )(kept, other)


def per_device(
    queries,
    fresh,
    kv_cache,
    cache_len,
    hidden_state,
    norm_gain,
    expert_ids,
    route_weight,
    gate_up,
    down,
):
    steps = queries.shape[0]
    owners = lax.axis_size("afd")
    chips = owners // 2
    turns = chips // 2
    cores = [(i, i ^ 1) for i in range(owners)]

    def swap(x):
        return lax.ppermute(x, "afd", cores)

    def route(t):
        return [(i, (i // 2 ^ distance(t, i % 2, chips)) * 2 + 1 - i % 2) for i in range(owners)]

    def send(x, t):
        return lax.ppermute(x, "afd", route(t))

    def send_back(x, t):
        return lax.ppermute(x, "afd", [(j, i) for i, j in route(t)])

    ids = expert_ids.transpose(2, 0, 1)
    weights = route_weight.transpose(2, 0, 1)
    resid, normed = attend(
        cache_len, ids, weights, queries, fresh, kv_cache, hidden_state, norm_gain
    )
    normed_other = swap(normed)
    sent = pack(steps, chips, normed, normed_other)
    own = [send(sent[t], t) for t in range(turns)]
    w_in, w_down = stage(gate_up, down)
    mix = mixer(steps, chips, normed, normed_other)
    own[0], w_in = lax.optimization_barrier((own[0], w_in))
    other = [swap(x) for x in own]
    summed = []
    for t in range(0, turns, TOGETHER):
        now = slice(t, t + TOGETHER)
        mine, theirs = experts(own[now], other[now], w_in, w_down)
        summed += [
            (a.astype(F32) + swap(b).astype(F32)).astype(BF16) for a, b in zip(mine, theirs)
        ]
    backs = [send_back(summed[t], t) for t in range(turns)]
    kept, given = combine(mix, resid, backs)
    return finish(queries.shape, kept, swap(given))


def solution(mesh):
    placed = (
        P(None, ("group", "afd"), None),
        P(None, ("group", "afd"), None),
        P(("group", "afd"), None, None),
        P(("group", "afd")),
        P(None, ("group", "afd"), None),
        P(),
        P(None, ("group", "afd"), None),
        P(None, ("group", "afd"), None),
        P("afd", None, None, None),
        P("afd", None, None),
    )
    return jax.shard_map(
        per_device,
        mesh=mesh,
        in_specs=placed,
        out_specs=P(None, ("group", "afd"), None),
        check_vma=False,
    )
```

```python
import functools
import jax
import jax.numpy as jnp
from jax import lax
from jax.experimental import pallas as pl
from jax.experimental.pallas import tpu as pltpu
from jax.sharding import PartitionSpec as P

HEADS = 32
HEAD = 224
EXPERTS = 8
TOP = 3
CAP = 2
PIECES = 4
LANES = 128
PARTS = 3
F32 = jnp.float32
BF16 = jnp.bfloat16
MIB = 1 << 20
VMEM = pl.BlockSpec(memory_space=pltpu.VMEM)
HBM = pl.BlockSpec(memory_space=pltpu.HBM)
TOGETHER = 4


def iota(shape, dim):
    return lax.broadcasted_iota(jnp.int32, shape, dim)


def in_hbm(*arrays):
    return [pltpu.with_memory_space_constraint(x, pltpu.HBM) for x in arrays]


def nt_dot(a, b):
    return lax.dot_general(a, b, (((1,), (1,)), ((), ())), preferred_element_type=F32)


def dot(a, b):
    return jnp.dot(a, b, preferred_element_type=F32)


def one_hot(mask):
    return jnp.where(mask, 1.0, 0.0).astype(BF16)


def distance(turn, core, chips):
    bits = (chips // 2).bit_length() - 1
    even = 0
    for b in range(bits):
        even = even + ((turn >> b) % 2 << (bits - b))
    return even ^ (core * (chips - 1))


def expert_at(turn, chips):
    place = lax.axis_index("afd")
    return (distance(turn, place % 2, chips) ^ (place // 2)) // (chips // EXPERTS)


def spread(ref, k, where, steps, rows, empty):
    out = jnp.full(where.shape, empty)
    for s in range(steps):
        for r in range(rows):
            out = jnp.where(where == s * rows + r, ref[k, s, r], out)
    return out


def tail(ids_ref, weight_ref, steps, rows):
    both = steps * rows
    lane = iota((both, LANES), 1)
    where = iota((both, 1), 0)
    mix = jnp.zeros((both, LANES), F32)
    named = jnp.zeros((both, LANES), F32)
    for k in range(TOP):
        hit = spread(ids_ref, k, where, steps, rows, -1) == lane % EXPERTS
        mix = mix + jnp.where(hit, spread(weight_ref, k, where, steps, rows, 0.0), 0.0)
        named = named + jnp.where(hit, 1.0, 0.0)
    out = jnp.where(lane // EXPERTS == PARTS, named, 0.0)
    for part in range(PARTS):
        term = mix.astype(BF16).astype(F32)
        out = jnp.where(lane // EXPERTS == part, term, out)
        mix = mix - term
    return out.astype(BF16)


def attend_kernel(
    len_hbm,
    ids_hbm,
    weight_hbm,
    q_hbm,
    fresh_hbm,
    kv_hbm,
    hid_hbm,
    gain_hbm,
    resid_ref,
    out_ref,
    len_ref,
    ids_ref,
    weight_ref,
    q_ref,
    fresh_ref,
    kv_ref,
    hid_ref,
    gain_ref,
    merged,
    sems,
):
    pairs = (
        (q_hbm, q_ref),
        (kv_hbm, kv_ref),
        (fresh_hbm, fresh_ref),
        (len_hbm, len_ref),
        (hid_hbm, hid_ref),
        (gain_hbm, gain_ref),
        (ids_hbm, ids_ref),
        (weight_hbm, weight_ref),
    )
    copies = [pltpu.make_async_copy(a, b, sems.at[i]) for i, (a, b) in enumerate(pairs)]
    for copy in copies:
        copy.start()
    steps, rows, width = q_ref.shape
    length = kv_ref.shape[2]
    both = steps * rows
    scale = HEAD ** (-0.5)
    copies[0].wait()
    q = jnp.concatenate([q_ref[s].astype(F32) for s in range(steps)], axis=0)
    heads = jnp.concatenate([q[:, h * HEAD : (h + 1) * HEAD] for h in range(HEADS)], axis=0)
    heads = heads.astype(BF16)
    for copy in copies[1:4]:
        copy.wait()
    kv = jnp.concatenate([kv_ref[r] for r in range(rows)], axis=1)
    new = jnp.concatenate([fresh_ref[s].astype(F32) for s in range(steps)], axis=0).astype(BF16)

    sub = iota((both, rows * length), 0)
    lane = iota((both, rows * length), 1)
    limit = jnp.zeros_like(lane)
    for r in range(rows):
        limit = jnp.where(lane // length == r, len_ref[r], limit)
    valid = (lane // length == sub % rows) & (lane % length < limit)
    sub = iota((both, both), 0)
    lane = iota((both, both), 1)
    valid_new = (lane % rows == sub % rows) & (lane // rows <= sub // rows)

    old_s = (dot(heads, kv[:HEAD]) * scale).reshape(HEADS, both, rows * length)
    new_s = (nt_dot(heads, new[:, :HEAD]) * scale).reshape(HEADS, both, both)
    old_s = jnp.where(valid[None], old_s, -1e30)
    new_s = jnp.where(valid_new[None], new_s, -1e30)
    top = jnp.maximum(
        jnp.max(old_s, axis=-1, keepdims=True), jnp.max(new_s, axis=-1, keepdims=True)
    )
    old_e = jnp.exp(old_s - top)
    new_e = jnp.exp(new_s - top)
    total = jnp.sum(old_e, axis=-1, keepdims=True) + jnp.sum(new_e, axis=-1, keepdims=True)
    share = 1.0 / total
    old_w = (old_e * share).reshape(HEADS * both, rows * length).astype(BF16)
    new_w = (new_e * share).reshape(HEADS * both, both).astype(BF16)
    attended = nt_dot(old_w, kv[HEAD:]) + dot(new_w, new[:, HEAD:])
    for h in range(HEADS):
        merged[:, h * HEAD : (h + 1) * HEAD] = attended[h * both : (h + 1) * both]
    for copy in copies[4:8]:
        copy.wait()
    hidden = jnp.concatenate([hid_ref[s].astype(F32) for s in range(steps)], axis=0)
    resid = hidden + merged[...]
    resid_ref[...] = resid
    meansq = jnp.mean(resid * resid, axis=-1, keepdims=True)
    gain = gain_ref[...].astype(F32)
    gain = jnp.concatenate([gain[i : i + 1] for i in range(width // LANES)], axis=1)
    normed = resid * lax.rsqrt(meansq + 1e-06) * gain
    out_ref[:, :width] = normed.astype(BF16)
    out_ref[:, width:] = tail(ids_ref, weight_ref, steps, rows)


def attend(cache_len, ids, weights, queries, fresh, kv_cache, hidden_state, norm_gain):
    steps, rows, width = queries.shape
    kv = kv_cache.transpose(0, 2, 1)
    gain = norm_gain.reshape(width // LANES, LANES)
    return pl.pallas_call(
        attend_kernel,
        out_shape=(
            jax.ShapeDtypeStruct((steps * rows, width), F32),
            jax.ShapeDtypeStruct((steps * rows, width + LANES), BF16),
        ),
        in_specs=[HBM] * 8,
        out_specs=(VMEM, VMEM),
        scratch_shapes=[
            pltpu.SMEM(cache_len.shape, jnp.int32),
            pltpu.SMEM(ids.shape, jnp.int32),
            pltpu.SMEM(weights.shape, F32),
            pltpu.VMEM(queries.shape, BF16),
            pltpu.VMEM(fresh.shape, BF16),
            pltpu.VMEM(kv.shape, BF16),
            pltpu.VMEM(hidden_state.shape, BF16),
            pltpu.VMEM(gain.shape, BF16),
            pltpu.VMEM((steps * rows, width), F32),
            pltpu.SemaphoreType.DMA((8,)),
        ],
        compiler_params=pltpu.CompilerParams(vmem_limit_bytes=24 * MIB),
        cost_estimate=pl.CostEstimate(
            flops=300_000_000, bytes_accessed=2_000_000, transcendentals=131072
        ),
        name="attend",
    )(*in_hbm(cache_len, ids, weights, queries, fresh, kv, hidden_state, gain))


def pack_kernel(steps, chips, own_ref, other_ref, *outs):
    both, width = own_ref.shape
    width -= LANES
    rows = both // steps
    piece = width // PIECES
    side_lines = steps * CAP
    lines = PIECES * 2 * side_lines
    tails = [ref[:, width:].astype(F32) for ref in (own_ref, other_ref)]
    tails = jnp.concatenate(tails * PIECES, axis=0).astype(BF16)
    count = 2 * both * PIECES
    row = iota((len(outs) * lines, LANES), 0)
    lane = iota((len(outs) * lines, LANES), 1)
    wanted = one_hot(lane == PARTS * EXPERTS + expert_at(row // lines, chips))
    named = nt_dot(wanted, tails)
    at = iota((count, count), 0)
    to = iota((count, count), 1)
    before = one_hot((at // rows == to // rows) & (at < to))
    rank = dot(named.astype(BF16), before)
    line = iota(named.shape, 0)
    col = iota(named.shape, 1)
    same = (line // CAP) % (lines // CAP) == col // rows
    picks = one_hot(same & (named > 0.5) & (rank == (line % CAP).astype(F32)))
    parts = [ref[:, :width].astype(F32) for ref in (own_ref, other_ref)]
    stacked = jnp.concatenate(
        [part[:, k * piece : (k + 1) * piece] for k in range(PIECES) for part in parts], axis=0
    ).astype(BF16)
    sent = dot(picks, stacked).astype(BF16)
    for t, out in enumerate(outs):
        out[...] = sent[t * lines : (t + 1) * lines]


def pack(steps, chips, own, other):
    both, width = own.shape
    shape = (PIECES * 2 * steps * CAP, (width - LANES) // PIECES)
    turns = chips // 2
    return pl.pallas_call(
        functools.partial(pack_kernel, steps, chips),
        out_shape=[jax.ShapeDtypeStruct(shape, BF16)] * turns,
        in_specs=[VMEM] * 2,
        out_specs=[VMEM] * turns,
        compiler_params=pltpu.CompilerParams(vmem_limit_bytes=24 * MIB),
        cost_estimate=pl.CostEstimate(
            flops=50_000_000, bytes_accessed=2_000_000, transcendentals=0
        ),
        name="pack",
    )(own, other)


def mixing(steps, chips, own_ref, other_ref):
    both, width = own_ref.shape
    width -= LANES
    rows = both // steps
    lines = PIECES * 2 * steps * CAP
    tails = [ref[:, width:].astype(F32) for ref in (own_ref, other_ref)]
    tails = jnp.concatenate(tails, axis=0).astype(BF16)
    count = chips // 2 * lines
    lane = iota((LANES, count), 0)
    expert = expert_at(iota((LANES, count), 1) // lines, chips)
    found = [dot(tails, one_hot(lane == part * EXPERTS + expert)) for part in range(PARTS + 1)]
    at = iota((2 * both, 2 * both), 1)
    to = iota((2 * both, 2 * both), 0)
    rank = dot(one_hot((at // rows == to // rows) & (at < to)), found[PARTS].astype(BF16))
    line = iota((2 * both, count), 1)
    row = iota((2 * both, count), 0)
    same = (line // CAP) % (2 * steps) == row // rows
    slot = same & (rank == (line % CAP).astype(F32))
    k_of = line // (2 * steps * CAP) % PIECES
    parts = [
        jnp.where(slot & (k_of == k), found[part], 0.0)
        for part in range(PARTS)
        for k in range(PIECES)
    ]
    return jnp.concatenate(parts, axis=0).astype(BF16)


def stage_kernel(gu_hbm, dn_hbm, gu, dn, sems):
    step = dn.shape[0] // 4
    pairs = []
    for i in range(4):
        part = pl.ds(i * step, step)
        pairs.append((gu_hbm.at[0, 0, part], gu.at[0, part]))
        pairs.append((gu_hbm.at[0, 1, part], gu.at[1, part]))
        pairs.append((dn_hbm.at[0, part], dn.at[part]))
    copies = [pltpu.make_async_copy(a, b, sems.at[i]) for i, (a, b) in enumerate(pairs)]
    for copy in copies:
        copy.start()
    for copy in copies:
        copy.wait()


def stage(gate_up, down):
    return pl.pallas_call(
        stage_kernel,
        out_shape=(
            jax.ShapeDtypeStruct(gate_up.shape[1:], BF16),
            jax.ShapeDtypeStruct(down.shape[1:], BF16),
        ),
        in_specs=[HBM, HBM],
        out_specs=(VMEM, VMEM),
        scratch_shapes=[pltpu.SemaphoreType.DMA((12,))],
        compiler_params=pltpu.CompilerParams(vmem_limit_bytes=16 * MIB),
        cost_estimate=pl.CostEstimate(flops=0, bytes_accessed=22_000_000, transcendentals=0),
        name="stage",
    )(*in_hbm(gate_up, down))


def mix_kernel(steps, chips, own_ref, other_ref, mix_ref):
    mix_ref[...] = mixing(steps, chips, own_ref, other_ref)


def mixer(steps, chips, own, other):
    lines = PIECES * 2 * steps * CAP
    shape = (PARTS * PIECES * 2 * own.shape[0], chips // 2 * lines)
    return pl.pallas_call(
        functools.partial(mix_kernel, steps, chips),
        out_shape=jax.ShapeDtypeStruct(shape, BF16),
        in_specs=[VMEM, VMEM],
        out_specs=VMEM,
        compiler_params=pltpu.CompilerParams(vmem_limit_bytes=24 * MIB),
        cost_estimate=pl.CostEstimate(
            flops=10_000_000, bytes_accessed=1_000_000, transcendentals=0
        ),
        name="mixer",
    )(own, other)


def expert_kernel(turns, *refs):
    own_refs, other_refs = refs[:turns], refs[turns : 2 * turns]
    w_in, w_down = refs[2 * turns : 2 * turns + 2]
    mine_refs = refs[2 * turns + 2 : 3 * turns + 2]
    theirs_refs = refs[3 * turns + 2 :]
    lines, piece = own_refs[0].shape
    per = lines // PIECES
    half = turns * per
    arrays = [ref[...].astype(F32) for ref in own_refs + other_refs]
    gate = upper = None
    for k in range(PIECES):
        x = [array[k * per : (k + 1) * per] for array in arrays]
        x = jnp.concatenate(x, axis=0).astype(BF16)
        cols = pl.ds(k * piece, piece)
        g, u = nt_dot(w_in[0, :, cols], x), nt_dot(w_in[1, :, cols], x)
        gate, upper = (g, u) if k == 0 else (gate + g, upper + u)
    act = (gate / (1.0 + jnp.exp(-gate)) * upper).T.astype(BF16)
    parts = [dot(act, w_down[:, k * piece : (k + 1) * piece]) for k in range(PIECES)]
    for first, now in ((half, theirs_refs), (0, mine_refs)):
        for t, ref in enumerate(now):
            start = first + t * per
            out = [part[start : start + per] for part in parts]
            ref[...] = jnp.concatenate(out, axis=0).astype(BF16)


def experts(own, other, gate_up, down):
    turns = len(own)
    shape = jax.ShapeDtypeStruct(own[0].shape, BF16)
    results = pl.pallas_call(
        functools.partial(expert_kernel, turns),
        out_shape=[shape] * (2 * turns),
        in_specs=[VMEM] * (2 * turns + 2),
        out_specs=[VMEM] * (2 * turns),
        compiler_params=pltpu.CompilerParams(vmem_limit_bytes=32 * MIB),
        cost_estimate=pl.CostEstimate(
            flops=800_000_000, bytes_accessed=12_000_000, transcendentals=16384
        ),
        name="experts",
    )(*own, *other, gate_up, down)
    return results[:turns], results[turns:]


def combine_kernel(mix_ref, resid_ref, *refs):
    back_refs, (kept_ref, sent_ref) = refs[:-2], refs[-2:]
    steps, rows, _ = kept_ref.shape
    both = steps * rows
    piece = back_refs[0].shape[1]
    product = dot(mix_ref[...], jnp.concatenate([ref[...] for ref in back_refs], axis=0))
    n = PIECES * 2 * both
    total = product[:n] + product[n : 2 * n] + product[2 * n :]
    for k in range(PIECES):
        cols = pl.ds(k * piece, piece)
        first = k * 2 * both
        kept = resid_ref[:, cols] + total[first : first + both]
        sent = total[first + both : first + 2 * both].astype(BF16)
        for s in range(steps):
            kept_ref[s, :, cols] = kept[s * rows : (s + 1) * rows]
            sent_ref[s, :, cols] = sent[s * rows : (s + 1) * rows]


def combine(shape, mix, resid, backs):
    return pl.pallas_call(
        combine_kernel,
        out_shape=(
            jax.ShapeDtypeStruct(shape, F32),
            jax.ShapeDtypeStruct(shape, BF16),
        ),
        in_specs=[VMEM] * (2 + len(backs)),
        out_specs=(VMEM, VMEM),
        compiler_params=pltpu.CompilerParams(vmem_limit_bytes=24 * MIB),
        cost_estimate=pl.CostEstimate(
            flops=100_000_000, bytes_accessed=1_000_000, transcendentals=0
        ),
        name="combine",
    )(mix, resid, *backs)


def per_device(
    queries,
    fresh,
    kv_cache,
    cache_len,
    hidden_state,
    norm_gain,
    expert_ids,
    route_weight,
    gate_up,
    down,
):
    steps = queries.shape[0]
    owners = lax.axis_size("afd")
    chips = owners // 2
    turns = chips // 2
    cores = [(i, i ^ 1) for i in range(owners)]

    def swap(x):
        return lax.ppermute(x, "afd", cores)

    def route(t):
        return [(i, (i // 2 ^ distance(t, i % 2, chips)) * 2 + 1 - i % 2) for i in range(owners)]

    def send(x, t):
        return lax.ppermute(x, "afd", route(t))

    def send_back(x, t):
        return lax.ppermute(x, "afd", [(j, i) for i, j in route(t)])

    ids = expert_ids.transpose(2, 0, 1)
    weights = route_weight.transpose(2, 0, 1)
    resid, normed = attend(
        cache_len, ids, weights, queries, fresh, kv_cache, hidden_state, norm_gain
    )
    normed_other = swap(normed)
    sent = pack(steps, chips, normed, normed_other)
    own = [send(sent[t], t) for t in range(turns)]
    w_in, w_down = stage(gate_up, down)
    mix = mixer(steps, chips, normed, normed_other)
    own[0], w_in = lax.optimization_barrier((own[0], w_in))
    other = [swap(x) for x in own]
    summed = []
    for t in range(0, turns, TOGETHER):
        now = slice(t, t + TOGETHER)
        mine, theirs = experts(own[now], other[now], w_in, w_down)
        summed += [
            (a.astype(F32) + swap(b).astype(F32)).astype(BF16) for a, b in zip(mine, theirs)
        ]
    backs = [send_back(summed[t], t) for t in range(turns)]
    kept, given = combine(queries.shape, mix, resid, backs)
    return (kept + swap(given).astype(F32)).astype(BF16)


def solution(mesh):
    placed = (
        P(None, ("group", "afd"), None),
        P(None, ("group", "afd"), None),
        P(("group", "afd"), None, None),
        P(("group", "afd")),
        P(None, ("group", "afd"), None),
        P(),
        P(None, ("group", "afd"), None),
        P(None, ("group", "afd"), None),
        P("afd", None, None, None),
        P("afd", None, None),
    )
    return jax.shard_map(
        per_device,
        mesh=mesh,
        in_specs=placed,
        out_specs=P(None, ("group", "afd"), None),
        check_vma=False,
    )
```

```python
import functools
import jax
import jax.numpy as jnp
from jax import lax
from jax.experimental import pallas as pl
from jax.experimental.pallas import tpu as pltpu
from jax.sharding import PartitionSpec as P

HEADS = 32
HEAD = 224
EXPERTS = 8
TOP = 3
CAP = 2
PIECES = 4
LANES = 128
PARTS = 3
F32 = jnp.float32
BF16 = jnp.bfloat16
MIB = 1 << 20
VMEM = pl.BlockSpec(memory_space=pltpu.VMEM)
HBM = pl.BlockSpec(memory_space=pltpu.HBM)
TOGETHER = 4


def iota(shape, dim):
    return lax.broadcasted_iota(jnp.int32, shape, dim)


def in_hbm(*arrays):
    return [pltpu.with_memory_space_constraint(x, pltpu.HBM) for x in arrays]


def nt_dot(a, b):
    return lax.dot_general(a, b, (((1,), (1,)), ((), ())), preferred_element_type=F32)


def dot(a, b):
    return jnp.dot(a, b, preferred_element_type=F32)


def one_hot(mask):
    return jnp.where(mask, 1.0, 0.0).astype(BF16)


def distance(turn, core, chips):
    bits = (chips // 2).bit_length() - 1
    even = 0
    for b in range(bits):
        even = even + ((turn >> b) % 2 << (bits - b))
    return even ^ (core * (chips - 1))


def expert_at(turn, chips):
    place = lax.axis_index("afd")
    return (distance(turn, place % 2, chips) ^ (place // 2)) // (chips // EXPERTS)


def spread(ref, k, where, steps, rows, empty):
    out = jnp.full(where.shape, empty)
    for s in range(steps):
        for r in range(rows):
            out = jnp.where(where == s * rows + r, ref[k, s, r], out)
    return out


def tail(ids_ref, weight_ref, steps, rows):
    both = steps * rows
    lane = iota((both, LANES), 1)
    where = iota((both, 1), 0)
    mix = jnp.zeros((both, LANES), F32)
    named = jnp.zeros((both, LANES), F32)
    for k in range(TOP):
        hit = spread(ids_ref, k, where, steps, rows, -1) == lane % EXPERTS
        mix = mix + jnp.where(hit, spread(weight_ref, k, where, steps, rows, 0.0), 0.0)
        named = named + jnp.where(hit, 1.0, 0.0)
    out = jnp.where(lane // EXPERTS == PARTS, named, 0.0)
    for part in range(PARTS):
        term = mix.astype(BF16).astype(F32)
        out = jnp.where(lane // EXPERTS == part, term, out)
        mix = mix - term
    return out.astype(BF16)


def attend_kernel(
    len_hbm,
    ids_hbm,
    weight_hbm,
    q_hbm,
    fresh_hbm,
    kv_hbm,
    hid_hbm,
    gain_hbm,
    resid_ref,
    out_ref,
    len_ref,
    ids_ref,
    weight_ref,
    q_ref,
    fresh_ref,
    kv_ref,
    hid_ref,
    gain_ref,
    merged,
    sems,
):
    pairs = (
        (q_hbm, q_ref),
        (kv_hbm, kv_ref),
        (fresh_hbm, fresh_ref),
        (len_hbm, len_ref),
        (hid_hbm, hid_ref),
        (gain_hbm, gain_ref),
        (ids_hbm, ids_ref),
        (weight_hbm, weight_ref),
    )
    copies = [pltpu.make_async_copy(a, b, sems.at[i]) for i, (a, b) in enumerate(pairs)]
    for copy in copies:
        copy.start()
    steps, rows, width = q_ref.shape
    length = kv_ref.shape[2]
    both = steps * rows
    scale = HEAD ** (-0.5)
    copies[0].wait()
    q = jnp.concatenate([q_ref[s].astype(F32) for s in range(steps)], axis=0)
    heads = jnp.concatenate([q[:, h * HEAD : (h + 1) * HEAD] for h in range(HEADS)], axis=0)
    heads = heads.astype(BF16)
    for copy in copies[1:4]:
        copy.wait()
    kv = jnp.concatenate([kv_ref[r] for r in range(rows)], axis=1)
    new = jnp.concatenate([fresh_ref[s].astype(F32) for s in range(steps)], axis=0).astype(BF16)

    sub = iota((both, rows * length), 0)
    lane = iota((both, rows * length), 1)
    limit = jnp.zeros_like(lane)
    for r in range(rows):
        limit = jnp.where(lane // length == r, len_ref[r], limit)
    valid = (lane // length == sub % rows) & (lane % length < limit)
    sub = iota((both, both), 0)
    lane = iota((both, both), 1)
    valid_new = (lane % rows == sub % rows) & (lane // rows <= sub // rows)

    old_s = (dot(heads, kv[:HEAD]) * scale).reshape(HEADS, both, rows * length)
    new_s = (nt_dot(heads, new[:, :HEAD]) * scale).reshape(HEADS, both, both)
    old_s = jnp.where(valid[None], old_s, -1e30)
    new_s = jnp.where(valid_new[None], new_s, -1e30)
    top = jnp.maximum(
        jnp.max(old_s, axis=-1, keepdims=True), jnp.max(new_s, axis=-1, keepdims=True)
    )
    old_e = jnp.exp(old_s - top)
    new_e = jnp.exp(new_s - top)
    total = jnp.sum(old_e, axis=-1, keepdims=True) + jnp.sum(new_e, axis=-1, keepdims=True)
    share = 1.0 / total
    old_w = (old_e * share).reshape(HEADS * both, rows * length).astype(BF16)
    new_w = (new_e * share).reshape(HEADS * both, both).astype(BF16)
    attended = nt_dot(old_w, kv[HEAD:]) + dot(new_w, new[:, HEAD:])
    for h in range(HEADS):
        merged[:, h * HEAD : (h + 1) * HEAD] = attended[h * both : (h + 1) * both]
    for copy in copies[4:8]:
        copy.wait()
    hidden = jnp.concatenate([hid_ref[s].astype(F32) for s in range(steps)], axis=0)
    resid = hidden + merged[...]
    resid_ref[...] = resid
    meansq = jnp.mean(resid * resid, axis=-1, keepdims=True)
    gain = gain_ref[...].astype(F32)
    gain = jnp.concatenate([gain[i : i + 1] for i in range(width // LANES)], axis=1)
    normed = resid * lax.rsqrt(meansq + 1e-06) * gain
    out_ref[:, :width] = normed.astype(BF16)
    out_ref[:, width:] = tail(ids_ref, weight_ref, steps, rows)


def attend(cache_len, ids, weights, queries, fresh, kv_cache, hidden_state, norm_gain):
    steps, rows, width = queries.shape
    kv = kv_cache.transpose(0, 2, 1)
    gain = norm_gain.reshape(width // LANES, LANES)
    return pl.pallas_call(
        attend_kernel,
        out_shape=(
            jax.ShapeDtypeStruct((steps * rows, width), F32),
            jax.ShapeDtypeStruct((steps * rows, width + LANES), BF16),
        ),
        in_specs=[HBM] * 8,
        out_specs=(VMEM, VMEM),
        scratch_shapes=[
            pltpu.SMEM(cache_len.shape, jnp.int32),
            pltpu.SMEM(ids.shape, jnp.int32),
            pltpu.SMEM(weights.shape, F32),
            pltpu.VMEM(queries.shape, BF16),
            pltpu.VMEM(fresh.shape, BF16),
            pltpu.VMEM(kv.shape, BF16),
            pltpu.VMEM(hidden_state.shape, BF16),
            pltpu.VMEM(gain.shape, BF16),
            pltpu.VMEM((steps * rows, width), F32),
            pltpu.SemaphoreType.DMA((8,)),
        ],
        compiler_params=pltpu.CompilerParams(vmem_limit_bytes=24 * MIB),
        cost_estimate=pl.CostEstimate(
            flops=300_000_000, bytes_accessed=2_000_000, transcendentals=131072
        ),
        name="attend",
    )(*in_hbm(cache_len, ids, weights, queries, fresh, kv, hidden_state, gain))


def pack_kernel(steps, chips, own_ref, other_ref, *outs):
    both, width = own_ref.shape
    width -= LANES
    rows = both // steps
    piece = width // PIECES
    side_lines = steps * CAP
    lines = PIECES * 2 * side_lines
    tails = [ref[:, width:].astype(F32) for ref in (own_ref, other_ref)]
    tails = jnp.concatenate(tails * PIECES, axis=0).astype(BF16)
    count = 2 * both * PIECES
    row = iota((len(outs) * lines, LANES), 0)
    lane = iota((len(outs) * lines, LANES), 1)
    wanted = one_hot(lane == PARTS * EXPERTS + expert_at(row // lines, chips))
    named = nt_dot(wanted, tails)
    at = iota((count, count), 0)
    to = iota((count, count), 1)
    before = one_hot((at // rows == to // rows) & (at < to))
    rank = dot(named.astype(BF16), before)
    line = iota(named.shape, 0)
    col = iota(named.shape, 1)
    same = (line // CAP) % (lines // CAP) == col // rows
    picks = one_hot(same & (named > 0.5) & (rank == (line % CAP).astype(F32)))
    parts = [ref[:, :width].astype(F32) for ref in (own_ref, other_ref)]
    stacked = jnp.concatenate(
        [part[:, k * piece : (k + 1) * piece] for k in range(PIECES) for part in parts], axis=0
    ).astype(BF16)
    sent = dot(picks, stacked).astype(BF16)
    for t, out in enumerate(outs):
        out[...] = sent[t * lines : (t + 1) * lines]


def pack(steps, chips, own, other):
    both, width = own.shape
    shape = (PIECES * 2 * steps * CAP, (width - LANES) // PIECES)
    turns = chips // 2
    return pl.pallas_call(
        functools.partial(pack_kernel, steps, chips),
        out_shape=[jax.ShapeDtypeStruct(shape, BF16)] * turns,
        in_specs=[VMEM] * 2,
        out_specs=[VMEM] * turns,
        compiler_params=pltpu.CompilerParams(vmem_limit_bytes=24 * MIB),
        cost_estimate=pl.CostEstimate(
            flops=50_000_000, bytes_accessed=2_000_000, transcendentals=0
        ),
        name="pack",
    )(own, other)


def mixing(steps, chips, own_ref, other_ref):
    both, width = own_ref.shape
    width -= LANES
    rows = both // steps
    lines = PIECES * 2 * steps * CAP
    tails = [ref[:, width:].astype(F32) for ref in (own_ref, other_ref)]
    tails = jnp.concatenate(tails, axis=0).astype(BF16)
    count = chips // 2 * lines
    lane = iota((LANES, count), 0)
    expert = expert_at(iota((LANES, count), 1) // lines, chips)
    found = [dot(tails, one_hot(lane == part * EXPERTS + expert)) for part in range(PARTS + 1)]
    at = iota((2 * both, 2 * both), 1)
    to = iota((2 * both, 2 * both), 0)
    rank = dot(one_hot((at // rows == to // rows) & (at < to)), found[PARTS].astype(BF16))
    line = iota((2 * both, count), 1)
    row = iota((2 * both, count), 0)
    same = (line // CAP) % (2 * steps) == row // rows
    slot = same & (rank == (line % CAP).astype(F32))
    k_of = line // (2 * steps * CAP) % PIECES
    parts = [
        jnp.where(slot & (k_of == k), found[part], 0.0)
        for part in range(PARTS)
        for k in range(PIECES)
    ]
    return jnp.concatenate(parts, axis=0).astype(BF16)


def stage_kernel(gu_hbm, dn_hbm, gu, dn, sems):
    step = dn.shape[0] // 4
    pairs = []
    for i in range(4):
        part = pl.ds(i * step, step)
        pairs.append((gu_hbm.at[0, 0, part], gu.at[0, part]))
        pairs.append((gu_hbm.at[0, 1, part], gu.at[1, part]))
        pairs.append((dn_hbm.at[0, part], dn.at[part]))
    copies = [pltpu.make_async_copy(a, b, sems.at[i]) for i, (a, b) in enumerate(pairs)]
    for copy in copies:
        copy.start()
    for copy in copies:
        copy.wait()


def stage(gate_up, down):
    return pl.pallas_call(
        stage_kernel,
        out_shape=(
            jax.ShapeDtypeStruct(gate_up.shape[1:], BF16),
            jax.ShapeDtypeStruct(down.shape[1:], BF16),
        ),
        in_specs=[HBM, HBM],
        out_specs=(VMEM, VMEM),
        scratch_shapes=[pltpu.SemaphoreType.DMA((12,))],
        compiler_params=pltpu.CompilerParams(vmem_limit_bytes=16 * MIB),
        cost_estimate=pl.CostEstimate(flops=0, bytes_accessed=22_000_000, transcendentals=0),
        name="stage",
    )(*in_hbm(gate_up, down))


def mix_kernel(steps, chips, own_ref, other_ref, mix_ref):
    mix_ref[...] = mixing(steps, chips, own_ref, other_ref)


def mixer(steps, chips, own, other):
    lines = PIECES * 2 * steps * CAP
    shape = (PARTS * PIECES * 2 * own.shape[0], chips // 2 * lines)
    return pl.pallas_call(
        functools.partial(mix_kernel, steps, chips),
        out_shape=jax.ShapeDtypeStruct(shape, BF16),
        in_specs=[VMEM, VMEM],
        out_specs=VMEM,
        compiler_params=pltpu.CompilerParams(vmem_limit_bytes=24 * MIB),
        cost_estimate=pl.CostEstimate(
            flops=10_000_000, bytes_accessed=1_000_000, transcendentals=0
        ),
        name="mixer",
    )(own, other)


def expert_kernel(turns, *refs):
    own_refs, other_refs = refs[:turns], refs[turns : 2 * turns]
    w_in, w_down = refs[2 * turns : 2 * turns + 2]
    mine_refs = refs[2 * turns + 2 : 3 * turns + 2]
    theirs_refs = refs[3 * turns + 2 :]
    lines, piece = own_refs[0].shape
    per = lines // PIECES
    half = turns * per
    arrays = [ref[...].astype(F32) for ref in own_refs + other_refs]
    gate = upper = None
    for k in range(PIECES):
        x = [array[k * per : (k + 1) * per] for array in arrays]
        x = jnp.concatenate(x, axis=0).astype(BF16)
        for part in range(2):
            cut = x[:, part * piece // 2 : (part + 1) * piece // 2]
            cols = pl.ds(k * piece + part * piece // 2, piece // 2)
            g, u = nt_dot(w_in[0, :, cols], cut), nt_dot(w_in[1, :, cols], cut)
            gate, upper = (g, u) if gate is None else (gate + g, upper + u)
    act = (gate / (1.0 + jnp.exp(-gate)) * upper).T.astype(BF16)
    parts = [dot(act, w_down[:, k * piece : (k + 1) * piece]) for k in range(PIECES)]
    for first, now in ((half, theirs_refs), (0, mine_refs)):
        for t, ref in enumerate(now):
            start = first + t * per
            out = [part[start : start + per] for part in parts]
            ref[...] = jnp.concatenate(out, axis=0).astype(BF16)


def experts(own, other, gate_up, down):
    turns = len(own)
    shape = jax.ShapeDtypeStruct(own[0].shape, BF16)
    results = pl.pallas_call(
        functools.partial(expert_kernel, turns),
        out_shape=[shape] * (2 * turns),
        in_specs=[VMEM] * (2 * turns + 2),
        out_specs=[VMEM] * (2 * turns),
        compiler_params=pltpu.CompilerParams(vmem_limit_bytes=32 * MIB),
        cost_estimate=pl.CostEstimate(
            flops=800_000_000, bytes_accessed=12_000_000, transcendentals=16384
        ),
        name="experts",
    )(*own, *other, gate_up, down)
    return results[:turns], results[turns:]


def combine_kernel(mix_ref, resid_ref, *refs):
    back_refs, (kept_ref, sent_ref) = refs[:-2], refs[-2:]
    both = resid_ref.shape[0]
    piece = back_refs[0].shape[1]
    product = dot(mix_ref[...], jnp.concatenate([ref[...] for ref in back_refs], axis=0))
    n = PIECES * 2 * both
    total = product[:n] + product[n : 2 * n] + product[2 * n :]
    for k in range(PIECES):
        cols = pl.ds(k * piece, piece)
        first = k * 2 * both
        kept_ref[:, cols] = resid_ref[:, cols] + total[first : first + both]
        sent_ref[:, cols] = total[first + both : first + 2 * both].astype(BF16)


def combine(mix, resid, backs):
    return pl.pallas_call(
        combine_kernel,
        out_shape=(
            jax.ShapeDtypeStruct(resid.shape, F32),
            jax.ShapeDtypeStruct(resid.shape, BF16),
        ),
        in_specs=[VMEM] * (2 + len(backs)),
        out_specs=(VMEM, VMEM),
        compiler_params=pltpu.CompilerParams(vmem_limit_bytes=24 * MIB),
        cost_estimate=pl.CostEstimate(
            flops=100_000_000, bytes_accessed=1_000_000, transcendentals=0
        ),
        name="combine",
    )(mix, resid, *backs)


def finish_kernel(kept_ref, other_ref, out_ref):
    steps, rows, _ = out_ref.shape
    done = (kept_ref[...] + other_ref[...].astype(F32)).astype(BF16)
    for s in range(steps):
        out_ref[s] = done[s * rows : (s + 1) * rows]


def finish(shape, kept, other):
    return pl.pallas_call(
        finish_kernel,
        out_shape=jax.ShapeDtypeStruct(shape, BF16),
        in_specs=[VMEM, VMEM],
        out_specs=VMEM,
        compiler_params=pltpu.CompilerParams(vmem_limit_bytes=24 * MIB),
        cost_estimate=pl.CostEstimate(flops=100_000, bytes_accessed=500_000, transcendentals=0),
        name="finish",
    )(kept, other)


def per_device(
    queries,
    fresh,
    kv_cache,
    cache_len,
    hidden_state,
    norm_gain,
    expert_ids,
    route_weight,
    gate_up,
    down,
):
    steps = queries.shape[0]
    owners = lax.axis_size("afd")
    chips = owners // 2
    turns = chips // 2
    cores = [(i, i ^ 1) for i in range(owners)]

    def swap(x):
        return lax.ppermute(x, "afd", cores)

    def route(t):
        return [(i, (i // 2 ^ distance(t, i % 2, chips)) * 2 + 1 - i % 2) for i in range(owners)]

    def send(x, t):
        return lax.ppermute(x, "afd", route(t))

    def send_back(x, t):
        return lax.ppermute(x, "afd", [(j, i) for i, j in route(t)])

    ids = expert_ids.transpose(2, 0, 1)
    weights = route_weight.transpose(2, 0, 1)
    resid, normed = attend(
        cache_len, ids, weights, queries, fresh, kv_cache, hidden_state, norm_gain
    )
    normed_other = swap(normed)
    sent = pack(steps, chips, normed, normed_other)
    own = [send(sent[t], t) for t in range(turns)]
    w_in, w_down = stage(gate_up, down)
    mix = mixer(steps, chips, normed, normed_other)
    own[0], w_in = lax.optimization_barrier((own[0], w_in))
    other = [swap(x) for x in own]
    summed = []
    for t in range(0, turns, TOGETHER):
        now = slice(t, t + TOGETHER)
        mine, theirs = experts(own[now], other[now], w_in, w_down)
        summed += [
            (a.astype(F32) + swap(b).astype(F32)).astype(BF16) for a, b in zip(mine, theirs)
        ]
    backs = [send_back(summed[t], t) for t in range(turns)]
    kept, given = combine(mix, resid, backs)
    return finish(queries.shape, kept, swap(given))


def solution(mesh):
    placed = (
        P(None, ("group", "afd"), None),
        P(None, ("group", "afd"), None),
        P(("group", "afd"), None, None),
        P(("group", "afd")),
        P(None, ("group", "afd"), None),
        P(),
        P(None, ("group", "afd"), None),
        P(None, ("group", "afd"), None),
        P("afd", None, None, None),
        P("afd", None, None),
    )
    return jax.shard_map(
        per_device,
        mesh=mesh,
        in_specs=placed,
        out_specs=P(None, ("group", "afd"), None),
        check_vma=False,
    )
```
